32 devices in a mesh: dp: 32 (over z, y, x, core).
Axes of the slice: x: 2, y: 2, z: 4, core: 2. Of those that a mesh axis runs over, the one named last changes fastest.
Arguments:
- token_ids: int32 [256, 512], P('dp'), may hold values from 0 to 30521
- lengths: int32 [256], P('dp'), may hold values from 85 to 512, as said below
- gate_noise: float32 [1284], replicated, may hold values from 0.02 to 0.98
- lagrange: float32 [2], replicated, may hold values from 1 to 3
- teacher_table: bfloat16 [31034, 256], replicated, may hold values from -0.29882812 to 0.29882812
- teacher_flat: bfloat16 [790016], replicated, may hold values from -5 to 7
- word_table: float32 [31232, 256], P('dp'), may hold values from -0.3 to 0.3
- table_first: float32 [31232, 256], P('dp'), may hold values from -3.5762787e-07 to 3.5762787e-07
- table_second: float32 [31232, 256], P('dp'), may hold values from 2.917711e-16 to 1.1670845e-15
- layer_flat: float32 [860160], P('dp'), may hold values from -5 to 7
- flat_first: float32 [860160], P('dp'), may hold values from -1.4305115e-06 to 1.4305115e-06
- flat_second: float32 [860160], P('dp'), may hold values from 4.668338e-15 to 1.8673351e-14
Outputs:
- table_out: float32 [31232, 256], P('dp')
- table_first_out: float32 [31232, 256], P('dp')
- table_second_out: float32 [31232, 256], P('dp')
- flat_out: float32 [860160], P('dp')
- flat_first_out: float32 [860160], P('dp')
- flat_second_out: float32 [860160], P('dp')
- total_loss: float32 [], replicated
- grad_norm: float32 [], replicated
The draws below stay inside these ranges and needn't reach their ends.
Inputs may be any that keep to these rules, and one draw needn't show every extreme that they name: `lengths`: the first of each device's 8 sequences is its longest; the longest on device d (from 0) is 170 + 342 * d // (devices - 1), the others are at least half of it.
All inputs are finite; a program needn't handle non-finite values.
Results may differ from the reference program's by a relative error of at most 0.0061.
Values may be sent and summed in bfloat16 or wider, within the bound.
A program may use at most 256 MiB of HBM per device.

```python
import math
import jax
import jax.numpy as jnp
from jax import lax

D = 256
HEADS = 4
FF = 1024
VOCAB = 30522
LEN = 512
SEQ_DEV = 8
ADAM_STEP = 10
SEQS = 256
NPAR = 856836
TPAR = 790016
NFLAT = 860160
VROWS = 31232


def layer_entries(student):
    square = D * D
    root_width = 1.0 / math.sqrt(D)
    entries = [(square, 2.5 * root_width, 0.0), (square, 2.5 * root_width, 0.0), (square, root_width, 0.0), (square, 4.0 * root_width, 0.0)]
    if student:
        entries = entries + [(square, root_width, 0.0)]
    entries = entries + [(D * FF, root_width, 0.0), (FF * D, 1.0 / math.sqrt(FF), 0.0)]
    for row_number in range(10):
        entries = entries + [(D, 0.2, 1.0 if row_number in (0, 2, 4) else 0.0)]
    entries = entries + [(FF, 0.2, 0.0)]
    if student:
        entries = entries + [(D + HEADS + FF, 1.5, 1.0)]
    return entries


def layer_draw(key, total_len, student):
    positions = jnp.arange(total_len)
    spreads = jnp.full((total_len,), 0.05, jnp.float32)
    centres = jnp.zeros((total_len,), jnp.float32)
    offset = 0
    for length, spread, centre in layer_entries(student):
        inside = (positions >= offset) & (positions < offset + length)
        spreads = jnp.where(inside, spread, spreads)
        centres = jnp.where(inside, centre, centres)
        offset = offset + length
    unit_draw = jnp.clip(jax.random.normal(key, (total_len,), jnp.float32), -4.0, 4.0)
    return centres + spreads * unit_draw


def draw_layer_flat(key, part):
    return layer_draw(key, NFLAT, True)


def draw_teacher_flat(key, part):
    return layer_draw(key, TPAR, False).astype(jnp.bfloat16)


def draw_lengths(key, part):
    row_index = jnp.arange(SEQS)
    device_index = row_index // SEQ_DEV
    groups = SEQS // SEQ_DEV
    longest = LEN // 3 + (LEN - LEN // 3) * device_index // max(groups - 1, 1)
    shortest = (longest + 1) // 2
    random_draw = jax.random.randint(key, (SEQS,), 0, LEN)
    drawn_lengths = shortest + random_draw % (longest - shortest + 1)
    return jnp.where(row_index % SEQ_DEV == 0, longest, drawn_lengths).astype(jnp.int32)


def set_ends(values, stream_key, low, top_value):
    place = [jax.random.randint(jax.random.fold_in(stream_key, axis), (), 0, length) for axis, length in enumerate(values.shape)]
    widest = values.shape.index(max(values.shape))
    next_to = place[:widest] + [(place[widest] + 1) % values.shape[widest]] + place[widest + 1:]
    return values.at[tuple(place)].set(low).at[tuple(next_to)].set(top_value)


def steps_of(stream_key, extent, cuts, least, top_value):
    loudness = 1.0
    for dim, parts in cuts:
        draws = jax.random.uniform(jax.random.fold_in(jax.random.fold_in(stream_key, 6), dim), (parts,), jnp.float32, least / len(cuts), top_value / len(cuts))
        loudness = loudness * jnp.repeat(jnp.exp(draws), extent[dim] // parts).reshape((-1,) + (1,) * (len(extent) - 1 - dim))
    return loudness


def gaussian(own_key, dims, scale, bound, split=(), held_as=jnp.bfloat16):
    values = scale * jax.random.normal(own_key, dims, jnp.float32)
    if split:
        values = values * steps_of(own_key, dims, split, -0.22, 0.18)
    return jnp.clip(values, -bound, bound).astype(held_as)


def setup_inputs(seed: int = 0) -> dict:
    splits = jax.random.split(jax.random.key(seed), 13)
    return {
        "token_ids": set_ends(jax.random.randint(splits[0], (SEQS, LEN), 0, VOCAB), jax.random.fold_in(splits[0], 1), 0, VOCAB - 1).astype(jnp.int32),
        "lengths": draw_lengths(jax.random.fold_in(splits[12], 71), 0),
        "gate_noise": jnp.clip(jax.random.uniform(splits[2], (D + HEADS + FF,), jnp.float32, 0.02, 0.98), 0.02, 0.98),
        "lagrange": jnp.clip(jax.random.uniform(splits[3], (2,), jnp.float32, 1.0, 3.0), 1.0, 3.0),
        "teacher_table": gaussian(splits[4], (VOCAB + LEN, D), 0.05, 0.29882812),
        "teacher_flat": draw_teacher_flat(jax.random.fold_in(splits[12], 71), 0),
        "word_table": gaussian(splits[6], (VROWS, D), 0.05, 0.3, ((0, 32),), jnp.float32),
        "table_first": gaussian(splits[7], (VROWS, D), (0.11 * 0.0005 / NPAR ** 0.5), 3.5762786865234375e-07, ((0, 32),), jnp.float32),
        "table_second": jnp.clip(jnp.exp(math.log(1.1670844522534561e-15) - 1.3862944 * jax.random.uniform(splits[8], (VROWS, D), jnp.float32) ** steps_of(splits[8], (VROWS, D), ((0, 32),), -0.2, 0.2)), 2.9177111306336403e-16, 1.1670844522534561e-15),
        "layer_flat": draw_layer_flat(jax.random.fold_in(splits[12], 71), 0),
        "flat_first": gaussian(splits[10], (NFLAT,), (0.11 * 0.002 / NPAR ** 0.5), 1.430511474609375e-06, ((0, 32),), jnp.float32),
        "flat_second": jnp.clip(jnp.exp(math.log(1.8673351236055298e-14) - 1.3862944 * jax.random.uniform(splits[11], (NFLAT,), jnp.float32) ** steps_of(splits[11], (NFLAT,), ((0, 32),), -0.2, 0.2)), 4.6683378090138245e-15, 1.8673351236055298e-14),
    }


clip_norm = 0.002
learn_rate = 0.015
beta_one = 0.9
beta_two = 0.999
adam_eps = 1e-08
decay_rate = 0.01
sparse_target = 0.3
relaxation_heat = 2.0 / 3.0
widened_left_limit = -0.1
widened_right_limit = 1.1
norm_eps = 1e-12

@jax.custom_vjp
def low(v):
    return lax.optimization_barrier(v.astype(jnp.bfloat16)).astype(jnp.float32)

@jax.custom_vjp
def low_back(v):
    return v

def low_keep(v):
    return (low(v), None)

def low_pass(kept, grad):
    return (grad,)

def back_keep(v):
    return (v, None)

def back_low(kept, grad):
    return (low(grad),)
low.defvjp(low_keep, low_pass)
low_back.defvjp(back_keep, back_low)

def round_both(values):
    return low_back(low(values))

def matmul_high(left, right):
    return jnp.matmul(left, right, precision=lax.Precision.HIGHEST)

def layout(student):
    square = (D, D)
    entries = [('w_query', square), ('w_key', square), ('w_value', square), ('w_output', square)]
    if student:
        entries = entries + [('w_align', square)]
    entries = entries + [('w_up', (D, FF)), ('w_down', (FF, D)), ('vectors', (10, D)), ('b_up', (FF,))]
    if student:
        entries = entries + [('gate_logits', (D + HEADS + FF,))]
    return entries

def unpack(flat_vector, student):
    pieces = {}
    offset = 0
    for entry_name, entry_shape in layout(student):
        length = math.prod(entry_shape)
        pieces[entry_name] = flat_vector[offset:offset + length].reshape(entry_shape)
        offset = offset + length
    return pieces

def layer_norm(inputs, gain_row, bias_row):
    row_mean = lax.optimization_barrier(jnp.mean(inputs, axis=-1, keepdims=True))
    centred = inputs - row_mean
    variance = lax.optimization_barrier(jnp.mean(centred * centred, axis=-1, keepdims=True))
    return centred * lax.rsqrt(variance + norm_eps) * gain_row + bias_row

def gate_values(mask_logodds, flat_random_sample):
    logistic_function = jax.nn.sigmoid((jnp.log(flat_random_sample) - jnp.log(1.0 - flat_random_sample) + mask_logodds) / relaxation_heat)
    return jnp.clip(logistic_function * (widened_right_limit - widened_left_limit) + widened_left_limit, 0.0, 1.0)

def lagrangian(mask_logodds, lagrange):
    survival_probability = jax.nn.sigmoid(mask_logodds - relaxation_heat * math.log(-widened_left_limit / widened_right_limit))
    head_dim = D // HEADS
    kept_hidden = jnp.mean(survival_probability[:D])
    kept_rest = 4.0 * head_dim * jnp.sum(survival_probability[D:D + HEADS]) + 2.0 * jnp.sum(survival_probability[D + HEADS:])
    expected = kept_hidden * kept_rest / (4.0 * D + 2.0 * FF)
    excess = expected - sparse_target
    return lagrange[0] * excess + lagrange[1] * excess * excess

def run_layer(table_rows, weights, token_ids, key_valid, gate_set):
    gate_hidden, gate_heads, gate_inner = gate_set
    seq_count, seq_span = token_ids.shape
    vectors = weights['vectors']
    embedded = jnp.take(table_rows, token_ids, axis=0) + table_rows[VOCAB:VOCAB + seq_span][None]
    start_f = layer_norm(embedded, vectors[0], vectors[1]) * gate_hidden
    start_low = low(start_f)
    head_split = (seq_count, seq_span, HEADS, D // HEADS)
    queries = round_both(matmul_high(start_low, weights['w_query']) + vectors[6]).reshape(head_split)
    keys_all = round_both(matmul_high(start_low, weights['w_key'])).reshape(head_split)
    values = round_both(matmul_high(start_low, weights['w_value']) + vectors[7]).reshape(head_split)
    factor = (D // HEADS) ** (-0.5)
    scores = low_back(jnp.einsum('sqhd,skhd->shqk', queries, keys_all, precision=lax.Precision.HIGHEST) * factor)
    scores = jnp.where(key_valid[:, None, None, :] > 0, scores, -1e+30)
    shares = low(jax.nn.softmax(scores, axis=-1))
    context = low_back(jnp.einsum('shqk,skhd->sqhd', shares, values, precision=lax.Precision.HIGHEST))
    gated_low = low(context * gate_heads[:, None]).reshape(seq_count, seq_span, D)
    branch = low_back(matmul_high(gated_low, weights['w_output']) + vectors[8])
    middle = layer_norm(start_f + gate_hidden * branch, vectors[2], vectors[3])
    pre_up = low_back(matmul_high(low(middle), weights['w_up']) + weights['b_up'])
    up_low = low(jax.nn.gelu(pre_up, approximate=False) * gate_inner)
    down_out = low_back(matmul_high(up_low, weights['w_down']) + vectors[9])
    return layer_norm(middle + gate_hidden * down_out, vectors[4], vectors[5])

def adam_step(weight, first_old, second, clipped):
    first_new = beta_one * first_old + (1.0 - beta_one) * clipped
    second_new = beta_two * second + (1.0 - beta_two) * clipped * clipped
    first_hat = first_new / (1.0 - beta_one ** ADAM_STEP)
    second_hat = second_new / (1.0 - beta_two ** ADAM_STEP)
    weight_new = weight - learn_rate * (first_hat / (jnp.sqrt(second_hat) + adam_eps) + decay_rate * weight)
    return (weight_new, first_new, second_new)

def reference(token_ids, lengths, gate_noise, lagrange, teacher_table, teacher_flat, word_table, table_first, table_second, layer_flat, flat_first, flat_second):
    token_total = jnp.sum(lengths).astype(jnp.float32)
    teacher_rows = teacher_table.astype(jnp.float32)
    teacher_weights = unpack(teacher_flat.astype(jnp.float32), False)
    all_open = (jnp.ones((D,), jnp.float32), jnp.ones((HEADS,), jnp.float32), jnp.ones((FF,), jnp.float32))
    id_groups = token_ids.reshape(-1, SEQ_DEV, LEN)
    length_groups = lengths.reshape(-1, SEQ_DEV)

    def objective(table_master, flat_master):
        table_low = low(table_master)
        weights = unpack(low(flat_master), True)
        gate_all = gate_values(weights['gate_logits'], gate_noise)
        gate_set = (gate_all[:D], gate_all[D:D + HEADS], gate_all[D + HEADS:])

        def group_term(running, group_in):
            group_ids, group_lengths = group_in
            key_valid = (jnp.arange(LEN)[None, :] < group_lengths[:, None]).astype(jnp.float32)
            target_out = run_layer(teacher_rows, teacher_weights, group_ids, key_valid, all_open)
            student_out = run_layer(table_low, weights, group_ids, key_valid, gate_set)
            aligned = low_back(matmul_high(low(student_out), weights['w_align']))
            differ = aligned - target_out
            return (running + jnp.sum(lax.optimization_barrier(jnp.mean(differ * differ, axis=-1)) * key_valid), None)
        distill, _ = lax.scan(jax.checkpoint(group_term), jnp.zeros((), jnp.float32), (id_groups, length_groups))
        return distill / token_total + lagrangian(weights['gate_logits'], lagrange)
    total_loss, pull_back = jax.vjp(objective, word_table, layer_flat)
    table_grad, flat_grad = pull_back(jnp.ones((), jnp.float32))
    grad_norm = jnp.sqrt(jnp.sum(table_grad * table_grad) + jnp.sum(flat_grad * flat_grad))
    factor = jnp.minimum(1.0, clip_norm / (grad_norm + 1e-06))
    table_out, table_first_out, table_second_out = adam_step(word_table, table_first, table_second, table_grad * factor)
    flat_out, flat_first_out, flat_second_out = adam_step(layer_flat, flat_first, flat_second, flat_grad * factor)
    return (table_out, table_first_out, table_second_out, flat_out, flat_first_out, flat_second_out, total_loss, grad_norm)
```

```python
import functools
import math

import jax
import jax.numpy as jnp
from jax import lax
from jax.experimental import pallas as pl
from jax.experimental.pallas import tpu as pltpu
from jax.sharding import PartitionSpec as P

D = 256
HEADS = 4
HD = D // HEADS
FF = 1024
LEN = 512
VOCAB = 30522
NPAR = 856836
LANES = 128
norm_eps = 1e-12
f32 = jnp.float32
bf16 = jnp.bfloat16
VMEM_LIMIT = 56 * 2**20

C_GH = 10 * D
C_HEAD = 11 * D
C_BUP = 12 * D
C_GI = 12 * D + FF
C_ROWS = 12 * D + 2 * FF
A_BUP = 10 * D
A_GH = 10 * D + FF
A_HEAD = 11 * D + FF
A_GI = 12 * D + FF
A_ROWS = 12 * D + 2 * FF
R_UP = 5 * 512
R_DOWN = R_UP + 2048
R_VEC = R_DOWN + 2048
R_BUP = R_VEC + 20
R_LOGIT = R_BUP + 8
R_USED = R_LOGIT + 11


def nn(left, right):
    return jnp.dot(left, right, preferred_element_type=f32)


def nt(left, right):
    return lax.dot_general(left, right, (((1,), (1,)), ((), ())), preferred_element_type=f32)


def chunks(span):
    return [(c, min(256, span - c)) for c in range(0, span, 256)]


def wide(col_ref, row, rows, width):
    col = col_ref[row : row + rows, :]
    return jnp.concatenate([col] * (width // LANES), axis=1) if width > LANES else col


def lanes_in(values):
    total = values[:, :LANES]
    for c in range(LANES, values.shape[1], LANES):
        total = total + values[:, c : c + LANES]
    return total


def eye(size):
    return (
        lax.broadcasted_iota(jnp.int32, (size, size), 0)
        == lax.broadcasted_iota(jnp.int32, (size, size), 1)
    ).astype(bf16)


def standardise(x):
    mean = jnp.sum(x, axis=0, keepdims=True) * (1.0 / D)
    centred = x - mean
    variance = jnp.sum(centred * centred, axis=0, keepdims=True) * (1.0 / D)
    scale = lax.rsqrt(variance + norm_eps)
    return centred * scale, scale


def standardise_back(dx, hat, scale):
    mean_one = jnp.sum(dx, axis=0, keepdims=True) * (1.0 / D)
    mean_two = jnp.sum(dx * hat, axis=0, keepdims=True) * (1.0 / D)
    return scale * (dx - mean_one - hat * mean_two)


def gelu_parts(x):
    half_erf = 0.5 * lax.erf(x * (2.0**-0.5)) + 0.5
    return half_erf


def forward_body(span, offset, length, student, rows_ref, pos_ref, col_ref, w, sc, eyes):
    for c, width in chunks(span):
        tokens = rows_ref[pl.ds(offset + c, width), :]
        embedded = nt(eyes[D], tokens) + pos_ref[:, c : c + width]
        hat, scale = standardise(embedded)
        start = hat * wide(col_ref, 0, D, width) + wide(col_ref, D, D, width)
        if student:
            sc["hat0"][:, c : c + width] = hat
            sc["scale"][0:1, c : c + width] = scale
            start = start * wide(col_ref, C_GH, D, width)
        sc["start"][:, c : c + width] = start
        start_low = start.astype(bf16)
        sc["start_low"][:, c : c + width] = start_low
        factor = HD**-0.5
        q = nn(w["qkvT"][0:D, :], start_low) + wide(col_ref, 6 * D, D, width)
        sc["qkv"][0:D, c : c + width] = q.astype(bf16)
        k = nn(w["qkvT"][D : 2 * D, :], start_low).astype(bf16)
        sc["qkv"][D : 2 * D, c : c + width] = k
        v = (nn(w["qkvT"][2 * D : 3 * D, :], start_low) + wide(col_ref, 7 * D, D, width)).astype(
            bf16
        )
        sc["qkv"][2 * D : 3 * D, c : c + width] = v
        for h in range(HEADS):
            sc["k_rows"][h, c : c + width, :] = nt(eyes[width], k[h * HD : (h + 1) * HD, :]).astype(
                bf16
            )
            if student:
                sc["v_rows"][h, c : c + width, :] = nt(
                    eyes[width], v[h * HD : (h + 1) * HD, :]
                ).astype(bf16)
    for c, width in chunks(span):
        valid = lax.broadcasted_iota(jnp.int32, (span, width), 0) < length
        for h in range(HEADS):
            q_h = sc["qkv"][h * HD : (h + 1) * HD, c : c + width] * bf16(HD**-0.5)
            scores = jnp.where(valid, nn(sc["k_rows"][h, 0:span, :], q_h), -1e30)
            shares = jnp.exp(scores - jnp.max(scores, axis=0, keepdims=True))
            shares_low = (shares * (1.0 / jnp.sum(shares, axis=0, keepdims=True))).astype(bf16)
            if student:
                sc["shares"][h, 0:span, c : c + width] = shares_low
            context = nn(sc["qkv"][2 * D + h * HD : 2 * D + (h + 1) * HD, 0:span], shares_low)
            if student:
                sc["context"][h * HD : (h + 1) * HD, c : c + width] = context
                context = context * wide(col_ref, C_HEAD + h * HD, HD, width)
            sc["gated"][h * HD : (h + 1) * HD, c : c + width] = context.astype(bf16)
    for c, width in chunks(span):
        branch = nn(w["oT"][...], sc["gated"][:, c : c + width]) + wide(col_ref, 8 * D, D, width)
        if student:
            sc["branch"][:, c : c + width] = branch
            branch = branch * wide(col_ref, C_GH, D, width)
        hat, scale = standardise(sc["start"][:, c : c + width] + branch)
        middle = hat * wide(col_ref, 2 * D, D, width) + wide(col_ref, 3 * D, D, width)
        if student:
            sc["hat1"][:, c : c + width] = hat
            sc["scale"][1:2, c : c + width] = scale
        middle_low = middle.astype(bf16)
        if student:
            sc["middle_low"][:, c : c + width] = middle_low
        for r in range(0, FF, D):
            pre = nn(w["upT"][r : r + D, :], middle_low) + wide(col_ref, C_BUP + r, D, width)
            cdf = 0.5 * lax.erf(pre * (2.0**-0.5)) + 0.5
            act = pre * cdf
            if student:
                inner = wide(col_ref, C_GI + r, D, width)
                pdf = jnp.exp(pre * pre * -0.5) * (1.0 / math.sqrt(2.0 * math.pi))
                sc["act"][r : r + D, c : c + width] = act
                sc["slope"][r : r + D, c : c + width] = (cdf + pre * pdf) * inner
                act = act * inner
            sc["up"][r : r + D, c : c + width] = act.astype(bf16)
        down = nn(w["downT"][...], sc["up"][:, c : c + width]) + wide(col_ref, 9 * D, D, width)
        if student:
            sc["down"][:, c : c + width] = down
            down = down * wide(col_ref, C_GH, D, width)
        hat, scale = standardise(middle + down)
        out = hat * wide(col_ref, 4 * D, D, width) + wide(col_ref, 5 * D, D, width)
        if student:
            sc["hat2"][:, c : c + width] = hat
            sc["scale"][2:3, c : c + width] = scale
        sc["out"][:, c : c + width] = out


def backward_body(span, length, factor, target_ref, col_ref, w, sc, acc, add_ref, loss_ref, grad_ref, pos_add):
    def add(row, values):
        add_ref[row : row + values.shape[0], :] += lanes_in(values)

    for c, width in chunks(span):
        cols = slice(c, c + width)
        out_low = sc["out"][:, cols].astype(bf16)
        sc["out_low"][:, cols] = out_low
        differ = nn(w["aT"][...], out_low) - target_ref[0, :, cols]
        token_valid = (lax.broadcasted_iota(jnp.int32, (1, width), 1) + c < length).astype(f32)
        loss_ref[0:1, cols] += (
            jnp.sum(differ * differ, axis=0, keepdims=True) * (1.0 / D) * token_valid
        )
        d_aligned = (differ * (token_valid * factor)).astype(bf16)
        sc["d_aligned"][:, cols] = d_aligned
        d_out = nn(w["a"][...], d_aligned)
        hat = sc["hat2"][:, cols]
        add(4 * D, d_out * hat)
        add(5 * D, d_out)
        d_second = standardise_back(d_out * wide(col_ref, 4 * D, D, width), hat, sc["scale"][2:3, cols])
        add(A_GH, d_second * sc["down"][:, cols])
        d_down = (d_second * wide(col_ref, C_GH, D, width)).astype(bf16)
        sc["d_down"][:, cols] = d_down
        add(9 * D, d_down.astype(f32))
        for r in range(0, FF, D):
            d_up = nn(w["down"][r : r + D, :], d_down)
            add(A_GI + r, d_up * sc["act"][r : r + D, cols])
            d_pre = (d_up * sc["slope"][r : r + D, cols]).astype(bf16)
            sc["d_pre"][r : r + D, cols] = d_pre
            add(A_BUP + r, d_pre.astype(f32))
        d_middle = d_second + nn(w["up"][...], sc["d_pre"][:, cols])
        hat = sc["hat1"][:, cols]
        add(2 * D, d_middle * hat)
        add(3 * D, d_middle)
        d_first = standardise_back(
            d_middle * wide(col_ref, 2 * D, D, width), hat, sc["scale"][1:2, cols]
        )
        sc["d_first"][:, cols] = d_first
        add(A_GH, d_first * sc["branch"][:, cols])
        d_branch = (d_first * wide(col_ref, C_GH, D, width)).astype(bf16)
        sc["d_branch"][:, cols] = d_branch
        add(8 * D, d_branch.astype(f32))
        d_gated = nn(w["o"][...], d_branch)
        context = sc["context"][:, cols]
        add(A_HEAD, d_gated * context)
        d_context = d_gated * wide(col_ref, C_HEAD, D, width)
        sc["d_context"][:, cols] = d_context.astype(bf16)
        dot_rows = d_context * context
        for h in range(HEADS):
            sc["delta"][h : h + 1, cols] = jnp.sum(
                dot_rows[h * HD : (h + 1) * HD, :], axis=0, keepdims=True
            )
    full = slice(0, span)
    acc["a"][...] += nt(sc["out_low"][:, full], sc["d_aligned"][:, full])
    acc["down"][...] += nt(sc["up"][:, full], sc["d_down"][:, full])
    acc["up"][...] += nt(sc["middle_low"][:, full], sc["d_pre"][:, full])
    acc["o"][...] += nt(sc["gated"][:, full], sc["d_branch"][:, full])
    for h in range(HEADS):
        rows = slice(h * HD, (h + 1) * HD)
        d_value = nt(sc["d_context"][rows, full], sc["shares"][h, 0:span, 0:span])
        sc["d_qkv"][2 * D + h * HD : 2 * D + (h + 1) * HD, full] = d_value.astype(bf16)
        d_key = None
        for c, width in chunks(span):
            cols = slice(c, c + width)
            d_shares = nn(sc["v_rows"][h, 0:span, :], sc["d_context"][rows, cols])
            d_scores = (
                sc["shares"][h, 0:span, cols].astype(f32) * (d_shares - sc["delta"][h : h + 1, cols])
            ).astype(bf16)
            sc["d_qkv"][rows, cols] = (
                nn(sc["qkv"][D + h * HD : D + (h + 1) * HD, full], d_scores) * (HD**-0.5)
            ).astype(bf16)
            part = nt(sc["qkv"][rows, cols], d_scores)
            d_key = part if d_key is None else d_key + part
        sc["d_qkv"][D + h * HD : D + (h + 1) * HD, full] = (d_key * (HD**-0.5)).astype(bf16)
    acc["qkv"][...] += nt(sc["start_low"][:, full], sc["d_qkv"][:, full])
    for c, width in chunks(span):
        cols = slice(c, c + width)
        add(6 * D, sc["d_qkv"][0:D, cols].astype(f32))
        add(7 * D, sc["d_qkv"][2 * D : 3 * D, cols].astype(f32))
        d_start = sc["d_first"][:, cols] + nn(w["qkv"][...], sc["d_qkv"][:, cols])
        hat = sc["hat0"][:, cols]
        gain = wide(col_ref, 0, D, width)
        add(A_GH, d_start * (hat * gain + wide(col_ref, D, D, width)))
        d_norm = d_start * wide(col_ref, C_GH, D, width)
        add(0, d_norm * hat)
        add(D, d_norm)
        d_embedded = standardise_back(d_norm * gain, hat, sc["scale"][0:1, cols])
        pos_add[:, cols] += d_embedded
        grad_ref[0, :, cols] = d_embedded.astype(bf16)
    if span < LEN:
        grad_ref[0, :, span:LEN] = jnp.zeros((D, LEN - span), bf16)


SPANS = (256, 384, 512)


def by_span(length, body):
    for i, span in enumerate(SPANS):
        low = SPANS[i - 1] if i else 0
        test = length > low
        if i == 0:
            test = length <= span
        elif i < len(SPANS) - 1:
            test = (length > low) & (length <= span)
        pl.when(test)(functools.partial(body, span))


def set_up(pos_in, pos_ref, eyes_refs):
    for size, ref in eyes_refs.items():
        ref[...] = eye(size)
    for c in range(0, LEN, 256):
        pos_ref[:, c : c + 256] = nt(eyes_refs[256][...], pos_in[c : c + 256, :])


TEACHER_W = (("qkvT", (3 * D, D)), ("oT", (D, D)), ("upT", (FF, D)), ("downT", (D, FF)))
STUDENT_W = TEACHER_W + (
    ("aT", (D, D)),
    ("qkv", (D, 3 * D)),
    ("o", (D, D)),
    ("a", (D, D)),
    ("up", (D, FF)),
    ("down", (FF, D)),
)
TEACHER_S = (
    ("start", (D, LEN), f32),
    ("start_low", (D, LEN), bf16),
    ("qkv", (3 * D, LEN), bf16),
    ("k_rows", (HEADS, LEN, HD), bf16),
    ("gated", (D, LEN), bf16),
    ("up", (FF, LEN), bf16),
)
STUDENT_S = TEACHER_S + (
    ("hat0", (D, LEN), f32),
    ("hat1", (D, LEN), f32),
    ("hat2", (D, LEN), f32),
    ("scale", (8, LEN), f32),
    ("v_rows", (HEADS, LEN, HD), bf16),
    ("shares", (HEADS, LEN, LEN), bf16),
    ("context", (D, LEN), f32),
    ("branch", (D, LEN), f32),
    ("middle_low", (D, LEN), bf16),
    ("act", (FF, LEN), f32),
    ("slope", (FF, LEN), f32),
    ("down", (D, LEN), f32),
    ("out", (D, LEN), f32),
    ("out_low", (D, LEN), bf16),
    ("d_aligned", (D, LEN), bf16),
    ("d_down", (D, LEN), bf16),
    ("d_pre", (FF, LEN), bf16),
    ("d_first", (D, LEN), f32),
    ("d_branch", (D, LEN), bf16),
    ("d_context", (D, LEN), bf16),
    ("delta", (8, LEN), f32),
    ("d_qkv", (3 * D, LEN), bf16),
)
ACCS = (
    ("qkv", (D, 3 * D)),
    ("o", (D, D)),
    ("a", (D, D)),
    ("up", (D, FF)),
    ("down", (FF, D)),
)


def teacher_kernel(len_ref, off_ref, rows_ref, pos_in, col_ref, *rest):
    w = {name: rest[i] for i, (name, _) in enumerate(TEACHER_W)}
    out_ref = rest[len(TEACHER_W)]
    scratch = rest[len(TEACHER_W) + 1 :]
    sc = {entry[0]: scratch[i] for i, entry in enumerate(TEACHER_S)}
    pos_ref, eye_one, eye_two = scratch[len(TEACHER_S) :]
    s = pl.program_id(0)
    sc["out"] = out_ref.at[0]

    @pl.when(s == 0)
    def _():
        set_up(pos_in, pos_ref, {128: eye_one, 256: eye_two})

    eyes = {128: eye_one, 256: eye_two}

    class Read:
        def __getitem__(self, size):
            return eyes[size][...]

    length = len_ref[s]

    def body(span):
        offset = pl.multiple_of(off_ref[s], 16)
        forward_body(span, offset, length, False, rows_ref, pos_ref, col_ref, w, sc, Read())

    by_span(length, body)


def student_kernel(len_ref, off_ref, fac_ref, rows_ref, pos_in, target_ref, col_ref, slope_in, lag_in, *rest):
    w = {name: rest[i] for i, (name, _) in enumerate(STUDENT_W)}
    rest = rest[len(STUDENT_W) :]
    flat_ref, grad_ref, pos_add, loss_ref = rest[:4]
    scratch = rest[4:]
    sc = {entry[0]: scratch[i] for i, entry in enumerate(STUDENT_S)}
    scratch = scratch[len(STUDENT_S) :]
    acc = {entry[0]: scratch[i] for i, entry in enumerate(ACCS)}
    add_ref, pos_ref, eye_one, eye_two = scratch[len(ACCS) :]
    s = pl.program_id(0)

    @pl.when(s == 0)
    def _():
        set_up(pos_in, pos_ref, {128: eye_one, 256: eye_two})
        for ref in list(acc.values()) + [add_ref, pos_add, loss_ref]:
            ref[...] = jnp.zeros(ref.shape, f32)

    eyes = {128: eye_one, 256: eye_two}

    class Read:
        def __getitem__(self, size):
            return eyes[size][...]

    length = len_ref[s]

    def body(span):
        offset = pl.multiple_of(off_ref[s], 16)
        forward_body(span, offset, length, True, rows_ref, pos_ref, col_ref, w, sc, Read())
        backward_body(
            span, length, fac_ref[0], target_ref, col_ref, w, sc, acc, add_ref, loss_ref, grad_ref, pos_add
        )

    by_span(length, body)

    @pl.when(s == pl.num_programs(0) - 1)
    def _():
        for i in range(3):
            for j in range(2):
                at = i * D + j * LANES
                flat_ref[pl.ds(512 * i + j, D, stride=2), :] = acc["qkv"][:, at : at + LANES]
        for j in range(2):
            lanes = slice(j * LANES, (j + 1) * LANES)
            flat_ref[pl.ds(512 * 3 + j, D, stride=2), :] = acc["o"][:, lanes]
            flat_ref[pl.ds(512 * 4 + j, D, stride=2), :] = acc["a"][:, lanes]
            flat_ref[pl.ds(R_DOWN + j, FF, stride=2), :] = acc["down"][:, lanes]
        for j in range(8):
            flat_ref[pl.ds(R_UP + j, D, stride=8), :] = acc["up"][:, j * LANES : (j + 1) * LANES]
        ones = jnp.ones((8, LANES), f32)

        def summed(row, rows):
            return lax.dot_general(
                ones,
                add_ref[row : row + rows, :],
                (((1,), (1,)), ((), ())),
                preferred_element_type=f32,
                precision=lax.Precision.HIGHEST,
            )

        for i in range(10):
            sums = summed(i * D, D)
            for j in range(2):
                flat_ref[R_VEC + 2 * i + j : R_VEC + 2 * i + j + 1, :] = sums[
                    0:1, j * LANES : (j + 1) * LANES
                ]
        sums = summed(A_BUP, FF)
        for j in range(8):
            flat_ref[R_BUP + j : R_BUP + j + 1, :] = sums[0:1, j * LANES : (j + 1) * LANES]
        hidden = summed(A_GH, D)
        group = (
            lax.broadcasted_iota(jnp.int32, (D, LANES), 0) // HD
            == lax.broadcasted_iota(jnp.int32, (D, LANES), 1)
        ).astype(f32)
        heads = jnp.dot(
            summed(A_HEAD, D), group, preferred_element_type=f32, precision=lax.Precision.HIGHEST
        )
        inner = summed(A_GI, FF)
        moved = pltpu.roll(jnp.concatenate([inner, jnp.zeros((8, LANES), f32)], axis=1), HEADS, 1)
        lane = lax.broadcasted_iota(jnp.int32, (8, LANES), 1)
        first = jnp.where(lane < HEADS, heads, moved[:, :LANES])
        tail = [hidden[:, :LANES], hidden[:, LANES:], first] + [
            moved[:, j * LANES : (j + 1) * LANES] for j in range(1, 9)
        ]
        for j, piece in enumerate(tail):
            flat_ref[R_LOGIT + j : R_LOGIT + j + 1, :] = (
                piece[0:1] * slope_in[j : j + 1, :] + lag_in[j : j + 1, :]
            )
        flat_ref[R_USED:, :] = jnp.zeros((flat_ref.shape[0] - R_USED, LANES), f32)


def whole_spec():
    return pl.BlockSpec(memory_space=pltpu.VMEM)


def smem_spec():
    return pl.BlockSpec(memory_space=pltpu.SMEM)


def seq_spec():
    return pl.BlockSpec((1, D, LEN), lambda s: (s, 0, 0))


def extra_scratch():
    return [
        pltpu.VMEM((D, LEN), f32),
        pltpu.VMEM((128, 128), bf16),
        pltpu.VMEM((256, 256), bf16),
    ]


def run_teacher(lengths, offsets, rows, places, columns, weights):
    seqs = lengths.shape[0]
    return pl.pallas_call(
        teacher_kernel,
        grid=(seqs,),
        out_shape=jax.ShapeDtypeStruct((seqs, D, LEN), f32),
        in_specs=[smem_spec(), smem_spec()] + [whole_spec()] * (3 + len(TEACHER_W)),
        out_specs=seq_spec(),
        scratch_shapes=[pltpu.VMEM(shape, kind) for _, shape, kind in TEACHER_S] + extra_scratch(),
        compiler_params=pltpu.CompilerParams(vmem_limit_bytes=VMEM_LIMIT),
        name="teacher",
    )(lengths, offsets, rows, places, columns, *[weights[name] for name, _ in TEACHER_W])


def run_student(lengths, offsets, factor, rows, places, target, columns, slopes, lag, weights, flat_rows):
    seqs = lengths.shape[0]
    return pl.pallas_call(
        student_kernel,
        grid=(seqs,),
        out_shape=(
            jax.ShapeDtypeStruct((flat_rows, LANES), f32),
            jax.ShapeDtypeStruct((seqs, D, LEN), bf16),
            jax.ShapeDtypeStruct((D, LEN), f32),
            jax.ShapeDtypeStruct((8, LEN), f32),
        ),
        in_specs=[smem_spec()] * 3
        + [whole_spec()] * 2
        + [seq_spec()]
        + [whole_spec()] * (3 + len(STUDENT_W)),
        out_specs=(
            pl.BlockSpec((flat_rows, LANES), lambda s: (0, 0)),
            seq_spec(),
            pl.BlockSpec((D, LEN), lambda s: (0, 0)),
            pl.BlockSpec((8, LEN), lambda s: (0, 0)),
        ),
        scratch_shapes=[pltpu.VMEM(shape, kind) for _, shape, kind in STUDENT_S]
        + [pltpu.VMEM(shape, f32) for _, shape in ACCS]
        + [pltpu.VMEM((A_ROWS, LANES), f32)]
        + extra_scratch(),
        compiler_params=pltpu.CompilerParams(vmem_limit_bytes=VMEM_LIMIT),
        name="student",
    )(
        lengths,
        offsets,
        factor,
        rows,
        places,
        target,
        columns,
        slopes,
        lag,
        *[weights[name] for name, _ in STUDENT_W],
    )


clip_norm = 0.002
learn_rate = 0.015
beta_one = 0.9
beta_two = 0.999
adam_eps = 1e-08
decay_rate = 0.01
sparse_target = 0.3
ADAM_STEP = 10
relaxation_heat = 2.0 / 3.0
widened_left_limit = -0.1
widened_right_limit = 1.1


def layout(student):
    square = (D, D)
    entries = [("w_query", square), ("w_key", square), ("w_value", square), ("w_output", square)]
    if student:
        entries = entries + [("w_align", square)]
    entries = entries + [
        ("w_up", (D, FF)),
        ("w_down", (FF, D)),
        ("vectors", (10, D)),
        ("b_up", (FF,)),
    ]
    if student:
        entries = entries + [("gate_logits", (D + HEADS + FF,))]
    return entries


def unpack(flat_vector, student):
    pieces = {}
    offset = 0
    for entry_name, entry_shape in layout(student):
        length = math.prod(entry_shape)
        pieces[entry_name] = flat_vector[offset : offset + length].reshape(entry_shape)
        offset = offset + length
    return pieces


def gate_values(mask_logodds, flat_random_sample):
    logistic_function = jax.nn.sigmoid(
        (jnp.log(flat_random_sample) - jnp.log(1.0 - flat_random_sample) + mask_logodds)
        / relaxation_heat
    )
    return jnp.clip(
        logistic_function * (widened_right_limit - widened_left_limit) + widened_left_limit,
        0.0,
        1.0,
    )


def lagrangian(mask_logodds, lagrange):
    survival_probability = jax.nn.sigmoid(
        mask_logodds - relaxation_heat * math.log(-widened_left_limit / widened_right_limit)
    )
    kept_hidden = jnp.mean(survival_probability[:D])
    kept_rest = 4.0 * HD * jnp.sum(survival_probability[D : D + HEADS]) + 2.0 * jnp.sum(
        survival_probability[D + HEADS :]
    )
    expected = kept_hidden * kept_rest / (4.0 * D + 2.0 * FF)
    excess = expected - sparse_target
    return lagrange[0] * excess + lagrange[1] * excess * excess


def adam_step(weight, first_old, second, clipped):
    first_new = beta_one * first_old + (1.0 - beta_one) * clipped
    second_new = beta_two * second + (1.0 - beta_two) * clipped * clipped
    first_hat = first_new / (1.0 - beta_one**ADAM_STEP)
    second_hat = second_new / (1.0 - beta_two**ADAM_STEP)
    weight_new = weight - learn_rate * (
        first_hat / (jnp.sqrt(second_hat) + adam_eps) + decay_rate * weight
    )
    return (weight_new, first_new, second_new)


def kernel_weights(pieces, student):
    w = {}
    w["qkv"] = jnp.concatenate([pieces["w_query"], pieces["w_key"], pieces["w_value"]], axis=1)
    w["qkvT"] = w["qkv"].T
    for name, source in (("o", "w_output"), ("up", "w_up"), ("down", "w_down")):
        w[name] = pieces[source]
        w[name + "T"] = pieces[source].T
    if student:
        w["a"] = pieces["w_align"]
        w["aT"] = w["a"].T
    return w


def columns_of(pieces, gates=None):
    vectors = pieces["vectors"].astype(f32).reshape(-1)
    bias = pieces["b_up"].astype(f32)
    if gates is None:
        gates = jnp.ones((D + HEADS + FF,), f32)
    parts = [vectors, gates[:D], jnp.repeat(gates[D : D + HEADS], HD), bias, gates[D + HEADS :]]
    column = jnp.concatenate(parts)
    return jnp.broadcast_to(column[:, None], (column.shape[0], LANES))


def pad_rows(values):
    return jnp.pad(values, (0, 16 * LANES - values.shape[0])).reshape(16, LANES)


def per_device(
    devices,
    token_ids,
    lengths,
    gate_noise,
    lagrange,
    teacher_table,
    teacher_flat,
    word_table,
    table_first,
    table_second,
    layer_flat,
    flat_first,
    flat_second,
):
    seqs = token_ids.shape[0]
    half = seqs // 2
    mates = [(i, devices - 1 - i) for i in range(devices)]
    sent = jnp.concatenate(
        [token_ids[half:], jnp.pad(lengths[half:], (0, LEN - half)).reshape(1, LEN)]
    )
    got = lax.ppermute(sent, "dp", mates)
    ids = jnp.concatenate([token_ids[:half], got[:half]])
    lens = jnp.concatenate([lengths[:half], got[half, :half]])
    offsets = jnp.arange(seqs, dtype=jnp.int32) * LEN

    table_rows = lax.all_gather(word_table.astype(bf16), "dp", axis=0, tiled=True)
    flat_rows = lax.all_gather(layer_flat.astype(bf16), "dp", axis=0, tiled=True)
    global_count = lax.psum(jnp.sum(lengths).astype(f32), "dp")
    factor = ((2.0 / D) / global_count).reshape(1)

    teacher = unpack(teacher_flat, False)
    target = run_teacher(
        lens,
        offsets,
        jnp.take(teacher_table, ids.reshape(-1), axis=0),
        teacher_table[VOCAB : VOCAB + LEN],
        columns_of(teacher),
        kernel_weights(teacher, False),
    )

    pieces = unpack(flat_rows, True)
    logits = pieces["gate_logits"].astype(f32)
    gates, gate_back = jax.vjp(lambda x: gate_values(x, gate_noise), logits)
    slopes = gate_back(jnp.ones_like(gates))[0]
    lag_value, lag_back = jax.vjp(lambda x: lagrangian(x, lagrange), logits)
    lag_weight = jnp.where(lax.axis_index("dp") == 0, 1.0, 0.0).astype(f32)
    flat_term, grad_rows, place_grad, loss_rows = run_student(
        lens,
        offsets,
        factor,
        jnp.take(table_rows, ids.reshape(-1), axis=0),
        table_rows[VOCAB : VOCAB + LEN],
        target,
        columns_of(pieces, gates),
        pad_rows(slopes),
        pad_rows(lag_back(lag_weight)[0]),
        kernel_weights(pieces, True),
        flat_rows.shape[0] // LANES,
    )
    global_sum = lax.psum(jnp.sum(loss_rows), "dp")
    updates = jnp.transpose(grad_rows, (0, 2, 1)).reshape(seqs * LEN, D).astype(f32)
    index = jnp.concatenate([ids.reshape(-1), VOCAB + jnp.arange(LEN, dtype=jnp.int32)])
    updates = jnp.concatenate([updates, place_grad.T])
    table_term = jnp.zeros((table_rows.shape[0], D), f32).at[index].add(updates)
    table_grad = lax.psum_scatter(table_term, "dp", scatter_dimension=0, tiled=True)
    flat_grad = lax.psum_scatter(flat_term.reshape(-1), "dp", scatter_dimension=0, tiled=True)
    squares = jnp.sum(table_grad * table_grad) + jnp.sum(flat_grad * flat_grad)
    grad_norm = jnp.sqrt(lax.psum(squares, "dp"))
    clip = jnp.minimum(1.0, clip_norm / (grad_norm + 1e-06))
    total_loss = global_sum / global_count + lag_value
    table_new = adam_step(word_table, table_first, table_second, table_grad * clip)
    flat_new = adam_step(layer_flat, flat_first, flat_second, flat_grad * clip)
    return (*table_new, *flat_new, total_loss, grad_norm)


def solution(mesh):
    row, flat, copied = P("dp", None), P("dp"), P()
    in_specs = (row, flat, copied, copied, copied, copied, row, row, row, flat, flat, flat)
    out_specs = (row, row, row, flat, flat, flat, copied, copied)
    return jax.shard_map(
        functools.partial(per_device, mesh.shape["dp"]),
        mesh=mesh,
        in_specs=in_specs,
        out_specs=out_specs,
        check_vma=False,
    )
```

```python
import functools
import math

import jax
import jax.numpy as jnp
from jax import lax
from jax.experimental import pallas as pl
from jax.experimental.pallas import tpu as pltpu
from jax.sharding import PartitionSpec as P

D = 256
HEADS = 4
HD = D // HEADS
FF = 1024
LEN = 512
VOCAB = 30522
NPAR = 856836
LANES = 128
norm_eps = 1e-12
f32 = jnp.float32
bf16 = jnp.bfloat16
VMEM_LIMIT = 56 * 2**20

C_GH = 10 * D
C_HEAD = 11 * D
C_BUP = 12 * D
C_GI = 12 * D + FF
C_ROWS = 12 * D + 2 * FF
A_BUP = 10 * D
A_GH = 10 * D + FF
A_HEAD = 11 * D + FF
A_GI = 12 * D + FF
A_ROWS = 12 * D + 2 * FF
R_UP = 5 * 512
R_DOWN = R_UP + 2048
R_VEC = R_DOWN + 2048
R_BUP = R_VEC + 20
R_LOGIT = R_BUP + 8
R_USED = R_LOGIT + 11


def nn(left, right):
    return jnp.dot(left, right, preferred_element_type=f32)


def nt(left, right):
    return lax.dot_general(left, right, (((1,), (1,)), ((), ())), preferred_element_type=f32)


def chunks(span):
    return [(c, min(256, span - c)) for c in range(0, span, 256)]


def wide(col_ref, row, rows, width):
    col = col_ref[row : row + rows, :]
    return jnp.concatenate([col] * (width // LANES), axis=1) if width > LANES else col


def lanes_in(values):
    total = values[:, :LANES]
    for c in range(LANES, values.shape[1], LANES):
        total = total + values[:, c : c + LANES]
    return total


def eye(size):
    return (
        lax.broadcasted_iota(jnp.int32, (size, size), 0)
        == lax.broadcasted_iota(jnp.int32, (size, size), 1)
    ).astype(bf16)


def standardise(x):
    mean = jnp.sum(x, axis=0, keepdims=True) * (1.0 / D)
    centred = x - mean
    variance = jnp.sum(centred * centred, axis=0, keepdims=True) * (1.0 / D)
    scale = lax.rsqrt(variance + norm_eps)
    return centred * scale, scale


def standardise_back(dx, hat, scale):
    mean_one = jnp.sum(dx, axis=0, keepdims=True) * (1.0 / D)
    mean_two = jnp.sum(dx * hat, axis=0, keepdims=True) * (1.0 / D)
    return scale * (dx - mean_one - hat * mean_two)


def gelu_parts(x):
    half_erf = 0.5 * lax.erf(x * (2.0**-0.5)) + 0.5
    return half_erf


def forward_body(span, offset, length, student, rows_ref, pos_ref, col_ref, w, sc, eyes):
    for c, width in chunks(span):
        tokens = rows_ref[pl.ds(offset + c, width), :]
        embedded = nt(eyes[D], tokens) + pos_ref[:, c : c + width]
        hat, scale = standardise(embedded)
        start = hat * wide(col_ref, 0, D, width) + wide(col_ref, D, D, width)
        if student:
            sc["hat0"][:, c : c + width] = hat
            sc["scale"][0:1, c : c + width] = scale
            start = start * wide(col_ref, C_GH, D, width)
        sc["start"][:, c : c + width] = start
        start_low = start.astype(bf16)
        sc["start_low"][:, c : c + width] = start_low
        factor = HD**-0.5
        q = nn(w["qkvT"][0:D, :], start_low) + wide(col_ref, 6 * D, D, width)
        sc["qkv"][0:D, c : c + width] = q.astype(bf16)
        k = nn(w["qkvT"][D : 2 * D, :], start_low).astype(bf16)
        sc["qkv"][D : 2 * D, c : c + width] = k
        v = (nn(w["qkvT"][2 * D : 3 * D, :], start_low) + wide(col_ref, 7 * D, D, width)).astype(
            bf16
        )
        sc["qkv"][2 * D : 3 * D, c : c + width] = v
        for h in range(HEADS):
            sc["k_rows"][h, c : c + width, :] = nt(eyes[width], k[h * HD : (h + 1) * HD, :]).astype(
                bf16
            )
            if student:
                sc["v_rows"][h, c : c + width, :] = nt(
                    eyes[width], v[h * HD : (h + 1) * HD, :]
                ).astype(bf16)
    for c, width in chunks(span):
        valid = lax.broadcasted_iota(jnp.int32, (span, width), 0) < length
        for h in range(HEADS):
            q_h = sc["qkv"][h * HD : (h + 1) * HD, c : c + width] * bf16(HD**-0.5)
            scores = jnp.where(valid, nn(sc["k_rows"][h, 0:span, :], q_h), -1e30)
            shares = jnp.exp(scores - jnp.max(scores, axis=0, keepdims=True))
            shares_low = (shares * (1.0 / jnp.sum(shares, axis=0, keepdims=True))).astype(bf16)
            if student:
                sc["shares"][h, 0:span, c : c + width] = shares_low
            context = nn(sc["qkv"][2 * D + h * HD : 2 * D + (h + 1) * HD, 0:span], shares_low)
            if student:
                sc["context"][h * HD : (h + 1) * HD, c : c + width] = context
                context = context * wide(col_ref, C_HEAD + h * HD, HD, width)
            sc["gated"][h * HD : (h + 1) * HD, c : c + width] = context.astype(bf16)
    for c, width in chunks(span):
        branch = nn(w["oT"][...], sc["gated"][:, c : c + width]) + wide(col_ref, 8 * D, D, width)
        if student:
            sc["branch"][:, c : c + width] = branch
            branch = branch * wide(col_ref, C_GH, D, width)
        hat, scale = standardise(sc["start"][:, c : c + width] + branch)
        middle = hat * wide(col_ref, 2 * D, D, width) + wide(col_ref, 3 * D, D, width)
        if student:
            sc["hat1"][:, c : c + width] = hat
            sc["scale"][1:2, c : c + width] = scale
        middle_low = middle.astype(bf16)
        if student:
            sc["middle_low"][:, c : c + width] = middle_low
        for r in range(0, FF, D):
            pre = nn(w["upT"][r : r + D, :], middle_low) + wide(col_ref, C_BUP + r, D, width)
            cdf = 0.5 * lax.erf(pre * (2.0**-0.5)) + 0.5
            act = pre * cdf
            if student:
                inner = wide(col_ref, C_GI + r, D, width)
                pdf = jnp.exp(pre * pre * -0.5) * (1.0 / math.sqrt(2.0 * math.pi))
                sc["act"][r : r + D, c : c + width] = act
                sc["slope"][r : r + D, c : c + width] = (cdf + pre * pdf) * inner
                act = act * inner
            sc["up"][r : r + D, c : c + width] = act.astype(bf16)
        down = nn(w["downT"][...], sc["up"][:, c : c + width]) + wide(col_ref, 9 * D, D, width)
        if student:
            sc["down"][:, c : c + width] = down
            down = down * wide(col_ref, C_GH, D, width)
        hat, scale = standardise(middle + down)
        out = hat * wide(col_ref, 4 * D, D, width) + wide(col_ref, 5 * D, D, width)
        if student:
            sc["hat2"][:, c : c + width] = hat
            sc["scale"][2:3, c : c + width] = scale
        sc["out"][:, c : c + width] = out


def backward_body(span, length, factor, target_ref, col_ref, w, sc, acc, add_ref, loss_ref, grad_ref, pos_add, eyes):
    def add(row, values):
        add_ref[row : row + values.shape[0], :] += lanes_in(values)

    for c, width in chunks(span):
        cols = slice(c, c + width)
        out_low = sc["out"][:, cols].astype(bf16)
        sc["out_low"][:, cols] = out_low
        differ = nn(w["aT"][...], out_low) - target_ref[0, :, cols]
        token_valid = (lax.broadcasted_iota(jnp.int32, (1, width), 1) + c < length).astype(f32)
        loss_ref[0:1, cols] += (
            jnp.sum(differ * differ, axis=0, keepdims=True) * (1.0 / D) * token_valid
        )
        d_aligned = (differ * (token_valid * factor)).astype(bf16)
        sc["d_aligned"][:, cols] = d_aligned
        d_out = nn(w["a"][...], d_aligned)
        hat = sc["hat2"][:, cols]
        add(4 * D, d_out * hat)
        add(5 * D, d_out)
        d_second = standardise_back(d_out * wide(col_ref, 4 * D, D, width), hat, sc["scale"][2:3, cols])
        add(A_GH, d_second * sc["down"][:, cols])
        d_down = (d_second * wide(col_ref, C_GH, D, width)).astype(bf16)
        sc["d_down"][:, cols] = d_down
        add(9 * D, d_down.astype(f32))
        for r in range(0, FF, D):
            d_up = nn(w["down"][r : r + D, :], d_down)
            add(A_GI + r, d_up * sc["act"][r : r + D, cols])
            d_pre = (d_up * sc["slope"][r : r + D, cols]).astype(bf16)
            sc["d_pre"][r : r + D, cols] = d_pre
            add(A_BUP + r, d_pre.astype(f32))
        d_middle = d_second + nn(w["up"][...], sc["d_pre"][:, cols])
        hat = sc["hat1"][:, cols]
        add(2 * D, d_middle * hat)
        add(3 * D, d_middle)
        d_first = standardise_back(
            d_middle * wide(col_ref, 2 * D, D, width), hat, sc["scale"][1:2, cols]
        )
        sc["d_first"][:, cols] = d_first
        add(A_GH, d_first * sc["branch"][:, cols])
        d_branch = (d_first * wide(col_ref, C_GH, D, width)).astype(bf16)
        sc["d_branch"][:, cols] = d_branch
        add(8 * D, d_branch.astype(f32))
        d_gated = nn(w["o"][...], d_branch)
        context = sc["context"][:, cols]
        add(A_HEAD, d_gated * context)
        d_context = d_gated * wide(col_ref, C_HEAD, D, width)
        sc["d_context"][:, cols] = d_context.astype(bf16)
        dot_rows = d_context * context
        for h in range(HEADS):
            sc["delta"][h : h + 1, cols] = jnp.sum(
                dot_rows[h * HD : (h + 1) * HD, :], axis=0, keepdims=True
            )
    full = slice(0, span)
    acc["a"][...] += nt(sc["out_low"][:, full], sc["d_aligned"][:, full])
    acc["down"][...] += nt(sc["up"][:, full], sc["d_down"][:, full])
    acc["up"][...] += nt(sc["middle_low"][:, full], sc["d_pre"][:, full])
    acc["o"][...] += nt(sc["gated"][:, full], sc["d_branch"][:, full])
    for h in range(HEADS):
        rows = slice(h * HD, (h + 1) * HD)
        d_value = nt(sc["d_context"][rows, full], sc["shares"][h, 0:span, 0:span])
        sc["d_qkv"][2 * D + h * HD : 2 * D + (h + 1) * HD, full] = d_value.astype(bf16)
        d_key = None
        for c, width in chunks(span):
            cols = slice(c, c + width)
            d_shares = nn(sc["v_rows"][h, 0:span, :], sc["d_context"][rows, cols])
            d_scores = (
                sc["shares"][h, 0:span, cols].astype(f32) * (d_shares - sc["delta"][h : h + 1, cols])
            ).astype(bf16)
            sc["d_qkv"][rows, cols] = (
                nn(sc["qkv"][D + h * HD : D + (h + 1) * HD, full], d_scores) * (HD**-0.5)
            ).astype(bf16)
            part = nt(sc["qkv"][rows, cols], d_scores)
            d_key = part if d_key is None else d_key + part
        sc["d_qkv"][D + h * HD : D + (h + 1) * HD, full] = (d_key * (HD**-0.5)).astype(bf16)
    acc["qkv"][...] += nt(sc["start_low"][:, full], sc["d_qkv"][:, full])
    for c, width in chunks(span):
        cols = slice(c, c + width)
        add(6 * D, sc["d_qkv"][0:D, cols].astype(f32))
        add(7 * D, sc["d_qkv"][2 * D : 3 * D, cols].astype(f32))
        d_start = sc["d_first"][:, cols] + nn(w["qkv"][...], sc["d_qkv"][:, cols])
        hat = sc["hat0"][:, cols]
        gain = wide(col_ref, 0, D, width)
        add(A_GH, d_start * (hat * gain + wide(col_ref, D, D, width)))
        d_norm = d_start * wide(col_ref, C_GH, D, width)
        add(0, d_norm * hat)
        add(D, d_norm)
        d_embedded = standardise_back(d_norm * gain, hat, sc["scale"][0:1, cols])
        pos_add[:, cols] += d_embedded
        d_low = d_embedded.astype(bf16)
        grad_ref[0, :, cols] = d_low
        sc["grad_rows"][cols, :] = nt(eyes[width], d_low)
    if span < LEN:
        grad_ref[0, :, span:LEN] = jnp.zeros((D, LEN - span), bf16)


SPANS = (256, 384, 512)


def by_span(length, body):
    for i, span in enumerate(SPANS):
        low = SPANS[i - 1] if i else 0
        test = length > low
        if i == 0:
            test = length <= span
        elif i < len(SPANS) - 1:
            test = (length > low) & (length <= span)
        pl.when(test)(functools.partial(body, span))


def set_up(pos_in, pos_ref, eyes_refs):
    for size, ref in eyes_refs.items():
        ref[...] = eye(size)
    for c in range(0, LEN, 256):
        pos_ref[:, c : c + 256] = nt(eyes_refs[256][...], pos_in[c : c + 256, :])


TEACHER_W = (("qkvT", (3 * D, D)), ("oT", (D, D)), ("upT", (FF, D)), ("downT", (D, FF)))
STUDENT_W = TEACHER_W + (
    ("aT", (D, D)),
    ("qkv", (D, 3 * D)),
    ("o", (D, D)),
    ("a", (D, D)),
    ("up", (D, FF)),
    ("down", (FF, D)),
)
TEACHER_S = (
    ("start", (D, LEN), f32),
    ("start_low", (D, LEN), bf16),
    ("qkv", (3 * D, LEN), bf16),
    ("k_rows", (HEADS, LEN, HD), bf16),
    ("gated", (D, LEN), bf16),
    ("up", (FF, LEN), bf16),
)
STUDENT_S = TEACHER_S + (
    ("hat0", (D, LEN), f32),
    ("hat1", (D, LEN), f32),
    ("hat2", (D, LEN), f32),
    ("scale", (8, LEN), f32),
    ("v_rows", (HEADS, LEN, HD), bf16),
    ("shares", (HEADS, LEN, LEN), bf16),
    ("context", (D, LEN), f32),
    ("branch", (D, LEN), f32),
    ("middle_low", (D, LEN), bf16),
    ("act", (FF, LEN), f32),
    ("slope", (FF, LEN), f32),
    ("down", (D, LEN), f32),
    ("out", (D, LEN), f32),
    ("out_low", (D, LEN), bf16),
    ("d_aligned", (D, LEN), bf16),
    ("d_down", (D, LEN), bf16),
    ("d_pre", (FF, LEN), bf16),
    ("d_first", (D, LEN), f32),
    ("d_branch", (D, LEN), bf16),
    ("d_context", (D, LEN), bf16),
    ("delta", (8, LEN), f32),
    ("d_qkv", (3 * D, LEN), bf16),
    ("grad_rows", (LEN, D), f32),
)
ACCS = (
    ("qkv", (D, 3 * D)),
    ("o", (D, D)),
    ("a", (D, D)),
    ("up", (D, FF)),
    ("down", (FF, D)),
)


def teacher_kernel(len_ref, off_ref, rows_ref, pos_in, col_ref, *rest):
    w = {name: rest[i] for i, (name, _) in enumerate(TEACHER_W)}
    out_ref = rest[len(TEACHER_W)]
    scratch = rest[len(TEACHER_W) + 1 :]
    sc = {entry[0]: scratch[i] for i, entry in enumerate(TEACHER_S)}
    pos_ref, eye_one, eye_two = scratch[len(TEACHER_S) :]
    s = pl.program_id(0)
    sc["out"] = out_ref.at[0]

    @pl.when(s == 0)
    def _():
        set_up(pos_in, pos_ref, {128: eye_one, 256: eye_two})

    eyes = {128: eye_one, 256: eye_two}

    class Read:
        def __getitem__(self, size):
            return eyes[size][...]

    length = len_ref[s]

    def body(span):
        offset = pl.multiple_of(off_ref[s], 16)
        forward_body(span, offset, length, False, rows_ref, pos_ref, col_ref, w, sc, Read())

    by_span(length, body)


def student_kernel(flat_len, len_ref, off_ref, slot_ref, fac_ref, rows_ref, pos_in, target_ref, col_ref, slope_in, lag_in, *rest):
    w = {name: rest[i] for i, (name, _) in enumerate(STUDENT_W)}
    rest = rest[len(STUDENT_W) :]
    flat_ref, grad_ref, packed_ref, loss_ref = rest[:4]
    scratch = rest[4:]
    sc = {entry[0]: scratch[i] for i, entry in enumerate(STUDENT_S)}
    scratch = scratch[len(STUDENT_S) :]
    acc = {entry[0]: scratch[i] for i, entry in enumerate(ACCS)}
    add_ref, pos_add, slots_f32, pos_ref, eye_one, eye_two = scratch[len(ACCS) :]
    s = pl.program_id(0)

    @pl.when(s == 0)
    def _():
        set_up(pos_in, pos_ref, {128: eye_one, 256: eye_two})
        for ref in list(acc.values()) + [add_ref, pos_add, loss_ref, slots_f32]:
            ref[...] = jnp.zeros(ref.shape, f32)

    eyes = {128: eye_one, 256: eye_two}

    class Read:
        def __getitem__(self, size):
            return eyes[size][...]

    length = len_ref[s]

    def body(span):
        offset = pl.multiple_of(off_ref[s], 16)
        forward_body(span, offset, length, True, rows_ref, pos_ref, col_ref, w, sc, Read())
        backward_body(
            span, length, fac_ref[0], target_ref, col_ref, w, sc, acc, add_ref, loss_ref, grad_ref, pos_add, Read()
        )

    by_span(length, body)

    def place(step, carry):
        for u in range(8):
            at = step * 8 + u
            slot = slot_ref[s, at]
            slots_f32[pl.ds(slot, 1), :] = sc["grad_rows"][pl.ds(at, 1), :]
        return carry

    lax.fori_loop(0, (length + 7) // 8, place, 0)

    @pl.when(s == pl.num_programs(0) - 1)
    def _():
        for i in range(3):
            for j in range(2):
                at = i * D + j * LANES
                flat_ref[pl.ds(512 * i + j, D, stride=2), :] = acc["qkv"][:, at : at + LANES]
        for j in range(2):
            lanes = slice(j * LANES, (j + 1) * LANES)
            flat_ref[pl.ds(512 * 3 + j, D, stride=2), :] = acc["o"][:, lanes]
            flat_ref[pl.ds(512 * 4 + j, D, stride=2), :] = acc["a"][:, lanes]
            flat_ref[pl.ds(R_DOWN + j, FF, stride=2), :] = acc["down"][:, lanes]
        for j in range(8):
            flat_ref[pl.ds(R_UP + j, D, stride=8), :] = acc["up"][:, j * LANES : (j + 1) * LANES]
        ones = jnp.ones((8, LANES), f32)

        def summed(row, rows):
            return lax.dot_general(
                ones,
                add_ref[row : row + rows, :],
                (((1,), (1,)), ((), ())),
                preferred_element_type=f32,
                precision=lax.Precision.HIGHEST,
            )

        for i in range(10):
            sums = summed(i * D, D)
            for j in range(2):
                flat_ref[R_VEC + 2 * i + j : R_VEC + 2 * i + j + 1, :] = sums[
                    0:1, j * LANES : (j + 1) * LANES
                ]
        sums = summed(A_BUP, FF)
        for j in range(8):
            flat_ref[R_BUP + j : R_BUP + j + 1, :] = sums[0:1, j * LANES : (j + 1) * LANES]
        hidden = summed(A_GH, D)
        group = (
            lax.broadcasted_iota(jnp.int32, (D, LANES), 0) // HD
            == lax.broadcasted_iota(jnp.int32, (D, LANES), 1)
        ).astype(f32)
        heads = jnp.dot(
            summed(A_HEAD, D), group, preferred_element_type=f32, precision=lax.Precision.HIGHEST
        )
        inner = summed(A_GI, FF)
        moved = pltpu.roll(jnp.concatenate([inner, jnp.zeros((8, LANES), f32)], axis=1), HEADS, 1)
        lane = lax.broadcasted_iota(jnp.int32, (8, LANES), 1)
        first = jnp.where(lane < HEADS, heads, moved[:, :LANES])
        tail = [hidden[:, :LANES], hidden[:, LANES:], first] + [
            moved[:, j * LANES : (j + 1) * LANES] for j in range(1, 9)
        ]
        for j, piece in enumerate(tail):
            flat_ref[R_LOGIT + j : R_LOGIT + j + 1, :] = (
                piece[0:1] * slope_in[j : j + 1, :] + lag_in[j : j + 1, :]
            )
        flat_ref[R_USED:flat_len, :] = jnp.zeros((flat_len - R_USED, LANES), f32)
        for j in range(2):
            flat_ref[pl.ds(flat_len + j, LEN, stride=2), :] = jnp.transpose(
                pos_add[j * LANES : (j + 1) * LANES, :]
            )
        packed_ref[...] = slots_f32[0 : packed_ref.shape[0], :].astype(bf16)


def whole_spec():
    return pl.BlockSpec(memory_space=pltpu.VMEM)


def smem_spec():
    return pl.BlockSpec(memory_space=pltpu.SMEM)


def seq_spec():
    return pl.BlockSpec((1, D, LEN), lambda s: (s, 0, 0))


def extra_scratch():
    return [
        pltpu.VMEM((D, LEN), f32),
        pltpu.VMEM((128, 128), bf16),
        pltpu.VMEM((256, 256), bf16),
    ]


def run_teacher(lengths, offsets, rows, places, columns, weights):
    seqs = lengths.shape[0]
    return pl.pallas_call(
        teacher_kernel,
        grid=(seqs,),
        out_shape=jax.ShapeDtypeStruct((seqs, D, LEN), f32),
        in_specs=[smem_spec(), smem_spec()] + [whole_spec()] * (3 + len(TEACHER_W)),
        out_specs=seq_spec(),
        scratch_shapes=[pltpu.VMEM(shape, kind) for _, shape, kind in TEACHER_S] + extra_scratch(),
        compiler_params=pltpu.CompilerParams(vmem_limit_bytes=VMEM_LIMIT),
        name="teacher",
    )(lengths, offsets, rows, places, columns, *[weights[name] for name, _ in TEACHER_W])


def run_student(
    lengths, offsets, slots, factor, rows, places, target, columns, slopes, lag, weights, flat_len, slot_rows
):
    seqs = lengths.shape[0]
    return pl.pallas_call(
        functools.partial(student_kernel, flat_len),
        grid=(seqs,),
        out_shape=(
            jax.ShapeDtypeStruct((flat_len + 2 * LEN, LANES), f32),
            jax.ShapeDtypeStruct((seqs, D, LEN), bf16),
            jax.ShapeDtypeStruct((slot_rows, D), bf16),
            jax.ShapeDtypeStruct((8, LEN), f32),
        ),
        in_specs=[smem_spec()] * 4
        + [whole_spec()] * 2
        + [seq_spec()]
        + [whole_spec()] * (3 + len(STUDENT_W)),
        out_specs=(
            pl.BlockSpec((flat_len + 2 * LEN, LANES), lambda s: (0, 0)),
            seq_spec(),
            pl.BlockSpec((slot_rows, D), lambda s: (0, 0)),
            pl.BlockSpec((8, LEN), lambda s: (0, 0)),
        ),
        scratch_shapes=[pltpu.VMEM(shape, kind) for _, shape, kind in STUDENT_S]
        + [pltpu.VMEM(shape, f32) for _, shape in ACCS]
        + [
            pltpu.VMEM((A_ROWS, LANES), f32),
            pltpu.VMEM((D, LEN), f32),
            pltpu.VMEM((slot_rows + 8, D), f32),
        ]
        + extra_scratch(),
        compiler_params=pltpu.CompilerParams(vmem_limit_bytes=VMEM_LIMIT),
        name="student",
    )(
        lengths,
        offsets,
        slots,
        factor,
        rows,
        places,
        target,
        columns,
        slopes,
        lag,
        *[weights[name] for name, _ in STUDENT_W],
    )


MESH = pl.DeviceIdType.MESH


def room(n):
    return min(LANES, max(32, 8 * LEN // n))


def greet_all(me, n):
    barrier = pltpu.get_barrier_semaphore()

    def signal(k, carry):
        pl.semaphore_signal(barrier, inc=1, device_id=(me ^ k,), device_id_type=MESH)
        return carry

    lax.fori_loop(1, n, signal, 0)
    pl.semaphore_wait(barrier, n - 1)


def copy_to(source, target, send, receive, device):
    return pltpu.make_async_remote_copy(
        src_ref=source,
        dst_ref=target,
        send_sem=send,
        recv_sem=receive,
        device_id=(device,),
        device_id_type=MESH,
    )


def route_kernel(n, owner_ref, local_ref, stat_ref, slot_ref, got_ref, tile_ref, send_sem, recv_sem):
    me = lax.axis_index("dp")
    cap = room(n)
    seqs = owner_ref.shape[0]
    upper = (
        lax.broadcasted_iota(jnp.int32, (256, 256), 0)
        <= lax.broadcasted_iota(jnp.int32, (256, 256), 1)
    ).astype(bf16)
    base = jnp.zeros((n, 1), f32)
    listed = jnp.zeros((n, LANES), f32)
    for s in range(seqs):
        for c in range(0, LEN, 256):
            owner = owner_ref[s : s + 1, c : c + 256]
            mine = (lax.broadcasted_iota(jnp.int32, (n, 256), 0) == owner).astype(f32)
            before = nn(mine.astype(bf16), upper)
            rank = jnp.sum(mine * (before - 1.0 + base), axis=0, keepdims=True).astype(jnp.int32)
            fits = (owner >= 0) & (rank < cap)
            slot_ref[s : s + 1, c : c + 256] = jnp.where(fits, owner * cap + rank, n * cap)
            place = (
                lax.broadcasted_iota(jnp.int32, (LANES, 256), 0) == jnp.where(fits, rank, -1)
            ).astype(f32)
            listed = listed + lax.dot_general(
                mine * local_ref[s : s + 1, c : c + 256],
                place,
                (((1,), (1,)), ((), ())),
                preferred_element_type=f32,
                precision=lax.Precision.HIGHEST,
            )
            base = base + before[:, 255:256]
    over = jnp.max(base, axis=0, keepdims=True) > cap
    lane = lax.broadcasted_iota(jnp.int32, (n, LANES), 1)
    tile_ref[...] = jnp.zeros(tile_ref.shape, jnp.int32)
    tile_ref[pl.ds(0, n, stride=8), :] = (listed + 0.5).astype(jnp.int32) - 1
    tile_ref[pl.ds(1, n, stride=8), :] = jnp.where(
        lane == 0, stat_ref[0], jnp.where(lane == 1, over.astype(jnp.int32), 0)
    )
    greet_all(me, n)

    def tile(ref, i):
        return ref.at[pl.ds(pl.multiple_of(i * 8, 8), 8), :]

    def copy(k):
        return copy_to(
            tile(tile_ref, me ^ k), tile(got_ref, me), send_sem.at[k], recv_sem.at[k], me ^ k
        )

    def start(k, carry):
        copy(k).start()
        return carry

    def finish(k, carry):
        copy(k).wait()
        return carry

    lax.fori_loop(1, n, start, 0)
    own = pl.ds(pl.multiple_of(me * 8, 8), 8)
    got_ref[own, :] = tile_ref[own, :]
    lax.fori_loop(1, n, finish, 0)


def run_route(n, owner, local, stat):
    return pl.pallas_call(
        functools.partial(route_kernel, n),
        out_shape=(
            jax.ShapeDtypeStruct(owner.shape, jnp.int32),
            jax.ShapeDtypeStruct((8 * n, LANES), jnp.int32),
        ),
        in_specs=[whole_spec(), whole_spec(), smem_spec()],
        out_specs=(whole_spec(), whole_spec()),
        scratch_shapes=[
            pltpu.VMEM((8 * n, LANES), jnp.int32),
            pltpu.SemaphoreType.DMA((n,)),
            pltpu.SemaphoreType.DMA((n,)),
        ],
        compiler_params=pltpu.CompilerParams(
            collective_id=1, has_side_effects=True, vmem_limit_bytes=VMEM_LIMIT
        ),
        name="route",
    )(owner, local, stat)


def plan(n, flat_len):
    chips = n // 2
    plane = 2 ** ((chips.bit_length() - 1) // 2)
    flat_seg = flat_len // n
    flat_pad = -(-flat_seg // 16) * 16
    place_seg = 2 * LEN // n
    return plane, chips // plane, flat_seg, flat_pad, place_seg, flat_pad + -(-place_seg // 16) * 16


def place_tile(n):
    return max(8, 2 * LEN // n)


def exchange_kernel(n, flat_len, sparse, *refs):
    plane, planes, flat_seg, flat_pad, place_seg, seg = plan(n, flat_len)
    chips = n // 2
    cap = room(n)
    tile = place_tile(n)
    flat_ref, loss_ref = refs[:2]
    refs = refs[2:]
    if sparse:
        packed_ref, list_ref = refs[:2]
        refs = refs[2:]
    else:
        given_ref = refs[0]
        refs = refs[1:]
    table_ref, sums_ref, stat_out = refs[:3]
    (stage, one_in, two_out, two_in, total, three_out, three_in, place_in, stat_in) = refs[3:12]
    refs = refs[12:]
    if sparse:
        rows_in = refs[0]
        refs = refs[1:]
    one_sem, two_sem, three_sem, place_sem, stat_sem, row_sem = refs
    me = lax.axis_index("dp")
    core = lax.rem(me, 2)
    chip = me // 2
    mid = lax.rem(chip, plane)
    high = chip // plane
    vrows = table_ref.shape[0]

    greet_all(me, n)
    pad = jnp.zeros((16, LANES), f32)
    for o in range(n):
        spot = stage.at[o % 2, o // 2]
        if flat_pad > flat_seg:
            spot[flat_pad - 16 : flat_pad, :] = pad
        if seg > flat_pad + place_seg:
            spot[seg - 16 : seg, :] = pad
        spot[0:flat_seg, :] = flat_ref[o * flat_seg : (o + 1) * flat_seg, :]
        at = flat_len + o * place_seg
        spot[flat_pad : flat_pad + place_seg, :] = flat_ref[at : at + place_seg, :]
    first = copy_to(stage.at[1 - core], one_in, one_sem.at[0], one_sem.at[1], me ^ 1)
    first.start()

    if sparse:

        def bucket(ref, i):
            return ref.at[pl.ds(pl.multiple_of(i * cap, cap), cap), :]

        def row_copy(k):
            return copy_to(
                bucket(packed_ref, me ^ k), bucket(rows_in, me), row_sem.at[0, k], row_sem.at[1, k], me ^ k
            )

        def start_row(i, carry):
            row_copy(n - i).start()
            return carry

        lax.fori_loop(1, n, start_row, 0)
        own = pl.ds(pl.multiple_of(me * cap, cap), cap)
        rows_in[own, :] = packed_ref[own, :]

    first.wait()
    for m in range(plane):
        for h in range(planes):
            c = h * plane + m
            two_out[m, h] = (stage[core, c] + one_in[c]).astype(bf16)
    second = []
    for k in range(1, plane):
        m = lax.rem(mid + k, plane)
        second.append(
            copy_to(
                two_out.at[m],
                two_in.at[k - 1],
                two_sem.at[0, k],
                two_sem.at[1, k],
                (high * plane + m) * 2 + core,
            )
        )
        second[-1].start()
    for copy in second:
        copy.wait()
    for h in range(planes):
        c = h * plane + mid
        value = stage[core, c] + one_in[c]
        for k in range(1, plane):
            value = value + two_in[k - 1, h].astype(f32)
        total[h] = value
        three_out[h] = value.astype(bf16)
    third = []
    for k in range(1, planes):
        h = lax.rem(high + k, planes)
        third.append(
            copy_to(
                three_out.at[h],
                three_in.at[k - 1],
                three_sem.at[0, k],
                three_sem.at[1, k],
                (h * plane + mid) * 2 + core,
            )
        )
        third[-1].start()
    for copy in third:
        copy.wait()
    value = total[high]
    for k in range(1, planes):
        value = value + three_in[k - 1].astype(f32)
    total[0] = value
    sums_ref[...] = value[:flat_pad]

    owners = range(VOCAB // vrows, (VOCAB + LEN - 1) // vrows + 1)
    place_out = total.at[0, pl.ds(flat_pad, tile), :]
    place_spot = pl.ds(pl.multiple_of(me * tile, 8), tile)
    for i, o in enumerate(owners):
        place_copy = copy_to(
            place_out, place_in.at[place_spot, :], place_sem.at[0, i], place_sem.at[1, me], o
        )
        pl.when(me != o)(place_copy.start)

    squares = jnp.sum(jnp.sum(value * value, axis=0, keepdims=True), axis=1, keepdims=True)
    if sparse:
        def add_pair(i, carry):
            pl.when(i > 0)(lambda: row_copy(2 * i).wait_recv())
            row_copy(2 * i + 1).wait_recv()
            a = chip ^ i
            lists = jnp.concatenate(
                [
                    list_ref[pl.ds(pl.multiple_of(a * 16 + 8 * j, 8), 8), :][0:1, :cap]
                    for j in range(2)
                ],
                axis=1,
            )
            pick = (lax.broadcasted_iota(jnp.int32, (vrows, 2 * cap), 0) == lists).astype(bf16)
            both = rows_in[pl.ds(pl.multiple_of(a * 2 * cap, 2 * cap), 2 * cap), :]
            table_ref[...] += nn(pick, both)
            return carry

        table_ref[...] = jnp.zeros(table_ref.shape, f32)
        lax.fori_loop(0, chips, add_pair, 0)
    else:
        table_ref[...] = given_ref[...]
    grads = table_ref[...]
    squares = squares + jnp.sum(
        jnp.sum(grads * grads, axis=0, keepdims=True), axis=1, keepdims=True
    )
    loss = jnp.sum(jnp.sum(loss_ref[...], axis=0, keepdims=True), axis=1, keepdims=True)
    lane = lax.broadcasted_iota(jnp.int32, (8, LANES), 1)
    stat_out[...] = jnp.where(lane == 0, squares, jnp.where(lane == 1, loss, 0.0))

    def stat_copy(k):
        return copy_to(
            stat_out, stat_in.at[me], stat_sem.at[0, k], stat_sem.at[1, k], me ^ k
        )

    def start_stat(k, carry):
        stat_copy(k).start()
        return carry

    def finish_stat(k, carry):
        stat_copy(k).wait()
        return carry

    lax.fori_loop(1, n, start_stat, 0)
    stat_in[me] = stat_out[...]

    for i, o in enumerate(owners):

        @pl.when(me == o)
        def _():
            place_in[place_spot, :] = place_out[...]

            def wait_place(j, carry):
                copy_to(
                    place_out,
                    place_in.at[pl.ds(pl.multiple_of(j * tile, 8), tile), :],
                    place_sem.at[0, i],
                    place_sem.at[1, j],
                    me ^ 1,
                ).wait_recv()
                return carry

            lax.fori_loop(0, o, wait_place, 0)
            lax.fori_loop(o + 1, n, wait_place, 0)
            low = max(0, o * vrows - VOCAB)
            top = min(LEN, (o + 1) * vrows - VOCAB)
            at = VOCAB + low - o * vrows
            if tile > place_seg:
                for d in range(n):
                    place_in[d * place_seg : (d + 1) * place_seg, :] = place_in[
                        d * tile : d * tile + place_seg, :
                    ]
            for j in range(2):
                table_ref[at : at + top - low, j * LANES : (j + 1) * LANES] += place_in[
                    pl.ds(2 * low + j, top - low, stride=2), :
                ]

    lax.fori_loop(1, n, finish_stat, 0)
    stat_out[...] = jnp.sum(stat_in[...], axis=0)
    for i, o in enumerate(owners):
        place_copy = copy_to(
            place_out, place_in.at[place_spot, :], place_sem.at[0, i], place_sem.at[1, me], o
        )
        pl.when(me != o)(place_copy.wait_send)
    if sparse:

        def finish_row(k, carry):
            row_copy(k).wait_send()
            return carry

        lax.fori_loop(1, n, finish_row, 0)


def run_exchange(n, vrows, flat_grads, loss_rows, sparse, given):
    flat_len = flat_grads.shape[0] - 2 * LEN
    plane, planes, flat_seg, flat_pad, place_seg, seg = plan(n, flat_len)
    count = len(range(VOCAB // vrows, (VOCAB + LEN - 1) // vrows + 1))
    dma = pltpu.SemaphoreType.DMA
    return pl.pallas_call(
        functools.partial(exchange_kernel, n, flat_len, sparse),
        out_shape=(
            jax.ShapeDtypeStruct((vrows, D), f32),
            jax.ShapeDtypeStruct((flat_pad, LANES), f32),
            jax.ShapeDtypeStruct((8, LANES), f32),
        ),
        in_specs=[whole_spec()] * (2 + len(given)),
        out_specs=(whole_spec(),) * 3,
        scratch_shapes=[
            pltpu.VMEM((2, n // 2, seg, LANES), f32),
            pltpu.VMEM((n // 2, seg, LANES), f32),
            pltpu.VMEM((plane, planes, seg, LANES), bf16),
            pltpu.VMEM((plane - 1, planes, seg, LANES), bf16),
            pltpu.VMEM((planes, seg, LANES), f32),
            pltpu.VMEM((planes, seg, LANES), bf16),
            pltpu.VMEM((planes - 1, seg, LANES), bf16),
            pltpu.VMEM((n * place_tile(n), LANES), f32),
            pltpu.VMEM((n, 8, LANES), f32),
        ]
        + ([pltpu.VMEM((n * room(n), D), bf16)] if sparse else [])
        + [dma((2,)), dma((2, plane)), dma((2, planes)), dma((2, max(n, count))), dma((2, n)), dma((2, n))],
        compiler_params=pltpu.CompilerParams(
            collective_id=2 if sparse else 3, has_side_effects=True, vmem_limit_bytes=VMEM_LIMIT
        ),
        name="exchange" if sparse else "exchange_dense",
    )(flat_grads, loss_rows, *given)


clip_norm = 0.002
learn_rate = 0.015
beta_one = 0.9
beta_two = 0.999
adam_eps = 1e-08
decay_rate = 0.01
sparse_target = 0.3
ADAM_STEP = 10
relaxation_heat = 2.0 / 3.0
widened_left_limit = -0.1
widened_right_limit = 1.1


def layout(student):
    square = (D, D)
    entries = [("w_query", square), ("w_key", square), ("w_value", square), ("w_output", square)]
    if student:
        entries = entries + [("w_align", square)]
    entries = entries + [
        ("w_up", (D, FF)),
        ("w_down", (FF, D)),
        ("vectors", (10, D)),
        ("b_up", (FF,)),
    ]
    if student:
        entries = entries + [("gate_logits", (D + HEADS + FF,))]
    return entries


def unpack(flat_vector, student):
    pieces = {}
    offset = 0
    for entry_name, entry_shape in layout(student):
        length = math.prod(entry_shape)
        pieces[entry_name] = flat_vector[offset : offset + length].reshape(entry_shape)
        offset = offset + length
    return pieces


def gate_values(mask_logodds, flat_random_sample):
    logistic_function = jax.nn.sigmoid(
        (jnp.log(flat_random_sample) - jnp.log(1.0 - flat_random_sample) + mask_logodds)
        / relaxation_heat
    )
    return jnp.clip(
        logistic_function * (widened_right_limit - widened_left_limit) + widened_left_limit,
        0.0,
        1.0,
    )


def lagrangian(mask_logodds, lagrange):
    survival_probability = jax.nn.sigmoid(
        mask_logodds - relaxation_heat * math.log(-widened_left_limit / widened_right_limit)
    )
    kept_hidden = jnp.mean(survival_probability[:D])
    kept_rest = 4.0 * HD * jnp.sum(survival_probability[D : D + HEADS]) + 2.0 * jnp.sum(
        survival_probability[D + HEADS :]
    )
    expected = kept_hidden * kept_rest / (4.0 * D + 2.0 * FF)
    excess = expected - sparse_target
    return lagrange[0] * excess + lagrange[1] * excess * excess


def adam_step(weight, first_old, second, clipped):
    first_new = beta_one * first_old + (1.0 - beta_one) * clipped
    second_new = beta_two * second + (1.0 - beta_two) * clipped * clipped
    first_hat = first_new / (1.0 - beta_one**ADAM_STEP)
    second_hat = second_new / (1.0 - beta_two**ADAM_STEP)
    weight_new = weight - learn_rate * (
        first_hat / (jnp.sqrt(second_hat) + adam_eps) + decay_rate * weight
    )
    return (weight_new, first_new, second_new)


def kernel_weights(pieces, student):
    w = {}
    w["qkv"] = jnp.concatenate([pieces["w_query"], pieces["w_key"], pieces["w_value"]], axis=1)
    w["qkvT"] = w["qkv"].T
    for name, source in (("o", "w_output"), ("up", "w_up"), ("down", "w_down")):
        w[name] = pieces[source]
        w[name + "T"] = pieces[source].T
    if student:
        w["a"] = pieces["w_align"]
        w["aT"] = w["a"].T
    return w


def columns_of(pieces, gates=None):
    vectors = pieces["vectors"].astype(f32).reshape(-1)
    bias = pieces["b_up"].astype(f32)
    if gates is None:
        gates = jnp.ones((D + HEADS + FF,), f32)
    parts = [vectors, gates[:D], jnp.repeat(gates[D : D + HEADS], HD), bias, gates[D + HEADS :]]
    column = jnp.concatenate(parts)
    return jnp.broadcast_to(column[:, None], (column.shape[0], LANES))


def pad_rows(values):
    return jnp.pad(values, (0, 16 * LANES - values.shape[0])).reshape(16, LANES)


def rows_of(table, ids):
    return table.at[ids.reshape(-1)].get(mode="promise_in_bounds")


def per_device(
    devices,
    token_ids,
    lengths,
    gate_noise,
    lagrange,
    teacher_table,
    teacher_flat,
    word_table,
    table_first,
    table_second,
    layer_flat,
    flat_first,
    flat_second,
):
    seqs = token_ids.shape[0]
    half = seqs // 2
    vrows = word_table.shape[0]
    flat_len = layer_flat.shape[0] * devices // LANES
    own = layer_flat.shape[0]
    own_rows = -(-own // D)
    pad = -(vrows + own_rows) % 16
    block = vrows + own_rows + pad
    shard = jnp.concatenate(
        [
            word_table.astype(bf16),
            jnp.pad(layer_flat.astype(bf16), (0, own_rows * D - own)).reshape(own_rows, D),
            jnp.zeros((pad, D), bf16),
        ]
    )
    gathered = lax.all_gather(shard, "dp", axis=0, tiled=True)

    mates = [(i, devices - 1 - i) for i in range(devices)]
    sent = jnp.concatenate(
        [token_ids[half:], jnp.pad(lengths[half:], (0, LEN - half)).reshape(1, LEN)]
    )
    got = lax.ppermute(sent, "dp", mates)
    ids = jnp.concatenate([token_ids[:half], got[:half]])
    lens = jnp.concatenate([lengths[:half], got[half, :half]])
    offsets = jnp.arange(seqs, dtype=jnp.int32) * LEN

    owner = ids // vrows
    valid = jnp.arange(LEN)[None, :] < lens[:, None]
    slots, listed = run_route(
        devices,
        jnp.where(valid, owner, -1),
        (ids - owner * vrows + 1).astype(f32),
        jnp.sum(lens).reshape(1),
    )
    stats = listed.reshape(devices, 8, LANES)[:, 1, :2]
    global_count = jnp.sum(stats[:, 0]).astype(f32)
    crowded = jnp.max(stats[:, 1]) > 0
    factor = ((2.0 / D) / global_count).reshape(1)

    teacher = unpack(teacher_flat, False)
    target = run_teacher(
        lens,
        offsets,
        rows_of(teacher_table, ids),
        teacher_table[VOCAB : VOCAB + LEN],
        columns_of(teacher),
        kernel_weights(teacher, False),
    )

    blocks = gathered.reshape(devices, block, D)
    flat_low = blocks[:, vrows : vrows + own_rows].reshape(devices, -1)[:, :own].reshape(-1)
    pieces = unpack(flat_low, True)
    logits = pieces["gate_logits"].astype(f32)
    gates, gate_back = jax.vjp(lambda x: gate_values(x, gate_noise), logits)
    slopes = gate_back(jnp.ones_like(gates))[0]
    lag_value, lag_back = jax.vjp(lambda x: lagrangian(x, lagrange), logits)
    lag_weight = jnp.where(lax.axis_index("dp") == 0, 1.0, 0.0).astype(f32)
    places = []
    for o in range(VOCAB // vrows, (VOCAB + LEN - 1) // vrows + 1):
        low, top = max(VOCAB, o * vrows), min(VOCAB + LEN, (o + 1) * vrows)
        places.append(gathered[o * (block - vrows) + low : o * (block - vrows) + top])
    flat_grads, grad_rows, packed, loss_rows = run_student(
        lens,
        offsets,
        slots,
        factor,
        rows_of(gathered, ids + owner * (block - vrows)),
        jnp.concatenate(places) if len(places) > 1 else places[0],
        target,
        columns_of(pieces, gates),
        pad_rows(slopes),
        pad_rows(lag_back(lag_weight)[0]),
        kernel_weights(pieces, True),
        flat_len,
        devices * room(devices),
    )

    def from_slots(_):
        return run_exchange(devices, vrows, flat_grads, loss_rows, True, (packed, listed))

    def from_rows(_):
        updates = jnp.transpose(grad_rows, (0, 2, 1)).reshape(seqs * LEN, D).astype(f32)
        table = jnp.zeros((devices * vrows, D), f32).at[ids.reshape(-1)].add(updates)
        table = lax.psum_scatter(table, "dp", scatter_dimension=0, tiled=True)
        return run_exchange(devices, vrows, flat_grads, loss_rows, False, (table,))

    table_grad, sums, totals = lax.cond(crowded, from_rows, from_slots, 0)
    flat_grad = sums[: own // LANES].reshape(-1)
    grad_norm = jnp.sqrt(totals[0, 0])
    clip = jnp.minimum(1.0, clip_norm / (grad_norm + 1e-06))
    total_loss = totals[0, 1] / global_count + lag_value
    table_new = adam_step(word_table, table_first, table_second, table_grad * clip)
    flat_new = adam_step(layer_flat, flat_first, flat_second, flat_grad * clip)
    return (*table_new, *flat_new, total_loss, grad_norm)


def solution(mesh):
    row, flat, copied = P("dp", None), P("dp"), P()
    in_specs = (row, flat, copied, copied, copied, copied, row, row, row, flat, flat, flat)
    out_specs = (row, row, row, flat, flat, flat, copied, copied)
    return jax.shard_map(
        functools.partial(per_device, mesh.shape["dp"]),
        mesh=mesh,
        in_specs=in_specs,
        out_specs=out_specs,
        check_vma=False,
    )
```

```python
import functools
import math

import jax
import jax.numpy as jnp
from jax import lax
from jax.experimental import pallas as pl
from jax.experimental.pallas import tpu as pltpu
from jax.sharding import PartitionSpec as P

D = 256
HEADS = 4
HD = D // HEADS
FF = 1024
LEN = 512
VOCAB = 30522
NPAR = 856836
LANES = 128
norm_eps = 1e-12
clip_norm = 0.002
learn_rate = 0.015
beta_one = 0.9
beta_two = 0.999
adam_eps = 1e-08
decay_rate = 0.01
sparse_target = 0.3
ADAM_STEP = 10
relaxation_heat = 2.0 / 3.0
widened_left_limit = -0.1
widened_right_limit = 1.1
f32 = jnp.float32
bf16 = jnp.bfloat16
VMEM_LIMIT = 60 * 2**20

C_GH = 10 * D
C_HEAD = 11 * D
C_BUP = 12 * D
C_GI = 12 * D + FF
C_ROWS = 12 * D + 2 * FF
A_BUP = 10 * D
A_GH = 10 * D + FF
A_HEAD = 11 * D + FF
A_GI = 12 * D + FF
A_ROWS = 12 * D + 2 * FF
R_UP = 5 * 512
R_DOWN = R_UP + 2048
R_VEC = R_DOWN + 2048
R_BUP = R_VEC + 20
R_LOGIT = R_BUP + 8
R_USED = R_LOGIT + 11


def nn(left, right):
    return jnp.dot(left, right, preferred_element_type=f32)


def nt(left, right):
    return lax.dot_general(left, right, (((1,), (1,)), ((), ())), preferred_element_type=f32)


def chunks(span):
    return [(c, min(256, span - c)) for c in range(0, span, 256)]


def wide(col_ref, row, rows, width):
    col = col_ref[row : row + rows, :]
    return jnp.concatenate([col] * (width // LANES), axis=1) if width > LANES else col


def lanes_in(values):
    total = values[:, :LANES]
    for c in range(LANES, values.shape[1], LANES):
        total = total + values[:, c : c + LANES]
    return total


def eye(size):
    return (
        lax.broadcasted_iota(jnp.int32, (size, size), 0)
        == lax.broadcasted_iota(jnp.int32, (size, size), 1)
    ).astype(bf16)


def standardise(x):
    mean = jnp.sum(x, axis=0, keepdims=True) * (1.0 / D)
    centred = x - mean
    variance = jnp.sum(centred * centred, axis=0, keepdims=True) * (1.0 / D)
    scale = lax.rsqrt(variance + norm_eps)
    return centred * scale, scale


def standardise_back(dx, hat, scale):
    mean_one = jnp.sum(dx, axis=0, keepdims=True) * (1.0 / D)
    mean_two = jnp.sum(dx * hat, axis=0, keepdims=True) * (1.0 / D)
    return scale * (dx - mean_one - hat * mean_two)


def gelu_parts(x):
    half_erf = 0.5 * lax.erf(x * (2.0**-0.5)) + 0.5
    return half_erf


def forward_body(span, length, student, embed, pos_ref, col_ref, w, sc, eyes):
    for c, width in chunks(span):
        embedded = embed(c, width) + pos_ref[:, c : c + width]
        hat, scale = standardise(embedded)
        start = hat * wide(col_ref, 0, D, width) + wide(col_ref, D, D, width)
        if student:
            sc["hat0"][:, c : c + width] = hat
            sc["scale"][0:1, c : c + width] = scale
            start = start * wide(col_ref, C_GH, D, width)
        sc["start"][:, c : c + width] = start
        start_low = start.astype(bf16)
        sc["start_low"][:, c : c + width] = start_low
        factor = HD**-0.5
        q = nn(w["qkvT"][0:D, :], start_low) + wide(col_ref, 6 * D, D, width)
        sc["qkv"][0:D, c : c + width] = q.astype(bf16)
        k = nn(w["qkvT"][D : 2 * D, :], start_low).astype(bf16)
        sc["qkv"][D : 2 * D, c : c + width] = k
        v = (nn(w["qkvT"][2 * D : 3 * D, :], start_low) + wide(col_ref, 7 * D, D, width)).astype(
            bf16
        )
        sc["qkv"][2 * D : 3 * D, c : c + width] = v
        for h in range(HEADS):
            sc["k_rows"][h, c : c + width, :] = nt(eyes[width], k[h * HD : (h + 1) * HD, :]).astype(
                bf16
            )
            if student:
                sc["v_rows"][h, c : c + width, :] = nt(
                    eyes[width], v[h * HD : (h + 1) * HD, :]
                ).astype(bf16)
    for c, width in chunks(span):
        valid = lax.broadcasted_iota(jnp.int32, (span, width), 0) < length
        for h in range(HEADS):
            q_h = sc["qkv"][h * HD : (h + 1) * HD, c : c + width] * bf16(HD**-0.5)
            scores = jnp.where(valid, nn(sc["k_rows"][h, 0:span, :], q_h), -1e30)
            shares = jnp.exp(scores - jnp.max(scores, axis=0, keepdims=True))
            shares_low = (shares * (1.0 / jnp.sum(shares, axis=0, keepdims=True))).astype(bf16)
            if student:
                sc["shares"][h, 0:span, c : c + width] = shares_low
            context = nn(sc["qkv"][2 * D + h * HD : 2 * D + (h + 1) * HD, 0:span], shares_low)
            if student:
                sc["context"][h * HD : (h + 1) * HD, c : c + width] = context
                context = context * wide(col_ref, C_HEAD + h * HD, HD, width)
            sc["gated"][h * HD : (h + 1) * HD, c : c + width] = context.astype(bf16)
    for c, width in chunks(span):
        branch = nn(w["oT"][...], sc["gated"][:, c : c + width]) + wide(col_ref, 8 * D, D, width)
        if student:
            sc["branch"][:, c : c + width] = branch
            branch = branch * wide(col_ref, C_GH, D, width)
        hat, scale = standardise(sc["start"][:, c : c + width] + branch)
        middle = hat * wide(col_ref, 2 * D, D, width) + wide(col_ref, 3 * D, D, width)
        if student:
            sc["hat1"][:, c : c + width] = hat
            sc["scale"][1:2, c : c + width] = scale
        middle_low = middle.astype(bf16)
        if student:
            sc["middle_low"][:, c : c + width] = middle_low
        for r in range(0, FF, D):
            pre = nn(w["upT"][r : r + D, :], middle_low) + wide(col_ref, C_BUP + r, D, width)
            cdf = 0.5 * lax.erf(pre * (2.0**-0.5)) + 0.5
            act = pre * cdf
            if student:
                inner = wide(col_ref, C_GI + r, D, width)
                pdf = jnp.exp(pre * pre * -0.5) * (1.0 / math.sqrt(2.0 * math.pi))
                sc["act"][r : r + D, c : c + width] = act
                sc["slope"][r : r + D, c : c + width] = (cdf + pre * pdf) * inner
                act = act * inner
            sc["up"][r : r + D, c : c + width] = act.astype(bf16)
        down = nn(w["downT"][...], sc["up"][:, c : c + width]) + wide(col_ref, 9 * D, D, width)
        if student:
            sc["down"][:, c : c + width] = down
            down = down * wide(col_ref, C_GH, D, width)
        hat, scale = standardise(middle + down)
        out = hat * wide(col_ref, 4 * D, D, width) + wide(col_ref, 5 * D, D, width)
        if student:
            sc["hat2"][:, c : c + width] = hat
            sc["scale"][2:3, c : c + width] = scale
        sc["out"][:, c : c + width] = out


def backward_body(span, length, factor, target_ref, col_ref, w, sc, acc, add_ref, loss_ref, grad_ref, pos_add):
    def add(row, values):
        add_ref[row : row + values.shape[0], :] += lanes_in(values)

    for c, width in chunks(span):
        cols = slice(c, c + width)
        out_low = sc["out"][:, cols].astype(bf16)
        sc["out_low"][:, cols] = out_low
        differ = nn(w["aT"][...], out_low) - target_ref[0, :, cols]
        token_valid = (lax.broadcasted_iota(jnp.int32, (1, width), 1) + c < length).astype(f32)
        loss_ref[0:1, cols] += (
            jnp.sum(differ * differ, axis=0, keepdims=True) * (1.0 / D) * token_valid
        )
        d_aligned = (differ * (token_valid * factor)).astype(bf16)
        sc["d_aligned"][:, cols] = d_aligned
        d_out = nn(w["a"][...], d_aligned)
        hat = sc["hat2"][:, cols]
        add(4 * D, d_out * hat)
        add(5 * D, d_out)
        d_second = standardise_back(d_out * wide(col_ref, 4 * D, D, width), hat, sc["scale"][2:3, cols])
        add(A_GH, d_second * sc["down"][:, cols])
        d_down = (d_second * wide(col_ref, C_GH, D, width)).astype(bf16)
        sc["d_down"][:, cols] = d_down
        add(9 * D, d_down.astype(f32))
        for r in range(0, FF, D):
            d_up = nn(w["down"][r : r + D, :], d_down)
            add(A_GI + r, d_up * sc["act"][r : r + D, cols])
            d_pre = (d_up * sc["slope"][r : r + D, cols]).astype(bf16)
            sc["d_pre"][r : r + D, cols] = d_pre
            add(A_BUP + r, d_pre.astype(f32))
        d_middle = d_second + nn(w["up"][...], sc["d_pre"][:, cols])
        hat = sc["hat1"][:, cols]
        add(2 * D, d_middle * hat)
        add(3 * D, d_middle)
        d_first = standardise_back(
            d_middle * wide(col_ref, 2 * D, D, width), hat, sc["scale"][1:2, cols]
        )
        sc["d_first"][:, cols] = d_first
        add(A_GH, d_first * sc["branch"][:, cols])
        d_branch = (d_first * wide(col_ref, C_GH, D, width)).astype(bf16)
        sc["d_branch"][:, cols] = d_branch
        add(8 * D, d_branch.astype(f32))
        d_gated = nn(w["o"][...], d_branch)
        context = sc["context"][:, cols]
        add(A_HEAD, d_gated * context)
        d_context = d_gated * wide(col_ref, C_HEAD, D, width)
        sc["d_context"][:, cols] = d_context.astype(bf16)
        dot_rows = d_context * context
        for h in range(HEADS):
            sc["delta"][h : h + 1, cols] = jnp.sum(
                dot_rows[h * HD : (h + 1) * HD, :], axis=0, keepdims=True
            )
    full = slice(0, span)
    acc["a"][...] += nt(sc["out_low"][:, full], sc["d_aligned"][:, full])
    acc["down"][...] += nt(sc["up"][:, full], sc["d_down"][:, full])
    acc["up"][...] += nt(sc["middle_low"][:, full], sc["d_pre"][:, full])
    acc["o"][...] += nt(sc["gated"][:, full], sc["d_branch"][:, full])
    for h in range(HEADS):
        rows = slice(h * HD, (h + 1) * HD)
        d_value = nt(sc["d_context"][rows, full], sc["shares"][h, 0:span, 0:span])
        sc["d_qkv"][2 * D + h * HD : 2 * D + (h + 1) * HD, full] = d_value.astype(bf16)
        d_key = None
        for c, width in chunks(span):
            cols = slice(c, c + width)
            d_shares = nn(sc["v_rows"][h, 0:span, :], sc["d_context"][rows, cols])
            d_scores = (
                sc["shares"][h, 0:span, cols].astype(f32) * (d_shares - sc["delta"][h : h + 1, cols])
            ).astype(bf16)
            sc["d_qkv"][rows, cols] = (
                nn(sc["qkv"][D + h * HD : D + (h + 1) * HD, full], d_scores) * (HD**-0.5)
            ).astype(bf16)
            part = nt(sc["qkv"][rows, cols], d_scores)
            d_key = part if d_key is None else d_key + part
        sc["d_qkv"][D + h * HD : D + (h + 1) * HD, full] = (d_key * (HD**-0.5)).astype(bf16)
    acc["qkv"][...] += nt(sc["start_low"][:, full], sc["d_qkv"][:, full])
    for c, width in chunks(span):
        cols = slice(c, c + width)
        add(6 * D, sc["d_qkv"][0:D, cols].astype(f32))
        add(7 * D, sc["d_qkv"][2 * D : 3 * D, cols].astype(f32))
        d_start = sc["d_first"][:, cols] + nn(w["qkv"][...], sc["d_qkv"][:, cols])
        hat = sc["hat0"][:, cols]
        gain = wide(col_ref, 0, D, width)
        add(A_GH, d_start * (hat * gain + wide(col_ref, D, D, width)))
        d_norm = d_start * wide(col_ref, C_GH, D, width)
        add(0, d_norm * hat)
        add(D, d_norm)
        d_embedded = standardise_back(d_norm * gain, hat, sc["scale"][0:1, cols])
        pos_add[:, cols] += d_embedded
        d_low = d_embedded.astype(bf16)
        grad_ref[0, :, cols] = d_low
    if span < LEN:
        grad_ref[0, :, span:LEN] = jnp.zeros((D, LEN - span), bf16)


def mark_slots(span, slot, perm_ref):
    step = 512

    def mark(i, carry):
        rows = pl.ds(pl.multiple_of(i * step, step), step)
        seen = lax.broadcasted_iota(jnp.int32, (step, span), 0) == slot - i * step
        perm_ref[rows, 0:span] = seen.astype(f32).astype(bf16)
        return carry

    lax.fori_loop(0, perm_ref.shape[0] // step, mark, 0)


def pack_rows(span, perm_ref, grad_ref, packed_ref):
    step = 2048

    def add(i, carry):
        rows = pl.ds(pl.multiple_of(i * step, step), step)
        packed_ref[rows, :] += nt(perm_ref[rows, 0:span], grad_ref[0, :, 0:span]).astype(bf16)
        return carry

    lax.fori_loop(0, packed_ref.shape[0] // step, add, 0)


SPANS = (256, 384, 512)


def by_span(length, body):
    for i, span in enumerate(SPANS):
        low = SPANS[i - 1] if i else 0
        test = length > low
        if i == 0:
            test = length <= span
        elif i < len(SPANS) - 1:
            test = (length > low) & (length <= span)
        pl.when(test)(functools.partial(body, span))


def set_up(pos_in, pos_ref, eyes_refs):
    for size, ref in eyes_refs.items():
        ref[...] = eye(size)
    for c in range(0, LEN, 256):
        pos_ref[:, c : c + 256] = nt(eyes_refs[256][...], pos_in[c : c + 256, :])


TEACHER_W = (
    ("qkv", (D, 3 * D)),
    ("qkvT", (3 * D, D)),
    ("o", (D, D)),
    ("oT", (D, D)),
    ("up", (D, FF)),
    ("upT", (FF, D)),
    ("down", (FF, D)),
    ("downT", (D, FF)),
)
STUDENT_W = TEACHER_W + (("a", (D, D)), ("aT", (D, D)))


def spread(col_ref, at, row):
    col_ref[at : at + LANES, :] = jnp.transpose(jnp.broadcast_to(row, (LANES, LANES)))


def load_weights(flat, w, col_ref, one, student):
    squares = [("qkv", 0), ("qkv", D), ("qkv", 2 * D), ("o", 0)] + ([("a", 0)] if student else [])
    for i, (name, at) in enumerate(squares):
        for j in range(2):
            lanes = slice(at + j * LANES, at + (j + 1) * LANES)
            w[name][:, lanes] = flat[pl.ds(512 * i + j, D, stride=2), :].astype(bf16)
    base = 512 * len(squares)
    for j in range(8):
        w["up"][:, j * LANES : (j + 1) * LANES] = flat[pl.ds(base + j, D, stride=8), :].astype(bf16)
    base = base + 2048
    for j in range(2):
        w["down"][:, j * LANES : (j + 1) * LANES] = flat[pl.ds(base + j, FF, stride=2), :].astype(
            bf16
        )
    base = base + 2048
    for i in range(20):
        spread(col_ref, i * LANES, flat[base + i : base + i + 1, :])
    for j in range(8):
        spread(col_ref, C_BUP + j * LANES, flat[base + 20 + j : base + 21 + j, :])
    unit = one[...]
    for name in ("qkv", "o", "up") + (("a",) if student else ()):
        for b in range(0, w[name].shape[1], D):
            w[name + "T"][b : b + D, :] = nt(unit, w[name][:, b : b + D]).astype(bf16)
    for b in range(0, FF, D):
        w["downT"][:, b : b + D] = nt(unit, w["down"][b : b + D, :]).astype(bf16)


def total_of(x):
    return jnp.sum(jnp.sum(x, axis=0, keepdims=True), axis=1, keepdims=True)


def head_groups():
    return (
        lax.broadcasted_iota(jnp.int32, (D, LANES), 0) // HD
        == lax.broadcasted_iota(jnp.int32, (D, LANES), 1)
    ).astype(f32)


def load_gates(logits, noise, lagrange_ref, lag_weight, col_ref, slope_ref, lag_ref):
    index = lax.broadcasted_iota(
        jnp.int32, logits.shape, 0
    ) * LANES + lax.broadcasted_iota(jnp.int32, logits.shape, 1)
    hidden, heads = index < D, (index >= D) & (index < D + HEADS)
    inner = (index >= D + HEADS) & (index < D + HEADS + FF)
    logistic = jax.nn.sigmoid((jnp.log(noise) - jnp.log(1.0 - noise) + logits) / relaxation_heat)
    spanned = widened_right_limit - widened_left_limit
    stretched = logistic * spanned + widened_left_limit
    gates = jnp.clip(stretched, 0.0, 1.0)
    inside = jnp.where((stretched > 0.0) & (stretched < 1.0), 1.0, 0.0)
    inside = jnp.where((stretched == 0.0) | (stretched == 1.0), 0.5, inside)
    slope_ref[...] = inside * logistic * (1.0 - logistic) * (spanned / relaxation_heat)
    keep = jax.nn.sigmoid(
        logits - relaxation_heat * math.log(-widened_left_limit / widened_right_limit)
    )
    kept = total_of(jnp.where(hidden, keep, 0.0)) * (1.0 / D)
    rest = total_of(jnp.where(heads, keep * (4.0 * HD), 0.0) + jnp.where(inner, keep * 2.0, 0.0))
    scale = 1.0 / (4.0 * D + 2.0 * FF)
    excess = kept * rest * scale - sparse_target
    rate = (lagrange_ref[0] + 2.0 * lagrange_ref[1] * excess) * (scale * lag_weight)
    share = jnp.where(hidden, rest * (1.0 / D), 0.0)
    share = share + kept * (jnp.where(heads, 4.0 * HD, 0.0) + jnp.where(inner, 2.0, 0.0))
    lag_ref[...] = rate * share * (keep * (1.0 - keep))
    for j in range(2):
        spread(col_ref, C_GH + j * LANES, gates[j : j + 1, :])
    wide_heads = lax.dot_general(
        jnp.broadcast_to(gates[2:3, :], (8, LANES)),
        head_groups(),
        (((1,), (1,)), ((), ())),
        preferred_element_type=f32,
        precision=lax.Precision.HIGHEST,
    )
    for j in range(2):
        spread(col_ref, C_HEAD + j * LANES, wide_heads[0:1, j * LANES : (j + 1) * LANES])
    run = jnp.concatenate([gates[j : j + 1, :] for j in range(2, 11)], axis=1)
    run = pltpu.roll(jnp.broadcast_to(run, (8, 9 * LANES)), 9 * LANES - HEADS, 1)
    for j in range(8):
        spread(col_ref, C_GI + j * LANES, run[0:1, j * LANES : (j + 1) * LANES])
    return lagrange_ref[0] * excess + lagrange_ref[1] * excess * excess


TEACHER_S = (
    ("start", (D, LEN), f32),
    ("start_low", (D, LEN), bf16),
    ("qkv", (3 * D, LEN), bf16),
    ("k_rows", (HEADS, LEN, HD), bf16),
    ("gated", (D, LEN), bf16),
    ("up", (FF, LEN), bf16),
)
STUDENT_S = TEACHER_S + (
    ("hat0", (D, LEN), f32),
    ("hat1", (D, LEN), f32),
    ("hat2", (D, LEN), f32),
    ("scale", (8, LEN), f32),
    ("v_rows", (HEADS, LEN, HD), bf16),
    ("shares", (HEADS, LEN, LEN), bf16),
    ("context", (D, LEN), f32),
    ("branch", (D, LEN), f32),
    ("middle_low", (D, LEN), bf16),
    ("act", (FF, LEN), f32),
    ("slope", (FF, LEN), f32),
    ("down", (D, LEN), f32),
    ("out", (D, LEN), f32),
    ("out_low", (D, LEN), bf16),
    ("d_aligned", (D, LEN), bf16),
    ("d_down", (D, LEN), bf16),
    ("d_pre", (FF, LEN), bf16),
    ("d_first", (D, LEN), f32),
    ("d_branch", (D, LEN), bf16),
    ("d_context", (D, LEN), bf16),
    ("delta", (8, LEN), f32),
    ("d_qkv", (3 * D, LEN), bf16),
)
ACCS = (
    ("qkv", (D, 3 * D)),
    ("o", (D, D)),
    ("a", (D, D)),
    ("up", (D, FF)),
    ("down", (FF, D)),
)


class Eyes:
    def __init__(self, one, two):
        self.refs = {128: one, 256: two}

    def __getitem__(self, size):
        return self.refs[size][...]


def student_kernel(n, flat_len, sparse, len_ref, fac_ref, lagrange_ref, noise_ref, flat_in, pos_in, target_ref, *rest):
    plane, planes, flat_seg = plan(n, flat_len)[:3]
    cap = room(n)
    if sparse:
        slot_ref, rows_ref = rest[:2]
        rest = rest[2:]
    else:
        rows_ref = rest[0]
        rest = rest[1:]
    flat_ref, grad_ref, loss_ref = rest[:3]
    rest = rest[3:]
    if sparse:
        packed_ref, rows_all, perm_ref = rest[0], rest[1], rest[2]
        rest = rest[3:]
    w = {entry[0]: rest[i] for i, entry in enumerate(STUDENT_W)}
    rest = rest[len(STUDENT_W) :]
    sc = {entry[0]: rest[i] for i, entry in enumerate(STUDENT_S)}
    rest = rest[len(STUDENT_S) :]
    acc = {entry[0]: rest[i] for i, entry in enumerate(ACCS)}
    add_ref, pos_add, slope_ref, lag_ref, col_ref, pos_ref, eye_one, eye_two = rest[len(ACCS) :]
    s = pl.program_id(0)
    eyes = Eyes(eye_one, eye_two)

    @pl.when(s == 0)
    def _():
        set_up(pos_in, pos_ref, eyes.refs)
        for o in range(n):
            c = o // 2
            flat_ref[o * flat_seg : (o + 1) * flat_seg, :] = flat_in[
                o % 2, c % plane, c // plane, :, :
            ].astype(f32)[:flat_seg]
        load_weights(flat_ref, w, col_ref, eye_two, True)
        lag_value = load_gates(
            flat_ref[R_LOGIT : R_LOGIT + 16, :],
            noise_ref[...],
            lagrange_ref,
            fac_ref[1],
            col_ref,
            slope_ref,
            lag_ref,
        )
        for ref in list(acc.values()) + [add_ref, pos_add]:
            ref[...] = jnp.zeros(ref.shape, f32)
        row = lax.broadcasted_iota(jnp.int32, (8, LEN), 0)
        loss_ref[...] = jnp.where(row == 1, lag_value, 0.0)
        if sparse:
            packed_ref[...] = jnp.zeros(packed_ref.shape, bf16)
            for o in range(n):
                rows_all[:, o * cap : (o + 1) * cap] = rows_ref[o]

    length = len_ref[s]

    def body(span):
        if sparse:
            mark_slots(span, slot_ref[pl.ds(s, 1), 0:span], perm_ref)

        def embed(c, width):
            if sparse:
                return nn(rows_all[...], perm_ref[:, c : c + width])
            at = pl.multiple_of(s * LEN + c, 128)
            return nt(eyes[D], rows_ref[pl.ds(at, width), :])

        forward_body(span, length, True, embed, pos_ref, col_ref, w, sc, eyes)
        backward_body(
            span, length, fac_ref[0], target_ref, col_ref, w, sc, acc, add_ref, loss_ref, grad_ref, pos_add
        )
        if sparse:
            pack_rows(span, perm_ref, grad_ref, packed_ref)

    by_span(length, body)

    @pl.when(s == pl.num_programs(0) - 1)
    def _():
        for i in range(3):
            for j in range(2):
                at = i * D + j * LANES
                flat_ref[pl.ds(512 * i + j, D, stride=2), :] = acc["qkv"][:, at : at + LANES]
        for j in range(2):
            lanes = slice(j * LANES, (j + 1) * LANES)
            flat_ref[pl.ds(512 * 3 + j, D, stride=2), :] = acc["o"][:, lanes]
            flat_ref[pl.ds(512 * 4 + j, D, stride=2), :] = acc["a"][:, lanes]
            flat_ref[pl.ds(R_DOWN + j, FF, stride=2), :] = acc["down"][:, lanes]
        for j in range(8):
            flat_ref[pl.ds(R_UP + j, D, stride=8), :] = acc["up"][:, j * LANES : (j + 1) * LANES]
        ones = jnp.ones((8, LANES), f32)

        def summed(row, rows):
            return lax.dot_general(
                ones,
                add_ref[row : row + rows, :],
                (((1,), (1,)), ((), ())),
                preferred_element_type=f32,
                precision=lax.Precision.HIGHEST,
            )

        for i in range(10):
            sums = summed(i * D, D)
            for j in range(2):
                flat_ref[R_VEC + 2 * i + j : R_VEC + 2 * i + j + 1, :] = sums[
                    0:1, j * LANES : (j + 1) * LANES
                ]
        sums = summed(A_BUP, FF)
        for j in range(8):
            flat_ref[R_BUP + j : R_BUP + j + 1, :] = sums[0:1, j * LANES : (j + 1) * LANES]
        hidden = summed(A_GH, D)
        heads = jnp.dot(
            summed(A_HEAD, D),
            head_groups(),
            preferred_element_type=f32,
            precision=lax.Precision.HIGHEST,
        )
        inner = summed(A_GI, FF)
        moved = pltpu.roll(jnp.concatenate([inner, jnp.zeros((8, LANES), f32)], axis=1), HEADS, 1)
        lane = lax.broadcasted_iota(jnp.int32, (8, LANES), 1)
        first = jnp.where(lane < HEADS, heads, moved[:, :LANES])
        tail = [hidden[:, :LANES], hidden[:, LANES:], first] + [
            moved[:, j * LANES : (j + 1) * LANES] for j in range(1, 9)
        ]
        for j, piece in enumerate(tail):
            flat_ref[R_LOGIT + j : R_LOGIT + j + 1, :] = (
                piece[0:1] * slope_ref[j : j + 1, :] + lag_ref[j : j + 1, :]
            )
        flat_ref[R_USED:flat_len, :] = jnp.zeros((flat_len - R_USED, LANES), f32)
        for j in range(2):
            flat_ref[pl.ds(flat_len + j, LEN, stride=2), :] = jnp.transpose(
                pos_add[j * LANES : (j + 1) * LANES, :]
            )


def whole_spec():
    return pl.BlockSpec(memory_space=pltpu.VMEM)


def smem_spec():
    return pl.BlockSpec(memory_space=pltpu.SMEM)


def seq_spec():
    return pl.BlockSpec((1, D, LEN), lambda s: (s, 0, 0))


def common_scratch():
    return [
        pltpu.VMEM((C_ROWS, LANES), f32),
        pltpu.VMEM((D, LEN), f32),
        pltpu.VMEM((128, 128), bf16),
        pltpu.VMEM((256, 256), bf16),
    ]


def run_student(n, flat_len, sparse, lengths, factors, lagrange, noise, flat_all, places, target, given):
    seqs = lengths.shape[0]
    slot_rows = n * room(n)
    shapes = [
        jax.ShapeDtypeStruct((flat_len + 2 * LEN, LANES), f32),
        jax.ShapeDtypeStruct((seqs, D, LEN), bf16),
        jax.ShapeDtypeStruct((8, LEN), f32),
    ]
    out_specs = [whole_spec(), seq_spec(), whole_spec()]
    scratch = []
    if sparse:
        shapes.append(jax.ShapeDtypeStruct((slot_rows, D), bf16))
        out_specs.append(whole_spec())
        scratch = [pltpu.VMEM((D, slot_rows), bf16), pltpu.VMEM((slot_rows, LEN), bf16)]
    return pl.pallas_call(
        functools.partial(student_kernel, n, flat_len, sparse),
        grid=(seqs,),
        out_shape=tuple(shapes),
        in_specs=[smem_spec()] * 3
        + [whole_spec()] * 3
        + [seq_spec()]
        + [whole_spec()] * len(given),
        out_specs=tuple(out_specs),
        scratch_shapes=scratch
        + [pltpu.VMEM(shape, bf16) for _, shape in STUDENT_W]
        + [pltpu.VMEM(shape, kind) for _, shape, kind in STUDENT_S]
        + [pltpu.VMEM(shape, f32) for _, shape in ACCS]
        + [
            pltpu.VMEM((A_ROWS, LANES), f32),
            pltpu.VMEM((D, LEN), f32),
            pltpu.VMEM((16, LANES), f32),
            pltpu.VMEM((16, LANES), f32),
        ]
        + common_scratch(),
        compiler_params=pltpu.CompilerParams(vmem_limit_bytes=VMEM_LIMIT),
        name="student" if sparse else "student_dense",
    )(lengths, factors, lagrange, noise, flat_all, places, target, *given)


MESH = pl.DeviceIdType.MESH


def room(n):
    return LANES if 8 * LEN // n >= LANES else 0


def greet_all(me, n):
    barrier = pltpu.get_barrier_semaphore()

    def signal(k, carry):
        pl.semaphore_signal(barrier, inc=1, device_id=(me ^ k,), device_id_type=MESH)
        return carry

    lax.fori_loop(1, n, signal, 0)
    pl.semaphore_wait(barrier, n - 1)


def copy_to(source, target, send, receive, device):
    return pltpu.make_async_remote_copy(
        src_ref=source,
        dst_ref=target,
        send_sem=send,
        recv_sem=receive,
        device_id=(device,),
        device_id_type=MESH,
    )


def list_rows(n, owner_ref, local_ref, stat, slot_ref, tile_ref):
    cap = room(n)
    upper = (
        lax.broadcasted_iota(jnp.int32, (256, 256), 0)
        <= lax.broadcasted_iota(jnp.int32, (256, 256), 1)
    ).astype(bf16)
    base = jnp.zeros((n, 1), f32)
    listed = jnp.zeros((n, LANES), f32)
    for s in range(owner_ref.shape[0]):
        for c in range(0, LEN, 256):
            owner = owner_ref[s : s + 1, c : c + 256]
            mine = (lax.broadcasted_iota(jnp.int32, (n, 256), 0) == owner).astype(f32)
            before = nn(mine.astype(bf16), upper)
            rank = jnp.sum(mine * (before - 1.0 + base), axis=0, keepdims=True).astype(jnp.int32)
            fits = (owner >= 0) & (rank < cap)
            slot_ref[s : s + 1, c : c + 256] = jnp.where(fits, owner * cap + rank, n * cap)
            place = (
                lax.broadcasted_iota(jnp.int32, (LANES, 256), 0) == jnp.where(fits, rank, -1)
            ).astype(f32)
            listed = listed + lax.dot_general(
                mine * local_ref[s : s + 1, c : c + 256],
                place,
                (((1,), (1,)), ((), ())),
                preferred_element_type=f32,
                precision=lax.Precision.HIGHEST,
            )
            base = base + before[:, 255:256]
    over = jnp.max(base, axis=0, keepdims=True) > cap
    lane = lax.broadcasted_iota(jnp.int32, (n, LANES), 1)
    tile_ref[...] = jnp.zeros(tile_ref.shape, jnp.int32)
    tile_ref[pl.ds(0, n, stride=8), :] = (listed + 0.5).astype(jnp.int32) - 1
    tile_ref[pl.ds(1, n, stride=8), :] = jnp.where(
        lane == 0, stat, jnp.where(lane == 1, over.astype(jnp.int32), 0)
    )


def place_parts(vrows):
    parts = []
    for o in range(VOCAB // vrows, (VOCAB + LEN - 1) // vrows + 1):
        low, top = max(VOCAB, o * vrows), min(VOCAB + LEN, (o + 1) * vrows)
        parts.append((o, low - o * vrows, low - VOCAB, top - low))
    return parts


def round_up(value, step):
    return -(-value // step) * step


def pair_lists(list_ref, a, cap):
    return jnp.concatenate(
        [list_ref[pl.ds(pl.multiple_of(a * 16 + 8 * j, 8), 8), :][0:1, :cap] for j in range(2)],
        axis=1,
    )


def fetch_kernel(
    n, flat_len, owner_ref, local_ref, stat_ref, len_ref, rows_ref, pos_in, flat_in, table_ref, own_flat, *rest
):
    plane, planes, flat_seg, flat_pad = plan(n, flat_len)[:4]
    cap = room(n)
    vrows = table_ref.shape[0]
    parts = place_parts(vrows)
    out_ref, got_out, flat_out, place_out = rest[:4]
    rest = rest[4:]
    if cap:
        slot_ref, rows_out = rest[:2]
        rest = rest[2:]
    w = {entry[0]: rest[i] for i, entry in enumerate(TEACHER_W)}
    rest = rest[len(TEACHER_W) :]
    sc = {entry[0]: rest[i] for i, entry in enumerate(TEACHER_S)}
    rest = rest[len(TEACHER_S) :]
    tile_ref, got_ref, flat_all, place_all, pad_ref, flat_f32 = rest[:6]
    list_sem, a_sem, b_sem, c_sem, pa_sem, pb_sem, pc_sem = rest[6:13]
    col_ref, pos_ref, eye_one, eye_two = rest[13:17]
    if cap:
        table_turned, row_send, rows_in, row_sem = rest[17:]
    eyes = Eyes(eye_one, eye_two)
    s = pl.program_id(0)
    seqs = owner_ref.shape[0]
    me = lax.axis_index("dp")
    core = lax.rem(me, 2)
    chip = me // 2
    mid = lax.rem(chip, plane)
    high = chip // plane

    def device(h, m, c):
        return (h * plane + m) * 2 + c

    def tile(ref, i):
        return ref.at[pl.ds(pl.multiple_of(i * 8, 8), 8), :]

    def list_copy(k):
        return copy_to(
            tile(tile_ref, me ^ k), tile(got_ref, me), list_sem.at[0, k], list_sem.at[1, k], me ^ k
        )

    def row_copy(k):
        return copy_to(
            row_send.at[me ^ k], rows_in.at[me], row_sem.at[0, k], row_sem.at[1, k], me ^ k
        )

    def flat_copies(stage):
        copies = []
        if stage == 0:
            spot = flat_all.at[core, mid, high]
            for k in range(1, planes):
                to = device(lax.rem(high + k, planes), mid, core)
                copies.append(copy_to(spot, spot, a_sem.at[0, k], a_sem.at[1, k], to))
        elif stage == 1:
            spot = flat_all.at[core, mid]
            for k in range(1, plane):
                to = device(high, lax.rem(mid + k, plane), core)
                copies.append(copy_to(spot, spot, b_sem.at[0, k], b_sem.at[1, k], to))
        else:
            spot = flat_all.at[core]
            copies.append(copy_to(spot, spot, c_sem.at[0], c_sem.at[1], me ^ 1))
        return copies

    def place_copies(stage, i):
        o, _, _, count = parts[i]
        chip_o = o // 2
        high_o, mid_o, core_o = chip_o // plane, chip_o % plane, o % 2
        spot = place_all.at[i, pl.ds(0, round_up(count, 16)), :]
        same_core, same_mid, same_high = core == core_o, mid == mid_o, high == high_o
        copies = []
        if stage == 0:
            for k in range(1, planes):
                to = device((high_o + k) % planes, mid_o, core_o)
                copies.append(copy_to(spot, spot, pa_sem.at[0, i, k], pa_sem.at[1, i, 0], to))
            sends = same_core & same_mid & same_high
            receives = same_core & same_mid & (high != high_o)
        elif stage == 1:
            for k in range(1, plane):
                to = device(high, (mid_o + k) % plane, core_o)
                copies.append(copy_to(spot, spot, pb_sem.at[0, i, k], pb_sem.at[1, i, 0], to))
            sends = same_core & same_mid
            receives = same_core & (mid != mid_o)
        else:
            copies.append(copy_to(spot, spot, pc_sem.at[0, i], pc_sem.at[1, i], me ^ 1))
            sends = same_core
            receives = core != core_o
        return copies, sends, receives

    def start_stage(stage):
        for copy in flat_copies(stage):
            copy.start()
        for i in range(len(parts)):
            copies, sends, _ = place_copies(stage, i)

            @pl.when(sends)
            def _():
                for copy in copies:
                    copy.start()

    def finish_stage(stage):
        for copy in flat_copies(stage):
            copy.wait()
        for i in range(len(parts)):
            copies, sends, receives = place_copies(stage, i)

            @pl.when(sends)
            def _():
                for copy in copies:
                    copy.wait_send()

            @pl.when(receives)
            def _():
                copies[0].wait_recv()

    @pl.when(s == 0)
    def _():
        greet_all(me, n)
        pad_ref[...] = jnp.zeros(pad_ref.shape, f32)
        pad_ref[0:flat_seg, :] = own_flat[...]
        flat_all[core, mid, high] = pad_ref[...].astype(bf16)
        for i, (o, at, _, count) in enumerate(parts):

            @pl.when(me == o)
            def _():
                full = round_up(count, 16)
                part = table_ref[at : at + count, :]
                if full > count:
                    part = jnp.concatenate([part, jnp.zeros((full - count, D), f32)], axis=0)
                place_all[i, 0:full, :] = part.astype(bf16)

        start_stage(0)
        if cap:
            list_rows(n, owner_ref, local_ref, stat_ref[0], slot_ref, tile_ref)
        else:
            tile_ref[...] = jnp.zeros(tile_ref.shape, jnp.int32) + stat_ref[0]

        def start_list(k, carry):
            list_copy(k).start()
            return carry

        lax.fori_loop(1, n, start_list, 0)
        own = pl.ds(pl.multiple_of(me * 8, 8), 8)
        got_ref[own, :] = tile_ref[own, :]
        set_up(pos_in, pos_ref, eyes.refs)
        if cap:
            table_turned[...] = nt(eye_two[...], table_ref[...].astype(bf16)).astype(bf16)

        def finish_list(k, carry):
            list_copy(k).wait()
            return carry

        lax.fori_loop(1, n, finish_list, 0)

        def serve(step, carry):
            i = n // 2 - 1 - step
            a = chip ^ i
            pick = (
                lax.broadcasted_iota(jnp.int32, (vrows, 2 * cap), 0) == pair_lists(got_ref, a, cap)
            ).astype(bf16)
            both = nn(table_turned[...], pick).astype(bf16)
            for j in range(2):
                row_send[2 * a + j] = both[:, j * cap : (j + 1) * cap]
                k = 2 * i + (core ^ j)
                pl.when(k > 0)(row_copy(k).start)
            return carry

        if cap:
            lax.fori_loop(0, n // 2, serve, 0)
            rows_in[me] = row_send[me]
        flat_f32[...] = flat_in[...].astype(f32)
        load_weights(flat_f32, w, col_ref, eye_two, False)

    @pl.when(s == 2)
    def _():
        finish_stage(0)
        start_stage(1)

    @pl.when(s == 4)
    def _():
        finish_stage(1)
        start_stage(2)

    sc["out"] = out_ref.at[0]
    length = len_ref[s]
    from_me = jnp.where(s < seqs // 2, me, n - 1 - me)
    longest = LEN // 3 + (LEN - LEN // 3) * from_me // (n - 1)

    def body(span):
        def embed(c, width):
            at = pl.multiple_of(s * LEN + c, 128)
            return nt(eyes[D], rows_ref[pl.ds(at, width), :])

        forward_body(span, length, False, embed, pos_ref, col_ref, w, sc, eyes)

    by_span(longest, body)

    @pl.when(s == seqs - 1)
    def _():
        finish_stage(2)

        def finish_row(k, carry):
            row_copy(k).wait()
            return carry

        if cap:
            lax.fori_loop(1, n, finish_row, 0)
            rows_out[...] = rows_in[...]
        got_out[...] = got_ref[...]
        flat_out[...] = flat_all[...]
        place_out[...] = place_all[...]


def run_fetch(n, flat_len, owner, local, stat, lengths, rows, places, teacher, table, own_flat):
    plane, planes, flat_seg, flat_pad = plan(n, flat_len)[:4]
    seqs, cap, vrows = owner.shape[0], room(n), table.shape[0]
    parts = place_parts(vrows)
    most = max(round_up(part[3], 16) for part in parts)
    dma = pltpu.SemaphoreType.DMA
    got = ((8 * n, LANES), jnp.int32)
    fetched = ((n, D, cap), bf16)
    flat_all = ((2, plane, planes, flat_pad, LANES), bf16)
    place_all = ((len(parts), most, D), bf16)
    shapes = [((seqs, D, LEN), f32), got, flat_all, place_all]
    extra = []
    if cap:
        shapes += [(owner.shape, jnp.int32), fetched]
        extra = [
            pltpu.VMEM((D, vrows), bf16),
            pltpu.VMEM(*fetched),
            pltpu.VMEM(*fetched),
            dma((2, n)),
        ]
    return pl.pallas_call(
        functools.partial(fetch_kernel, n, flat_len),
        grid=(seqs,),
        out_shape=tuple(jax.ShapeDtypeStruct(shape, kind) for shape, kind in shapes),
        in_specs=[whole_spec()] * 2 + [smem_spec()] * 2 + [whole_spec()] * 5,
        out_specs=(seq_spec(),) + (whole_spec(),) * (len(shapes) - 1),
        scratch_shapes=[pltpu.VMEM(shape, bf16) for _, shape in TEACHER_W]
        + [pltpu.VMEM(shape, kind) for _, shape, kind in TEACHER_S]
        + [
            pltpu.VMEM(*got),
            pltpu.VMEM(*got),
            pltpu.VMEM(*flat_all),
            pltpu.VMEM(*place_all),
            pltpu.VMEM((flat_pad, LANES), f32),
            pltpu.VMEM(teacher.shape, f32),
            dma((2, n)),
            dma((2, planes)),
            dma((2, plane)),
            dma((2,)),
            dma((2, len(parts), planes)),
            dma((2, len(parts), plane)),
            dma((2, len(parts))),
        ]
        + common_scratch()
        + extra,
        compiler_params=pltpu.CompilerParams(
            collective_id=1, has_side_effects=True, vmem_limit_bytes=VMEM_LIMIT
        ),
        name="teacher",
    )(owner, local, stat, lengths, rows, places, teacher, table, own_flat)


def plan(n, flat_len):
    chips = n // 2
    plane = 2 ** ((chips.bit_length() - 1) // 2)
    flat_seg = flat_len // n
    flat_pad = round_up(flat_seg, 16)
    place_seg = 2 * LEN // n
    return plane, chips // plane, flat_seg, flat_pad, place_seg, flat_pad + round_up(place_seg, 16)


def place_tile(n):
    return max(8, 2 * LEN // n)


def exchange_kernel(n, flat_len, sparse, *refs):
    plane, planes, flat_seg, flat_pad, place_seg, seg = plan(n, flat_len)
    chips = n // 2
    cap = room(n)
    tile = place_tile(n)
    flat_ref, loss_ref = refs[:2]
    refs = refs[2:]
    if sparse:
        packed_ref, list_ref = refs[:2]
        refs = refs[2:]
    else:
        given_ref = refs[0]
        refs = refs[1:]
    table_ref, sums_ref, stat_out = refs[:3]
    (stage, one_in, two_out, two_in, total, three_out, three_in, place_in, stat_in) = refs[3:12]
    refs = refs[12:]
    if sparse:
        rows_in = refs[0]
        refs = refs[1:]
    one_sem, two_sem, three_sem, place_sem, stat_sem, row_sem = refs
    me = lax.axis_index("dp")
    core = lax.rem(me, 2)
    chip = me // 2
    mid = lax.rem(chip, plane)
    high = chip // plane
    vrows = table_ref.shape[0]

    greet_all(me, n)
    pad = jnp.zeros((16, LANES), f32)
    for o in range(n):
        spot = stage.at[o % 2, o // 2]
        if flat_pad > flat_seg:
            spot[flat_pad - 16 : flat_pad, :] = pad
        if seg > flat_pad + place_seg:
            spot[seg - 16 : seg, :] = pad
        spot[0:flat_seg, :] = flat_ref[o * flat_seg : (o + 1) * flat_seg, :]
        at = flat_len + o * place_seg
        spot[flat_pad : flat_pad + place_seg, :] = flat_ref[at : at + place_seg, :]
    first = copy_to(stage.at[1 - core], one_in, one_sem.at[0], one_sem.at[1], me ^ 1)
    first.start()

    if sparse:

        def bucket(ref, i):
            return ref.at[pl.ds(pl.multiple_of(i * cap, cap), cap), :]

        def row_copy(k):
            return copy_to(
                bucket(packed_ref, me ^ k), bucket(rows_in, me), row_sem.at[0, k], row_sem.at[1, k], me ^ k
            )

        def start_row(i, carry):
            row_copy(n - i).start()
            return carry

        lax.fori_loop(1, n, start_row, 0)
        own = pl.ds(pl.multiple_of(me * cap, cap), cap)
        rows_in[own, :] = packed_ref[own, :]

    first.wait()
    for m in range(plane):
        for h in range(planes):
            c = h * plane + m
            two_out[m, h] = (stage[core, c] + one_in[c]).astype(bf16)
    second = []
    for k in range(1, plane):
        m = lax.rem(mid + k, plane)
        second.append(
            copy_to(
                two_out.at[m],
                two_in.at[k - 1],
                two_sem.at[0, k],
                two_sem.at[1, k],
                (high * plane + m) * 2 + core,
            )
        )
        second[-1].start()
    for copy in second:
        copy.wait()
    for h in range(planes):
        c = h * plane + mid
        value = stage[core, c] + one_in[c]
        for k in range(1, plane):
            value = value + two_in[k - 1, h].astype(f32)
        total[h] = value
        three_out[h] = value.astype(bf16)
    third = []
    for k in range(1, planes):
        h = lax.rem(high + k, planes)
        third.append(
            copy_to(
                three_out.at[h],
                three_in.at[k - 1],
                three_sem.at[0, k],
                three_sem.at[1, k],
                (h * plane + mid) * 2 + core,
            )
        )
        third[-1].start()
    for copy in third:
        copy.wait()
    value = total[high]
    for k in range(1, planes):
        value = value + three_in[k - 1].astype(f32)
    total[0] = value
    sums_ref[...] = value[:flat_pad]

    owners = range(VOCAB // vrows, (VOCAB + LEN - 1) // vrows + 1)
    place_out = total.at[0, pl.ds(flat_pad, tile), :]
    place_spot = pl.ds(pl.multiple_of(me * tile, 8), tile)
    for i, o in enumerate(owners):
        place_copy = copy_to(
            place_out, place_in.at[place_spot, :], place_sem.at[0, i], place_sem.at[1, me], o
        )
        pl.when(me != o)(place_copy.start)

    squares = jnp.sum(jnp.sum(value * value, axis=0, keepdims=True), axis=1, keepdims=True)
    if sparse:
        def add_pair(i, carry):
            pl.when(i > 0)(lambda: row_copy(2 * i).wait_recv())
            row_copy(2 * i + 1).wait_recv()
            a = chip ^ i
            lists = pair_lists(list_ref, a, cap)
            pick = (lax.broadcasted_iota(jnp.int32, (vrows, 2 * cap), 0) == lists).astype(bf16)
            both = rows_in[pl.ds(pl.multiple_of(a * 2 * cap, 2 * cap), 2 * cap), :]
            table_ref[...] += nn(pick, both)
            return carry

        table_ref[...] = jnp.zeros(table_ref.shape, f32)
        lax.fori_loop(0, chips, add_pair, 0)
    else:
        table_ref[...] = given_ref[...]
    grads = table_ref[...]
    squares = squares + jnp.sum(
        jnp.sum(grads * grads, axis=0, keepdims=True), axis=1, keepdims=True
    )
    loss = jnp.sum(loss_ref[0:1, :], axis=1, keepdims=True)
    lane = lax.broadcasted_iota(jnp.int32, (8, LANES), 1)
    stat_out[...] = jnp.where(lane == 0, squares, jnp.where(lane == 1, loss, 0.0))

    def stat_copy(k):
        return copy_to(
            stat_out, stat_in.at[me], stat_sem.at[0, k], stat_sem.at[1, k], me ^ k
        )

    def start_stat(k, carry):
        stat_copy(k).start()
        return carry

    def finish_stat(k, carry):
        stat_copy(k).wait()
        return carry

    lax.fori_loop(1, n, start_stat, 0)
    stat_in[me] = stat_out[...]

    for i, o in enumerate(owners):

        @pl.when(me == o)
        def _():
            place_in[place_spot, :] = place_out[...]

            def wait_place(j, carry):
                copy_to(
                    place_out,
                    place_in.at[pl.ds(pl.multiple_of(j * tile, 8), tile), :],
                    place_sem.at[0, i],
                    place_sem.at[1, j],
                    me ^ 1,
                ).wait_recv()
                return carry

            lax.fori_loop(0, o, wait_place, 0)
            lax.fori_loop(o + 1, n, wait_place, 0)
            low = max(0, o * vrows - VOCAB)
            top = min(LEN, (o + 1) * vrows - VOCAB)
            at = VOCAB + low - o * vrows
            if tile > place_seg:
                for d in range(n):
                    place_in[d * place_seg : (d + 1) * place_seg, :] = place_in[
                        d * tile : d * tile + place_seg, :
                    ]
            for j in range(2):
                table_ref[at : at + top - low, j * LANES : (j + 1) * LANES] += place_in[
                    pl.ds(2 * low + j, top - low, stride=2), :
                ]

    lax.fori_loop(1, n, finish_stat, 0)
    stat_out[...] = jnp.sum(stat_in[...], axis=0)
    for i, o in enumerate(owners):
        place_copy = copy_to(
            place_out, place_in.at[place_spot, :], place_sem.at[0, i], place_sem.at[1, me], o
        )
        pl.when(me != o)(place_copy.wait_send)
    if sparse:

        def finish_row(k, carry):
            row_copy(k).wait_send()
            return carry

        lax.fori_loop(1, n, finish_row, 0)


def run_exchange(n, vrows, flat_grads, loss_rows, sparse, given):
    flat_len = flat_grads.shape[0] - 2 * LEN
    plane, planes, flat_seg, flat_pad, place_seg, seg = plan(n, flat_len)
    count = len(range(VOCAB // vrows, (VOCAB + LEN - 1) // vrows + 1))
    dma = pltpu.SemaphoreType.DMA
    return pl.pallas_call(
        functools.partial(exchange_kernel, n, flat_len, sparse),
        out_shape=(
            jax.ShapeDtypeStruct((vrows, D), f32),
            jax.ShapeDtypeStruct((flat_pad, LANES), f32),
            jax.ShapeDtypeStruct((8, LANES), f32),
        ),
        in_specs=[whole_spec()] * (2 + len(given)),
        out_specs=(whole_spec(),) * 3,
        scratch_shapes=[
            pltpu.VMEM((2, n // 2, seg, LANES), f32),
            pltpu.VMEM((n // 2, seg, LANES), f32),
            pltpu.VMEM((plane, planes, seg, LANES), bf16),
            pltpu.VMEM((plane - 1, planes, seg, LANES), bf16),
            pltpu.VMEM((planes, seg, LANES), f32),
            pltpu.VMEM((planes, seg, LANES), bf16),
            pltpu.VMEM((planes - 1, seg, LANES), bf16),
            pltpu.VMEM((n * place_tile(n), LANES), f32),
            pltpu.VMEM((n, 8, LANES), f32),
        ]
        + ([pltpu.VMEM((n * room(n), D), bf16)] if sparse else [])
        + [dma((2,)), dma((2, plane)), dma((2, planes)), dma((2, max(n, count))), dma((2, n)), dma((2, n))],
        compiler_params=pltpu.CompilerParams(
            collective_id=2 if sparse else 3, has_side_effects=True, vmem_limit_bytes=VMEM_LIMIT
        ),
        name="exchange" if sparse else "exchange_dense",
    )(flat_grads, loss_rows, *given)


def adam_step(weight, first_old, second, clipped):
    first_new = beta_one * first_old + (1.0 - beta_one) * clipped
    second_new = beta_two * second + (1.0 - beta_two) * clipped * clipped
    first_hat = first_new / (1.0 - beta_one**ADAM_STEP)
    second_hat = second_new / (1.0 - beta_two**ADAM_STEP)
    weight_new = weight - learn_rate * (
        first_hat / (jnp.sqrt(second_hat) + adam_eps) + decay_rate * weight
    )
    return (weight_new, first_new, second_new)


def rows_of(table, ids):
    return table.at[ids.reshape(-1)].get(mode="promise_in_bounds")


def ring_gather(devices, block):
    me = lax.axis_index("dp")
    rows = block.shape[0]
    onward = [(i, (i + 1) % devices) for i in range(devices)]

    def step(i, state):
        block, whole = state
        whole = lax.dynamic_update_slice(whole, block, (lax.rem(me - i + devices, devices) * rows, 0))
        return lax.ppermute(block, "dp", onward), whole

    whole = jnp.zeros((devices * rows, block.shape[1]), block.dtype)
    return lax.fori_loop(0, devices, step, (block, whole))[1]


def ring_scatter(devices, whole):
    me = lax.axis_index("dp")
    rows = whole.shape[0] // devices
    onward = [(i, (i + 1) % devices) for i in range(devices)]

    def part(i):
        at = lax.rem(me - 1 - i + 2 * devices, devices) * rows
        return lax.dynamic_slice(whole, (at, 0), (rows, whole.shape[1]))

    def step(i, total):
        return lax.ppermute(total, "dp", onward) + part(i)

    return lax.fori_loop(1, devices, step, part(0))


def per_device(
    devices,
    token_ids,
    lengths,
    gate_noise,
    lagrange,
    teacher_table,
    teacher_flat,
    word_table,
    table_first,
    table_second,
    layer_flat,
    flat_first,
    flat_second,
):
    seqs = token_ids.shape[0]
    half = seqs // 2
    vrows = word_table.shape[0]
    own = layer_flat.shape[0]
    flat_len = own * devices // LANES

    mates = [(i, devices - 1 - i) for i in range(devices)]
    sent = jnp.concatenate(
        [token_ids[half:], jnp.pad(lengths[half:], (0, LEN - half)).reshape(1, LEN)]
    )
    got = lax.ppermute(sent, "dp", mates)
    ids = jnp.concatenate([token_ids[:half], got[:half]])
    lens = jnp.concatenate([lengths[:half], got[half, :half]])

    owner = ids // vrows
    valid = jnp.arange(LEN)[None, :] < lens[:, None]
    target, listed, flat_all, place_all, *routed = run_fetch(
        devices,
        flat_len,
        jnp.where(valid, owner, -1),
        (ids - owner * vrows + 1).astype(f32),
        jnp.sum(lens).reshape(1),
        lens,
        rows_of(teacher_table, ids),
        teacher_table[VOCAB : VOCAB + LEN],
        teacher_flat.reshape(-1, LANES),
        word_table,
        layer_flat.reshape(-1, LANES),
    )
    stats = listed.reshape(devices, 8, LANES)[:, 1, :2]
    global_count = jnp.sum(stats[:, 0]).astype(f32)
    lag_weight = jnp.where(lax.axis_index("dp") == 0, 1.0, 0.0).astype(f32)
    factors = jnp.stack([(2.0 / D) / global_count, lag_weight])
    noise = jnp.pad(gate_noise, (0, 16 * LANES - gate_noise.shape[0]), constant_values=0.5)
    places = [place_all[i, : part[3]] for i, part in enumerate(place_parts(vrows))]
    shared = (
        lens,
        factors,
        lagrange,
        noise.reshape(16, LANES),
        flat_all,
        jnp.concatenate(places) if len(places) > 1 else places[0],
        target,
    )

    def from_slots():
        slots, fetched = routed
        flat_grads, _, loss_rows, packed = run_student(
            devices, flat_len, True, *shared, (slots, fetched)
        )
        result = run_exchange(devices, vrows, flat_grads, loss_rows, True, (packed, listed))
        return (*result, loss_rows)

    def from_rows():
        if routed:
            table = ring_gather(devices, word_table.astype(bf16))
        else:
            table = lax.all_gather(word_table.astype(bf16), "dp", axis=0, tiled=True)
        flat_grads, grad_rows, loss_rows = run_student(
            devices, flat_len, False, *shared, (rows_of(table, ids),)
        )
        updates = jnp.transpose(grad_rows, (0, 2, 1)).reshape(seqs * LEN, D).astype(f32)
        table = jnp.zeros((devices * vrows, D), f32).at[ids.reshape(-1)].add(updates)
        if routed:
            table = ring_scatter(devices, table)
        else:
            table = lax.psum_scatter(table, "dp", scatter_dimension=0, tiled=True)
        result = run_exchange(devices, vrows, flat_grads, loss_rows, False, (table,))
        return (*result, loss_rows)

    if routed:
        crowded = jnp.max(stats[:, 1])
        _, table_grad, sums, totals, loss_rows = lax.while_loop(
            lambda state: state[0] > 0,
            lambda state: (jnp.zeros_like(state[0]), *from_rows()),
            (crowded, *from_slots()),
        )
    else:
        table_grad, sums, totals, loss_rows = from_rows()
    lag_value = loss_rows[1, 0]
    flat_grad = sums[: own // LANES].reshape(-1)
    grad_norm = jnp.sqrt(totals[0, 0])
    clip = jnp.minimum(1.0, clip_norm / (grad_norm + 1e-06))
    total_loss = totals[0, 1] / global_count + lag_value
    table_new = adam_step(word_table, table_first, table_second, table_grad * clip)
    flat_new = adam_step(layer_flat, flat_first, flat_second, flat_grad * clip)
    return (*table_new, *flat_new, total_loss, grad_norm)


def solution(mesh):
    row, flat, copied = P("dp", None), P("dp"), P()
    in_specs = (row, flat, copied, copied, copied, copied, row, row, row, flat, flat, flat)
    out_specs = (row, row, row, flat, flat, flat, copied, copied)
    return jax.shard_map(
        functools.partial(per_device, mesh.shape["dp"]),
        mesh=mesh,
        in_specs=in_specs,
        out_specs=out_specs,
        check_vma=False,
    )
```

```python
import functools
import math

import jax
import jax.numpy as jnp
from jax import lax
from jax.experimental import pallas as pl
from jax.experimental.pallas import tpu as pltpu
from jax.sharding import PartitionSpec as P

D = 256
HEADS = 4
HD = D // HEADS
FF = 1024
LEN = 512
VOCAB = 30522
NPAR = 856836
LANES = 128
norm_eps = 1e-12
clip_norm = 0.002
learn_rate = 0.015
beta_one = 0.9
beta_two = 0.999
adam_eps = 1e-08
decay_rate = 0.01
sparse_target = 0.3
ADAM_STEP = 10
relaxation_heat = 2.0 / 3.0
widened_left_limit = -0.1
widened_right_limit = 1.1
f32 = jnp.float32
bf16 = jnp.bfloat16
VMEM_LIMIT = 60 * 2**20

C_GH = 10 * D
C_HEAD = 11 * D
C_BUP = 12 * D
C_GI = 12 * D + FF
C_ROWS = 12 * D + 2 * FF
A_BUP = 10 * D
A_GH = 10 * D + FF
A_HEAD = 11 * D + FF
A_GI = 12 * D + FF
A_ROWS = 12 * D + 2 * FF
R_UP = 5 * 512
R_DOWN = R_UP + 2048
R_VEC = R_DOWN + 2048
R_BUP = R_VEC + 20
R_LOGIT = R_BUP + 8
R_USED = R_LOGIT + 11


def nn(left, right):
    return jnp.dot(left, right, preferred_element_type=f32)


def nt(left, right):
    return lax.dot_general(left, right, (((1,), (1,)), ((), ())), preferred_element_type=f32)


def chunks(span):
    return [(c, min(256, span - c)) for c in range(0, span, 256)]


def wide(col_ref, row, rows, width):
    col = col_ref[row : row + rows, :]
    return jnp.concatenate([col] * (width // LANES), axis=1) if width > LANES else col


def lanes_in(values):
    total = values[:, :LANES]
    for c in range(LANES, values.shape[1], LANES):
        total = total + values[:, c : c + LANES]
    return total


def eye(size):
    return (
        lax.broadcasted_iota(jnp.int32, (size, size), 0)
        == lax.broadcasted_iota(jnp.int32, (size, size), 1)
    ).astype(bf16)


def standardise(x):
    mean = jnp.sum(x, axis=0, keepdims=True) * (1.0 / D)
    centred = x - mean
    variance = jnp.sum(centred * centred, axis=0, keepdims=True) * (1.0 / D)
    scale = lax.rsqrt(variance + norm_eps)
    return centred * scale, scale


def standardise_back(dx, hat, scale):
    mean_one = jnp.sum(dx, axis=0, keepdims=True) * (1.0 / D)
    mean_two = jnp.sum(dx * hat, axis=0, keepdims=True) * (1.0 / D)
    return scale * (dx - mean_one - hat * mean_two)


def gelu_parts(x):
    half_erf = 0.5 * lax.erf(x * (2.0**-0.5)) + 0.5
    return half_erf


def start_part(c, width, student, embed, pos_ref, col_ref, w, sc, eyes):
    cols = pl.ds(c, width)
    embedded = embed(c, width) + pos_ref[:, cols]
    hat, scale = standardise(embedded)
    start = hat * wide(col_ref, 0, D, width) + wide(col_ref, D, D, width)
    if student:
        sc["hat0"][:, cols] = hat
        sc["scale"][0:1, cols] = scale
        start = start * wide(col_ref, C_GH, D, width)
    sc["start"][:, cols] = start
    start_low = start.astype(bf16)
    if student:
        sc["start_low"][:, cols] = start_low
    q = nn(w["qkvT"][0:D, :], start_low) + wide(col_ref, 6 * D, D, width)
    sc["qkv"][0:D, cols] = q.astype(bf16)
    k = nn(w["qkvT"][D : 2 * D, :], start_low).astype(bf16)
    sc["qkv"][D : 2 * D, cols] = k
    v = (nn(w["qkvT"][2 * D : 3 * D, :], start_low) + wide(col_ref, 7 * D, D, width)).astype(bf16)
    sc["qkv"][2 * D : 3 * D, cols] = v
    for h in range(HEADS):
        rows = slice(h * HD, (h + 1) * HD)
        sc["k_rows"][h, cols, :] = nt(eyes[width], k[rows, :]).astype(bf16)
        if student:
            sc["v_rows"][h, cols, :] = nt(eyes[width], v[rows, :]).astype(bf16)


def attend(span, length, student, col_ref, sc):
    for c, width in chunks(span):
        valid = lax.broadcasted_iota(jnp.int32, (span, width), 0) < length
        for h in range(HEADS):
            q_h = sc["qkv"][h * HD : (h + 1) * HD, c : c + width] * bf16(HD**-0.5)
            scores = jnp.where(valid, nn(sc["k_rows"][h, 0:span, :], q_h), -1e30)
            shares = jnp.exp(scores - jnp.max(scores, axis=0, keepdims=True))
            shares_low = (shares * (1.0 / jnp.sum(shares, axis=0, keepdims=True))).astype(bf16)
            if student:
                sc["shares"][h, 0:span, c : c + width] = shares_low
            context = nn(sc["qkv"][2 * D + h * HD : 2 * D + (h + 1) * HD, 0:span], shares_low)
            if student:
                sc["context"][h * HD : (h + 1) * HD, c : c + width] = context
                context = context * wide(col_ref, C_HEAD + h * HD, HD, width)
            sc["gated"][h * HD : (h + 1) * HD, c : c + width] = context.astype(bf16)


def middle_part(c, width, student, col_ref, w, sc):
    cols = pl.ds(c, width)
    branch = nn(w["oT"][...], sc["gated"][:, cols]) + wide(col_ref, 8 * D, D, width)
    if student:
        sc["branch"][:, 0:width] = branch
        branch = branch * wide(col_ref, C_GH, D, width)
    hat, scale = standardise(sc["start"][:, cols] + branch)
    middle = hat * wide(col_ref, 2 * D, D, width) + wide(col_ref, 3 * D, D, width)
    if student:
        sc["hat1"][:, 0:width] = hat
        sc["scale"][1:2, cols] = scale
    middle_low = middle.astype(bf16)
    if student:
        sc["middle_low"][:, 0:width] = middle_low
    for r in range(0, FF, D):
        pre = nn(w["upT"][r : r + D, :], middle_low) + wide(col_ref, C_BUP + r, D, width)
        cdf = 0.5 * lax.erf(pre * (2.0**-0.5)) + 0.5
        act = pre * cdf
        if student:
            inner = wide(col_ref, C_GI + r, D, width)
            pdf = jnp.exp(pre * pre * -0.5) * (1.0 / math.sqrt(2.0 * math.pi))
            sc["act"][r : r + D, 0:width] = act
            sc["slope"][r : r + D, 0:width] = (cdf + pre * pdf) * inner
            act = act * inner
        sc["up"][r : r + D, 0:width] = act.astype(bf16)
    down = nn(w["downT"][...], sc["up"][:, 0:width]) + wide(col_ref, 9 * D, D, width)
    if student:
        sc["down"][:, 0:width] = down
        down = down * wide(col_ref, C_GH, D, width)
    hat, scale = standardise(middle + down)
    out = hat * wide(col_ref, 4 * D, D, width) + wide(col_ref, 5 * D, D, width)
    return out, hat, scale


def add_lanes(add_ref, row, values):
    add_ref[row : row + values.shape[0], :] += lanes_in(values)


def back_part(c, width, length, factor, out, hat, scale, target_ref, col_ref, w, sc, acc, add_ref, loss_ref):
    cols = pl.ds(c, width)
    here = slice(0, width)
    add = functools.partial(add_lanes, add_ref)
    out_low = out.astype(bf16)
    differ = nn(w["aT"][...], out_low) - target_ref[0, :, cols]
    token_valid = (lax.broadcasted_iota(jnp.int32, (1, width), 1) + c < length).astype(f32)
    loss_ref[0:1, cols] += jnp.sum(differ * differ, axis=0, keepdims=True) * (1.0 / D) * token_valid
    d_aligned = (differ * (token_valid * factor)).astype(bf16)
    acc["a"][...] += nt(out_low, d_aligned)
    d_out = nn(w["a"][...], d_aligned)
    add(4 * D, d_out * hat)
    add(5 * D, d_out)
    d_second = standardise_back(d_out * wide(col_ref, 4 * D, D, width), hat, scale)
    add(A_GH, d_second * sc["down"][:, here])
    d_down = (d_second * wide(col_ref, C_GH, D, width)).astype(bf16)
    add(9 * D, d_down.astype(f32))
    acc["down"][...] += nt(sc["up"][:, here], d_down)
    for r in range(0, FF, D):
        d_up = nn(w["down"][r : r + D, :], d_down)
        add(A_GI + r, d_up * sc["act"][r : r + D, here])
        d_pre = (d_up * sc["slope"][r : r + D, here]).astype(bf16)
        sc["d_pre"][r : r + D, here] = d_pre
        add(A_BUP + r, d_pre.astype(f32))
    d_middle = d_second + nn(w["up"][...], sc["d_pre"][:, here])
    acc["up"][...] += nt(sc["middle_low"][:, here], sc["d_pre"][:, here])
    hat = sc["hat1"][:, here]
    add(2 * D, d_middle * hat)
    add(3 * D, d_middle)
    d_first = standardise_back(
        d_middle * wide(col_ref, 2 * D, D, width), hat, sc["scale"][1:2, cols]
    )
    sc["d_first"][:, cols] = d_first
    add(A_GH, d_first * sc["branch"][:, here])
    d_branch = (d_first * wide(col_ref, C_GH, D, width)).astype(bf16)
    add(8 * D, d_branch.astype(f32))
    acc["o"][...] += nt(sc["gated"][:, cols], d_branch)
    d_gated = nn(w["o"][...], d_branch)
    context = sc["context"][:, cols]
    add(A_HEAD, d_gated * context)
    d_context = d_gated * wide(col_ref, C_HEAD, D, width)
    sc["d_context"][:, cols] = d_context.astype(bf16)
    dot_rows = d_context * context
    for h in range(HEADS):
        sc["delta"][h : h + 1, cols] = jnp.sum(
            dot_rows[h * HD : (h + 1) * HD, :], axis=0, keepdims=True
        )


def attend_back(span, sc):
    full = slice(0, span)
    for h in range(HEADS):
        rows = slice(h * HD, (h + 1) * HD)
        d_value = nt(sc["d_context"][rows, full], sc["shares"][h, 0:span, 0:span])
        sc["d_qkv"][2 * D + h * HD : 2 * D + (h + 1) * HD, full] = d_value.astype(bf16)
        d_key = None
        for c, width in chunks(span):
            cols = slice(c, c + width)
            d_shares = nn(sc["v_rows"][h, 0:span, :], sc["d_context"][rows, cols])
            d_scores = (
                sc["shares"][h, 0:span, cols].astype(f32) * (d_shares - sc["delta"][h : h + 1, cols])
            ).astype(bf16)
            sc["d_qkv"][rows, cols] = (
                nn(sc["qkv"][D + h * HD : D + (h + 1) * HD, full], d_scores) * (HD**-0.5)
            ).astype(bf16)
            part = nt(sc["qkv"][rows, cols], d_scores)
            d_key = part if d_key is None else d_key + part
        sc["d_qkv"][D + h * HD : D + (h + 1) * HD, full] = (d_key * (HD**-0.5)).astype(bf16)


def end_part(c, width, col_ref, w, sc, acc, add_ref, grad_ref, pos_add):
    cols = pl.ds(c, width)
    add = functools.partial(add_lanes, add_ref)
    acc["qkv"][...] += nt(sc["start_low"][:, cols], sc["d_qkv"][:, cols])
    add(6 * D, sc["d_qkv"][0:D, cols].astype(f32))
    add(7 * D, sc["d_qkv"][2 * D : 3 * D, cols].astype(f32))
    d_start = sc["d_first"][:, cols] + nn(w["qkv"][...], sc["d_qkv"][:, cols])
    hat = sc["hat0"][:, cols]
    gain = wide(col_ref, 0, D, width)
    add(A_GH, d_start * (hat * gain + wide(col_ref, D, D, width)))
    d_norm = d_start * wide(col_ref, C_GH, D, width)
    add(0, d_norm * hat)
    add(D, d_norm)
    d_embedded = standardise_back(d_norm * gain, hat, sc["scale"][0:1, cols])
    pos_add[:, cols] += d_embedded
    grad_ref[0, :, cols] = d_embedded.astype(bf16)


def by_part(length, body):
    def step(i, carry):
        body(pl.multiple_of(i * 256, 256), 256)
        return carry

    lax.fori_loop(0, jnp.where(length > 384, 2, 1), step, 0)
    pl.when((length > 256) & (length <= 384))(lambda: body(256, 128))


def mark_slots(slot, perm_ref):
    step = 512
    width = slot.shape[1]

    def mark(i, carry):
        rows = pl.ds(pl.multiple_of(i * step, step), step)
        seen = lax.broadcasted_iota(jnp.int32, (step, width), 0) == slot - i * step
        perm_ref[rows, :] = seen.astype(f32).astype(bf16)
        return carry

    lax.fori_loop(0, perm_ref.shape[0] // step, mark, 0)


def pack_rows(span, perm_ref, grad_ref, packed_ref):
    step = 1024

    def add(i, carry):
        rows = pl.ds(pl.multiple_of(i * step, step), step)
        packed_ref[rows, :] += nt(perm_ref[rows, 0:span], grad_ref[0, :, 0:span]).astype(bf16)
        return carry

    lax.fori_loop(0, packed_ref.shape[0] // step, add, 0)


SPANS = (256, 384, 512)


def by_span(length, body):
    for i, span in enumerate(SPANS):
        low = SPANS[i - 1] if i else 0
        test = length > low
        if i == 0:
            test = length <= span
        elif i < len(SPANS) - 1:
            test = (length > low) & (length <= span)
        pl.when(test)(functools.partial(body, span))


def set_up(pos_in, pos_ref, eyes_refs):
    for size, ref in eyes_refs.items():
        ref[...] = eye(size)
    for c in range(0, LEN, 256):
        pos_ref[:, c : c + 256] = nt(eyes_refs[256][...], pos_in[c : c + 256, :])


TEACHER_W = (
    ("qkv", (D, 3 * D)),
    ("qkvT", (3 * D, D)),
    ("o", (D, D)),
    ("oT", (D, D)),
    ("up", (D, FF)),
    ("upT", (FF, D)),
    ("down", (FF, D)),
    ("downT", (D, FF)),
)
STUDENT_W = TEACHER_W + (("a", (D, D)), ("aT", (D, D)))


def spread(col_ref, at, row):
    col_ref[at : at + LANES, :] = jnp.transpose(jnp.broadcast_to(row, (LANES, LANES)))


def load_weights(flat, w, col_ref, one, student):
    squares = [("qkv", 0), ("qkv", D), ("qkv", 2 * D), ("o", 0)] + ([("a", 0)] if student else [])
    for i, (name, at) in enumerate(squares):
        for j in range(2):
            lanes = slice(at + j * LANES, at + (j + 1) * LANES)
            w[name][:, lanes] = flat[pl.ds(512 * i + j, D, stride=2), :].astype(bf16)
    base = 512 * len(squares)
    for j in range(8):
        w["up"][:, j * LANES : (j + 1) * LANES] = flat[pl.ds(base + j, D, stride=8), :].astype(bf16)
    base = base + 2048
    for j in range(2):
        w["down"][:, j * LANES : (j + 1) * LANES] = flat[pl.ds(base + j, FF, stride=2), :].astype(
            bf16
        )
    base = base + 2048
    for i in range(20):
        spread(col_ref, i * LANES, flat[base + i : base + i + 1, :])
    for j in range(8):
        spread(col_ref, C_BUP + j * LANES, flat[base + 20 + j : base + 21 + j, :])
    unit = one[...]
    for name in ("qkv", "o", "up") + (("a",) if student else ()):
        for b in range(0, w[name].shape[1], D):
            w[name + "T"][b : b + D, :] = nt(unit, w[name][:, b : b + D]).astype(bf16)
    for b in range(0, FF, D):
        w["downT"][:, b : b + D] = nt(unit, w["down"][b : b + D, :]).astype(bf16)


def total_of(x):
    return jnp.sum(jnp.sum(x, axis=0, keepdims=True), axis=1, keepdims=True)


def head_groups():
    return (
        lax.broadcasted_iota(jnp.int32, (D, LANES), 0) // HD
        == lax.broadcasted_iota(jnp.int32, (D, LANES), 1)
    ).astype(f32)


def load_gates(logits, noise, lagrange_ref, lag_weight, col_ref, slope_ref, lag_ref):
    index = lax.broadcasted_iota(
        jnp.int32, logits.shape, 0
    ) * LANES + lax.broadcasted_iota(jnp.int32, logits.shape, 1)
    hidden, heads = index < D, (index >= D) & (index < D + HEADS)
    inner = (index >= D + HEADS) & (index < D + HEADS + FF)
    logistic = jax.nn.sigmoid((jnp.log(noise) - jnp.log(1.0 - noise) + logits) / relaxation_heat)
    spanned = widened_right_limit - widened_left_limit
    stretched = logistic * spanned + widened_left_limit
    gates = jnp.clip(stretched, 0.0, 1.0)
    inside = jnp.where((stretched > 0.0) & (stretched < 1.0), 1.0, 0.0)
    inside = jnp.where((stretched == 0.0) | (stretched == 1.0), 0.5, inside)
    slope_ref[...] = inside * logistic * (1.0 - logistic) * (spanned / relaxation_heat)
    keep = jax.nn.sigmoid(
        logits - relaxation_heat * math.log(-widened_left_limit / widened_right_limit)
    )
    kept = total_of(jnp.where(hidden, keep, 0.0)) * (1.0 / D)
    rest = total_of(jnp.where(heads, keep * (4.0 * HD), 0.0) + jnp.where(inner, keep * 2.0, 0.0))
    scale = 1.0 / (4.0 * D + 2.0 * FF)
    excess = kept * rest * scale - sparse_target
    rate = (lagrange_ref[0] + 2.0 * lagrange_ref[1] * excess) * (scale * lag_weight)
    share = jnp.where(hidden, rest * (1.0 / D), 0.0)
    share = share + kept * (jnp.where(heads, 4.0 * HD, 0.0) + jnp.where(inner, 2.0, 0.0))
    lag_ref[...] = rate * share * (keep * (1.0 - keep))
    for j in range(2):
        spread(col_ref, C_GH + j * LANES, gates[j : j + 1, :])
    wide_heads = lax.dot_general(
        jnp.broadcast_to(gates[2:3, :], (8, LANES)),
        head_groups(),
        (((1,), (1,)), ((), ())),
        preferred_element_type=f32,
        precision=lax.Precision.HIGHEST,
    )
    for j in range(2):
        spread(col_ref, C_HEAD + j * LANES, wide_heads[0:1, j * LANES : (j + 1) * LANES])
    run = jnp.concatenate([gates[j : j + 1, :] for j in range(2, 11)], axis=1)
    run = pltpu.roll(jnp.broadcast_to(run, (8, 9 * LANES)), 9 * LANES - HEADS, 1)
    for j in range(8):
        spread(col_ref, C_GI + j * LANES, run[0:1, j * LANES : (j + 1) * LANES])
    return lagrange_ref[0] * excess + lagrange_ref[1] * excess * excess


TEACHER_S = (
    ("start", (D, LEN), f32),
    ("qkv", (3 * D, LEN), bf16),
    ("k_rows", (HEADS, LEN, HD), bf16),
    ("gated", (D, LEN), bf16),
    ("up", (FF, 256), bf16),
)
STUDENT_S = TEACHER_S + (
    ("start_low", (D, LEN), bf16),
    ("hat0", (D, LEN), f32),
    ("hat1", (D, 256), f32),
    ("scale", (8, LEN), f32),
    ("v_rows", (HEADS, LEN, HD), bf16),
    ("shares", (HEADS, LEN, LEN), bf16),
    ("context", (D, LEN), f32),
    ("branch", (D, 256), f32),
    ("middle_low", (D, 256), bf16),
    ("act", (FF, 256), f32),
    ("slope", (FF, 256), f32),
    ("down", (D, 256), f32),
    ("d_pre", (FF, 256), bf16),
    ("d_first", (D, LEN), f32),
    ("d_context", (D, LEN), bf16),
    ("delta", (8, LEN), f32),
    ("d_qkv", (3 * D, LEN), bf16),
)
ACCS = (
    ("qkv", (D, 3 * D)),
    ("o", (D, D)),
    ("a", (D, D)),
    ("up", (D, FF)),
    ("down", (FF, D)),
)


class Eyes:
    def __init__(self, one, two):
        self.refs = {128: one, 256: two}

    def __getitem__(self, size):
        return self.refs[size][...]


def student_kernel(n, flat_len, sparse, len_ref, fac_ref, lagrange_ref, noise_ref, flat_in, pos_in, target_ref, *rest):
    plane, planes, flat_seg = plan(n, flat_len)[:3]
    cap = room(n)
    if sparse:
        slot_ref, rows_ref = rest[:2]
        rest = rest[2:]
    else:
        rows_ref = rest[0]
        rest = rest[1:]
    flat_ref, grad_ref, loss_ref = rest[:3]
    rest = rest[3:]
    if sparse:
        packed_ref, rows_all, perm_ref, slot_now = rest[:4]
        rest = rest[4:]
    w = {entry[0]: rest[i] for i, entry in enumerate(STUDENT_W)}
    rest = rest[len(STUDENT_W) :]
    sc = {entry[0]: rest[i] for i, entry in enumerate(STUDENT_S)}
    rest = rest[len(STUDENT_S) :]
    acc = {entry[0]: rest[i] for i, entry in enumerate(ACCS)}
    add_ref, pos_add, slope_ref, lag_ref, col_ref, pos_ref, eye_one, eye_two = rest[len(ACCS) :]
    s = pl.program_id(0)
    eyes = Eyes(eye_one, eye_two)

    @pl.when(s == 0)
    def _():
        set_up(pos_in, pos_ref, eyes.refs)
        for o in range(n):
            c = o // 2
            flat_ref[o * flat_seg : (o + 1) * flat_seg, :] = flat_in[
                o % 2, c % plane, c // plane, :, :
            ].astype(f32)[:flat_seg]
        load_weights(flat_ref, w, col_ref, eye_two, True)
        lag_value = load_gates(
            flat_ref[R_LOGIT : R_LOGIT + 16, :],
            noise_ref[...],
            lagrange_ref,
            fac_ref[1],
            col_ref,
            slope_ref,
            lag_ref,
        )
        for ref in list(acc.values()) + [add_ref, pos_add]:
            ref[...] = jnp.zeros(ref.shape, f32)
        row = lax.broadcasted_iota(jnp.int32, (8, LEN), 0)
        loss_ref[...] = jnp.where(row == 1, lag_value, 0.0)
        if sparse:
            packed_ref[...] = jnp.zeros(packed_ref.shape, bf16)
            for o in range(n):
                rows_all[:, o * cap : (o + 1) * cap] = rows_ref[o]

    length = len_ref[s]

    def embed(c, width):
        if sparse:
            mark_slots(slot_now[0:1, pl.ds(c, width)], perm_ref.at[:, pl.ds(c, width)])
            return nn(rows_all[...], perm_ref[:, pl.ds(c, width)])
        at = pl.multiple_of(s * LEN + c, 128)
        return nt(eyes[D], rows_ref[pl.ds(at, width), :])

    def between(c, width):
        out, hat, scale = middle_part(c, width, True, col_ref, w, sc)
        back_part(
            c, width, length, fac_ref[0], out, hat, scale, target_ref, col_ref, w, sc, acc, add_ref, loss_ref
        )

    grad_ref[0, :, 256:LEN] = jnp.zeros((D, LEN - 256), bf16)
    if sparse:
        slot_now[0:1, :] = slot_ref[pl.ds(s, 1), :]
    by_part(
        length, lambda c, width: start_part(c, width, True, embed, pos_ref, col_ref, w, sc, eyes)
    )
    by_span(length, lambda span: attend(span, length, True, col_ref, sc))
    by_part(length, between)
    by_span(length, lambda span: attend_back(span, sc))
    by_part(
        length,
        lambda c, width: end_part(c, width, col_ref, w, sc, acc, add_ref, grad_ref, pos_add),
    )
    if sparse:
        by_span(length, lambda span: pack_rows(span, perm_ref, grad_ref, packed_ref))

    @pl.when(s == pl.num_programs(0) - 1)
    def _():
        for i in range(3):
            for j in range(2):
                at = i * D + j * LANES
                flat_ref[pl.ds(512 * i + j, D, stride=2), :] = acc["qkv"][:, at : at + LANES]
        for j in range(2):
            lanes = slice(j * LANES, (j + 1) * LANES)
            flat_ref[pl.ds(512 * 3 + j, D, stride=2), :] = acc["o"][:, lanes]
            flat_ref[pl.ds(512 * 4 + j, D, stride=2), :] = acc["a"][:, lanes]
            flat_ref[pl.ds(R_DOWN + j, FF, stride=2), :] = acc["down"][:, lanes]
        for j in range(8):
            flat_ref[pl.ds(R_UP + j, D, stride=8), :] = acc["up"][:, j * LANES : (j + 1) * LANES]
        ones = jnp.ones((8, LANES), f32)

        def summed(row, rows):
            return lax.dot_general(
                ones,
                add_ref[row : row + rows, :],
                (((1,), (1,)), ((), ())),
                preferred_element_type=f32,
                precision=lax.Precision.HIGHEST,
            )

        for i in range(10):
            sums = summed(i * D, D)
            for j in range(2):
                flat_ref[R_VEC + 2 * i + j : R_VEC + 2 * i + j + 1, :] = sums[
                    0:1, j * LANES : (j + 1) * LANES
                ]
        sums = summed(A_BUP, FF)
        for j in range(8):
            flat_ref[R_BUP + j : R_BUP + j + 1, :] = sums[0:1, j * LANES : (j + 1) * LANES]
        hidden = summed(A_GH, D)
        heads = jnp.dot(
            summed(A_HEAD, D),
            head_groups(),
            preferred_element_type=f32,
            precision=lax.Precision.HIGHEST,
        )
        inner = summed(A_GI, FF)
        moved = pltpu.roll(jnp.concatenate([inner, jnp.zeros((8, LANES), f32)], axis=1), HEADS, 1)
        lane = lax.broadcasted_iota(jnp.int32, (8, LANES), 1)
        first = jnp.where(lane < HEADS, heads, moved[:, :LANES])
        tail = [hidden[:, :LANES], hidden[:, LANES:], first] + [
            moved[:, j * LANES : (j + 1) * LANES] for j in range(1, 9)
        ]
        for j, piece in enumerate(tail):
            flat_ref[R_LOGIT + j : R_LOGIT + j + 1, :] = (
                piece[0:1] * slope_ref[j : j + 1, :] + lag_ref[j : j + 1, :]
            )
        flat_ref[R_USED:flat_len, :] = jnp.zeros((flat_len - R_USED, LANES), f32)
        for j in range(2):
            flat_ref[pl.ds(flat_len + j, LEN, stride=2), :] = jnp.transpose(
                pos_add[j * LANES : (j + 1) * LANES, :]
            )


def whole_spec():
    return pl.BlockSpec(memory_space=pltpu.VMEM)


def smem_spec():
    return pl.BlockSpec(memory_space=pltpu.SMEM)


def seq_spec():
    return pl.BlockSpec((1, D, LEN), lambda s: (s, 0, 0))


def common_scratch():
    return [
        pltpu.VMEM((C_ROWS, LANES), f32),
        pltpu.VMEM((D, LEN), f32),
        pltpu.VMEM((128, 128), bf16),
        pltpu.VMEM((256, 256), bf16),
    ]


def run_student(n, flat_len, sparse, lengths, factors, lagrange, noise, flat_all, places, target, given):
    seqs = lengths.shape[0]
    slot_rows = n * room(n)
    shapes = [
        jax.ShapeDtypeStruct((flat_len + 2 * LEN, LANES), f32),
        jax.ShapeDtypeStruct((seqs, D, LEN), bf16),
        jax.ShapeDtypeStruct((8, LEN), f32),
    ]
    out_specs = [whole_spec(), seq_spec(), whole_spec()]
    scratch = []
    if sparse:
        shapes.append(jax.ShapeDtypeStruct((slot_rows, D), bf16))
        out_specs.append(whole_spec())
        scratch = [
            pltpu.VMEM((D, slot_rows), bf16),
            pltpu.VMEM((slot_rows, LEN), bf16),
            pltpu.VMEM((8, LEN), jnp.int32),
        ]
    return pl.pallas_call(
        functools.partial(student_kernel, n, flat_len, sparse),
        grid=(seqs,),
        out_shape=tuple(shapes),
        in_specs=[smem_spec()] * 3
        + [whole_spec()] * 3
        + [seq_spec()]
        + [whole_spec()] * len(given),
        out_specs=tuple(out_specs),
        scratch_shapes=scratch
        + [pltpu.VMEM(shape, bf16) for _, shape in STUDENT_W]
        + [pltpu.VMEM(shape, kind) for _, shape, kind in STUDENT_S]
        + [pltpu.VMEM(shape, f32) for _, shape in ACCS]
        + [
            pltpu.VMEM((A_ROWS, LANES), f32),
            pltpu.VMEM((D, LEN), f32),
            pltpu.VMEM((16, LANES), f32),
            pltpu.VMEM((16, LANES), f32),
        ]
        + common_scratch(),
        compiler_params=pltpu.CompilerParams(vmem_limit_bytes=VMEM_LIMIT),
        name="student" if sparse else "student_dense",
    )(lengths, factors, lagrange, noise, flat_all, places, target, *given)


MESH = pl.DeviceIdType.MESH


def room(n):
    return LANES if 8 * LEN // n >= LANES else 0


def greet_all(me, n):
    barrier = pltpu.get_barrier_semaphore()

    def signal(k, carry):
        pl.semaphore_signal(barrier, inc=1, device_id=(me ^ k,), device_id_type=MESH)
        return carry

    lax.fori_loop(1, n, signal, 0)
    pl.semaphore_wait(barrier, n - 1)


def copy_to(source, target, send, receive, device):
    return pltpu.make_async_remote_copy(
        src_ref=source,
        dst_ref=target,
        send_sem=send,
        recv_sem=receive,
        device_id=(device,),
        device_id_type=MESH,
    )


def list_rows(n, owner_ref, local_ref, stat, slot_ref, tile_ref):
    cap = room(n)
    upper = (
        lax.broadcasted_iota(jnp.int32, (256, 256), 0)
        <= lax.broadcasted_iota(jnp.int32, (256, 256), 1)
    ).astype(bf16)
    base = jnp.zeros((n, 1), f32)
    listed = jnp.zeros((n, LANES), f32)
    for s in range(owner_ref.shape[0]):
        for c in range(0, LEN, 256):
            owner = owner_ref[s : s + 1, c : c + 256]
            mine = (lax.broadcasted_iota(jnp.int32, (n, 256), 0) == owner).astype(f32)
            before = nn(mine.astype(bf16), upper)
            rank = jnp.sum(mine * (before - 1.0 + base), axis=0, keepdims=True).astype(jnp.int32)
            fits = (owner >= 0) & (rank < cap)
            slot_ref[s : s + 1, c : c + 256] = jnp.where(fits, owner * cap + rank, n * cap)
            place = (
                lax.broadcasted_iota(jnp.int32, (LANES, 256), 0) == jnp.where(fits, rank, -1)
            ).astype(f32)
            listed = listed + lax.dot_general(
                mine * local_ref[s : s + 1, c : c + 256],
                place,
                (((1,), (1,)), ((), ())),
                preferred_element_type=f32,
                precision=lax.Precision.HIGHEST,
            )
            base = base + before[:, 255:256]
    over = jnp.max(base, axis=0, keepdims=True) > cap
    lane = lax.broadcasted_iota(jnp.int32, (n, LANES), 1)
    tile_ref[...] = jnp.zeros(tile_ref.shape, jnp.int32)
    tile_ref[pl.ds(0, n, stride=8), :] = (listed + 0.5).astype(jnp.int32) - 1
    tile_ref[pl.ds(1, n, stride=8), :] = jnp.where(
        lane == 0, stat, jnp.where(lane == 1, over.astype(jnp.int32), 0)
    )


def place_parts(vrows):
    parts = []
    for o in range(VOCAB // vrows, (VOCAB + LEN - 1) // vrows + 1):
        low, top = max(VOCAB, o * vrows), min(VOCAB + LEN, (o + 1) * vrows)
        parts.append((o, low - o * vrows, low - VOCAB, top - low))
    return parts


def round_up(value, step):
    return -(-value // step) * step


def pair_lists(list_ref, a, cap):
    return jnp.concatenate(
        [list_ref[pl.ds(pl.multiple_of(a * 16 + 8 * j, 8), 8), :][0:1, :cap] for j in range(2)],
        axis=1,
    )


def fetch_kernel(
    n, flat_len, owner_ref, local_ref, stat_ref, len_ref, block_ref, row_ref, words_in, pos_in, flat_in, table_ref, own_flat, *rest
):
    plane, planes, flat_seg, flat_pad = plan(n, flat_len)[:4]
    cap = room(n)
    vrows = table_ref.shape[0]
    parts = place_parts(vrows)
    out_ref, got_out, flat_out, place_out = rest[:4]
    rest = rest[4:]
    if cap:
        slot_ref, rows_out = rest[:2]
        rest = rest[2:]
    w = {entry[0]: rest[i] for i, entry in enumerate(TEACHER_W)}
    rest = rest[len(TEACHER_W) :]
    sc = {entry[0]: rest[i] for i, entry in enumerate(TEACHER_S)}
    rest = rest[len(TEACHER_S) :]
    tile_ref, got_ref, flat_all, place_all, pad_ref, flat_f32 = rest[:6]
    list_sem, a_sem, b_sem, c_sem, pa_sem, pb_sem, pc_sem = rest[6:13]
    col_ref, pos_ref, eye_one, eye_two = rest[13:17]
    words, picked, word_sem = rest[17:20]
    if cap:
        table_turned, row_send, rows_in, row_sem = rest[20:]
    eyes = Eyes(eye_one, eye_two)
    s = pl.program_id(0)
    seqs = owner_ref.shape[0]
    me = lax.axis_index("dp")
    core = lax.rem(me, 2)
    chip = me // 2
    mid = lax.rem(chip, plane)
    high = chip // plane

    def device(h, m, c):
        return (h * plane + m) * 2 + c

    def tile(ref, i):
        return ref.at[pl.ds(pl.multiple_of(i * 8, 8), 8), :]

    def list_copy(k):
        return copy_to(
            tile(tile_ref, me ^ k), tile(got_ref, me), list_sem.at[0, k], list_sem.at[1, k], me ^ k
        )

    def row_copy(k):
        return copy_to(
            row_send.at[me ^ k], rows_in.at[me], row_sem.at[0, k], row_sem.at[1, k], me ^ k
        )

    def flat_copies(stage):
        copies = []
        if stage == 0:
            spot = flat_all.at[core, mid, high]
            for k in range(1, planes):
                to = device(lax.rem(high + k, planes), mid, core)
                copies.append(copy_to(spot, spot, a_sem.at[0, k], a_sem.at[1, k], to))
        elif stage == 1:
            spot = flat_all.at[core, mid]
            for k in range(1, plane):
                to = device(high, lax.rem(mid + k, plane), core)
                copies.append(copy_to(spot, spot, b_sem.at[0, k], b_sem.at[1, k], to))
        else:
            spot = flat_all.at[core]
            copies.append(copy_to(spot, spot, c_sem.at[0], c_sem.at[1], me ^ 1))
        return copies

    def place_copies(stage, i):
        o, _, _, count = parts[i]
        chip_o = o // 2
        high_o, mid_o, core_o = chip_o // plane, chip_o % plane, o % 2
        spot = place_all.at[i, pl.ds(0, round_up(count, 16)), :]
        same_core, same_mid, same_high = core == core_o, mid == mid_o, high == high_o
        copies = []
        if stage == 0:
            for k in range(1, planes):
                to = device((high_o + k) % planes, mid_o, core_o)
                copies.append(copy_to(spot, spot, pa_sem.at[0, i, k], pa_sem.at[1, i, 0], to))
            sends = same_core & same_mid & same_high
            receives = same_core & same_mid & (high != high_o)
        elif stage == 1:
            for k in range(1, plane):
                to = device(high, (mid_o + k) % plane, core_o)
                copies.append(copy_to(spot, spot, pb_sem.at[0, i, k], pb_sem.at[1, i, 0], to))
            sends = same_core & same_mid
            receives = same_core & (mid != mid_o)
        else:
            copies.append(copy_to(spot, spot, pc_sem.at[0, i], pc_sem.at[1, i], me ^ 1))
            sends = same_core
            receives = core != core_o
        return copies, sends, receives

    def start_stage(stage):
        for copy in flat_copies(stage):
            copy.start()
        for i in range(len(parts)):
            copies, sends, _ = place_copies(stage, i)

            @pl.when(sends)
            def _():
                for copy in copies:
                    copy.start()

    def finish_stage(stage):
        for copy in flat_copies(stage):
            copy.wait()
        for i in range(len(parts)):
            copies, sends, receives = place_copies(stage, i)

            @pl.when(sends)
            def _():
                for copy in copies:
                    copy.wait_send()

            @pl.when(receives)
            def _():
                copies[0].wait_recv()

    known = words.shape[0] * 16
    word_copy = pltpu.make_async_copy(
        words_in.at[pl.ds(0, known), :], words.reshape(known, D), word_sem
    )

    @pl.when(s == 0)
    def _():
        word_copy.start()
        picked[...] = jnp.zeros(picked.shape, f32)
        greet_all(me, n)
        pad_ref[...] = jnp.zeros(pad_ref.shape, f32)
        pad_ref[0:flat_seg, :] = own_flat[...]
        flat_all[core, mid, high] = pad_ref[...].astype(bf16)
        for i, (o, at, _, count) in enumerate(parts):

            @pl.when(me == o)
            def _():
                full = round_up(count, 16)
                part = table_ref[at : at + count, :]
                if full > count:
                    part = jnp.concatenate([part, jnp.zeros((full - count, D), f32)], axis=0)
                place_all[i, 0:full, :] = part.astype(bf16)

        start_stage(0)
        if cap:
            list_rows(n, owner_ref, local_ref, stat_ref[0], slot_ref, tile_ref)
        else:
            tile_ref[...] = jnp.zeros(tile_ref.shape, jnp.int32) + stat_ref[0]

        def start_list(k, carry):
            list_copy(k).start()
            return carry

        lax.fori_loop(1, n, start_list, 0)
        own = pl.ds(pl.multiple_of(me * 8, 8), 8)
        got_ref[own, :] = tile_ref[own, :]
        set_up(pos_in, pos_ref, eyes.refs)
        if cap:
            table_turned[...] = nt(eye_two[...], table_ref[...].astype(bf16)).astype(bf16)

        def finish_list(k, carry):
            list_copy(k).wait()
            return carry

        lax.fori_loop(1, n, finish_list, 0)

        def serve(step, carry):
            i = n // 2 - 1 - step
            a = chip ^ i
            pick = (
                lax.broadcasted_iota(jnp.int32, (vrows, 2 * cap), 0) == pair_lists(got_ref, a, cap)
            ).astype(bf16)
            both = nn(table_turned[...], pick).astype(bf16)
            for j in range(2):
                row_send[2 * a + j] = both[:, j * cap : (j + 1) * cap]
                k = 2 * i + (core ^ j)
                pl.when(k > 0)(row_copy(k).start)
            return carry

        if cap:
            lax.fori_loop(0, n // 2, serve, 0)
            rows_in[me] = row_send[me]
        flat_f32[...] = flat_in[...].astype(f32)
        load_weights(flat_f32, w, col_ref, eye_two, False)
        word_copy.wait()

    @pl.when(s == 2)
    def _():
        finish_stage(0)
        start_stage(1)

    @pl.when(s == 4)
    def _():
        finish_stage(1)
        start_stage(2)

    length = len_ref[s]
    from_me = jnp.where(s < seqs // 2, me, n - 1 - me)
    longest = LEN // 3 + (LEN - LEN // 3) * from_me // (n - 1)

    def pick_eight(g, carry):
        rows = []
        for u in range(8):
            block = words[block_ref[s, g * 8 + u]].astype(f32)
            mine = lax.broadcasted_iota(jnp.int32, (16, D), 0) == row_ref[s, g * 8 + u]
            rows.append(jnp.sum(jnp.where(mine, block, 0.0), axis=0, keepdims=True))
        picked[pl.ds(pl.multiple_of(g * 8, 8), 8), :] = jnp.concatenate(rows, axis=0)
        return carry

    lax.fori_loop(0, (longest + 7) // 8, pick_eight, 0)

    def embed(c, width):
        return nt(eyes[D], picked[pl.ds(c, width), :].astype(bf16))

    def finish(c, width):
        out_ref[0, :, pl.ds(c, width)] = middle_part(c, width, False, col_ref, w, sc)[0]

    def body(span):
        for c, width in chunks(span):
            start_part(c, width, False, embed, pos_ref, col_ref, w, sc, eyes)
        attend(span, length, False, col_ref, sc)
        for c, width in chunks(span):
            finish(c, width)

    by_span(longest, body)

    @pl.when(s == seqs - 1)
    def _():
        finish_stage(2)

        def finish_row(k, carry):
            row_copy(k).wait()
            return carry

        if cap:
            lax.fori_loop(1, n, finish_row, 0)
            rows_out[...] = rows_in[...]
        got_out[...] = got_ref[...]
        flat_out[...] = flat_all[...]
        place_out[...] = place_all[...]


def run_fetch(n, flat_len, owner, local, stat, lengths, blocks, rows, words, places, teacher, table, own_flat):
    plane, planes, flat_seg, flat_pad = plan(n, flat_len)[:4]
    seqs, cap, vrows = owner.shape[0], room(n), table.shape[0]
    parts = place_parts(vrows)
    most = max(round_up(part[3], 16) for part in parts)
    dma = pltpu.SemaphoreType.DMA
    got = ((8 * n, LANES), jnp.int32)
    fetched = ((n, D, cap), bf16)
    flat_all = ((2, plane, planes, flat_pad, LANES), bf16)
    place_all = ((len(parts), most, D), bf16)
    shapes = [((seqs, D, LEN), f32), got, flat_all, place_all]
    extra = []
    if cap:
        shapes += [(owner.shape, jnp.int32), fetched]
        extra = [
            pltpu.VMEM((D, vrows), bf16),
            pltpu.VMEM(*fetched),
            pltpu.VMEM(*fetched),
            dma((2, n)),
        ]
    return pl.pallas_call(
        functools.partial(fetch_kernel, n, flat_len),
        grid=(seqs,),
        out_shape=tuple(jax.ShapeDtypeStruct(shape, kind) for shape, kind in shapes),
        in_specs=[whole_spec()] * 2
        + [smem_spec()] * 4
        + [pl.BlockSpec(memory_space=pl.ANY)]
        + [whole_spec()] * 4,
        out_specs=(seq_spec(),) + (whole_spec(),) * (len(shapes) - 1),
        scratch_shapes=[pltpu.VMEM(shape, bf16) for _, shape in TEACHER_W]
        + [pltpu.VMEM(shape, kind) for _, shape, kind in TEACHER_S]
        + [
            pltpu.VMEM(*got),
            pltpu.VMEM(*got),
            pltpu.VMEM(*flat_all),
            pltpu.VMEM(*place_all),
            pltpu.VMEM((flat_pad, LANES), f32),
            pltpu.VMEM(teacher.shape, f32),
            dma((2, n)),
            dma((2, planes)),
            dma((2, plane)),
            dma((2,)),
            dma((2, len(parts), planes)),
            dma((2, len(parts), plane)),
            dma((2, len(parts))),
        ]
        + common_scratch()
        + [pltpu.VMEM((words.shape[0] // 16, 16, D), bf16), pltpu.VMEM((LEN, D), f32), dma]
        + extra,
        compiler_params=pltpu.CompilerParams(
            collective_id=1, has_side_effects=True, vmem_limit_bytes=VMEM_LIMIT
        ),
        name="teacher",
    )(owner, local, stat, lengths, blocks, rows, words, places, teacher, table, own_flat)


def plan(n, flat_len):
    chips = n // 2
    plane = 2 ** ((chips.bit_length() - 1) // 2)
    flat_seg = flat_len // n
    flat_pad = round_up(flat_seg, 16)
    place_seg = 2 * LEN // n
    return plane, chips // plane, flat_seg, flat_pad, place_seg, flat_pad + round_up(place_seg, 16)


def place_tile(n):
    return max(8, 2 * LEN // n)


def exchange_kernel(n, flat_len, sparse, *refs):
    plane, planes, flat_seg, flat_pad, place_seg, seg = plan(n, flat_len)
    chips = n // 2
    cap = room(n)
    tile = place_tile(n)
    flat_ref, loss_ref = refs[:2]
    refs = refs[2:]
    if sparse:
        packed_ref, list_ref = refs[:2]
        refs = refs[2:]
    else:
        given_ref = refs[0]
        refs = refs[1:]
    table_ref, sums_ref, stat_out = refs[:3]
    (stage, one_in, two_out, two_in, total, three_out, three_in, place_in, stat_in) = refs[3:12]
    refs = refs[12:]
    if sparse:
        rows_in = refs[0]
        refs = refs[1:]
    one_sem, two_sem, three_sem, place_sem, stat_sem, row_sem = refs
    me = lax.axis_index("dp")
    core = lax.rem(me, 2)
    chip = me // 2
    mid = lax.rem(chip, plane)
    high = chip // plane
    vrows = table_ref.shape[0]

    greet_all(me, n)
    pad = jnp.zeros((16, LANES), f32)
    for o in range(n):
        spot = stage.at[o % 2, o // 2]
        if flat_pad > flat_seg:
            spot[flat_pad - 16 : flat_pad, :] = pad
        if seg > flat_pad + place_seg:
            spot[seg - 16 : seg, :] = pad
        spot[0:flat_seg, :] = flat_ref[o * flat_seg : (o + 1) * flat_seg, :]
        at = flat_len + o * place_seg
        spot[flat_pad : flat_pad + place_seg, :] = flat_ref[at : at + place_seg, :]
    first = copy_to(stage.at[1 - core], one_in, one_sem.at[0], one_sem.at[1], me ^ 1)
    first.start()

    if sparse:

        def bucket(ref, i):
            return ref.at[pl.ds(pl.multiple_of(i * cap, cap), cap), :]

        def row_copy(k):
            return copy_to(
                bucket(packed_ref, me ^ k), bucket(rows_in, me), row_sem.at[0, k], row_sem.at[1, k], me ^ k
            )

        def start_row(i, carry):
            row_copy(n - i).start()
            return carry

        lax.fori_loop(1, n, start_row, 0)
        own = pl.ds(pl.multiple_of(me * cap, cap), cap)
        rows_in[own, :] = packed_ref[own, :]

    first.wait()
    for m in range(plane):
        for h in range(planes):
            c = h * plane + m
            two_out[m, h] = (stage[core, c] + one_in[c]).astype(bf16)
    second = []
    for k in range(1, plane):
        m = lax.rem(mid + k, plane)
        second.append(
            copy_to(
                two_out.at[m],
                two_in.at[k - 1],
                two_sem.at[0, k],
                two_sem.at[1, k],
                (high * plane + m) * 2 + core,
            )
        )
        second[-1].start()
    for copy in second:
        copy.wait()
    for h in range(planes):
        c = h * plane + mid
        value = stage[core, c] + one_in[c]
        for k in range(1, plane):
            value = value + two_in[k - 1, h].astype(f32)
        total[h] = value
        three_out[h] = value.astype(bf16)
    third = []
    for k in range(1, planes):
        h = lax.rem(high + k, planes)
        third.append(
            copy_to(
                three_out.at[h],
                three_in.at[k - 1],
                three_sem.at[0, k],
                three_sem.at[1, k],
                (h * plane + mid) * 2 + core,
            )
        )
        third[-1].start()
    for copy in third:
        copy.wait()
    value = total[high]
    for k in range(1, planes):
        value = value + three_in[k - 1].astype(f32)
    total[0] = value
    sums_ref[...] = value[:flat_pad]

    owners = range(VOCAB // vrows, (VOCAB + LEN - 1) // vrows + 1)
    place_out = total.at[0, pl.ds(flat_pad, tile), :]
    place_spot = pl.ds(pl.multiple_of(me * tile, 8), tile)
    for i, o in enumerate(owners):
        place_copy = copy_to(
            place_out, place_in.at[place_spot, :], place_sem.at[0, i], place_sem.at[1, me], o
        )
        pl.when(me != o)(place_copy.start)

    squares = jnp.sum(jnp.sum(value * value, axis=0, keepdims=True), axis=1, keepdims=True)
    if sparse:
        def add_pair(i, carry):
            pl.when(i > 0)(lambda: row_copy(2 * i).wait_recv())
            row_copy(2 * i + 1).wait_recv()
            a = chip ^ i
            lists = pair_lists(list_ref, a, cap)
            pick = (lax.broadcasted_iota(jnp.int32, (vrows, 2 * cap), 0) == lists).astype(bf16)
            both = rows_in[pl.ds(pl.multiple_of(a * 2 * cap, 2 * cap), 2 * cap), :]
            table_ref[...] += nn(pick, both)
            return carry

        table_ref[...] = jnp.zeros(table_ref.shape, f32)
        lax.fori_loop(0, chips, add_pair, 0)
    else:
        table_ref[...] = given_ref[...]
    grads = table_ref[...]
    squares = squares + jnp.sum(
        jnp.sum(grads * grads, axis=0, keepdims=True), axis=1, keepdims=True
    )
    loss = jnp.sum(loss_ref[0:1, :], axis=1, keepdims=True)
    lane = lax.broadcasted_iota(jnp.int32, (8, LANES), 1)
    stat_out[...] = jnp.where(lane == 0, squares, jnp.where(lane == 1, loss, 0.0))

    def stat_copy(k):
        return copy_to(
            stat_out, stat_in.at[me], stat_sem.at[0, k], stat_sem.at[1, k], me ^ k
        )

    def start_stat(k, carry):
        stat_copy(k).start()
        return carry

    def finish_stat(k, carry):
        stat_copy(k).wait()
        return carry

    lax.fori_loop(1, n, start_stat, 0)
    stat_in[me] = stat_out[...]

    for i, o in enumerate(owners):

        @pl.when(me == o)
        def _():
            place_in[place_spot, :] = place_out[...]

            def wait_place(j, carry):
                copy_to(
                    place_out,
                    place_in.at[pl.ds(pl.multiple_of(j * tile, 8), tile), :],
                    place_sem.at[0, i],
                    place_sem.at[1, j],
                    me ^ 1,
                ).wait_recv()
                return carry

            lax.fori_loop(0, o, wait_place, 0)
            lax.fori_loop(o + 1, n, wait_place, 0)
            low = max(0, o * vrows - VOCAB)
            top = min(LEN, (o + 1) * vrows - VOCAB)
            at = VOCAB + low - o * vrows
            if tile > place_seg:
                for d in range(n):
                    place_in[d * place_seg : (d + 1) * place_seg, :] = place_in[
                        d * tile : d * tile + place_seg, :
                    ]
            for j in range(2):
                table_ref[at : at + top - low, j * LANES : (j + 1) * LANES] += place_in[
                    pl.ds(2 * low + j, top - low, stride=2), :
                ]

    lax.fori_loop(1, n, finish_stat, 0)
    stat_out[...] = jnp.sum(stat_in[...], axis=0)
    for i, o in enumerate(owners):
        place_copy = copy_to(
            place_out, place_in.at[place_spot, :], place_sem.at[0, i], place_sem.at[1, me], o
        )
        pl.when(me != o)(place_copy.wait_send)
    if sparse:

        def finish_row(k, carry):
            row_copy(k).wait_send()
            return carry

        lax.fori_loop(1, n, finish_row, 0)


def run_exchange(n, vrows, flat_grads, loss_rows, sparse, given):
    flat_len = flat_grads.shape[0] - 2 * LEN
    plane, planes, flat_seg, flat_pad, place_seg, seg = plan(n, flat_len)
    count = len(range(VOCAB // vrows, (VOCAB + LEN - 1) // vrows + 1))
    dma = pltpu.SemaphoreType.DMA
    return pl.pallas_call(
        functools.partial(exchange_kernel, n, flat_len, sparse),
        out_shape=(
            jax.ShapeDtypeStruct((vrows, D), f32),
            jax.ShapeDtypeStruct((flat_pad, LANES), f32),
            jax.ShapeDtypeStruct((8, LANES), f32),
        ),
        in_specs=[whole_spec()] * (2 + len(given)),
        out_specs=(whole_spec(),) * 3,
        scratch_shapes=[
            pltpu.VMEM((2, n // 2, seg, LANES), f32),
            pltpu.VMEM((n // 2, seg, LANES), f32),
            pltpu.VMEM((plane, planes, seg, LANES), bf16),
            pltpu.VMEM((plane - 1, planes, seg, LANES), bf16),
            pltpu.VMEM((planes, seg, LANES), f32),
            pltpu.VMEM((planes, seg, LANES), bf16),
            pltpu.VMEM((planes - 1, seg, LANES), bf16),
            pltpu.VMEM((n * place_tile(n), LANES), f32),
            pltpu.VMEM((n, 8, LANES), f32),
        ]
        + ([pltpu.VMEM((n * room(n), D), bf16)] if sparse else [])
        + [dma((2,)), dma((2, plane)), dma((2, planes)), dma((2, max(n, count))), dma((2, n)), dma((2, n))],
        compiler_params=pltpu.CompilerParams(
            collective_id=2 if sparse else 3, has_side_effects=True, vmem_limit_bytes=VMEM_LIMIT
        ),
        name="exchange" if sparse else "exchange_dense",
    )(flat_grads, loss_rows, *given)


def adam_step(weight, first_old, second, clipped):
    first_new = beta_one * first_old + (1.0 - beta_one) * clipped
    second_new = beta_two * second + (1.0 - beta_two) * clipped * clipped
    first_hat = first_new / (1.0 - beta_one**ADAM_STEP)
    second_hat = second_new / (1.0 - beta_two**ADAM_STEP)
    weight_new = weight - learn_rate * (
        first_hat / (jnp.sqrt(second_hat) + adam_eps) + decay_rate * weight
    )
    return (weight_new, first_new, second_new)


def rows_of(table, ids):
    return table.at[ids.reshape(-1)].get(mode="promise_in_bounds")


def ring_gather(devices, block):
    me = lax.axis_index("dp")
    rows = block.shape[0]
    onward = [(i, (i + 1) % devices) for i in range(devices)]

    def step(i, state):
        block, whole = state
        whole = lax.dynamic_update_slice(whole, block, (lax.rem(me - i + devices, devices) * rows, 0))
        return lax.ppermute(block, "dp", onward), whole

    whole = jnp.zeros((devices * rows, block.shape[1]), block.dtype)
    return lax.fori_loop(0, devices, step, (block, whole))[1]


def ring_scatter(devices, whole):
    me = lax.axis_index("dp")
    rows = whole.shape[0] // devices
    onward = [(i, (i + 1) % devices) for i in range(devices)]

    def part(i):
        at = lax.rem(me - 1 - i + 2 * devices, devices) * rows
        return lax.dynamic_slice(whole, (at, 0), (rows, whole.shape[1]))

    def step(i, total):
        return lax.ppermute(total, "dp", onward) + part(i)

    return lax.fori_loop(1, devices, step, part(0))


def per_device(
    devices,
    token_ids,
    lengths,
    gate_noise,
    lagrange,
    teacher_table,
    teacher_flat,
    word_table,
    table_first,
    table_second,
    layer_flat,
    flat_first,
    flat_second,
):
    seqs = token_ids.shape[0]
    half = seqs // 2
    vrows = word_table.shape[0]
    own = layer_flat.shape[0]
    flat_len = own * devices // LANES

    mates = [(i, devices - 1 - i) for i in range(devices)]
    sent = jnp.concatenate(
        [token_ids[half:], jnp.pad(lengths[half:], (0, LEN - half)).reshape(1, LEN)]
    )
    got = lax.ppermute(sent, "dp", mates)
    ids = jnp.concatenate([token_ids[:half], got[:half]])
    lens = jnp.concatenate([lengths[:half], got[half, :half]])

    owner = ids // vrows
    valid = jnp.arange(LEN)[None, :] < lens[:, None]
    target, listed, flat_all, place_all, *routed = run_fetch(
        devices,
        flat_len,
        jnp.where(valid, owner, -1),
        (ids - owner * vrows + 1).astype(f32),
        jnp.sum(lens).reshape(1),
        lens,
        ids // 16,
        ids % 16,
        teacher_table,
        teacher_table[VOCAB : VOCAB + LEN],
        teacher_flat.reshape(-1, LANES),
        word_table,
        layer_flat.reshape(-1, LANES),
    )
    stats = listed.reshape(devices, 8, LANES)[:, 1, :2]
    global_count = jnp.sum(stats[:, 0]).astype(f32)
    lag_weight = jnp.where(lax.axis_index("dp") == 0, 1.0, 0.0).astype(f32)
    factors = jnp.stack([(2.0 / D) / global_count, lag_weight])
    noise = jnp.pad(gate_noise, (0, 16 * LANES - gate_noise.shape[0]), constant_values=0.5)
    places = [place_all[i, : part[3]] for i, part in enumerate(place_parts(vrows))]
    shared = (
        lens,
        factors,
        lagrange,
        noise.reshape(16, LANES),
        flat_all,
        jnp.concatenate(places) if len(places) > 1 else places[0],
        target,
    )

    def from_slots():
        slots, fetched = routed
        flat_grads, _, loss_rows, packed = run_student(
            devices, flat_len, True, *shared, (slots, fetched)
        )
        result = run_exchange(devices, vrows, flat_grads, loss_rows, True, (packed, listed))
        return (*result, loss_rows)

    def from_rows():
        if routed:
            table = ring_gather(devices, word_table.astype(bf16))
        else:
            table = lax.all_gather(word_table.astype(bf16), "dp", axis=0, tiled=True)
        flat_grads, grad_rows, loss_rows = run_student(
            devices, flat_len, False, *shared, (rows_of(table, ids),)
        )
        updates = jnp.transpose(grad_rows, (0, 2, 1)).reshape(seqs * LEN, D).astype(f32)
        table = jnp.zeros((devices * vrows, D), f32).at[ids.reshape(-1)].add(updates)
        if routed:
            table = ring_scatter(devices, table)
        else:
            table = lax.psum_scatter(table, "dp", scatter_dimension=0, tiled=True)
        result = run_exchange(devices, vrows, flat_grads, loss_rows, False, (table,))
        return (*result, loss_rows)

    if routed:
        crowded = jnp.max(stats[:, 1])
        _, table_grad, sums, totals, loss_rows = lax.while_loop(
            lambda state: state[0] > 0,
            lambda state: (jnp.zeros_like(state[0]), *from_rows()),
            (crowded, *from_slots()),
        )
    else:
        table_grad, sums, totals, loss_rows = from_rows()
    lag_value = loss_rows[1, 0]
    flat_grad = sums[: own // LANES].reshape(-1)
    grad_norm = jnp.sqrt(totals[0, 0])
    clip = jnp.minimum(1.0, clip_norm / (grad_norm + 1e-06))
    total_loss = totals[0, 1] / global_count + lag_value
    table_new = adam_step(word_table, table_first, table_second, table_grad * clip)
    flat_new = adam_step(layer_flat, flat_first, flat_second, flat_grad * clip)
    return (*table_new, *flat_new, total_loss, grad_norm)


def solution(mesh):
    row, flat, copied = P("dp", None), P("dp"), P()
    in_specs = (row, flat, copied, copied, copied, copied, row, row, row, flat, flat, flat)
    out_specs = (row, row, row, flat, flat, flat, copied, copied)
    return jax.shard_map(
        functools.partial(per_device, mesh.shape["dp"]),
        mesh=mesh,
        in_specs=in_specs,
        out_specs=out_specs,
        check_vma=False,
    )
```

```python
import functools
import math

import jax
import jax.numpy as jnp
from jax import lax
from jax.experimental import pallas as pl
from jax.experimental.pallas import tpu as pltpu
from jax.sharding import PartitionSpec as P

D = 256
HEADS = 4
HD = D // HEADS
FF = 1024
LEN = 512
VOCAB = 30522
NPAR = 856836
LANES = 128
norm_eps = 1e-12
clip_norm = 0.002
learn_rate = 0.015
beta_one = 0.9
beta_two = 0.999
adam_eps = 1e-08
decay_rate = 0.01
sparse_target = 0.3
ADAM_STEP = 10
relaxation_heat = 2.0 / 3.0
widened_left_limit = -0.1
widened_right_limit = 1.1
f32 = jnp.float32
bf16 = jnp.bfloat16
VMEM_LIMIT = 60 * 2**20

C_GH = 10 * D
C_HEAD = 11 * D
C_BUP = 12 * D
C_GI = 12 * D + FF
C_ROWS = 12 * D + 2 * FF
A_BUP = 10 * D
A_GH = 10 * D + FF
A_HEAD = 11 * D + FF
A_GI = 12 * D + FF
A_ROWS = 12 * D + 2 * FF
R_UP = 5 * 512
R_DOWN = R_UP + 2048
R_VEC = R_DOWN + 2048
R_BUP = R_VEC + 20
R_LOGIT = R_BUP + 8
R_USED = R_LOGIT + 11


def nn(left, right):
    return jnp.dot(left, right, preferred_element_type=f32)


def nt(left, right):
    return lax.dot_general(left, right, (((1,), (1,)), ((), ())), preferred_element_type=f32)


def chunks(span):
    return [(c, min(256, span - c)) for c in range(0, span, 256)]


def wide(col_ref, row, rows, width):
    col = col_ref[row : row + rows, :]
    return jnp.concatenate([col] * (width // LANES), axis=1) if width > LANES else col


def lanes_in(values):
    total = values[:, :LANES]
    for c in range(LANES, values.shape[1], LANES):
        total = total + values[:, c : c + LANES]
    return total


def eye(size):
    return (
        lax.broadcasted_iota(jnp.int32, (size, size), 0)
        == lax.broadcasted_iota(jnp.int32, (size, size), 1)
    ).astype(bf16)


def standardise(x):
    mean = jnp.sum(x, axis=0, keepdims=True) * (1.0 / D)
    centred = x - mean
    variance = jnp.sum(centred * centred, axis=0, keepdims=True) * (1.0 / D)
    scale = lax.rsqrt(variance + norm_eps)
    return centred * scale, scale


def standardise_back(dx, hat, scale):
    mean_one = jnp.sum(dx, axis=0, keepdims=True) * (1.0 / D)
    mean_two = jnp.sum(dx * hat, axis=0, keepdims=True) * (1.0 / D)
    return scale * (dx - mean_one - hat * mean_two)


def gelu_parts(x):
    half_erf = 0.5 * lax.erf(x * (2.0**-0.5)) + 0.5
    return half_erf


def start_part(c, width, student, embed, pos_ref, col_ref, w, sc, eyes):
    cols = pl.ds(c, width)
    embedded = embed(c, width) + pos_ref[:, cols]
    hat, scale = standardise(embedded)
    start = hat * wide(col_ref, 0, D, width) + wide(col_ref, D, D, width)
    if student:
        sc["hat0"][:, cols] = hat
        sc["scale"][0:1, cols] = scale
        start = start * wide(col_ref, C_GH, D, width)
    sc["start"][:, cols] = start
    start_low = start.astype(bf16)
    if student:
        sc["start_low"][:, cols] = start_low
    q = nn(w["qkvT"][0:D, :], start_low) + wide(col_ref, 6 * D, D, width)
    sc["qkv"][0:D, cols] = q.astype(bf16)
    k = nn(w["qkvT"][D : 2 * D, :], start_low).astype(bf16)
    sc["qkv"][D : 2 * D, cols] = k
    v = (nn(w["qkvT"][2 * D : 3 * D, :], start_low) + wide(col_ref, 7 * D, D, width)).astype(bf16)
    sc["qkv"][2 * D : 3 * D, cols] = v
    for h in range(HEADS):
        rows = slice(h * HD, (h + 1) * HD)
        sc["k_rows"][h, cols, :] = nt(eyes[width], k[rows, :]).astype(bf16)
        if student:
            sc["v_rows"][h, cols, :] = nt(eyes[width], v[rows, :]).astype(bf16)


def attend(span, length, student, col_ref, sc):
    for c, width in chunks(span):
        valid = lax.broadcasted_iota(jnp.int32, (span, width), 0) < length
        for h in range(HEADS):
            q_h = sc["qkv"][h * HD : (h + 1) * HD, c : c + width] * bf16(HD**-0.5)
            scores = jnp.where(valid, nn(sc["k_rows"][h, 0:span, :], q_h), -1e30)
            shares = jnp.exp(scores - jnp.max(scores, axis=0, keepdims=True))
            shares_low = (shares * (1.0 / jnp.sum(shares, axis=0, keepdims=True))).astype(bf16)
            if student:
                sc["shares"][h, 0:span, c : c + width] = shares_low
            context = nn(sc["qkv"][2 * D + h * HD : 2 * D + (h + 1) * HD, 0:span], shares_low)
            if student:
                sc["context"][h * HD : (h + 1) * HD, c : c + width] = context
                context = context * wide(col_ref, C_HEAD + h * HD, HD, width)
            sc["gated"][h * HD : (h + 1) * HD, c : c + width] = context.astype(bf16)


def middle_part(c, width, student, col_ref, w, sc):
    cols = pl.ds(c, width)
    branch = nn(w["oT"][...], sc["gated"][:, cols]) + wide(col_ref, 8 * D, D, width)
    if student:
        sc["branch"][:, 0:width] = branch
        branch = branch * wide(col_ref, C_GH, D, width)
    hat, scale = standardise(sc["start"][:, cols] + branch)
    middle = hat * wide(col_ref, 2 * D, D, width) + wide(col_ref, 3 * D, D, width)
    if student:
        sc["hat1"][:, 0:width] = hat
        sc["scale"][1:2, cols] = scale
    middle_low = middle.astype(bf16)
    if student:
        sc["middle_low"][:, 0:width] = middle_low
    for r in range(0, FF, D):
        pre = nn(w["upT"][r : r + D, :], middle_low) + wide(col_ref, C_BUP + r, D, width)
        cdf = 0.5 * lax.erf(pre * (2.0**-0.5)) + 0.5
        act = pre * cdf
        if student:
            inner = wide(col_ref, C_GI + r, D, width)
            pdf = jnp.exp(pre * pre * -0.5) * (1.0 / math.sqrt(2.0 * math.pi))
            sc["act"][r : r + D, 0:width] = act
            sc["slope"][r : r + D, 0:width] = (cdf + pre * pdf) * inner
            act = act * inner
        sc["up"][r : r + D, 0:width] = act.astype(bf16)
    down = nn(w["downT"][...], sc["up"][:, 0:width]) + wide(col_ref, 9 * D, D, width)
    if student:
        sc["down"][:, 0:width] = down
        down = down * wide(col_ref, C_GH, D, width)
    hat, scale = standardise(middle + down)
    out = hat * wide(col_ref, 4 * D, D, width) + wide(col_ref, 5 * D, D, width)
    return out, hat, scale


def add_lanes(add_ref, row, values):
    add_ref[row : row + values.shape[0], :] += lanes_in(values)


def back_part(c, width, length, factor, out, hat, scale, target_ref, col_ref, w, sc, acc, add_ref, loss_ref):
    cols = pl.ds(c, width)
    here = slice(0, width)
    add = functools.partial(add_lanes, add_ref)
    out_low = out.astype(bf16)
    differ = nn(w["aT"][...], out_low) - target_ref[0, :, cols]
    token_valid = (lax.broadcasted_iota(jnp.int32, (1, width), 1) + c < length).astype(f32)
    loss_ref[0:1, cols] += jnp.sum(differ * differ, axis=0, keepdims=True) * (1.0 / D) * token_valid
    d_aligned = (differ * (token_valid * factor)).astype(bf16)
    acc["a"][...] += nt(out_low, d_aligned)
    d_out = nn(w["a"][...], d_aligned)
    add(4 * D, d_out * hat)
    add(5 * D, d_out)
    d_second = standardise_back(d_out * wide(col_ref, 4 * D, D, width), hat, scale)
    add(A_GH, d_second * sc["down"][:, here])
    d_down = (d_second * wide(col_ref, C_GH, D, width)).astype(bf16)
    add(9 * D, d_down.astype(f32))
    acc["down"][...] += nt(sc["up"][:, here], d_down)
    for r in range(0, FF, D):
        d_up = nn(w["down"][r : r + D, :], d_down)
        add(A_GI + r, d_up * sc["act"][r : r + D, here])
        d_pre = (d_up * sc["slope"][r : r + D, here]).astype(bf16)
        sc["d_pre"][r : r + D, here] = d_pre
        add(A_BUP + r, d_pre.astype(f32))
    d_middle = d_second + nn(w["up"][...], sc["d_pre"][:, here])
    acc["up"][...] += nt(sc["middle_low"][:, here], sc["d_pre"][:, here])
    hat = sc["hat1"][:, here]
    add(2 * D, d_middle * hat)
    add(3 * D, d_middle)
    d_first = standardise_back(
        d_middle * wide(col_ref, 2 * D, D, width), hat, sc["scale"][1:2, cols]
    )
    sc["d_first"][:, cols] = d_first
    add(A_GH, d_first * sc["branch"][:, here])
    d_branch = (d_first * wide(col_ref, C_GH, D, width)).astype(bf16)
    add(8 * D, d_branch.astype(f32))
    acc["o"][...] += nt(sc["gated"][:, cols], d_branch)
    d_gated = nn(w["o"][...], d_branch)
    context = sc["context"][:, cols]
    add(A_HEAD, d_gated * context)
    d_context = d_gated * wide(col_ref, C_HEAD, D, width)
    sc["d_context"][:, cols] = d_context.astype(bf16)
    dot_rows = d_context * context
    for h in range(HEADS):
        sc["delta"][h : h + 1, cols] = jnp.sum(
            dot_rows[h * HD : (h + 1) * HD, :], axis=0, keepdims=True
        )


def attend_back(span, sc):
    full = slice(0, span)
    for h in range(HEADS):
        rows = slice(h * HD, (h + 1) * HD)
        d_value = nt(sc["d_context"][rows, full], sc["shares"][h, 0:span, 0:span])
        sc["d_qkv"][2 * D + h * HD : 2 * D + (h + 1) * HD, full] = d_value.astype(bf16)
        d_key = None
        for c, width in chunks(span):
            cols = slice(c, c + width)
            d_shares = nn(sc["v_rows"][h, 0:span, :], sc["d_context"][rows, cols])
            d_scores = (
                sc["shares"][h, 0:span, cols].astype(f32) * (d_shares - sc["delta"][h : h + 1, cols])
            ).astype(bf16)
            sc["d_qkv"][rows, cols] = (
                nn(sc["qkv"][D + h * HD : D + (h + 1) * HD, full], d_scores) * (HD**-0.5)
            ).astype(bf16)
            part = nt(sc["qkv"][rows, cols], d_scores)
            d_key = part if d_key is None else d_key + part
        sc["d_qkv"][D + h * HD : D + (h + 1) * HD, full] = (d_key * (HD**-0.5)).astype(bf16)


def end_part(c, width, col_ref, w, sc, acc, add_ref, grad_ref, pos_add):
    cols = pl.ds(c, width)
    add = functools.partial(add_lanes, add_ref)
    acc["qkv"][...] += nt(sc["start_low"][:, cols], sc["d_qkv"][:, cols])
    add(6 * D, sc["d_qkv"][0:D, cols].astype(f32))
    add(7 * D, sc["d_qkv"][2 * D : 3 * D, cols].astype(f32))
    d_start = sc["d_first"][:, cols] + nn(w["qkv"][...], sc["d_qkv"][:, cols])
    hat = sc["hat0"][:, cols]
    gain = wide(col_ref, 0, D, width)
    add(A_GH, d_start * (hat * gain + wide(col_ref, D, D, width)))
    d_norm = d_start * wide(col_ref, C_GH, D, width)
    add(0, d_norm * hat)
    add(D, d_norm)
    d_embedded = standardise_back(d_norm * gain, hat, sc["scale"][0:1, cols])
    pos_add[:, cols] += d_embedded
    grad_ref[0, :, cols] = d_embedded.astype(bf16)


def by_part(length, body):
    def step(i, carry):
        body(pl.multiple_of(i * 256, 256), 256)
        return carry

    lax.fori_loop(0, jnp.where(length > 384, 2, 1), step, 0)
    pl.when((length > 256) & (length <= 384))(lambda: body(256, 128))


def mark_slots(slot, perm_ref):
    step = 512
    width = slot.shape[1]

    def mark(i, carry):
        rows = pl.ds(pl.multiple_of(i * step, step), step)
        seen = lax.broadcasted_iota(jnp.int32, (step, width), 0) == slot - i * step
        perm_ref[rows, :] = seen.astype(f32).astype(bf16)
        return carry

    lax.fori_loop(0, perm_ref.shape[0] // step, mark, 0)


def pack_rows(span, perm_ref, grad_ref, packed_ref):
    step = 1024

    def add(i, carry):
        rows = pl.ds(pl.multiple_of(i * step, step), step)
        packed_ref[rows, :] += nt(perm_ref[rows, 0:span], grad_ref[0, :, 0:span]).astype(bf16)
        return carry

    lax.fori_loop(0, packed_ref.shape[0] // step, add, 0)


SPANS = (256, 384, 512)


def by_span(length, body):
    for i, span in enumerate(SPANS):
        low = SPANS[i - 1] if i else 0
        test = length > low
        if i == 0:
            test = length <= span
        elif i < len(SPANS) - 1:
            test = (length > low) & (length <= span)
        pl.when(test)(functools.partial(body, span))


def set_up(pos_in, pos_ref, eyes_refs):
    for size, ref in eyes_refs.items():
        ref[...] = eye(size)
    for c in range(0, LEN, 256):
        pos_ref[:, c : c + 256] = nt(eyes_refs[256][...], pos_in[c : c + 256, :])


TEACHER_W = (
    ("qkv", (D, 3 * D)),
    ("qkvT", (3 * D, D)),
    ("o", (D, D)),
    ("oT", (D, D)),
    ("up", (D, FF)),
    ("upT", (FF, D)),
    ("down", (FF, D)),
    ("downT", (D, FF)),
)
STUDENT_W = TEACHER_W + (("a", (D, D)), ("aT", (D, D)))


def spread(col_ref, at, row):
    col_ref[pl.ds(at, LANES), :] = jnp.transpose(jnp.broadcast_to(row, (LANES, LANES)))


def load_weights(flat, w, col_ref, one, student):
    squares = [("qkv", 0), ("qkv", D), ("qkv", 2 * D), ("o", 0)] + ([("a", 0)] if student else [])
    for i, (name, at) in enumerate(squares):
        for j in range(2):
            lanes = slice(at + j * LANES, at + (j + 1) * LANES)
            w[name][:, lanes] = flat[pl.ds(512 * i + j, D, stride=2), :].astype(bf16)
    base = 512 * len(squares)
    for j in range(8):
        w["up"][:, j * LANES : (j + 1) * LANES] = flat[pl.ds(base + j, D, stride=8), :].astype(bf16)
    base = base + 2048
    for j in range(2):
        w["down"][:, j * LANES : (j + 1) * LANES] = flat[pl.ds(base + j, FF, stride=2), :].astype(
            bf16
        )
    base = base + 2048
    for i in range(20):
        spread(col_ref, i * LANES, flat[base + i : base + i + 1, :])
    for j in range(8):
        spread(col_ref, C_BUP + j * LANES, flat[base + 20 + j : base + 21 + j, :])
    unit = one[...]
    for name in ("qkv", "o", "up") + (("a",) if student else ()):
        for b in range(0, w[name].shape[1], D):
            w[name + "T"][b : b + D, :] = nt(unit, w[name][:, b : b + D]).astype(bf16)
    for b in range(0, FF, D):
        w["downT"][:, b : b + D] = nt(unit, w["down"][b : b + D, :]).astype(bf16)


def total_of(x):
    return jnp.sum(jnp.sum(x, axis=0, keepdims=True), axis=1, keepdims=True)


def head_groups():
    return (
        lax.broadcasted_iota(jnp.int32, (D, LANES), 0) // HD
        == lax.broadcasted_iota(jnp.int32, (D, LANES), 1)
    ).astype(f32)


def load_gates(logits, noise, lagrange_ref, lag_weight, col_ref, slope_ref, lag_ref):
    index = lax.broadcasted_iota(
        jnp.int32, logits.shape, 0
    ) * LANES + lax.broadcasted_iota(jnp.int32, logits.shape, 1)
    hidden, heads = index < D, (index >= D) & (index < D + HEADS)
    inner = (index >= D + HEADS) & (index < D + HEADS + FF)
    logistic = jax.nn.sigmoid((jnp.log(noise) - jnp.log(1.0 - noise) + logits) / relaxation_heat)
    spanned = widened_right_limit - widened_left_limit
    stretched = logistic * spanned + widened_left_limit
    gates = jnp.clip(stretched, 0.0, 1.0)
    inside = jnp.where((stretched > 0.0) & (stretched < 1.0), 1.0, 0.0)
    inside = jnp.where((stretched == 0.0) | (stretched == 1.0), 0.5, inside)
    slope_ref[...] = inside * logistic * (1.0 - logistic) * (spanned / relaxation_heat)
    keep = jax.nn.sigmoid(
        logits - relaxation_heat * math.log(-widened_left_limit / widened_right_limit)
    )
    kept = total_of(jnp.where(hidden, keep, 0.0)) * (1.0 / D)
    rest = total_of(jnp.where(heads, keep * (4.0 * HD), 0.0) + jnp.where(inner, keep * 2.0, 0.0))
    scale = 1.0 / (4.0 * D + 2.0 * FF)
    excess = kept * rest * scale - sparse_target
    rate = (lagrange_ref[0] + 2.0 * lagrange_ref[1] * excess) * (scale * lag_weight)
    share = jnp.where(hidden, rest * (1.0 / D), 0.0)
    share = share + kept * (jnp.where(heads, 4.0 * HD, 0.0) + jnp.where(inner, 2.0, 0.0))
    lag_ref[...] = rate * share * (keep * (1.0 - keep))
    for j in range(2):
        spread(col_ref, C_GH + j * LANES, gates[j : j + 1, :])
    wide_heads = lax.dot_general(
        jnp.broadcast_to(gates[2:3, :], (8, LANES)),
        head_groups(),
        (((1,), (1,)), ((), ())),
        preferred_element_type=f32,
        precision=lax.Precision.HIGHEST,
    )
    for j in range(2):
        spread(col_ref, C_HEAD + j * LANES, wide_heads[0:1, j * LANES : (j + 1) * LANES])
    run = jnp.concatenate([gates[j : j + 1, :] for j in range(2, 11)], axis=1)
    run = pltpu.roll(jnp.broadcast_to(run, (8, 9 * LANES)), 9 * LANES - HEADS, 1)
    for j in range(8):
        spread(col_ref, C_GI + j * LANES, run[0:1, j * LANES : (j + 1) * LANES])
    return lagrange_ref[0] * excess + lagrange_ref[1] * excess * excess


TEACHER_S = (
    ("start", (D, LEN), f32),
    ("qkv", (3 * D, LEN), bf16),
    ("k_rows", (HEADS, LEN, HD), bf16),
    ("gated", (D, LEN), bf16),
    ("up", (FF, 256), bf16),
)
STUDENT_S = TEACHER_S + (
    ("start_low", (D, LEN), bf16),
    ("hat0", (D, LEN), f32),
    ("hat1", (D, 256), f32),
    ("scale", (8, LEN), f32),
    ("v_rows", (HEADS, LEN, HD), bf16),
    ("shares", (HEADS, LEN, LEN), bf16),
    ("context", (D, LEN), f32),
    ("branch", (D, 256), f32),
    ("middle_low", (D, 256), bf16),
    ("act", (FF, 256), f32),
    ("slope", (FF, 256), f32),
    ("down", (D, 256), f32),
    ("d_pre", (FF, 256), bf16),
    ("d_first", (D, LEN), f32),
    ("d_context", (D, LEN), bf16),
    ("delta", (8, LEN), f32),
    ("d_qkv", (3 * D, LEN), bf16),
)
ACCS = (
    ("qkv", (D, 3 * D)),
    ("o", (D, D)),
    ("a", (D, D)),
    ("up", (D, FF)),
    ("down", (FF, D)),
)


class Eyes:
    def __init__(self, one, two):
        self.refs = {128: one, 256: two}

    def __getitem__(self, size):
        return self.refs[size][...]


def student_kernel(n, flat_len, sparse, len_ref, fac_ref, lagrange_ref, noise_ref, flat_in, pos_in, target_ref, *rest):
    plane, planes, flat_seg = plan(n, flat_len)[:3]
    cap = room(n)
    if sparse:
        slot_ref, rows_ref = rest[:2]
        rest = rest[2:]
    else:
        rows_ref = rest[0]
        rest = rest[1:]
    flat_ref, grad_ref, loss_ref = rest[:3]
    rest = rest[3:]
    if sparse:
        packed_ref, rows_all, perm_ref, slot_now = rest[:4]
        rest = rest[4:]
    w = {entry[0]: rest[i] for i, entry in enumerate(STUDENT_W)}
    rest = rest[len(STUDENT_W) :]
    sc = {entry[0]: rest[i] for i, entry in enumerate(STUDENT_S)}
    rest = rest[len(STUDENT_S) :]
    acc = {entry[0]: rest[i] for i, entry in enumerate(ACCS)}
    add_ref, pos_add, slope_ref, lag_ref, col_ref, pos_ref, eye_one, eye_two = rest[len(ACCS) :]
    s = pl.program_id(0)
    eyes = Eyes(eye_one, eye_two)

    @pl.when(s == 0)
    def _():
        set_up(pos_in, pos_ref, eyes.refs)
        for o in range(n):
            c = o // 2
            flat_ref[o * flat_seg : (o + 1) * flat_seg, :] = flat_in[
                o % 2, c % plane, c // plane, :, :
            ].astype(f32)[:flat_seg]
        load_weights(flat_ref, w, col_ref, eye_two, True)
        lag_value = load_gates(
            flat_ref[R_LOGIT : R_LOGIT + 16, :],
            noise_ref[...],
            lagrange_ref,
            fac_ref[1],
            col_ref,
            slope_ref,
            lag_ref,
        )
        for ref in list(acc.values()) + [add_ref, pos_add]:
            ref[...] = jnp.zeros(ref.shape, f32)
        row = lax.broadcasted_iota(jnp.int32, (8, LEN), 0)
        loss_ref[...] = jnp.where(row == 1, lag_value, 0.0)
        if sparse:
            packed_ref[...] = jnp.zeros(packed_ref.shape, bf16)
            for o in range(n):
                rows_all[:, o * cap : (o + 1) * cap] = rows_ref[o]

    length = len_ref[s]

    def embed(c, width):
        if sparse:
            mark_slots(slot_now[0:1, pl.ds(c, width)], perm_ref.at[:, pl.ds(c, width)])
            return nn(rows_all[...], perm_ref[:, pl.ds(c, width)])
        at = pl.multiple_of(s * LEN + c, 128)
        return nt(eyes[D], rows_ref[pl.ds(at, width), :])

    def between(c, width):
        out, hat, scale = middle_part(c, width, True, col_ref, w, sc)
        back_part(
            c, width, length, fac_ref[0], out, hat, scale, target_ref, col_ref, w, sc, acc, add_ref, loss_ref
        )

    grad_ref[0, :, 256:LEN] = jnp.zeros((D, LEN - 256), bf16)
    if sparse:
        slot_now[0:1, :] = slot_ref[pl.ds(s, 1), :]
    by_part(
        length, lambda c, width: start_part(c, width, True, embed, pos_ref, col_ref, w, sc, eyes)
    )
    by_span(length, lambda span: attend(span, length, True, col_ref, sc))
    by_part(length, between)
    by_span(length, lambda span: attend_back(span, sc))
    by_part(
        length,
        lambda c, width: end_part(c, width, col_ref, w, sc, acc, add_ref, grad_ref, pos_add),
    )
    if sparse:
        by_span(length, lambda span: pack_rows(span, perm_ref, grad_ref, packed_ref))

    @pl.when(s == pl.num_programs(0) - 1)
    def _():
        for i in range(3):
            for j in range(2):
                at = i * D + j * LANES
                flat_ref[pl.ds(512 * i + j, D, stride=2), :] = acc["qkv"][:, at : at + LANES]
        for j in range(2):
            lanes = slice(j * LANES, (j + 1) * LANES)
            flat_ref[pl.ds(512 * 3 + j, D, stride=2), :] = acc["o"][:, lanes]
            flat_ref[pl.ds(512 * 4 + j, D, stride=2), :] = acc["a"][:, lanes]
            flat_ref[pl.ds(R_DOWN + j, FF, stride=2), :] = acc["down"][:, lanes]
        for j in range(8):
            flat_ref[pl.ds(R_UP + j, D, stride=8), :] = acc["up"][:, j * LANES : (j + 1) * LANES]
        ones = jnp.ones((8, LANES), f32)

        def summed(row, rows):
            return lax.dot_general(
                ones,
                add_ref[row : row + rows, :],
                (((1,), (1,)), ((), ())),
                preferred_element_type=f32,
                precision=lax.Precision.HIGHEST,
            )

        for i in range(10):
            sums = summed(i * D, D)
            for j in range(2):
                flat_ref[R_VEC + 2 * i + j : R_VEC + 2 * i + j + 1, :] = sums[
                    0:1, j * LANES : (j + 1) * LANES
                ]
        sums = summed(A_BUP, FF)
        for j in range(8):
            flat_ref[R_BUP + j : R_BUP + j + 1, :] = sums[0:1, j * LANES : (j + 1) * LANES]
        hidden = summed(A_GH, D)
        heads = jnp.dot(
            summed(A_HEAD, D),
            head_groups(),
            preferred_element_type=f32,
            precision=lax.Precision.HIGHEST,
        )
        inner = summed(A_GI, FF)
        moved = pltpu.roll(jnp.concatenate([inner, jnp.zeros((8, LANES), f32)], axis=1), HEADS, 1)
        lane = lax.broadcasted_iota(jnp.int32, (8, LANES), 1)
        first = jnp.where(lane < HEADS, heads, moved[:, :LANES])
        tail = [hidden[:, :LANES], hidden[:, LANES:], first] + [
            moved[:, j * LANES : (j + 1) * LANES] for j in range(1, 9)
        ]
        for j, piece in enumerate(tail):
            flat_ref[R_LOGIT + j : R_LOGIT + j + 1, :] = (
                piece[0:1] * slope_ref[j : j + 1, :] + lag_ref[j : j + 1, :]
            )
        flat_ref[R_USED:flat_len, :] = jnp.zeros((flat_len - R_USED, LANES), f32)
        for j in range(2):
            flat_ref[pl.ds(flat_len + j, LEN, stride=2), :] = jnp.transpose(
                pos_add[j * LANES : (j + 1) * LANES, :]
            )


def whole_spec():
    return pl.BlockSpec(memory_space=pltpu.VMEM)


def smem_spec():
    return pl.BlockSpec(memory_space=pltpu.SMEM)


def seq_spec():
    return pl.BlockSpec((1, D, LEN), lambda s: (s, 0, 0))


def common_scratch():
    return [
        pltpu.VMEM((C_ROWS, LANES), f32),
        pltpu.VMEM((D, LEN), f32),
        pltpu.VMEM((128, 128), bf16),
        pltpu.VMEM((256, 256), bf16),
    ]


def run_student(n, flat_len, sparse, lengths, factors, lagrange, noise, flat_all, places, target, given):
    seqs = lengths.shape[0]
    slot_rows = n * room(n)
    shapes = [
        jax.ShapeDtypeStruct((flat_len + 2 * LEN, LANES), f32),
        jax.ShapeDtypeStruct((seqs, D, LEN), bf16),
        jax.ShapeDtypeStruct((8, LEN), f32),
    ]
    out_specs = [whole_spec(), seq_spec(), whole_spec()]
    scratch = []
    if sparse:
        shapes.append(jax.ShapeDtypeStruct((slot_rows, D), bf16))
        out_specs.append(whole_spec())
        scratch = [
            pltpu.VMEM((D, slot_rows), bf16),
            pltpu.VMEM((slot_rows, LEN), bf16),
            pltpu.VMEM((8, LEN), jnp.int32),
        ]
    return pl.pallas_call(
        functools.partial(student_kernel, n, flat_len, sparse),
        grid=(seqs,),
        out_shape=tuple(shapes),
        in_specs=[smem_spec()] * 3
        + [whole_spec()] * 3
        + [seq_spec()]
        + [whole_spec()] * len(given),
        out_specs=tuple(out_specs),
        scratch_shapes=scratch
        + [pltpu.VMEM(shape, bf16) for _, shape in STUDENT_W]
        + [pltpu.VMEM(shape, kind) for _, shape, kind in STUDENT_S]
        + [pltpu.VMEM(shape, f32) for _, shape in ACCS]
        + [
            pltpu.VMEM((A_ROWS, LANES), f32),
            pltpu.VMEM((D, LEN), f32),
            pltpu.VMEM((16, LANES), f32),
            pltpu.VMEM((16, LANES), f32),
        ]
        + common_scratch(),
        compiler_params=pltpu.CompilerParams(vmem_limit_bytes=VMEM_LIMIT),
        name="student" if sparse else "student_dense",
    )(lengths, factors, lagrange, noise, flat_all, places, target, *given)


MESH = pl.DeviceIdType.MESH
ROW_CUTS = (8, 8)


def room(n):
    return LANES if 8 * LEN // n >= LANES else 0


def greet_all(me, n):
    barrier = pltpu.get_barrier_semaphore()

    def signal(k, carry):
        pl.semaphore_signal(barrier, inc=1, device_id=(me ^ k,), device_id_type=MESH)
        return carry

    lax.fori_loop(1, n, signal, 0)
    pl.semaphore_wait(barrier, n - 1)


def copy_to(source, target, send, receive, device):
    return pltpu.make_async_remote_copy(
        src_ref=source,
        dst_ref=target,
        send_sem=send,
        recv_sem=receive,
        device_id=(device,),
        device_id_type=MESH,
    )


def list_rows(n, owner_ref, local_ref, stat, slot_ref, tile_ref):
    cap = room(n)
    upper = (
        lax.broadcasted_iota(jnp.int32, (256, 256), 0)
        <= lax.broadcasted_iota(jnp.int32, (256, 256), 1)
    ).astype(bf16)

    def sequence(s, state):
        base, listed = state
        for c in range(0, LEN, 256):
            owner = owner_ref[pl.ds(s, 1), c : c + 256]
            mine = (lax.broadcasted_iota(jnp.int32, (n, 256), 0) == owner).astype(f32)
            before = nn(mine.astype(bf16), upper)
            rank = jnp.sum(mine * (before - 1.0 + base), axis=0, keepdims=True).astype(jnp.int32)
            fits = (owner >= 0) & (rank < cap)
            slot_ref[pl.ds(s, 1), c : c + 256] = jnp.where(fits, owner * cap + rank, n * cap)
            place = (
                lax.broadcasted_iota(jnp.int32, (LANES, 256), 0) == jnp.where(fits, rank, -1)
            ).astype(f32)
            listed = listed + lax.dot_general(
                mine * local_ref[pl.ds(s, 1), c : c + 256],
                place,
                (((1,), (1,)), ((), ())),
                preferred_element_type=f32,
                precision=lax.Precision.HIGHEST,
            )
            base = base + before[:, 255:256]
        return base, listed

    base, listed = lax.fori_loop(
        0,
        owner_ref.shape[0],
        sequence,
        (jnp.zeros((n, 1), f32), jnp.zeros((n, LANES), f32)),
    )
    over = jnp.max(base, axis=0, keepdims=True) > cap
    lane = lax.broadcasted_iota(jnp.int32, (n, LANES), 1)
    tile_ref[...] = jnp.zeros(tile_ref.shape, jnp.int32)
    tile_ref[pl.ds(0, n, stride=8), :] = (listed + 0.5).astype(jnp.int32) - 1
    tile_ref[pl.ds(1, n, stride=8), :] = jnp.where(
        lane == 0, stat, jnp.where(lane == 1, over.astype(jnp.int32), 0)
    )


def place_parts(vrows):
    parts = []
    for o in range(VOCAB // vrows, (VOCAB + LEN - 1) // vrows + 1):
        low, top = max(VOCAB, o * vrows), min(VOCAB + LEN, (o + 1) * vrows)
        parts.append((o, low - o * vrows, low - VOCAB, top - low))
    return parts


def round_up(value, step):
    return -(-value // step) * step


def pair_lists(list_ref, a, cap):
    return jnp.concatenate(
        [list_ref[pl.ds(pl.multiple_of(a * 16 + 8 * j, 8), 8), :][0:1, :cap] for j in range(2)],
        axis=1,
    )


def fetch_kernel(
    n, flat_len, owner_ref, local_ref, stat_ref, len_ref, block_ref, row_ref, words_in, pos_in, flat_in, table_ref, own_flat, *rest
):
    plane, planes, flat_seg, flat_pad = plan(n, flat_len)[:4]
    cap = room(n)
    vrows = table_ref.shape[0]
    parts = place_parts(vrows)
    out_ref, got_out, flat_out, place_out = rest[:4]
    rest = rest[4:]
    if cap:
        slot_ref, rows_out = rest[:2]
        rest = rest[2:]
    w = {entry[0]: rest[i] for i, entry in enumerate(TEACHER_W)}
    rest = rest[len(TEACHER_W) :]
    sc = {entry[0]: rest[i] for i, entry in enumerate(TEACHER_S)}
    rest = rest[len(TEACHER_S) :]
    tile_ref, got_ref, flat_all, place_all, pad_ref, flat_f32 = rest[:6]
    list_sem, a_sem, b_sem, c_sem, pa_sem, pb_sem, pc_sem = rest[6:13]
    col_ref, pos_ref, eye_one, eye_two = rest[13:17]
    words, picked, word_sem, out_sem = rest[17:21]
    if cap:
        table_turned, row_send, rows_in, row_sem = rest[21:]
    eyes = Eyes(eye_one, eye_two)
    s = pl.program_id(0)
    seqs = owner_ref.shape[0]
    me = lax.axis_index("dp")
    core = lax.rem(me, 2)
    chip = me // 2
    mid = lax.rem(chip, plane)
    high = chip // plane

    def device(h, m, c):
        return (h * plane + m) * 2 + c

    def tile(ref, i):
        return ref.at[pl.ds(pl.multiple_of(i * 8, 8), 8), :]

    def list_copy(k):
        return copy_to(
            tile(tile_ref, me ^ k), tile(got_ref, me), list_sem.at[0, k], list_sem.at[1, k], me ^ k
        )

    def row_copy(k):
        return copy_to(
            row_send.at[me ^ k], rows_in.at[me], row_sem.at[0, k], row_sem.at[1, k], me ^ k
        )

    def flat_copies(stage):
        copies = []
        if stage == 0:
            spot = flat_all.at[core, mid, high]
            for k in range(1, planes):
                to = device(lax.rem(high + k, planes), mid, core)
                copies.append(copy_to(spot, spot, a_sem.at[0, k], a_sem.at[1, k], to))
        elif stage == 1:
            spot = flat_all.at[core, mid]
            for k in range(1, plane):
                to = device(high, lax.rem(mid + k, plane), core)
                copies.append(copy_to(spot, spot, b_sem.at[0, k], b_sem.at[1, k], to))
        else:
            spot = flat_all.at[core]
            copies.append(copy_to(spot, spot, c_sem.at[0], c_sem.at[1], me ^ 1))
        return copies

    def place_copies(stage, i):
        o, _, _, count = parts[i]
        chip_o = o // 2
        high_o, mid_o, core_o = chip_o // plane, chip_o % plane, o % 2
        spot = place_all.at[i, pl.ds(0, round_up(count, 16)), :]
        same_core, same_mid, same_high = core == core_o, mid == mid_o, high == high_o
        copies = []
        if stage == 0:
            for k in range(1, planes):
                to = device((high_o + k) % planes, mid_o, core_o)
                copies.append(copy_to(spot, spot, pa_sem.at[0, i, k], pa_sem.at[1, i, 0], to))
            sends = same_core & same_mid & same_high
            receives = same_core & same_mid & (high != high_o)
        elif stage == 1:
            for k in range(1, plane):
                to = device(high, (mid_o + k) % plane, core_o)
                copies.append(copy_to(spot, spot, pb_sem.at[0, i, k], pb_sem.at[1, i, 0], to))
            sends = same_core & same_mid
            receives = same_core & (mid != mid_o)
        else:
            copies.append(copy_to(spot, spot, pc_sem.at[0, i], pc_sem.at[1, i], me ^ 1))
            sends = same_core
            receives = core != core_o
        return copies, sends, receives

    def start_stage(stage):
        for copy in flat_copies(stage):
            copy.start()
        for i in range(len(parts)):
            copies, sends, _ = place_copies(stage, i)

            @pl.when(sends)
            def _():
                for copy in copies:
                    copy.start()

    def finish_stage(stage):
        for copy in flat_copies(stage):
            copy.wait()
        for i in range(len(parts)):
            copies, sends, receives = place_copies(stage, i)

            @pl.when(sends)
            def _():
                for copy in copies:
                    copy.wait_send()

            @pl.when(receives)
            def _():
                copies[0].wait_recv()

    known = words.shape[0] * 16
    word_copy = pltpu.make_async_copy(
        words_in.at[pl.ds(0, known), :], words.reshape(known, D), word_sem
    )

    @pl.when(s == 0)
    def _():
        word_copy.start()
        picked[...] = jnp.zeros(picked.shape, f32)
        greet_all(me, n)
        pad_ref[...] = jnp.zeros(pad_ref.shape, f32)
        pad_ref[0:flat_seg, :] = own_flat[...]
        flat_all[core, mid, high] = pad_ref[...].astype(bf16)
        for i, (o, at, _, count) in enumerate(parts):

            @pl.when(me == o)
            def _():
                full = round_up(count, 16)
                part = table_ref[at : at + count, :]
                if full > count:
                    part = jnp.concatenate([part, jnp.zeros((full - count, D), f32)], axis=0)
                place_all[i, 0:full, :] = part.astype(bf16)

        start_stage(0)
        if cap:
            list_rows(n, owner_ref, local_ref, stat_ref[0], slot_ref, tile_ref)
        else:
            tile_ref[...] = jnp.zeros(tile_ref.shape, jnp.int32) + stat_ref[0]

        def start_list(k, carry):
            list_copy(k).start()
            return carry

        lax.fori_loop(1, n, start_list, 0)
        own = pl.ds(pl.multiple_of(me * 8, 8), 8)
        got_ref[own, :] = tile_ref[own, :]
        set_up(pos_in, pos_ref, eyes.refs)
        if cap:
            table_turned[...] = nt(eye_two[...], table_ref[...].astype(bf16)).astype(bf16)

        def finish_list(k, carry):
            list_copy(k).wait()
            return carry

        lax.fori_loop(1, n, finish_list, 0)

        def serve(step, carry):
            i = n // 2 - 1 - step
            a = chip ^ i
            pick = (
                lax.broadcasted_iota(jnp.int32, (vrows, 2 * cap), 0) == pair_lists(got_ref, a, cap)
            ).astype(bf16)
            both = nn(table_turned[...], pick).astype(bf16)
            for j in range(2):
                row_send[2 * a + j] = both[:, j * cap : (j + 1) * cap]
                k = 2 * i + (core ^ j)
                pl.when(k > 0)(row_copy(k).start)
            return carry

        if cap:
            lax.fori_loop(0, n // 2, serve, 0)
            rows_in[me] = row_send[me]
        step = 512
        whole = flat_in.shape[0] // step

        def unpack(i, carry):
            rows = pl.ds(pl.multiple_of(i * step, step), step)
            flat_f32[rows, :] = flat_in[rows, :].astype(f32)
            return carry

        lax.fori_loop(0, whole, unpack, 0)
        flat_f32[whole * step :, :] = flat_in[whole * step :, :].astype(f32)
        load_weights(flat_f32, w, col_ref, eye_two, False)
        word_copy.wait()

    @pl.when(s == 1)
    def _():
        finish_stage(0)
        start_stage(1)

    length = len_ref[s]
    from_me = jnp.where(s < seqs // 2, me, n - 1 - me)
    longest = LEN // 3 + (LEN - LEN // 3) * from_me // (n - 1)

    def pick_eight(g, carry):
        rows = []
        for u in range(8):
            block = words[block_ref[s, g * 8 + u]].astype(f32)
            mine = lax.broadcasted_iota(jnp.int32, (16, D), 0) == row_ref[s, g * 8 + u]
            rows.append(jnp.sum(jnp.where(mine, block, 0.0), axis=0, keepdims=True))
        picked[pl.ds(pl.multiple_of(g * 8, 8), 8), :] = jnp.concatenate(rows, axis=0)
        return carry

    lax.fori_loop(0, (longest + 7) // 8, pick_eight, 0)

    def embed(c, width):
        return nt(eyes[D], picked[pl.ds(c, width), :].astype(bf16))

    def finish(c, width):
        out_ref[0, :, pl.ds(c, width)] = middle_part(c, width, False, col_ref, w, sc)[0]

    def body(span):
        for c, width in chunks(span):
            start_part(c, width, False, embed, pos_ref, col_ref, w, sc, eyes)
        attend(span, length, False, col_ref, sc)
        for c, width in chunks(span):
            finish(c, width)

    by_span(longest, body)

    @pl.when(s == seqs - 2)
    def _():
        finish_stage(1)
        start_stage(2)

    @pl.when(s == seqs - 1)
    def _():
        finish_stage(2)

        def finish_row(k, carry):
            row_copy(k).wait()
            return carry

        if cap:
            lax.fori_loop(1, n, finish_row, 0)
        pairs = [(got_ref, got_out), (flat_all, flat_out), (place_all, place_out)]
        if cap:
            pairs.append((rows_in, rows_out))
        leaving = [
            pltpu.make_async_copy(source, target, out_sem.at[i])
            for i, (source, target) in enumerate(pairs)
        ]
        for copy in leaving:
            copy.start()
        for copy in leaving:
            copy.wait()


def run_fetch(n, flat_len, owner, local, stat, lengths, blocks, rows, words, places, teacher, table, own_flat):
    plane, planes, flat_seg, flat_pad = plan(n, flat_len)[:4]
    seqs, cap, vrows = owner.shape[0], room(n), table.shape[0]
    parts = place_parts(vrows)
    most = max(round_up(part[3], 16) for part in parts)
    dma = pltpu.SemaphoreType.DMA
    got = ((8 * n, LANES), jnp.int32)
    fetched = ((n, D, cap), bf16)
    flat_all = ((2, plane, planes, flat_pad, LANES), bf16)
    place_all = ((len(parts), most, D), bf16)
    shapes = [((seqs, D, LEN), f32), got, flat_all, place_all]
    far = pl.BlockSpec(memory_space=pl.ANY)
    out_specs = [seq_spec(), far, far, far]
    extra = []
    if cap:
        shapes += [(owner.shape, jnp.int32), fetched]
        out_specs += [whole_spec(), far]
        extra = [
            pltpu.VMEM((D, vrows), bf16),
            pltpu.VMEM(*fetched),
            pltpu.VMEM(*fetched),
            dma((2, n)),
        ]
    return pl.pallas_call(
        functools.partial(fetch_kernel, n, flat_len),
        grid=(seqs,),
        out_shape=tuple(jax.ShapeDtypeStruct(shape, kind) for shape, kind in shapes),
        in_specs=[whole_spec()] * 2
        + [smem_spec()] * 4
        + [pl.BlockSpec(memory_space=pl.ANY)]
        + [whole_spec()] * 4,
        out_specs=tuple(out_specs),
        scratch_shapes=[pltpu.VMEM(shape, bf16) for _, shape in TEACHER_W]
        + [pltpu.VMEM(shape, kind) for _, shape, kind in TEACHER_S]
        + [
            pltpu.VMEM(*got),
            pltpu.VMEM(*got),
            pltpu.VMEM(*flat_all),
            pltpu.VMEM(*place_all),
            pltpu.VMEM((flat_pad, LANES), f32),
            pltpu.VMEM(teacher.shape, f32),
            dma((2, n)),
            dma((2, planes)),
            dma((2, plane)),
            dma((2,)),
            dma((2, len(parts), planes)),
            dma((2, len(parts), plane)),
            dma((2, len(parts))),
        ]
        + common_scratch()
        + [pltpu.VMEM((words.shape[0] // 16, 16, D), bf16), pltpu.VMEM((LEN, D), f32), dma, dma((4,))]
        + extra,
        compiler_params=pltpu.CompilerParams(
            collective_id=1, has_side_effects=True, vmem_limit_bytes=VMEM_LIMIT
        ),
        name="teacher",
    )(owner, local, stat, lengths, blocks, rows, words, places, teacher, table, own_flat)


def plan(n, flat_len):
    chips = n // 2
    plane = 2 ** ((chips.bit_length() - 1) // 2)
    flat_seg = flat_len // n
    flat_pad = round_up(flat_seg, 16)
    place_seg = 2 * LEN // n
    return plane, chips // plane, flat_seg, flat_pad, place_seg, flat_pad + round_up(place_seg, 16)


def place_tile(n):
    return max(8, 2 * LEN // n)


def exchange_kernel(n, flat_len, sparse, *refs):
    plane, planes, flat_seg, flat_pad, place_seg, seg = plan(n, flat_len)
    chips = n // 2
    cap = room(n)
    tile = place_tile(n)
    flat_ref, loss_ref = refs[:2]
    refs = refs[2:]
    if sparse:
        packed_ref, list_ref = refs[:2]
        refs = refs[2:]
    else:
        given_ref = refs[0]
        refs = refs[1:]
    table_ref, sums_ref, stat_out = refs[:3]
    (stage, one_in, two_out, two_in, total, three_out, three_in, place_in, stat_in) = refs[3:12]
    refs = refs[12:]
    if sparse:
        rows_in = refs[0]
        refs = refs[1:]
    one_sem, two_sem, three_sem, place_sem, stat_sem, row_sem = refs
    me = lax.axis_index("dp")
    core = lax.rem(me, 2)
    chip = me // 2
    mid = lax.rem(chip, plane)
    high = chip // plane
    vrows = table_ref.shape[0]

    greet_all(me, n)
    pad = jnp.zeros((16, LANES), f32)
    for o in range(n):
        spot = stage.at[o % 2, o // 2]
        if flat_pad > flat_seg:
            spot[flat_pad - 16 : flat_pad, :] = pad
        if seg > flat_pad + place_seg:
            spot[seg - 16 : seg, :] = pad
        spot[0:flat_seg, :] = flat_ref[o * flat_seg : (o + 1) * flat_seg, :]
        at = flat_len + o * place_seg
        spot[flat_pad : flat_pad + place_seg, :] = flat_ref[at : at + place_seg, :]
    first = copy_to(stage.at[1 - core], one_in, one_sem.at[0], one_sem.at[1], me ^ 1)
    first.start()

    if sparse:

        def bucket(ref, i):
            return ref.at[pl.ds(pl.multiple_of(i * cap, cap), cap), :]

        def row_copy(k):
            return copy_to(
                bucket(packed_ref, me ^ k), bucket(rows_in, me), row_sem.at[0, k], row_sem.at[1, k], me ^ k
            )

        def start_row(i, carry):
            row_copy(n - i).start()
            return carry

        def start_rows(low, top):
            lax.fori_loop(low, top, start_row, 0)

        cuts = [1 + (n - 1) * part // 31 for part in ROW_CUTS] + [n]
        start_rows(1, cuts[0])
        own = pl.ds(pl.multiple_of(me * cap, cap), cap)
        rows_in[own, :] = packed_ref[own, :]

    first.wait()
    for m in range(plane):
        for h in range(planes):
            c = h * plane + m
            two_out[m, h] = (stage[core, c] + one_in[c]).astype(bf16)
    second = []
    for k in range(1, plane):
        m = lax.rem(mid + k, plane)
        second.append(
            copy_to(
                two_out.at[m],
                two_in.at[k - 1],
                two_sem.at[0, k],
                two_sem.at[1, k],
                (high * plane + m) * 2 + core,
            )
        )
        second[-1].start()
    if sparse:
        start_rows(cuts[0], cuts[1])
    for copy in second:
        copy.wait()
    for h in range(planes):
        c = h * plane + mid
        value = stage[core, c] + one_in[c]
        for k in range(1, plane):
            value = value + two_in[k - 1, h].astype(f32)
        total[h] = value
        three_out[h] = value.astype(bf16)
    third = []
    for k in range(1, planes):
        h = lax.rem(high + k, planes)
        third.append(
            copy_to(
                three_out.at[h],
                three_in.at[k - 1],
                three_sem.at[0, k],
                three_sem.at[1, k],
                (h * plane + mid) * 2 + core,
            )
        )
        third[-1].start()
    if sparse:
        start_rows(cuts[1], cuts[2])
    for copy in third:
        copy.wait()
    value = total[high]
    for k in range(1, planes):
        value = value + three_in[k - 1].astype(f32)
    total[0] = value
    sums_ref[...] = value[:flat_pad]

    owners = range(VOCAB // vrows, (VOCAB + LEN - 1) // vrows + 1)
    place_out = total.at[0, pl.ds(flat_pad, tile), :]
    place_spot = pl.ds(pl.multiple_of(me * tile, 8), tile)
    for i, o in enumerate(owners):
        place_copy = copy_to(
            place_out, place_in.at[place_spot, :], place_sem.at[0, i], place_sem.at[1, me], o
        )
        pl.when(me != o)(place_copy.start)

    squares = jnp.sum(jnp.sum(value * value, axis=0, keepdims=True), axis=1, keepdims=True)
    if sparse:
        def add_pair(i, carry):
            pl.when(i > 0)(lambda: row_copy(2 * i).wait_recv())
            row_copy(2 * i + 1).wait_recv()
            a = chip ^ i
            lists = pair_lists(list_ref, a, cap)
            pick = (lax.broadcasted_iota(jnp.int32, (vrows, 2 * cap), 0) == lists).astype(bf16)
            both = rows_in[pl.ds(pl.multiple_of(a * 2 * cap, 2 * cap), 2 * cap), :]
            table_ref[...] += nn(pick, both)
            return carry

        table_ref[...] = jnp.zeros(table_ref.shape, f32)
        lax.fori_loop(0, chips, add_pair, 0)
    else:
        table_ref[...] = given_ref[...]
    grads = table_ref[...]
    squares = squares + jnp.sum(
        jnp.sum(grads * grads, axis=0, keepdims=True), axis=1, keepdims=True
    )
    loss = jnp.sum(loss_ref[0:1, :], axis=1, keepdims=True)
    lane = lax.broadcasted_iota(jnp.int32, (8, LANES), 1)
    lag = jnp.where(me == 0, loss_ref[1:2, 0:1], 0.0)
    stat_out[...] = jnp.where(
        lane == 0, squares, jnp.where(lane == 1, loss, jnp.where(lane == 2, lag, 0.0))
    )

    def stat_copy(k):
        return copy_to(
            stat_out, stat_in.at[me], stat_sem.at[0, k], stat_sem.at[1, k], me ^ k
        )

    def start_stat(k, carry):
        stat_copy(k).start()
        return carry

    def finish_stat(k, carry):
        stat_copy(k).wait()
        return carry

    lax.fori_loop(1, n, start_stat, 0)
    stat_in[me] = stat_out[...]

    for i, o in enumerate(owners):

        @pl.when(me == o)
        def _():
            place_in[place_spot, :] = place_out[...]

            def wait_place(j, carry):
                copy_to(
                    place_out,
                    place_in.at[pl.ds(pl.multiple_of(j * tile, 8), tile), :],
                    place_sem.at[0, i],
                    place_sem.at[1, j],
                    me ^ 1,
                ).wait_recv()
                return carry

            lax.fori_loop(0, o, wait_place, 0)
            lax.fori_loop(o + 1, n, wait_place, 0)
            low = max(0, o * vrows - VOCAB)
            top = min(LEN, (o + 1) * vrows - VOCAB)
            at = VOCAB + low - o * vrows
            if tile > place_seg:
                for d in range(n):
                    place_in[d * place_seg : (d + 1) * place_seg, :] = place_in[
                        d * tile : d * tile + place_seg, :
                    ]
            for j in range(2):
                table_ref[at : at + top - low, j * LANES : (j + 1) * LANES] += place_in[
                    pl.ds(2 * low + j, top - low, stride=2), :
                ]

    lax.fori_loop(1, n, finish_stat, 0)
    sums = jnp.sum(stat_in[...], axis=0)
    norm = jnp.sqrt(sums[0:1, 0:1])
    clip = jnp.minimum(1.0, clip_norm / (norm + 1e-06))
    stat_out[...] = jnp.where(lane == 0, norm, jnp.where(lane == 3, clip, sums))
    for i, o in enumerate(owners):
        place_copy = copy_to(
            place_out, place_in.at[place_spot, :], place_sem.at[0, i], place_sem.at[1, me], o
        )
        pl.when(me != o)(place_copy.wait_send)
    if sparse:

        def finish_row(k, carry):
            row_copy(k).wait_send()
            return carry

        lax.fori_loop(1, n, finish_row, 0)


def run_exchange(n, vrows, flat_grads, loss_rows, sparse, given):
    flat_len = flat_grads.shape[0] - 2 * LEN
    plane, planes, flat_seg, flat_pad, place_seg, seg = plan(n, flat_len)
    count = len(range(VOCAB // vrows, (VOCAB + LEN - 1) // vrows + 1))
    dma = pltpu.SemaphoreType.DMA
    return pl.pallas_call(
        functools.partial(exchange_kernel, n, flat_len, sparse),
        out_shape=(
            jax.ShapeDtypeStruct((vrows, D), f32),
            jax.ShapeDtypeStruct((flat_pad, LANES), f32),
            jax.ShapeDtypeStruct((8, LANES), f32),
        ),
        in_specs=[whole_spec()] * (2 + len(given)),
        out_specs=(whole_spec(),) * 3,
        scratch_shapes=[
            pltpu.VMEM((2, n // 2, seg, LANES), f32),
            pltpu.VMEM((n // 2, seg, LANES), f32),
            pltpu.VMEM((plane, planes, seg, LANES), bf16),
            pltpu.VMEM((plane - 1, planes, seg, LANES), bf16),
            pltpu.VMEM((planes, seg, LANES), f32),
            pltpu.VMEM((planes, seg, LANES), bf16),
            pltpu.VMEM((planes - 1, seg, LANES), bf16),
            pltpu.VMEM((n * place_tile(n), LANES), f32),
            pltpu.VMEM((n, 8, LANES), f32),
        ]
        + ([pltpu.VMEM((n * room(n), D), bf16)] if sparse else [])
        + [dma((2,)), dma((2, plane)), dma((2, planes)), dma((2, max(n, count))), dma((2, n)), dma((2, n))],
        compiler_params=pltpu.CompilerParams(
            collective_id=2 if sparse else 3, has_side_effects=True, vmem_limit_bytes=VMEM_LIMIT
        ),
        name="exchange" if sparse else "exchange_dense",
    )(flat_grads, loss_rows, *given)


def adam_step(weight, first_old, second, clipped):
    first_new = beta_one * first_old + (1.0 - beta_one) * clipped
    second_new = beta_two * second + (1.0 - beta_two) * clipped * clipped
    first_hat = first_new / (1.0 - beta_one**ADAM_STEP)
    second_hat = second_new / (1.0 - beta_two**ADAM_STEP)
    weight_new = weight - learn_rate * (
        first_hat / (jnp.sqrt(second_hat) + adam_eps) + decay_rate * weight
    )
    return (weight_new, first_new, second_new)


def rows_of(table, ids):
    return table.at[ids.reshape(-1)].get(mode="promise_in_bounds")


def ring_gather(devices, block):
    me = lax.axis_index("dp")
    rows = block.shape[0]
    onward = [(i, (i + 1) % devices) for i in range(devices)]

    def step(i, state):
        block, whole = state
        whole = lax.dynamic_update_slice(whole, block, (lax.rem(me - i + devices, devices) * rows, 0))
        return lax.ppermute(block, "dp", onward), whole

    whole = jnp.zeros((devices * rows, block.shape[1]), block.dtype)
    return lax.fori_loop(0, devices, step, (block, whole))[1]


def ring_scatter(devices, whole):
    me = lax.axis_index("dp")
    rows = whole.shape[0] // devices
    onward = [(i, (i + 1) % devices) for i in range(devices)]

    def part(i):
        at = lax.rem(me - 1 - i + 2 * devices, devices) * rows
        return lax.dynamic_slice(whole, (at, 0), (rows, whole.shape[1]))

    def step(i, total):
        return lax.ppermute(total, "dp", onward) + part(i)

    return lax.fori_loop(1, devices, step, part(0))


def per_device(
    devices,
    token_ids,
    lengths,
    gate_noise,
    lagrange,
    teacher_table,
    teacher_flat,
    word_table,
    table_first,
    table_second,
    layer_flat,
    flat_first,
    flat_second,
):
    seqs = token_ids.shape[0]
    half = seqs // 2
    vrows = word_table.shape[0]
    own = layer_flat.shape[0]
    flat_len = own * devices // LANES

    before = jnp.arange(seqs)[None, :] < jnp.arange(seqs)[:, None]
    longer = (lengths[None, :] > lengths[:, None]) | (
        (lengths[None, :] == lengths[:, None]) & before
    )
    rank = jnp.sum(longer.astype(jnp.int32), axis=1)
    kept = [r for r in range(seqs) if r % 4 in (0, 3)]
    order = jnp.array(kept + [r for r in range(seqs) if r not in kept], jnp.int32)
    chosen = (rank[None, :] == order[:, None]).astype(jnp.int32)
    token_ids = jnp.sum(chosen[:, :, None] * token_ids[None], axis=1)
    lengths = jnp.sum(chosen * lengths[None], axis=1)

    mates = [(i, devices - 1 - i) for i in range(devices)]
    sent = jnp.concatenate(
        [token_ids[half:], jnp.pad(lengths[half:], (0, LEN - half)).reshape(1, LEN)]
    )
    got = lax.ppermute(sent, "dp", mates)
    ids = jnp.concatenate([token_ids[:half], got[:half]])
    lens = jnp.concatenate([lengths[:half], got[half, :half]])

    owner = ids // vrows
    valid = jnp.arange(LEN)[None, :] < lens[:, None]
    target, listed, flat_all, place_all, *routed = run_fetch(
        devices,
        flat_len,
        jnp.where(valid, owner, -1),
        (ids - owner * vrows + 1).astype(f32),
        jnp.sum(lens).reshape(1),
        lens,
        ids // 16,
        ids % 16,
        teacher_table,
        teacher_table[VOCAB : VOCAB + LEN],
        teacher_flat.reshape(-1, LANES),
        word_table,
        layer_flat.reshape(-1, LANES),
    )
    stats = listed.reshape(devices, 8, LANES)[:, 1, :2]
    global_count = jnp.sum(stats[:, 0]).astype(f32)
    lag_weight = jnp.where(lax.axis_index("dp") == 0, 1.0, 0.0).astype(f32)
    factors = jnp.stack([(2.0 / D) / global_count, lag_weight])
    noise = jnp.pad(gate_noise, (0, 16 * LANES - gate_noise.shape[0]), constant_values=0.5)
    places = [place_all[i, : part[3]] for i, part in enumerate(place_parts(vrows))]
    shared = (
        lens,
        factors,
        lagrange,
        noise.reshape(16, LANES),
        flat_all,
        jnp.concatenate(places) if len(places) > 1 else places[0],
        target,
    )

    def from_slots():
        slots, fetched = routed
        flat_grads, _, loss_rows, packed = run_student(
            devices, flat_len, True, *shared, (slots, fetched)
        )
        result = run_exchange(devices, vrows, flat_grads, loss_rows, True, (packed, listed))
        return result

    def from_rows(mark):
        if routed:
            words, _ = lax.optimization_barrier((word_table, mark))
            table = ring_gather(devices, words.astype(bf16))
        else:
            table = lax.all_gather(word_table.astype(bf16), "dp", axis=0, tiled=True)
        flat_grads, grad_rows, loss_rows = run_student(
            devices, flat_len, False, *shared, (rows_of(table, ids),)
        )
        updates = jnp.transpose(grad_rows, (0, 2, 1)).reshape(seqs * LEN, D).astype(f32)
        table = jnp.zeros((devices * vrows, D), f32).at[ids.reshape(-1)].add(updates)
        if routed:
            table = ring_scatter(devices, table)
        else:
            table = lax.psum_scatter(table, "dp", scatter_dimension=0, tiled=True)
        result = run_exchange(devices, vrows, flat_grads, loss_rows, False, (table,))
        return result

    if routed:
        crowded = jnp.max(stats[:, 1])
        _, table_grad, sums, totals = lax.while_loop(
            lambda state: state[0] > 0,
            lambda state: (jnp.zeros_like(state[0]), *from_rows(state[0])),
            (crowded, *from_slots()),
        )
    else:
        table_grad, sums, totals = from_rows(0)
    flat_grad = sums[: own // LANES].reshape(-1)
    grad_norm = totals[0, 0]
    clip = totals[0, 3]
    total_loss = totals[0, 1] / global_count + totals[0, 2]
    table_new = adam_step(word_table, table_first, table_second, table_grad * clip)
    flat_new = adam_step(layer_flat, flat_first, flat_second, flat_grad * clip)
    return (*table_new, *flat_new, total_loss, grad_norm)


def solution(mesh):
    row, flat, copied = P("dp", None), P("dp"), P()
    in_specs = (row, flat, copied, copied, copied, copied, row, row, row, flat, flat, flat)
    out_specs = (row, row, row, flat, flat, flat, copied, copied)
    return jax.shard_map(
        functools.partial(per_device, mesh.shape["dp"]),
        mesh=mesh,
        in_specs=in_specs,
        out_specs=out_specs,
        check_vma=False,
    )
```

```python
import functools
import math

import jax
import jax.numpy as jnp
from jax import lax
from jax.experimental import pallas as pl
from jax.experimental.pallas import tpu as pltpu
from jax.sharding import PartitionSpec as P

D = 256
HEADS = 4
HD = D // HEADS
FF = 1024
LEN = 512
VOCAB = 30522
NPAR = 856836
LANES = 128
norm_eps = 1e-12
clip_norm = 0.002
learn_rate = 0.015
beta_one = 0.9
beta_two = 0.999
adam_eps = 1e-08
decay_rate = 0.01
sparse_target = 0.3
ADAM_STEP = 10
relaxation_heat = 2.0 / 3.0
widened_left_limit = -0.1
widened_right_limit = 1.1
f32 = jnp.float32
bf16 = jnp.bfloat16
VMEM_LIMIT = 60 * 2**20

C_GH = 10 * D
C_HEAD = 11 * D
C_BUP = 12 * D
C_GI = 12 * D + FF
C_ROWS = 12 * D + 2 * FF
A_BUP = 10 * D
A_GH = 10 * D + FF
A_HEAD = 11 * D + FF
A_GI = 12 * D + FF
A_ROWS = 12 * D + 2 * FF
R_UP = 5 * 512
R_DOWN = R_UP + 2048
R_VEC = R_DOWN + 2048
R_BUP = R_VEC + 20
R_LOGIT = R_BUP + 8
R_USED = R_LOGIT + 11


def nn(left, right):
    return jnp.dot(left, right, preferred_element_type=f32)


def nt(left, right):
    return lax.dot_general(left, right, (((1,), (1,)), ((), ())), preferred_element_type=f32)


def chunks(span):
    return [(c, min(256, span - c)) for c in range(0, span, 256)]


def wide(col_ref, row, rows, width):
    col = col_ref[row : row + rows, :]
    return jnp.concatenate([col] * (width // LANES), axis=1) if width > LANES else col


def lanes_in(values):
    total = values[:, :LANES]
    for c in range(LANES, values.shape[1], LANES):
        total = total + values[:, c : c + LANES]
    return total


def eye(size):
    return (
        lax.broadcasted_iota(jnp.int32, (size, size), 0)
        == lax.broadcasted_iota(jnp.int32, (size, size), 1)
    ).astype(bf16)


def standardise(x):
    mean = jnp.sum(x, axis=0, keepdims=True) * (1.0 / D)
    centred = x - mean
    variance = jnp.sum(centred * centred, axis=0, keepdims=True) * (1.0 / D)
    scale = lax.rsqrt(variance + norm_eps)
    return centred * scale, scale


def standardise_back(dx, hat, scale):
    mean_one = jnp.sum(dx, axis=0, keepdims=True) * (1.0 / D)
    mean_two = jnp.sum(dx * hat, axis=0, keepdims=True) * (1.0 / D)
    return scale * (dx - mean_one - hat * mean_two)


def gelu_parts(x):
    half_erf = 0.5 * lax.erf(x * (2.0**-0.5)) + 0.5
    return half_erf


def start_part(c, width, student, embed, pos_ref, col_ref, w, sc, eyes):
    cols = pl.ds(c, width)
    embedded = embed(c, width) + pos_ref[:, cols]
    hat, scale = standardise(embedded)
    start = hat * wide(col_ref, 0, D, width) + wide(col_ref, D, D, width)
    if student:
        sc["hat0"][:, cols] = hat
        sc["scale"][0:1, cols] = scale
        start = start * wide(col_ref, C_GH, D, width)
    sc["start"][:, cols] = start
    start_low = start.astype(bf16)
    if student:
        sc["start_low"][:, cols] = start_low
    q = nn(w["qkvT"][0:D, :], start_low) + wide(col_ref, 6 * D, D, width)
    sc["qkv"][0:D, cols] = q.astype(bf16)
    k = nn(w["qkvT"][D : 2 * D, :], start_low).astype(bf16)
    sc["qkv"][D : 2 * D, cols] = k
    v = (nn(w["qkvT"][2 * D : 3 * D, :], start_low) + wide(col_ref, 7 * D, D, width)).astype(bf16)
    sc["qkv"][2 * D : 3 * D, cols] = v
    for h in range(HEADS):
        rows = slice(h * HD, (h + 1) * HD)
        sc["k_rows"][h, cols, :] = nt(eyes[width], k[rows, :]).astype(bf16)
        if student:
            sc["v_rows"][h, cols, :] = nt(eyes[width], v[rows, :]).astype(bf16)


def attend(span, length, student, col_ref, sc):
    for c, width in chunks(span):
        valid = lax.broadcasted_iota(jnp.int32, (span, width), 0) < length
        for h in range(HEADS):
            q_h = sc["qkv"][h * HD : (h + 1) * HD, c : c + width] * bf16(HD**-0.5)
            scores = jnp.where(valid, nn(sc["k_rows"][h, 0:span, :], q_h), -1e30)
            shares = jnp.exp(scores - jnp.max(scores, axis=0, keepdims=True))
            shares_low = (shares * (1.0 / jnp.sum(shares, axis=0, keepdims=True))).astype(bf16)
            if student:
                sc["shares"][h, 0:span, c : c + width] = shares_low
            context = nn(sc["qkv"][2 * D + h * HD : 2 * D + (h + 1) * HD, 0:span], shares_low)
            if student:
                sc["context"][h * HD : (h + 1) * HD, c : c + width] = context
                context = context * wide(col_ref, C_HEAD + h * HD, HD, width)
            sc["gated"][h * HD : (h + 1) * HD, c : c + width] = context.astype(bf16)


def middle_part(c, width, student, col_ref, w, sc):
    cols = pl.ds(c, width)
    branch = nn(w["oT"][...], sc["gated"][:, cols]) + wide(col_ref, 8 * D, D, width)
    if student:
        sc["branch"][:, 0:width] = branch
        branch = branch * wide(col_ref, C_GH, D, width)
    hat, scale = standardise(sc["start"][:, cols] + branch)
    middle = hat * wide(col_ref, 2 * D, D, width) + wide(col_ref, 3 * D, D, width)
    if student:
        sc["hat1"][:, 0:width] = hat
        sc["scale"][1:2, cols] = scale
    middle_low = middle.astype(bf16)
    if student:
        sc["middle_low"][:, 0:width] = middle_low
    for r in range(0, FF, D):
        pre = nn(w["upT"][r : r + D, :], middle_low) + wide(col_ref, C_BUP + r, D, width)
        cdf = 0.5 * lax.erf(pre * (2.0**-0.5)) + 0.5
        act = pre * cdf
        if student:
            inner = wide(col_ref, C_GI + r, D, width)
            pdf = jnp.exp(pre * pre * -0.5) * (1.0 / math.sqrt(2.0 * math.pi))
            sc["act"][r : r + D, 0:width] = act
            sc["slope"][r : r + D, 0:width] = (cdf + pre * pdf) * inner
            act = act * inner
        sc["up"][r : r + D, 0:width] = act.astype(bf16)
    down = nn(w["downT"][...], sc["up"][:, 0:width]) + wide(col_ref, 9 * D, D, width)
    if student:
        sc["down"][:, 0:width] = down
        down = down * wide(col_ref, C_GH, D, width)
    hat, scale = standardise(middle + down)
    out = hat * wide(col_ref, 4 * D, D, width) + wide(col_ref, 5 * D, D, width)
    return out, hat, scale


def add_lanes(add_ref, row, values):
    add_ref[row : row + values.shape[0], :] += lanes_in(values)


def back_part(c, width, length, factor, out, hat, scale, target_ref, col_ref, w, sc, acc, add_ref, loss_ref):
    cols = pl.ds(c, width)
    here = slice(0, width)
    add = functools.partial(add_lanes, add_ref)
    out_low = out.astype(bf16)
    differ = nn(w["aT"][...], out_low) - target_ref[0, :, cols]
    token_valid = (lax.broadcasted_iota(jnp.int32, (1, width), 1) + c < length).astype(f32)
    loss_ref[0:1, cols] += jnp.sum(differ * differ, axis=0, keepdims=True) * (1.0 / D) * token_valid
    d_aligned = (differ * (token_valid * factor)).astype(bf16)
    acc["a"][...] += nt(out_low, d_aligned)
    d_out = nn(w["a"][...], d_aligned)
    add(4 * D, d_out * hat)
    add(5 * D, d_out)
    d_second = standardise_back(d_out * wide(col_ref, 4 * D, D, width), hat, scale)
    add(A_GH, d_second * sc["down"][:, here])
    d_down = (d_second * wide(col_ref, C_GH, D, width)).astype(bf16)
    add(9 * D, d_down.astype(f32))
    acc["down"][...] += nt(sc["up"][:, here], d_down)
    for r in range(0, FF, D):
        d_up = nn(w["down"][r : r + D, :], d_down)
        add(A_GI + r, d_up * sc["act"][r : r + D, here])
        d_pre = (d_up * sc["slope"][r : r + D, here]).astype(bf16)
        sc["d_pre"][r : r + D, here] = d_pre
        add(A_BUP + r, d_pre.astype(f32))
    d_middle = d_second + nn(w["up"][...], sc["d_pre"][:, here])
    acc["up"][...] += nt(sc["middle_low"][:, here], sc["d_pre"][:, here])
    hat = sc["hat1"][:, here]
    add(2 * D, d_middle * hat)
    add(3 * D, d_middle)
    d_first = standardise_back(
        d_middle * wide(col_ref, 2 * D, D, width), hat, sc["scale"][1:2, cols]
    )
    sc["d_first"][:, cols] = d_first
    add(A_GH, d_first * sc["branch"][:, here])
    d_branch = (d_first * wide(col_ref, C_GH, D, width)).astype(bf16)
    add(8 * D, d_branch.astype(f32))
    acc["o"][...] += nt(sc["gated"][:, cols], d_branch)
    d_gated = nn(w["o"][...], d_branch)
    context = sc["context"][:, cols]
    add(A_HEAD, d_gated * context)
    d_context = d_gated * wide(col_ref, C_HEAD, D, width)
    sc["d_context"][:, cols] = d_context.astype(bf16)
    dot_rows = d_context * context
    for h in range(HEADS):
        sc["delta"][h : h + 1, cols] = jnp.sum(
            dot_rows[h * HD : (h + 1) * HD, :], axis=0, keepdims=True
        )


def attend_back(span, sc):
    full = slice(0, span)
    for h in range(HEADS):
        rows = slice(h * HD, (h + 1) * HD)
        d_value = nt(sc["d_context"][rows, full], sc["shares"][h, 0:span, 0:span])
        sc["d_qkv"][2 * D + h * HD : 2 * D + (h + 1) * HD, full] = d_value.astype(bf16)
        d_key = None
        for c, width in chunks(span):
            cols = slice(c, c + width)
            d_shares = nn(sc["v_rows"][h, 0:span, :], sc["d_context"][rows, cols])
            d_scores = (
                sc["shares"][h, 0:span, cols].astype(f32) * (d_shares - sc["delta"][h : h + 1, cols])
            ).astype(bf16)
            sc["d_qkv"][rows, cols] = (
                nn(sc["qkv"][D + h * HD : D + (h + 1) * HD, full], d_scores) * (HD**-0.5)
            ).astype(bf16)
            part = nt(sc["qkv"][rows, cols], d_scores)
            d_key = part if d_key is None else d_key + part
        sc["d_qkv"][D + h * HD : D + (h + 1) * HD, full] = (d_key * (HD**-0.5)).astype(bf16)


def end_part(c, width, col_ref, w, sc, acc, add_ref, grad_ref, pos_add):
    cols = pl.ds(c, width)
    add = functools.partial(add_lanes, add_ref)
    acc["qkv"][...] += nt(sc["start_low"][:, cols], sc["d_qkv"][:, cols])
    add(6 * D, sc["d_qkv"][0:D, cols].astype(f32))
    add(7 * D, sc["d_qkv"][2 * D : 3 * D, cols].astype(f32))
    d_start = sc["d_first"][:, cols] + nn(w["qkv"][...], sc["d_qkv"][:, cols])
    hat = sc["hat0"][:, cols]
    gain = wide(col_ref, 0, D, width)
    add(A_GH, d_start * (hat * gain + wide(col_ref, D, D, width)))
    d_norm = d_start * wide(col_ref, C_GH, D, width)
    add(0, d_norm * hat)
    add(D, d_norm)
    d_embedded = standardise_back(d_norm * gain, hat, sc["scale"][0:1, cols])
    pos_add[:, cols] += d_embedded
    grad_ref[0, :, cols] = d_embedded.astype(bf16)


def by_part(length, body):
    def step(i, carry):
        body(pl.multiple_of(i * 256, 256), 256)
        return carry

    lax.fori_loop(0, jnp.where(length > 384, 2, 1), step, 0)
    pl.when((length > 256) & (length <= 384))(lambda: body(256, 128))


def mark_slots(slot, perm_ref):
    step = 512
    width = slot.shape[1]

    def mark(i, carry):
        rows = pl.ds(pl.multiple_of(i * step, step), step)
        seen = lax.broadcasted_iota(jnp.int32, (step, width), 0) == slot - i * step
        perm_ref[rows, :] = seen.astype(f32).astype(bf16)
        return carry

    lax.fori_loop(0, perm_ref.shape[0] // step, mark, 0)


def pack_rows(span, perm_ref, grad_ref, packed_ref):
    step = 1024

    def add(i, carry):
        rows = pl.ds(pl.multiple_of(i * step, step), step)
        packed_ref[rows, :] += nt(perm_ref[rows, 0:span], grad_ref[0, :, 0:span]).astype(bf16)
        return carry

    lax.fori_loop(0, packed_ref.shape[0] // step, add, 0)


SPANS = (256, 384, 512)


def by_span(length, body):
    for i, span in enumerate(SPANS):
        low = SPANS[i - 1] if i else 0
        test = length > low
        if i == 0:
            test = length <= span
        elif i < len(SPANS) - 1:
            test = (length > low) & (length <= span)
        pl.when(test)(functools.partial(body, span))


def set_up(pos_in, pos_ref, eyes_refs):
    for size, ref in eyes_refs.items():
        ref[...] = eye(size)
    for c in range(0, LEN, 256):
        pos_ref[:, c : c + 256] = nt(eyes_refs[256][...], pos_in[c : c + 256, :])


TEACHER_W = (
    ("qkv", (D, 3 * D)),
    ("qkvT", (3 * D, D)),
    ("o", (D, D)),
    ("oT", (D, D)),
    ("up", (D, FF)),
    ("upT", (FF, D)),
    ("down", (FF, D)),
    ("downT", (D, FF)),
)
STUDENT_W = TEACHER_W + (("a", (D, D)), ("aT", (D, D)))


def spread(col_ref, at, row):
    col_ref[pl.ds(at, LANES), :] = jnp.transpose(jnp.broadcast_to(row, (LANES, LANES)))


def load_weights(flat, w, col_ref, one, student):
    squares = [("qkv", 0), ("qkv", D), ("qkv", 2 * D), ("o", 0)] + ([("a", 0)] if student else [])
    for i, (name, at) in enumerate(squares):
        for j in range(2):
            lanes = slice(at + j * LANES, at + (j + 1) * LANES)
            w[name][:, lanes] = flat[pl.ds(512 * i + j, D, stride=2), :].astype(bf16)
    base = 512 * len(squares)
    for j in range(8):
        w["up"][:, j * LANES : (j + 1) * LANES] = flat[pl.ds(base + j, D, stride=8), :].astype(bf16)
    base = base + 2048
    for j in range(2):
        w["down"][:, j * LANES : (j + 1) * LANES] = flat[pl.ds(base + j, FF, stride=2), :].astype(
            bf16
        )
    base = base + 2048
    for i in range(20):
        spread(col_ref, i * LANES, flat[base + i : base + i + 1, :])
    for j in range(8):
        spread(col_ref, C_BUP + j * LANES, flat[base + 20 + j : base + 21 + j, :])
    unit = one[...]
    for name in ("qkv", "o", "up") + (("a",) if student else ()):
        for b in range(0, w[name].shape[1], D):
            w[name + "T"][b : b + D, :] = nt(unit, w[name][:, b : b + D]).astype(bf16)
    for b in range(0, FF, D):
        w["downT"][:, b : b + D] = nt(unit, w["down"][b : b + D, :]).astype(bf16)


def total_of(x):
    return jnp.sum(jnp.sum(x, axis=0, keepdims=True), axis=1, keepdims=True)


def head_groups():
    return (
        lax.broadcasted_iota(jnp.int32, (D, LANES), 0) // HD
        == lax.broadcasted_iota(jnp.int32, (D, LANES), 1)
    ).astype(f32)


def load_gates(logits, noise, lagrange_ref, lag_weight, col_ref, slope_ref, lag_ref):
    index = lax.broadcasted_iota(
        jnp.int32, logits.shape, 0
    ) * LANES + lax.broadcasted_iota(jnp.int32, logits.shape, 1)
    hidden, heads = index < D, (index >= D) & (index < D + HEADS)
    inner = (index >= D + HEADS) & (index < D + HEADS + FF)
    logistic = jax.nn.sigmoid((jnp.log(noise) - jnp.log(1.0 - noise) + logits) / relaxation_heat)
    spanned = widened_right_limit - widened_left_limit
    stretched = logistic * spanned + widened_left_limit
    gates = jnp.clip(stretched, 0.0, 1.0)
    inside = jnp.where((stretched > 0.0) & (stretched < 1.0), 1.0, 0.0)
    inside = jnp.where((stretched == 0.0) | (stretched == 1.0), 0.5, inside)
    slope_ref[...] = inside * logistic * (1.0 - logistic) * (spanned / relaxation_heat)
    keep = jax.nn.sigmoid(
        logits - relaxation_heat * math.log(-widened_left_limit / widened_right_limit)
    )
    kept = total_of(jnp.where(hidden, keep, 0.0)) * (1.0 / D)
    rest = total_of(jnp.where(heads, keep * (4.0 * HD), 0.0) + jnp.where(inner, keep * 2.0, 0.0))
    scale = 1.0 / (4.0 * D + 2.0 * FF)
    excess = kept * rest * scale - sparse_target
    rate = (lagrange_ref[0] + 2.0 * lagrange_ref[1] * excess) * (scale * lag_weight)
    share = jnp.where(hidden, rest * (1.0 / D), 0.0)
    share = share + kept * (jnp.where(heads, 4.0 * HD, 0.0) + jnp.where(inner, 2.0, 0.0))
    lag_ref[...] = rate * share * (keep * (1.0 - keep))
    for j in range(2):
        spread(col_ref, C_GH + j * LANES, gates[j : j + 1, :])
    wide_heads = lax.dot_general(
        jnp.broadcast_to(gates[2:3, :], (8, LANES)),
        head_groups(),
        (((1,), (1,)), ((), ())),
        preferred_element_type=f32,
        precision=lax.Precision.HIGHEST,
    )
    for j in range(2):
        spread(col_ref, C_HEAD + j * LANES, wide_heads[0:1, j * LANES : (j + 1) * LANES])
    run = jnp.concatenate([gates[j : j + 1, :] for j in range(2, 11)], axis=1)
    run = pltpu.roll(jnp.broadcast_to(run, (8, 9 * LANES)), 9 * LANES - HEADS, 1)
    for j in range(8):
        spread(col_ref, C_GI + j * LANES, run[0:1, j * LANES : (j + 1) * LANES])
    return lagrange_ref[0] * excess + lagrange_ref[1] * excess * excess


TEACHER_S = (
    ("start", (D, LEN), f32),
    ("qkv", (3 * D, LEN), bf16),
    ("k_rows", (HEADS, LEN, HD), bf16),
    ("gated", (D, LEN), bf16),
    ("up", (FF, 256), bf16),
)
STUDENT_S = TEACHER_S + (
    ("start_low", (D, LEN), bf16),
    ("hat0", (D, LEN), f32),
    ("hat1", (D, 256), f32),
    ("scale", (8, LEN), f32),
    ("v_rows", (HEADS, LEN, HD), bf16),
    ("shares", (HEADS, LEN, LEN), bf16),
    ("context", (D, LEN), f32),
    ("branch", (D, 256), f32),
    ("middle_low", (D, 256), bf16),
    ("act", (FF, 256), f32),
    ("slope", (FF, 256), f32),
    ("down", (D, 256), f32),
    ("d_pre", (FF, 256), bf16),
    ("d_first", (D, LEN), f32),
    ("d_context", (D, LEN), bf16),
    ("delta", (8, LEN), f32),
    ("d_qkv", (3 * D, LEN), bf16),
)
ACCS = (
    ("qkv", (D, 3 * D)),
    ("o", (D, D)),
    ("a", (D, D)),
    ("up", (D, FF)),
    ("down", (FF, D)),
)


class Eyes:
    def __init__(self, one, two):
        self.refs = {128: one, 256: two}

    def __getitem__(self, size):
        return self.refs[size][...]


def student_kernel(n, flat_len, sparse, len_ref, fac_ref, lagrange_ref, noise_ref, flat_in, pos_in, target_ref, *rest):
    plane, planes, flat_seg = plan(n, flat_len)[:3]
    cap = room(n)
    if sparse:
        slot_ref, rows_ref = rest[:2]
        rest = rest[2:]
    else:
        rows_ref = rest[0]
        rest = rest[1:]
    flat_ref, grad_ref, loss_ref = rest[:3]
    rest = rest[3:]
    if sparse:
        packed_ref, rows_all, perm_ref, slot_now = rest[:4]
        rest = rest[4:]
    w = {entry[0]: rest[i] for i, entry in enumerate(STUDENT_W)}
    rest = rest[len(STUDENT_W) :]
    sc = {entry[0]: rest[i] for i, entry in enumerate(STUDENT_S)}
    rest = rest[len(STUDENT_S) :]
    acc = {entry[0]: rest[i] for i, entry in enumerate(ACCS)}
    add_ref, pos_add, slope_ref, lag_ref, col_ref, pos_ref, eye_one, eye_two = rest[len(ACCS) :]
    s = pl.program_id(0)
    eyes = Eyes(eye_one, eye_two)

    @pl.when(s == 0)
    def _():
        set_up(pos_in, pos_ref, eyes.refs)
        for o in range(n):
            c = o // 2
            flat_ref[o * flat_seg : (o + 1) * flat_seg, :] = flat_in[
                o % 2, c % plane, c // plane, :, :
            ].astype(f32)[:flat_seg]
        load_weights(flat_ref, w, col_ref, eye_two, True)
        lag_value = load_gates(
            flat_ref[R_LOGIT : R_LOGIT + 16, :],
            noise_ref[...],
            lagrange_ref,
            fac_ref[1],
            col_ref,
            slope_ref,
            lag_ref,
        )
        for ref in list(acc.values()) + [add_ref, pos_add]:
            ref[...] = jnp.zeros(ref.shape, f32)
        row = lax.broadcasted_iota(jnp.int32, (8, LEN), 0)
        loss_ref[...] = jnp.where(row == 1, lag_value, 0.0)
        if sparse:
            packed_ref[...] = jnp.zeros(packed_ref.shape, bf16)
            for o in range(n):
                rows_all[:, o * cap : (o + 1) * cap] = rows_ref[o]

    length = len_ref[s]

    def embed(c, width):
        if sparse:
            mark_slots(slot_now[0:1, pl.ds(c, width)], perm_ref.at[:, pl.ds(c, width)])
            return nn(rows_all[...], perm_ref[:, pl.ds(c, width)])
        at = pl.multiple_of(s * LEN + c, 128)
        return nt(eyes[D], rows_ref[pl.ds(at, width), :])

    def between(c, width):
        out, hat, scale = middle_part(c, width, True, col_ref, w, sc)
        back_part(
            c, width, length, fac_ref[0], out, hat, scale, target_ref, col_ref, w, sc, acc, add_ref, loss_ref
        )

    grad_ref[0, :, 256:LEN] = jnp.zeros((D, LEN - 256), bf16)
    if sparse:
        slot_now[0:1, :] = slot_ref[pl.ds(s, 1), :]
    by_part(
        length, lambda c, width: start_part(c, width, True, embed, pos_ref, col_ref, w, sc, eyes)
    )
    by_span(length, lambda span: attend(span, length, True, col_ref, sc))
    by_part(length, between)
    by_span(length, lambda span: attend_back(span, sc))
    by_part(
        length,
        lambda c, width: end_part(c, width, col_ref, w, sc, acc, add_ref, grad_ref, pos_add),
    )
    if sparse:
        by_span(length, lambda span: pack_rows(span, perm_ref, grad_ref, packed_ref))

    @pl.when(s == pl.num_programs(0) - 1)
    def _():
        for i in range(3):
            for j in range(2):
                at = i * D + j * LANES
                flat_ref[pl.ds(512 * i + j, D, stride=2), :] = acc["qkv"][:, at : at + LANES]
        for j in range(2):
            lanes = slice(j * LANES, (j + 1) * LANES)
            flat_ref[pl.ds(512 * 3 + j, D, stride=2), :] = acc["o"][:, lanes]
            flat_ref[pl.ds(512 * 4 + j, D, stride=2), :] = acc["a"][:, lanes]
            flat_ref[pl.ds(R_DOWN + j, FF, stride=2), :] = acc["down"][:, lanes]
        for j in range(8):
            flat_ref[pl.ds(R_UP + j, D, stride=8), :] = acc["up"][:, j * LANES : (j + 1) * LANES]
        ones = jnp.ones((8, LANES), f32)

        def summed(row, rows):
            return lax.dot_general(
                ones,
                add_ref[row : row + rows, :],
                (((1,), (1,)), ((), ())),
                preferred_element_type=f32,
                precision=lax.Precision.HIGHEST,
            )

        for i in range(10):
            sums = summed(i * D, D)
            for j in range(2):
                flat_ref[R_VEC + 2 * i + j : R_VEC + 2 * i + j + 1, :] = sums[
                    0:1, j * LANES : (j + 1) * LANES
                ]
        sums = summed(A_BUP, FF)
        for j in range(8):
            flat_ref[R_BUP + j : R_BUP + j + 1, :] = sums[0:1, j * LANES : (j + 1) * LANES]
        hidden = summed(A_GH, D)
        heads = jnp.dot(
            summed(A_HEAD, D),
            head_groups(),
            preferred_element_type=f32,
            precision=lax.Precision.HIGHEST,
        )
        inner = summed(A_GI, FF)
        moved = pltpu.roll(jnp.concatenate([inner, jnp.zeros((8, LANES), f32)], axis=1), HEADS, 1)
        lane = lax.broadcasted_iota(jnp.int32, (8, LANES), 1)
        first = jnp.where(lane < HEADS, heads, moved[:, :LANES])
        tail = [hidden[:, :LANES], hidden[:, LANES:], first] + [
            moved[:, j * LANES : (j + 1) * LANES] for j in range(1, 9)
        ]
        for j, piece in enumerate(tail):
            flat_ref[R_LOGIT + j : R_LOGIT + j + 1, :] = (
                piece[0:1] * slope_ref[j : j + 1, :] + lag_ref[j : j + 1, :]
            )
        flat_ref[R_USED:flat_len, :] = jnp.zeros((flat_len - R_USED, LANES), f32)
        for j in range(2):
            flat_ref[pl.ds(flat_len + j, LEN, stride=2), :] = jnp.transpose(
                pos_add[j * LANES : (j + 1) * LANES, :]
            )


def whole_spec():
    return pl.BlockSpec(memory_space=pltpu.VMEM)


def smem_spec():
    return pl.BlockSpec(memory_space=pltpu.SMEM)


def seq_spec():
    return pl.BlockSpec((1, D, LEN), lambda s: (s, 0, 0))


def common_scratch():
    return [
        pltpu.VMEM((C_ROWS, LANES), f32),
        pltpu.VMEM((D, LEN), f32),
        pltpu.VMEM((128, 128), bf16),
        pltpu.VMEM((256, 256), bf16),
    ]


def run_student(n, flat_len, sparse, lengths, factors, lagrange, noise, flat_all, places, target, given):
    seqs = lengths.shape[0]
    slot_rows = n * room(n)
    shapes = [
        jax.ShapeDtypeStruct((flat_len + 2 * LEN, LANES), f32),
        jax.ShapeDtypeStruct((seqs, D, LEN), bf16),
        jax.ShapeDtypeStruct((8, LEN), f32),
    ]
    out_specs = [whole_spec(), seq_spec(), whole_spec()]
    scratch = []
    if sparse:
        shapes.append(jax.ShapeDtypeStruct((slot_rows, D), bf16))
        out_specs.append(whole_spec())
        scratch = [
            pltpu.VMEM((D, slot_rows), bf16),
            pltpu.VMEM((slot_rows, LEN), bf16),
            pltpu.VMEM((8, LEN), jnp.int32),
        ]
    return pl.pallas_call(
        functools.partial(student_kernel, n, flat_len, sparse),
        grid=(seqs,),
        out_shape=tuple(shapes),
        in_specs=[smem_spec()] * 3
        + [whole_spec()] * 3
        + [seq_spec()]
        + [whole_spec()] * len(given),
        out_specs=tuple(out_specs),
        scratch_shapes=scratch
        + [pltpu.VMEM(shape, bf16) for _, shape in STUDENT_W]
        + [pltpu.VMEM(shape, kind) for _, shape, kind in STUDENT_S]
        + [pltpu.VMEM(shape, f32) for _, shape in ACCS]
        + [
            pltpu.VMEM((A_ROWS, LANES), f32),
            pltpu.VMEM((D, LEN), f32),
            pltpu.VMEM((16, LANES), f32),
            pltpu.VMEM((16, LANES), f32),
        ]
        + common_scratch(),
        compiler_params=pltpu.CompilerParams(vmem_limit_bytes=44 * 2**20),
        name="student" if sparse else "student_dense",
    )(lengths, factors, lagrange, noise, flat_all, places, target, *given)


MESH = pl.DeviceIdType.MESH
ROW_CUTS = (8, 8)


def room(n):
    return LANES if 8 * LEN // n >= LANES else 0


def filled(n):
    return room(n) - 16


def greet_all(me, n):
    barrier = pltpu.get_barrier_semaphore()

    def signal(k, carry):
        pl.semaphore_signal(barrier, inc=1, device_id=(me ^ k,), device_id_type=MESH)
        return carry

    lax.fori_loop(1, n, signal, 0)
    pl.semaphore_wait(barrier, n - 1)


def copy_to(source, target, send, receive, device):
    return pltpu.make_async_remote_copy(
        src_ref=source,
        dst_ref=target,
        send_sem=send,
        recv_sem=receive,
        device_id=(device,),
        device_id_type=MESH,
    )


def list_rows(n, owner_ref, local_ref, stat, slot_ref, tile_ref):
    cap = room(n)
    upper = (
        lax.broadcasted_iota(jnp.int32, (256, 256), 0)
        <= lax.broadcasted_iota(jnp.int32, (256, 256), 1)
    ).astype(bf16)

    def sequence(s, state):
        base, listed = state
        for c in range(0, LEN, 256):
            owner = owner_ref[pl.ds(s, 1), c : c + 256]
            mine = (lax.broadcasted_iota(jnp.int32, (n, 256), 0) == owner).astype(f32)
            before = nn(mine.astype(bf16), upper)
            rank = jnp.sum(mine * (before - 1.0 + base), axis=0, keepdims=True).astype(jnp.int32)
            fits = (owner >= 0) & (rank < filled(n))
            slot_ref[pl.ds(s, 1), c : c + 256] = jnp.where(fits, owner * cap + rank, n * cap)
            place = (
                lax.broadcasted_iota(jnp.int32, (LANES, 256), 0) == jnp.where(fits, rank, -1)
            ).astype(f32)
            listed = listed + lax.dot_general(
                mine * local_ref[pl.ds(s, 1), c : c + 256],
                place,
                (((1,), (1,)), ((), ())),
                preferred_element_type=f32,
                precision=lax.Precision.HIGHEST,
            )
            base = base + before[:, 255:256]
        return base, listed

    base, listed = lax.fori_loop(
        0,
        owner_ref.shape[0],
        sequence,
        (jnp.zeros((n, 1), f32), jnp.zeros((n, LANES), f32)),
    )
    over = jnp.max(base, axis=0, keepdims=True) > filled(n)
    lane = lax.broadcasted_iota(jnp.int32, (n, LANES), 1)
    tile_ref[...] = jnp.zeros(tile_ref.shape, jnp.int32)
    tile_ref[pl.ds(0, n, stride=8), :] = (listed + 0.5).astype(jnp.int32) - 1
    tile_ref[pl.ds(1, n, stride=8), :] = jnp.where(
        lane == 0, stat, jnp.where(lane == 1, over.astype(jnp.int32), 0)
    )


def place_parts(vrows):
    parts = []
    for o in range(VOCAB // vrows, (VOCAB + LEN - 1) // vrows + 1):
        low, top = max(VOCAB, o * vrows), min(VOCAB + LEN, (o + 1) * vrows)
        parts.append((o, low - o * vrows, low - VOCAB, top - low))
    return parts


def round_up(value, step):
    return -(-value // step) * step


def pair_lists(list_ref, a, cap):
    return jnp.concatenate(
        [list_ref[pl.ds(pl.multiple_of(a * 16 + 8 * j, 8), 8), :][0:1, :cap] for j in range(2)],
        axis=1,
    )


def fetch_kernel(
    n, flat_len, owner_ref, local_ref, stat_ref, len_ref, block_ref, row_ref, words_in, pos_in, flat_in, table_ref, own_flat, *rest
):
    plane, planes, flat_seg, flat_pad = plan(n, flat_len)[:4]
    cap = room(n)
    vrows = table_ref.shape[0]
    parts = place_parts(vrows)
    out_ref, got_out, flat_out, place_out = rest[:4]
    rest = rest[4:]
    if cap:
        slot_ref, rows_out = rest[:2]
        rest = rest[2:]
    w = {entry[0]: rest[i] for i, entry in enumerate(TEACHER_W)}
    rest = rest[len(TEACHER_W) :]
    sc = {entry[0]: rest[i] for i, entry in enumerate(TEACHER_S)}
    rest = rest[len(TEACHER_S) :]
    tile_ref, got_ref, flat_all, place_all, pad_ref, flat_f32 = rest[:6]
    list_sem, a_sem, b_sem, c_sem, pa_sem, pb_sem, pc_sem = rest[6:13]
    col_ref, pos_ref, eye_one, eye_two = rest[13:17]
    words, picked, word_sem, out_sem = rest[17:21]
    if cap:
        table_turned, row_send, rows_in, row_sem = rest[21:]
    eyes = Eyes(eye_one, eye_two)
    s = pl.program_id(0)
    seqs = owner_ref.shape[0]
    me = lax.axis_index("dp")
    core = lax.rem(me, 2)
    chip = me // 2
    mid = lax.rem(chip, plane)
    high = chip // plane

    def device(h, m, c):
        return (h * plane + m) * 2 + c

    def tile(ref, i):
        return ref.at[pl.ds(pl.multiple_of(i * 8, 8), 8), :]

    def list_copy(k):
        return copy_to(
            tile(tile_ref, me ^ k), tile(got_ref, me), list_sem.at[0, k], list_sem.at[1, k], me ^ k
        )

    def row_copy(k):
        return copy_to(
            row_send.at[me ^ k], rows_in.at[me], row_sem.at[0, k], row_sem.at[1, k], me ^ k
        )

    def flat_copies(stage):
        copies = []
        if stage == 0:
            spot = flat_all.at[core, mid, high]
            for k in range(1, planes):
                to = device(lax.rem(high + k, planes), mid, core)
                copies.append(copy_to(spot, spot, a_sem.at[0, k], a_sem.at[1, k], to))
        elif stage == 1:
            spot = flat_all.at[core, mid]
            for k in range(1, plane):
                to = device(high, lax.rem(mid + k, plane), core)
                copies.append(copy_to(spot, spot, b_sem.at[0, k], b_sem.at[1, k], to))
        else:
            spot = flat_all.at[core]
            copies.append(copy_to(spot, spot, c_sem.at[0], c_sem.at[1], me ^ 1))
        return copies

    def place_copies(stage, i):
        o, _, _, count = parts[i]
        chip_o = o // 2
        high_o, mid_o, core_o = chip_o // plane, chip_o % plane, o % 2
        spot = place_all.at[i, pl.ds(0, round_up(count, 16)), :]
        same_core, same_mid, same_high = core == core_o, mid == mid_o, high == high_o
        copies = []
        if stage == 0:
            for k in range(1, planes):
                to = device((high_o + k) % planes, mid_o, core_o)
                copies.append(copy_to(spot, spot, pa_sem.at[0, i, k], pa_sem.at[1, i, 0], to))
            sends = same_core & same_mid & same_high
            receives = same_core & same_mid & (high != high_o)
        elif stage == 1:
            for k in range(1, plane):
                to = device(high, (mid_o + k) % plane, core_o)
                copies.append(copy_to(spot, spot, pb_sem.at[0, i, k], pb_sem.at[1, i, 0], to))
            sends = same_core & same_mid
            receives = same_core & (mid != mid_o)
        else:
            copies.append(copy_to(spot, spot, pc_sem.at[0, i], pc_sem.at[1, i], me ^ 1))
            sends = same_core
            receives = core != core_o
        return copies, sends, receives

    def start_stage(stage):
        for copy in flat_copies(stage):
            copy.start()
        for i in range(len(parts)):
            copies, sends, _ = place_copies(stage, i)

            @pl.when(sends)
            def _():
                for copy in copies:
                    copy.start()

    def finish_stage(stage):
        for copy in flat_copies(stage):
            copy.wait()
        for i in range(len(parts)):
            copies, sends, receives = place_copies(stage, i)

            @pl.when(sends)
            def _():
                for copy in copies:
                    copy.wait_send()

            @pl.when(receives)
            def _():
                copies[0].wait_recv()

    known = words.shape[0] * 16
    word_copy = pltpu.make_async_copy(
        words_in.at[pl.ds(0, known), :], words.reshape(known, D), word_sem
    )

    @pl.when(s == 0)
    def _():
        word_copy.start()
        picked[...] = jnp.zeros(picked.shape, f32)
        greet_all(me, n)
        pad_ref[...] = jnp.zeros(pad_ref.shape, f32)
        pad_ref[0:flat_seg, :] = own_flat[...]
        flat_all[core, mid, high] = pad_ref[...].astype(bf16)
        for i, (o, at, _, count) in enumerate(parts):

            @pl.when(me == o)
            def _():
                full = round_up(count, 16)
                part = table_ref[at : at + count, :]
                if full > count:
                    part = jnp.concatenate([part, jnp.zeros((full - count, D), f32)], axis=0)
                place_all[i, 0:full, :] = part.astype(bf16)

        start_stage(0)
        if cap:
            list_rows(n, owner_ref, local_ref, stat_ref[0], slot_ref, tile_ref)
        else:
            tile_ref[...] = jnp.zeros(tile_ref.shape, jnp.int32) + stat_ref[0]

        def start_list(k, carry):
            list_copy(k).start()
            return carry

        lax.fori_loop(1, n, start_list, 0)
        own = pl.ds(pl.multiple_of(me * 8, 8), 8)
        got_ref[own, :] = tile_ref[own, :]
        set_up(pos_in, pos_ref, eyes.refs)
        if cap:
            table_turned[...] = nt(eye_two[...], table_ref[...].astype(bf16)).astype(bf16)

        def finish_list(k, carry):
            list_copy(k).wait()
            return carry

        lax.fori_loop(1, n, finish_list, 0)

        def serve(step, carry):
            i = n // 2 - 1 - step
            a = chip ^ i
            pick = (
                lax.broadcasted_iota(jnp.int32, (vrows, 2 * cap), 0) == pair_lists(got_ref, a, cap)
            ).astype(bf16)
            both = nn(table_turned[...], pick).astype(bf16)
            for j in range(2):
                row_send[2 * a + j] = both[:, j * cap : (j + 1) * cap]
                k = 2 * i + (core ^ j)
                pl.when(k > 0)(row_copy(k).start)
            return carry

        if cap:
            lax.fori_loop(0, n // 2, serve, 0)
            rows_in[me] = row_send[me]
        step = 512
        whole = flat_in.shape[0] // step

        def unpack(i, carry):
            rows = pl.ds(pl.multiple_of(i * step, step), step)
            flat_f32[rows, :] = flat_in[rows, :].astype(f32)
            return carry

        lax.fori_loop(0, whole, unpack, 0)
        flat_f32[whole * step :, :] = flat_in[whole * step :, :].astype(f32)
        load_weights(flat_f32, w, col_ref, eye_two, False)
        word_copy.wait()

    @pl.when(s == 1)
    def _():
        finish_stage(0)
        start_stage(1)

    length = len_ref[s]
    from_me = jnp.where(s < seqs // 2, me, n - 1 - me)
    longest = LEN // 3 + (LEN - LEN // 3) * from_me // (n - 1)

    def pick_eight(g, carry):
        rows = []
        for u in range(8):
            block = words[block_ref[s, g * 8 + u]].astype(f32)
            mine = lax.broadcasted_iota(jnp.int32, (16, D), 0) == row_ref[s, g * 8 + u]
            rows.append(jnp.sum(jnp.where(mine, block, 0.0), axis=0, keepdims=True))
        picked[pl.ds(pl.multiple_of(g * 8, 8), 8), :] = jnp.concatenate(rows, axis=0)
        return carry

    lax.fori_loop(0, (longest + 7) // 8, pick_eight, 0)

    def embed(c, width):
        return nt(eyes[D], picked[pl.ds(c, width), :].astype(bf16))

    def finish(c, width):
        out_ref[0, :, pl.ds(c, width)] = middle_part(c, width, False, col_ref, w, sc)[0]

    def body(span):
        for c, width in chunks(span):
            start_part(c, width, False, embed, pos_ref, col_ref, w, sc, eyes)
        attend(span, length, False, col_ref, sc)
        for c, width in chunks(span):
            finish(c, width)

    by_span(longest, body)

    @pl.when(s == seqs - 2)
    def _():
        finish_stage(1)
        start_stage(2)

    @pl.when(s == seqs - 1)
    def _():
        finish_stage(2)

        def finish_row(k, carry):
            row_copy(k).wait()
            return carry

        if cap:
            lax.fori_loop(1, n, finish_row, 0)
        pairs = [(got_ref, got_out), (flat_all, flat_out), (place_all, place_out)]
        if cap:
            pairs.append((rows_in, rows_out))
        leaving = [
            pltpu.make_async_copy(source, target, out_sem.at[i])
            for i, (source, target) in enumerate(pairs)
        ]
        for copy in leaving:
            copy.start()
        for copy in leaving:
            copy.wait()


def run_fetch(n, flat_len, owner, local, stat, lengths, blocks, rows, words, places, teacher, table, own_flat):
    plane, planes, flat_seg, flat_pad = plan(n, flat_len)[:4]
    seqs, cap, vrows = owner.shape[0], room(n), table.shape[0]
    parts = place_parts(vrows)
    most = max(round_up(part[3], 16) for part in parts)
    dma = pltpu.SemaphoreType.DMA
    got = ((8 * n, LANES), jnp.int32)
    fetched = ((n, D, cap), bf16)
    flat_all = ((2, plane, planes, flat_pad, LANES), bf16)
    place_all = ((len(parts), most, D), bf16)
    shapes = [((seqs, D, LEN), f32), got, flat_all, place_all]
    far = pl.BlockSpec(memory_space=pl.ANY)
    out_specs = [seq_spec(), far, far, far]
    extra = []
    if cap:
        shapes += [(owner.shape, jnp.int32), fetched]
        out_specs += [whole_spec(), far]
        extra = [
            pltpu.VMEM((D, vrows), bf16),
            pltpu.VMEM(*fetched),
            pltpu.VMEM(*fetched),
            dma((2, n)),
        ]
    return pl.pallas_call(
        functools.partial(fetch_kernel, n, flat_len),
        grid=(seqs,),
        out_shape=tuple(jax.ShapeDtypeStruct(shape, kind) for shape, kind in shapes),
        in_specs=[whole_spec()] * 2
        + [smem_spec()] * 4
        + [pl.BlockSpec(memory_space=pl.ANY)]
        + [whole_spec()] * 4,
        out_specs=tuple(out_specs),
        scratch_shapes=[pltpu.VMEM(shape, bf16) for _, shape in TEACHER_W]
        + [pltpu.VMEM(shape, kind) for _, shape, kind in TEACHER_S]
        + [
            pltpu.VMEM(*got),
            pltpu.VMEM(*got),
            pltpu.VMEM(*flat_all),
            pltpu.VMEM(*place_all),
            pltpu.VMEM((flat_pad, LANES), f32),
            pltpu.VMEM(teacher.shape, f32),
            dma((2, n)),
            dma((2, planes)),
            dma((2, plane)),
            dma((2,)),
            dma((2, len(parts), planes)),
            dma((2, len(parts), plane)),
            dma((2, len(parts))),
        ]
        + common_scratch()
        + [pltpu.VMEM((words.shape[0] // 16, 16, D), bf16), pltpu.VMEM((LEN, D), f32), dma, dma((4,))]
        + extra,
        compiler_params=pltpu.CompilerParams(
            collective_id=1, has_side_effects=True, vmem_limit_bytes=50 * 2**20
        ),
        name="teacher",
    )(owner, local, stat, lengths, blocks, rows, words, places, teacher, table, own_flat)


def plan(n, flat_len):
    chips = n // 2
    plane = 2 ** ((chips.bit_length() - 1) // 2)
    flat_seg = flat_len // n
    flat_pad = round_up(flat_seg, 16)
    place_seg = 2 * LEN // n
    return plane, chips // plane, flat_seg, flat_pad, place_seg, flat_pad + round_up(place_seg, 16)


def place_tile(n):
    return max(8, 2 * LEN // n)


def exchange_kernel(n, flat_len, sparse, *refs):
    plane, planes, flat_seg, flat_pad, place_seg, seg = plan(n, flat_len)
    chips = n // 2
    cap = room(n)
    tile = place_tile(n)
    flat_ref, loss_ref = refs[:2]
    refs = refs[2:]
    if sparse:
        packed_ref, list_ref = refs[:2]
        refs = refs[2:]
    else:
        given_ref = refs[0]
        refs = refs[1:]
    table_ref, sums_ref, stat_out = refs[:3]
    (stage, one_in, two_out, two_in, total, three_out, three_in, place_in, stat_in) = refs[3:12]
    refs = refs[12:]
    if sparse:
        rows_in = refs[0]
        refs = refs[1:]
    one_sem, two_sem, three_sem, place_sem, stat_sem, row_sem = refs
    me = lax.axis_index("dp")
    core = lax.rem(me, 2)
    chip = me // 2
    mid = lax.rem(chip, plane)
    high = chip // plane
    vrows = table_ref.shape[0]

    greet_all(me, n)
    pad = jnp.zeros((16, LANES), f32)
    for o in range(n):
        spot = stage.at[o % 2, o // 2]
        if flat_pad > flat_seg:
            spot[flat_pad - 16 : flat_pad, :] = pad
        if seg > flat_pad + place_seg:
            spot[seg - 16 : seg, :] = pad
        spot[0:flat_seg, :] = flat_ref[o * flat_seg : (o + 1) * flat_seg, :]
        at = flat_len + o * place_seg
        spot[flat_pad : flat_pad + place_seg, :] = flat_ref[at : at + place_seg, :]
    first = copy_to(stage.at[1 - core], one_in, one_sem.at[0], one_sem.at[1], me ^ 1)
    first.start()

    if sparse:

        def bucket(ref, i):
            return ref.at[pl.ds(pl.multiple_of(i * cap, cap), filled(n)), :]

        def row_copy(k):
            return copy_to(
                bucket(packed_ref, me ^ k), bucket(rows_in, me), row_sem.at[0, k], row_sem.at[1, k], me ^ k
            )

        def start_row(i, carry):
            row_copy(n - i).start()
            return carry

        def start_rows(low, top):
            lax.fori_loop(low, top, start_row, 0)

        cuts = [1 + (n - 1) * part // 31 for part in ROW_CUTS] + [n]
        start_rows(1, cuts[0])
        own = pl.ds(pl.multiple_of(me * cap, cap), cap)
        rows_in[own, :] = packed_ref[own, :]

        def unused(i, carry):
            at = pl.multiple_of(i * cap + filled(n), 16)
            rows_in[pl.ds(at, cap - filled(n)), :] = jnp.zeros((cap - filled(n), D), bf16)
            return carry

        lax.fori_loop(0, n, unused, 0)

    first.wait()
    for m in range(plane):
        for h in range(planes):
            c = h * plane + m
            two_out[m, h] = (stage[core, c] + one_in[c]).astype(bf16)
    second = []
    for k in range(1, plane):
        m = lax.rem(mid + k, plane)
        second.append(
            copy_to(
                two_out.at[m],
                two_in.at[k - 1],
                two_sem.at[0, k],
                two_sem.at[1, k],
                (high * plane + m) * 2 + core,
            )
        )
        second[-1].start()
    if sparse:
        start_rows(cuts[0], cuts[1])
    for copy in second:
        copy.wait()
    for h in range(planes):
        c = h * plane + mid
        value = stage[core, c] + one_in[c]
        for k in range(1, plane):
            value = value + two_in[k - 1, h].astype(f32)
        total[h] = value
        three_out[h] = value.astype(bf16)
    third = []
    for k in range(1, planes):
        h = lax.rem(high + k, planes)
        third.append(
            copy_to(
                three_out.at[h],
                three_in.at[k - 1],
                three_sem.at[0, k],
                three_sem.at[1, k],
                (h * plane + mid) * 2 + core,
            )
        )
        third[-1].start()
    if sparse:
        start_rows(cuts[1], cuts[2])
    for copy in third:
        copy.wait()
    value = total[high]
    for k in range(1, planes):
        value = value + three_in[k - 1].astype(f32)
    total[0] = value
    sums_ref[...] = value[:flat_pad]

    owners = range(VOCAB // vrows, (VOCAB + LEN - 1) // vrows + 1)
    place_out = total.at[0, pl.ds(flat_pad, tile), :]
    place_spot = pl.ds(pl.multiple_of(me * tile, 8), tile)
    for i, o in enumerate(owners):
        place_copy = copy_to(
            place_out, place_in.at[place_spot, :], place_sem.at[0, i], place_sem.at[1, me], o
        )
        pl.when(me != o)(place_copy.start)

    squares = jnp.sum(jnp.sum(value * value, axis=0, keepdims=True), axis=1, keepdims=True)
    if sparse:
        def add_pair(i, carry):
            pl.when(i > 0)(lambda: row_copy(2 * i).wait_recv())
            row_copy(2 * i + 1).wait_recv()
            a = chip ^ i
            lists = pair_lists(list_ref, a, cap)
            pick = (lax.broadcasted_iota(jnp.int32, (vrows, 2 * cap), 0) == lists).astype(bf16)
            both = rows_in[pl.ds(pl.multiple_of(a * 2 * cap, 2 * cap), 2 * cap), :]
            table_ref[...] += nn(pick, both)
            return carry

        table_ref[...] = jnp.zeros(table_ref.shape, f32)
        lax.fori_loop(0, chips, add_pair, 0)
    else:
        table_ref[...] = given_ref[...]
    grads = table_ref[...]
    squares = squares + jnp.sum(
        jnp.sum(grads * grads, axis=0, keepdims=True), axis=1, keepdims=True
    )
    loss = jnp.sum(loss_ref[0:1, :], axis=1, keepdims=True)
    lane = lax.broadcasted_iota(jnp.int32, (8, LANES), 1)
    lag = jnp.where(me == 0, loss_ref[1:2, 0:1], 0.0)
    stat_out[...] = jnp.where(
        lane == 0, squares, jnp.where(lane == 1, loss, jnp.where(lane == 2, lag, 0.0))
    )

    def stat_copy(k):
        return copy_to(
            stat_out, stat_in.at[me], stat_sem.at[0, k], stat_sem.at[1, k], me ^ k
        )

    def start_stat(k, carry):
        stat_copy(k).start()
        return carry

    def finish_stat(k, carry):
        stat_copy(k).wait()
        return carry

    lax.fori_loop(1, n, start_stat, 0)
    stat_in[me] = stat_out[...]

    for i, o in enumerate(owners):

        @pl.when(me == o)
        def _():
            place_in[place_spot, :] = place_out[...]

            def wait_place(j, carry):
                copy_to(
                    place_out,
                    place_in.at[pl.ds(pl.multiple_of(j * tile, 8), tile), :],
                    place_sem.at[0, i],
                    place_sem.at[1, j],
                    me ^ 1,
                ).wait_recv()
                return carry

            lax.fori_loop(0, o, wait_place, 0)
            lax.fori_loop(o + 1, n, wait_place, 0)
            low = max(0, o * vrows - VOCAB)
            top = min(LEN, (o + 1) * vrows - VOCAB)
            at = VOCAB + low - o * vrows
            if tile > place_seg:
                for d in range(n):
                    place_in[d * place_seg : (d + 1) * place_seg, :] = place_in[
                        d * tile : d * tile + place_seg, :
                    ]
            for j in range(2):
                table_ref[at : at + top - low, j * LANES : (j + 1) * LANES] += place_in[
                    pl.ds(2 * low + j, top - low, stride=2), :
                ]

    lax.fori_loop(1, n, finish_stat, 0)
    sums = jnp.sum(stat_in[...], axis=0)
    norm = jnp.sqrt(sums[0:1, 0:1])
    clip = jnp.minimum(1.0, clip_norm / (norm + 1e-06))
    stat_out[...] = jnp.where(lane == 0, norm, sums)
    table_ref[...] = table_ref[...] * clip
    sums_ref[...] = sums_ref[...] * clip
    for i, o in enumerate(owners):
        place_copy = copy_to(
            place_out, place_in.at[place_spot, :], place_sem.at[0, i], place_sem.at[1, me], o
        )
        pl.when(me != o)(place_copy.wait_send)
    if sparse:

        def finish_row(k, carry):
            row_copy(k).wait_send()
            return carry

        lax.fori_loop(1, n, finish_row, 0)


def run_exchange(n, vrows, flat_grads, loss_rows, sparse, given):
    flat_len = flat_grads.shape[0] - 2 * LEN
    plane, planes, flat_seg, flat_pad, place_seg, seg = plan(n, flat_len)
    count = len(range(VOCAB // vrows, (VOCAB + LEN - 1) // vrows + 1))
    dma = pltpu.SemaphoreType.DMA
    return pl.pallas_call(
        functools.partial(exchange_kernel, n, flat_len, sparse),
        out_shape=(
            jax.ShapeDtypeStruct((vrows, D), f32),
            jax.ShapeDtypeStruct((flat_pad, LANES), f32),
            jax.ShapeDtypeStruct((8, LANES), f32),
        ),
        in_specs=[whole_spec()] * (2 + len(given)),
        out_specs=(whole_spec(),) * 3,
        scratch_shapes=[
            pltpu.VMEM((2, n // 2, seg, LANES), f32),
            pltpu.VMEM((n // 2, seg, LANES), f32),
            pltpu.VMEM((plane, planes, seg, LANES), bf16),
            pltpu.VMEM((plane - 1, planes, seg, LANES), bf16),
            pltpu.VMEM((planes, seg, LANES), f32),
            pltpu.VMEM((planes, seg, LANES), bf16),
            pltpu.VMEM((planes - 1, seg, LANES), bf16),
            pltpu.VMEM((n * place_tile(n), LANES), f32),
            pltpu.VMEM((n, 8, LANES), f32),
        ]
        + ([pltpu.VMEM((n * room(n), D), bf16)] if sparse else [])
        + [dma((2,)), dma((2, plane)), dma((2, planes)), dma((2, max(n, count))), dma((2, n)), dma((2, n))],
        compiler_params=pltpu.CompilerParams(
            collective_id=2 if sparse else 3, has_side_effects=True, vmem_limit_bytes=24 * 2**20
        ),
        name="exchange" if sparse else "exchange_dense",
    )(flat_grads, loss_rows, *given)


def adam_step(weight, first_old, second, clipped):
    first_new = beta_one * first_old + (1.0 - beta_one) * clipped
    second_new = beta_two * second + (1.0 - beta_two) * clipped * clipped
    first_hat = first_new / (1.0 - beta_one**ADAM_STEP)
    second_hat = second_new / (1.0 - beta_two**ADAM_STEP)
    weight_new = weight - learn_rate * (
        first_hat / (jnp.sqrt(second_hat) + adam_eps) + decay_rate * weight
    )
    return (weight_new, first_new, second_new)


def rows_of(table, ids):
    return table.at[ids.reshape(-1)].get(mode="promise_in_bounds")


def ring_gather(devices, block):
    me = lax.axis_index("dp")
    rows = block.shape[0]
    onward = [(i, (i + 1) % devices) for i in range(devices)]

    def step(i, state):
        block, whole = state
        whole = lax.dynamic_update_slice(whole, block, (lax.rem(me - i + devices, devices) * rows, 0))
        return lax.ppermute(block, "dp", onward), whole

    whole = jnp.zeros((devices * rows, block.shape[1]), block.dtype)
    return lax.fori_loop(0, devices, step, (block, whole))[1]


def ring_scatter(devices, whole):
    me = lax.axis_index("dp")
    rows = whole.shape[0] // devices
    onward = [(i, (i + 1) % devices) for i in range(devices)]

    def part(i):
        at = lax.rem(me - 1 - i + 2 * devices, devices) * rows
        return lax.dynamic_slice(whole, (at, 0), (rows, whole.shape[1]))

    def step(i, total):
        return lax.ppermute(total, "dp", onward) + part(i)

    return lax.fori_loop(1, devices, step, part(0))


def per_device(
    devices,
    token_ids,
    lengths,
    gate_noise,
    lagrange,
    teacher_table,
    teacher_flat,
    word_table,
    table_first,
    table_second,
    layer_flat,
    flat_first,
    flat_second,
):
    seqs = token_ids.shape[0]
    half = seqs // 2
    vrows = word_table.shape[0]
    own = layer_flat.shape[0]
    flat_len = own * devices // LANES

    before = jnp.arange(seqs)[None, :] < jnp.arange(seqs)[:, None]
    longer = (lengths[None, :] > lengths[:, None]) | (
        (lengths[None, :] == lengths[:, None]) & before
    )
    rank = jnp.sum(longer.astype(jnp.int32), axis=1)
    kept = [r for r in range(seqs) if r % 4 in (0, 3)]
    order = jnp.array(kept + [r for r in range(seqs) if r not in kept], jnp.int32)
    chosen = (rank[None, :] == order[:, None]).astype(jnp.int32)
    token_ids = jnp.sum(chosen[:, :, None] * token_ids[None], axis=1)
    lengths = jnp.sum(chosen * lengths[None], axis=1)

    mates = [(i, devices - 1 - i) for i in range(devices)]
    sent = jnp.concatenate(
        [token_ids[half:], jnp.pad(lengths[half:], (0, LEN - half)).reshape(1, LEN)]
    )
    got = lax.ppermute(sent, "dp", mates)
    ids = jnp.concatenate([token_ids[:half], got[:half]])
    lens = jnp.concatenate([lengths[:half], got[half, :half]])

    owner = ids // vrows
    valid = jnp.arange(LEN)[None, :] < lens[:, None]
    target, listed, flat_all, place_all, *routed = run_fetch(
        devices,
        flat_len,
        jnp.where(valid, owner, -1),
        (ids - owner * vrows + 1).astype(f32),
        jnp.sum(lens).reshape(1),
        lens,
        ids // 16,
        ids % 16,
        teacher_table,
        teacher_table[VOCAB : VOCAB + LEN],
        teacher_flat.reshape(-1, LANES),
        word_table,
        layer_flat.reshape(-1, LANES),
    )
    stats = listed.reshape(devices, 8, LANES)[:, 1, :2]
    global_count = jnp.sum(stats[:, 0]).astype(f32)
    lag_weight = jnp.where(lax.axis_index("dp") == 0, 1.0, 0.0).astype(f32)
    factors = jnp.stack([(2.0 / D) / global_count, lag_weight])
    noise = jnp.pad(gate_noise, (0, 16 * LANES - gate_noise.shape[0]), constant_values=0.5)
    places = [place_all[i, : part[3]] for i, part in enumerate(place_parts(vrows))]
    shared = (
        lens,
        factors,
        lagrange,
        noise.reshape(16, LANES),
        flat_all,
        jnp.concatenate(places) if len(places) > 1 else places[0],
        target,
    )

    def from_slots():
        slots, fetched = routed
        flat_grads, _, loss_rows, packed = run_student(
            devices, flat_len, True, *shared, (slots, fetched)
        )
        result = run_exchange(devices, vrows, flat_grads, loss_rows, True, (packed, listed))
        return result

    def from_rows(mark):
        if routed:
            words, _ = lax.optimization_barrier((word_table, mark))
            table = ring_gather(devices, words.astype(bf16))
        else:
            table = lax.all_gather(word_table.astype(bf16), "dp", axis=0, tiled=True)
        flat_grads, grad_rows, loss_rows = run_student(
            devices, flat_len, False, *shared, (rows_of(table, ids),)
        )
        updates = jnp.transpose(grad_rows, (0, 2, 1)).reshape(seqs * LEN, D).astype(f32)
        table = jnp.zeros((devices * vrows, D), f32).at[ids.reshape(-1)].add(updates)
        if routed:
            table = ring_scatter(devices, table)
        else:
            table = lax.psum_scatter(table, "dp", scatter_dimension=0, tiled=True)
        result = run_exchange(devices, vrows, flat_grads, loss_rows, False, (table,))
        return result

    if routed:
        crowded = jnp.max(stats[:, 1])
        _, table_grad, sums, totals = lax.while_loop(
            lambda state: state[0] > 0,
            lambda state: (jnp.zeros_like(state[0]), *from_rows(state[0])),
            (crowded, *from_slots()),
        )
    else:
        table_grad, sums, totals = from_rows(0)
    flat_grad = sums[: own // LANES].reshape(-1)
    grad_norm = totals[0, 0]
    total_loss = totals[0, 1] / global_count + totals[0, 2]
    table_new = adam_step(word_table, table_first, table_second, table_grad)
    flat_new = adam_step(layer_flat, flat_first, flat_second, flat_grad)
    return (*table_new, *flat_new, total_loss, grad_norm)


def solution(mesh):
    row, flat, copied = P("dp", None), P("dp"), P()
    in_specs = (row, flat, copied, copied, copied, copied, row, row, row, flat, flat, flat)
    out_specs = (row, row, row, flat, flat, flat, copied, copied)
    return jax.shard_map(
        functools.partial(per_device, mesh.shape["dp"]),
        mesh=mesh,
        in_specs=in_specs,
        out_specs=out_specs,
        check_vma=False,
    )
```

```python
import functools
import math

import jax
import jax.numpy as jnp
from jax import lax
from jax.experimental import pallas as pl
from jax.experimental.pallas import tpu as pltpu
from jax.sharding import PartitionSpec as P

D = 256
HEADS = 4
HD = D // HEADS
FF = 1024
LEN = 512
VOCAB = 30522
NPAR = 856836
LANES = 128
norm_eps = 1e-12
clip_norm = 0.002
learn_rate = 0.015
beta_one = 0.9
beta_two = 0.999
adam_eps = 1e-08
decay_rate = 0.01
sparse_target = 0.3
ADAM_STEP = 10
relaxation_heat = 2.0 / 3.0
widened_left_limit = -0.1
widened_right_limit = 1.1
f32 = jnp.float32
bf16 = jnp.bfloat16
VMEM_LIMIT = 60 * 2**20

C_GH = 10 * D
C_HEAD = 11 * D
C_BUP = 12 * D
C_GI = 12 * D + FF
C_ROWS = 12 * D + 2 * FF
A_BUP = 10 * D
A_GH = 10 * D + FF
A_HEAD = 11 * D + FF
A_GI = 12 * D + FF
A_ROWS = 12 * D + 2 * FF
R_UP = 5 * 512
R_DOWN = R_UP + 2048
R_VEC = R_DOWN + 2048
R_BUP = R_VEC + 20
R_LOGIT = R_BUP + 8
R_USED = R_LOGIT + 11


def nn(left, right):
    return jnp.dot(left, right, preferred_element_type=f32)


def nt(left, right):
    return lax.dot_general(left, right, (((1,), (1,)), ((), ())), preferred_element_type=f32)


def chunks(span):
    return [(c, min(256, span - c)) for c in range(0, span, 256)]


def wide(col_ref, row, rows, width):
    col = col_ref[row : row + rows, :]
    return jnp.concatenate([col] * (width // LANES), axis=1) if width > LANES else col


def lanes_in(values):
    total = values[:, :LANES]
    for c in range(LANES, values.shape[1], LANES):
        total = total + values[:, c : c + LANES]
    return total


def eye(size):
    return (
        lax.broadcasted_iota(jnp.int32, (size, size), 0)
        == lax.broadcasted_iota(jnp.int32, (size, size), 1)
    ).astype(bf16)


def standardise(x):
    mean = jnp.sum(x, axis=0, keepdims=True) * (1.0 / D)
    centred = x - mean
    variance = jnp.sum(centred * centred, axis=0, keepdims=True) * (1.0 / D)
    scale = lax.rsqrt(variance + norm_eps)
    return centred * scale, scale


def standardise_back(dx, hat, scale):
    mean_one = jnp.sum(dx, axis=0, keepdims=True) * (1.0 / D)
    mean_two = jnp.sum(dx * hat, axis=0, keepdims=True) * (1.0 / D)
    return scale * (dx - mean_one - hat * mean_two)


def gelu_parts(x):
    half_erf = 0.5 * lax.erf(x * (2.0**-0.5)) + 0.5
    return half_erf


def start_part(c, width, student, embed, pos_ref, col_ref, w, sc, eyes):
    cols = pl.ds(c, width)
    embedded = embed(c, width) + pos_ref[:, cols]
    hat, scale = standardise(embedded)
    start = hat * wide(col_ref, 0, D, width) + wide(col_ref, D, D, width)
    if student:
        sc["hat0"][:, cols] = hat
        sc["scale"][0:1, cols] = scale
        start = start * wide(col_ref, C_GH, D, width)
    sc["start"][:, cols] = start
    start_low = start.astype(bf16)
    if student:
        sc["start_low"][:, cols] = start_low
    q = nn(w["qkvT"][0:D, :], start_low) + wide(col_ref, 6 * D, D, width)
    sc["qkv"][0:D, cols] = q.astype(bf16)
    k = nn(w["qkvT"][D : 2 * D, :], start_low).astype(bf16)
    sc["qkv"][D : 2 * D, cols] = k
    v = (nn(w["qkvT"][2 * D : 3 * D, :], start_low) + wide(col_ref, 7 * D, D, width)).astype(bf16)
    sc["qkv"][2 * D : 3 * D, cols] = v
    for h in range(HEADS):
        rows = slice(h * HD, (h + 1) * HD)
        sc["k_rows"][h, cols, :] = nt(eyes[width], k[rows, :]).astype(bf16)
        if student:
            sc["v_rows"][h, cols, :] = nt(eyes[width], v[rows, :]).astype(bf16)


def attend(span, length, student, col_ref, sc):
    for c, width in chunks(span):
        valid = lax.broadcasted_iota(jnp.int32, (span, width), 0) < length
        for h in range(HEADS):
            q_h = sc["qkv"][h * HD : (h + 1) * HD, c : c + width] * bf16(HD**-0.5)
            scores = jnp.where(valid, nn(sc["k_rows"][h, 0:span, :], q_h), -1e30)
            shares = jnp.exp(scores - jnp.max(scores, axis=0, keepdims=True))
            shares_low = (shares * (1.0 / jnp.sum(shares, axis=0, keepdims=True))).astype(bf16)
            if student:
                sc["shares"][h, 0:span, c : c + width] = shares_low
            context = nn(sc["qkv"][2 * D + h * HD : 2 * D + (h + 1) * HD, 0:span], shares_low)
            if student:
                sc["context"][h * HD : (h + 1) * HD, c : c + width] = context
                context = context * wide(col_ref, C_HEAD + h * HD, HD, width)
            sc["gated"][h * HD : (h + 1) * HD, c : c + width] = context.astype(bf16)


def middle_part(c, width, student, col_ref, w, sc):
    cols = pl.ds(c, width)
    branch = nn(w["oT"][...], sc["gated"][:, cols]) + wide(col_ref, 8 * D, D, width)
    if student:
        sc["branch"][:, 0:width] = branch
        branch = branch * wide(col_ref, C_GH, D, width)
    hat, scale = standardise(sc["start"][:, cols] + branch)
    middle = hat * wide(col_ref, 2 * D, D, width) + wide(col_ref, 3 * D, D, width)
    if student:
        sc["hat1"][:, 0:width] = hat
        sc["scale"][1:2, cols] = scale
    middle_low = middle.astype(bf16)
    if student:
        sc["middle_low"][:, 0:width] = middle_low
    for r in range(0, FF, D):
        pre = nn(w["upT"][r : r + D, :], middle_low) + wide(col_ref, C_BUP + r, D, width)
        cdf = 0.5 * lax.erf(pre * (2.0**-0.5)) + 0.5
        act = pre * cdf
        if student:
            inner = wide(col_ref, C_GI + r, D, width)
            pdf = jnp.exp(pre * pre * -0.5) * (1.0 / math.sqrt(2.0 * math.pi))
            sc["act"][r : r + D, 0:width] = act
            sc["slope"][r : r + D, 0:width] = (cdf + pre * pdf) * inner
            act = act * inner
        sc["up"][r : r + D, 0:width] = act.astype(bf16)
    down = nn(w["downT"][...], sc["up"][:, 0:width]) + wide(col_ref, 9 * D, D, width)
    if student:
        sc["down"][:, 0:width] = down
        down = down * wide(col_ref, C_GH, D, width)
    hat, scale = standardise(middle + down)
    out = hat * wide(col_ref, 4 * D, D, width) + wide(col_ref, 5 * D, D, width)
    return out, hat, scale


def add_lanes(add_ref, row, values):
    add_ref[row : row + values.shape[0], :] += lanes_in(values)


def back_part(c, width, length, factor, out, hat, scale, target_ref, col_ref, w, sc, acc, add_ref, loss_ref):
    cols = pl.ds(c, width)
    here = slice(0, width)
    add = functools.partial(add_lanes, add_ref)
    out_low = out.astype(bf16)
    differ = nn(w["aT"][...], out_low) - target_ref[0, :, cols]
    token_valid = (lax.broadcasted_iota(jnp.int32, (1, width), 1) + c < length).astype(f32)
    loss_ref[0:1, cols] += jnp.sum(differ * differ, axis=0, keepdims=True) * (1.0 / D) * token_valid
    d_aligned = (differ * (token_valid * factor)).astype(bf16)
    acc["a"][...] += nt(out_low, d_aligned)
    d_out = nn(w["a"][...], d_aligned)
    add(4 * D, d_out * hat)
    add(5 * D, d_out)
    d_second = standardise_back(d_out * wide(col_ref, 4 * D, D, width), hat, scale)
    add(A_GH, d_second * sc["down"][:, here])
    d_down = (d_second * wide(col_ref, C_GH, D, width)).astype(bf16)
    add(9 * D, d_down.astype(f32))
    acc["down"][...] += nt(sc["up"][:, here], d_down)
    for r in range(0, FF, D):
        d_up = nn(w["down"][r : r + D, :], d_down)
        add(A_GI + r, d_up * sc["act"][r : r + D, here])
        d_pre = (d_up * sc["slope"][r : r + D, here]).astype(bf16)
        sc["d_pre"][r : r + D, here] = d_pre
        add(A_BUP + r, d_pre.astype(f32))
    d_middle = d_second + nn(w["up"][...], sc["d_pre"][:, here])
    acc["up"][...] += nt(sc["middle_low"][:, here], sc["d_pre"][:, here])
    hat = sc["hat1"][:, here]
    add(2 * D, d_middle * hat)
    add(3 * D, d_middle)
    d_first = standardise_back(
        d_middle * wide(col_ref, 2 * D, D, width), hat, sc["scale"][1:2, cols]
    )
    sc["d_first"][:, cols] = d_first
    add(A_GH, d_first * sc["branch"][:, here])
    d_branch = (d_first * wide(col_ref, C_GH, D, width)).astype(bf16)
    add(8 * D, d_branch.astype(f32))
    acc["o"][...] += nt(sc["gated"][:, cols], d_branch)
    d_gated = nn(w["o"][...], d_branch)
    context = sc["context"][:, cols]
    add(A_HEAD, d_gated * context)
    d_context = d_gated * wide(col_ref, C_HEAD, D, width)
    sc["d_context"][:, cols] = d_context.astype(bf16)
    dot_rows = d_context * context
    for h in range(HEADS):
        sc["delta"][h : h + 1, cols] = jnp.sum(
            dot_rows[h * HD : (h + 1) * HD, :], axis=0, keepdims=True
        )


def attend_back(span, sc):
    full = slice(0, span)
    for h in range(HEADS):
        rows = slice(h * HD, (h + 1) * HD)
        d_value = nt(sc["d_context"][rows, full], sc["shares"][h, 0:span, 0:span])
        sc["d_qkv"][2 * D + h * HD : 2 * D + (h + 1) * HD, full] = d_value.astype(bf16)
        d_key = None
        for c, width in chunks(span):
            cols = slice(c, c + width)
            d_shares = nn(sc["v_rows"][h, 0:span, :], sc["d_context"][rows, cols])
            d_scores = (
                sc["shares"][h, 0:span, cols].astype(f32) * (d_shares - sc["delta"][h : h + 1, cols])
            ).astype(bf16)
            sc["d_qkv"][rows, cols] = (
                nn(sc["qkv"][D + h * HD : D + (h + 1) * HD, full], d_scores) * (HD**-0.5)
            ).astype(bf16)
            part = nt(sc["qkv"][rows, cols], d_scores)
            d_key = part if d_key is None else d_key + part
        sc["d_qkv"][D + h * HD : D + (h + 1) * HD, full] = (d_key * (HD**-0.5)).astype(bf16)


def end_part(c, width, col_ref, w, sc, acc, add_ref, grad_ref, pos_add):
    cols = pl.ds(c, width)
    add = functools.partial(add_lanes, add_ref)
    acc["qkv"][...] += nt(sc["start_low"][:, cols], sc["d_qkv"][:, cols])
    add(6 * D, sc["d_qkv"][0:D, cols].astype(f32))
    add(7 * D, sc["d_qkv"][2 * D : 3 * D, cols].astype(f32))
    d_start = sc["d_first"][:, cols] + nn(w["qkv"][...], sc["d_qkv"][:, cols])
    hat = sc["hat0"][:, cols]
    gain = wide(col_ref, 0, D, width)
    add(A_GH, d_start * (hat * gain + wide(col_ref, D, D, width)))
    d_norm = d_start * wide(col_ref, C_GH, D, width)
    add(0, d_norm * hat)
    add(D, d_norm)
    d_embedded = standardise_back(d_norm * gain, hat, sc["scale"][0:1, cols])
    pos_add[:, cols] += d_embedded
    grad_ref[0, :, cols] = d_embedded.astype(bf16)


def by_part(length, body):
    def step(i, carry):
        body(pl.multiple_of(i * 256, 256), 256)
        return carry

    lax.fori_loop(0, jnp.where(length > 384, 2, 1), step, 0)
    pl.when((length > 256) & (length <= 384))(lambda: body(256, 128))


def mark_slots(slot, perm_ref):
    step = 512
    width = slot.shape[1]

    def mark(i, carry):
        rows = pl.ds(pl.multiple_of(i * step, step), step)
        seen = lax.broadcasted_iota(jnp.int32, (step, width), 0) == slot - i * step
        perm_ref[rows, :] = seen.astype(f32).astype(bf16)
        return carry

    lax.fori_loop(0, perm_ref.shape[0] // step, mark, 0)


def pack_rows(span, perm_ref, grad_ref, packed_ref):
    step = 2048

    def add(i, carry):
        rows = pl.ds(pl.multiple_of(i * step, step), step)
        packed_ref[rows, :] += nt(perm_ref[rows, 0:span], grad_ref[0, :, 0:span]).astype(bf16)
        return carry

    lax.fori_loop(0, packed_ref.shape[0] // step, add, 0)


SPANS = (256, 384, 512)


def by_span(length, body):
    for i, span in enumerate(SPANS):
        low = SPANS[i - 1] if i else 0
        test = length > low
        if i == 0:
            test = length <= span
        elif i < len(SPANS) - 1:
            test = (length > low) & (length <= span)
        pl.when(test)(functools.partial(body, span))


def set_up(pos_in, pos_ref, eyes_refs):
    for size, ref in eyes_refs.items():
        ref[...] = eye(size)
    for c in range(0, LEN, 256):
        pos_ref[:, c : c + 256] = nt(eyes_refs[256][...], pos_in[c : c + 256, :])


TEACHER_W = (
    ("qkv", (D, 3 * D)),
    ("qkvT", (3 * D, D)),
    ("o", (D, D)),
    ("oT", (D, D)),
    ("up", (D, FF)),
    ("upT", (FF, D)),
    ("down", (FF, D)),
    ("downT", (D, FF)),
)
STUDENT_W = TEACHER_W + (("a", (D, D)), ("aT", (D, D)))


def spread(col_ref, at, row):
    col_ref[pl.ds(at, LANES), :] = jnp.transpose(jnp.broadcast_to(row, (LANES, LANES)))


def load_weights(flat, w, col_ref, one, student):
    squares = [("qkv", 0), ("qkv", D), ("qkv", 2 * D), ("o", 0)] + ([("a", 0)] if student else [])
    for i, (name, at) in enumerate(squares):
        for j in range(2):
            lanes = slice(at + j * LANES, at + (j + 1) * LANES)
            w[name][:, lanes] = flat[pl.ds(512 * i + j, D, stride=2), :].astype(bf16)
    base = 512 * len(squares)
    for j in range(8):
        w["up"][:, j * LANES : (j + 1) * LANES] = flat[pl.ds(base + j, D, stride=8), :].astype(bf16)
    base = base + 2048
    for j in range(2):
        w["down"][:, j * LANES : (j + 1) * LANES] = flat[pl.ds(base + j, FF, stride=2), :].astype(
            bf16
        )
    base = base + 2048
    for i in range(20):
        spread(col_ref, i * LANES, flat[base + i : base + i + 1, :])
    for j in range(8):
        spread(col_ref, C_BUP + j * LANES, flat[base + 20 + j : base + 21 + j, :])
    unit = one[...]
    for name in ("qkv", "o", "up") + (("a",) if student else ()):
        for b in range(0, w[name].shape[1], D):
            w[name + "T"][b : b + D, :] = nt(unit, w[name][:, b : b + D]).astype(bf16)
    for b in range(0, FF, D):
        w["downT"][:, b : b + D] = nt(unit, w["down"][b : b + D, :]).astype(bf16)


def total_of(x):
    return jnp.sum(jnp.sum(x, axis=0, keepdims=True), axis=1, keepdims=True)


def head_groups():
    return (
        lax.broadcasted_iota(jnp.int32, (D, LANES), 0) // HD
        == lax.broadcasted_iota(jnp.int32, (D, LANES), 1)
    ).astype(f32)


def load_gates(logits, noise, lagrange_ref, lag_weight, col_ref, slope_ref, lag_ref):
    index = lax.broadcasted_iota(
        jnp.int32, logits.shape, 0
    ) * LANES + lax.broadcasted_iota(jnp.int32, logits.shape, 1)
    hidden, heads = index < D, (index >= D) & (index < D + HEADS)
    inner = (index >= D + HEADS) & (index < D + HEADS + FF)
    logistic = jax.nn.sigmoid((jnp.log(noise) - jnp.log(1.0 - noise) + logits) / relaxation_heat)
    spanned = widened_right_limit - widened_left_limit
    stretched = logistic * spanned + widened_left_limit
    gates = jnp.clip(stretched, 0.0, 1.0)
    inside = jnp.where((stretched > 0.0) & (stretched < 1.0), 1.0, 0.0)
    inside = jnp.where((stretched == 0.0) | (stretched == 1.0), 0.5, inside)
    slope_ref[...] = inside * logistic * (1.0 - logistic) * (spanned / relaxation_heat)
    keep = jax.nn.sigmoid(
        logits - relaxation_heat * math.log(-widened_left_limit / widened_right_limit)
    )
    kept = total_of(jnp.where(hidden, keep, 0.0)) * (1.0 / D)
    rest = total_of(jnp.where(heads, keep * (4.0 * HD), 0.0) + jnp.where(inner, keep * 2.0, 0.0))
    scale = 1.0 / (4.0 * D + 2.0 * FF)
    excess = kept * rest * scale - sparse_target
    rate = (lagrange_ref[0] + 2.0 * lagrange_ref[1] * excess) * (scale * lag_weight)
    share = jnp.where(hidden, rest * (1.0 / D), 0.0)
    share = share + kept * (jnp.where(heads, 4.0 * HD, 0.0) + jnp.where(inner, 2.0, 0.0))
    lag_ref[...] = rate * share * (keep * (1.0 - keep))
    for j in range(2):
        spread(col_ref, C_GH + j * LANES, gates[j : j + 1, :])
    wide_heads = lax.dot_general(
        jnp.broadcast_to(gates[2:3, :], (8, LANES)),
        head_groups(),
        (((1,), (1,)), ((), ())),
        preferred_element_type=f32,
        precision=lax.Precision.HIGHEST,
    )
    for j in range(2):
        spread(col_ref, C_HEAD + j * LANES, wide_heads[0:1, j * LANES : (j + 1) * LANES])
    run = jnp.concatenate([gates[j : j + 1, :] for j in range(2, 11)], axis=1)
    run = pltpu.roll(jnp.broadcast_to(run, (8, 9 * LANES)), 9 * LANES - HEADS, 1)
    for j in range(8):
        spread(col_ref, C_GI + j * LANES, run[0:1, j * LANES : (j + 1) * LANES])
    return lagrange_ref[0] * excess + lagrange_ref[1] * excess * excess


TEACHER_S = (
    ("start", (D, LEN), f32),
    ("qkv", (3 * D, LEN), bf16),
    ("k_rows", (HEADS, LEN, HD), bf16),
    ("gated", (D, LEN), bf16),
    ("up", (FF, 256), bf16),
)
STUDENT_S = TEACHER_S + (
    ("start_low", (D, LEN), bf16),
    ("hat0", (D, LEN), f32),
    ("hat1", (D, 256), f32),
    ("scale", (8, LEN), f32),
    ("v_rows", (HEADS, LEN, HD), bf16),
    ("shares", (HEADS, LEN, LEN), bf16),
    ("context", (D, LEN), f32),
    ("branch", (D, 256), f32),
    ("middle_low", (D, 256), bf16),
    ("act", (FF, 256), f32),
    ("slope", (FF, 256), f32),
    ("down", (D, 256), f32),
    ("d_pre", (FF, 256), bf16),
    ("d_first", (D, LEN), f32),
    ("d_context", (D, LEN), bf16),
    ("delta", (8, LEN), f32),
    ("d_qkv", (3 * D, LEN), bf16),
)
ACCS = (
    ("qkv", (D, 3 * D)),
    ("o", (D, D)),
    ("a", (D, D)),
    ("up", (D, FF)),
    ("down", (FF, D)),
)


class Eyes:
    def __init__(self, one, two):
        self.refs = {128: one, 256: two}

    def __getitem__(self, size):
        return self.refs[size][...]


def student_kernel(n, flat_len, sparse, len_ref, fac_ref, lagrange_ref, noise_ref, flat_in, pos_in, target_ref, *rest):
    plane, planes, flat_seg = plan(n, flat_len)[:3]
    cap = room(n)
    if sparse:
        slot_ref, rows_ref = rest[:2]
        rest = rest[2:]
    else:
        rows_ref = rest[0]
        rest = rest[1:]
    flat_ref, grad_ref, loss_ref = rest[:3]
    rest = rest[3:]
    if sparse:
        packed_ref, rows_all, perm_ref, slot_now = rest[:4]
        rest = rest[4:]
    w = {entry[0]: rest[i] for i, entry in enumerate(STUDENT_W)}
    rest = rest[len(STUDENT_W) :]
    sc = {entry[0]: rest[i] for i, entry in enumerate(STUDENT_S)}
    rest = rest[len(STUDENT_S) :]
    acc = {entry[0]: rest[i] for i, entry in enumerate(ACCS)}
    add_ref, pos_add, slope_ref, lag_ref, col_ref, pos_ref, eye_one, eye_two = rest[len(ACCS) :]
    s = pl.program_id(0)
    eyes = Eyes(eye_one, eye_two)

    @pl.when(s == 0)
    def _():
        set_up(pos_in, pos_ref, eyes.refs)
        for o in range(n):
            c = o // 2
            flat_ref[o * flat_seg : (o + 1) * flat_seg, :] = flat_in[
                o % 2, c % plane, c // plane, :, :
            ].astype(f32)[:flat_seg]
        load_weights(flat_ref, w, col_ref, eye_two, True)
        lag_value = load_gates(
            flat_ref[R_LOGIT : R_LOGIT + 16, :],
            noise_ref[...],
            lagrange_ref,
            fac_ref[1],
            col_ref,
            slope_ref,
            lag_ref,
        )
        for ref in list(acc.values()) + [add_ref, pos_add]:
            ref[...] = jnp.zeros(ref.shape, f32)
        row = lax.broadcasted_iota(jnp.int32, (8, LEN), 0)
        loss_ref[...] = jnp.where(row == 1, lag_value, 0.0)
        if sparse:
            packed_ref[...] = jnp.zeros(packed_ref.shape, bf16)
            for o in range(n):
                rows_all[:, o * cap : (o + 1) * cap] = rows_ref[o]

    length = len_ref[s]

    def embed(c, width):
        if sparse:
            mark_slots(slot_now[0:1, pl.ds(c, width)], perm_ref.at[:, pl.ds(c, width)])
            return nn(rows_all[...], perm_ref[:, pl.ds(c, width)])
        at = pl.multiple_of(s * LEN + c, 128)
        return nt(eyes[D], rows_ref[pl.ds(at, width), :])

    def between(c, width):
        out, hat, scale = middle_part(c, width, True, col_ref, w, sc)
        back_part(
            c, width, length, fac_ref[0], out, hat, scale, target_ref, col_ref, w, sc, acc, add_ref, loss_ref
        )

    grad_ref[0, :, 256:LEN] = jnp.zeros((D, LEN - 256), bf16)
    if sparse:
        slot_now[0:1, :] = slot_ref[pl.ds(s, 1), :]
    by_part(
        length, lambda c, width: start_part(c, width, True, embed, pos_ref, col_ref, w, sc, eyes)
    )
    by_span(length, lambda span: attend(span, length, True, col_ref, sc))
    by_part(length, between)
    by_span(length, lambda span: attend_back(span, sc))
    by_part(
        length,
        lambda c, width: end_part(c, width, col_ref, w, sc, acc, add_ref, grad_ref, pos_add),
    )
    if sparse:
        by_span(length, lambda span: pack_rows(span, perm_ref, grad_ref, packed_ref))

    @pl.when(s == pl.num_programs(0) - 1)
    def _():
        for i in range(3):
            for j in range(2):
                at = i * D + j * LANES
                flat_ref[pl.ds(512 * i + j, D, stride=2), :] = acc["qkv"][:, at : at + LANES]
        for j in range(2):
            lanes = slice(j * LANES, (j + 1) * LANES)
            flat_ref[pl.ds(512 * 3 + j, D, stride=2), :] = acc["o"][:, lanes]
            flat_ref[pl.ds(512 * 4 + j, D, stride=2), :] = acc["a"][:, lanes]
            flat_ref[pl.ds(R_DOWN + j, FF, stride=2), :] = acc["down"][:, lanes]
        for j in range(8):
            flat_ref[pl.ds(R_UP + j, D, stride=8), :] = acc["up"][:, j * LANES : (j + 1) * LANES]
        ones = jnp.ones((8, LANES), f32)

        def summed(row, rows):
            return lax.dot_general(
                ones,
                add_ref[row : row + rows, :],
                (((1,), (1,)), ((), ())),
                preferred_element_type=f32,
                precision=lax.Precision.HIGHEST,
            )

        for i in range(10):
            sums = summed(i * D, D)
            for j in range(2):
                flat_ref[R_VEC + 2 * i + j : R_VEC + 2 * i + j + 1, :] = sums[
                    0:1, j * LANES : (j + 1) * LANES
                ]
        sums = summed(A_BUP, FF)
        for j in range(8):
            flat_ref[R_BUP + j : R_BUP + j + 1, :] = sums[0:1, j * LANES : (j + 1) * LANES]
        hidden = summed(A_GH, D)
        heads = jnp.dot(
            summed(A_HEAD, D),
            head_groups(),
            preferred_element_type=f32,
            precision=lax.Precision.HIGHEST,
        )
        inner = summed(A_GI, FF)
        moved = pltpu.roll(jnp.concatenate([inner, jnp.zeros((8, LANES), f32)], axis=1), HEADS, 1)
        lane = lax.broadcasted_iota(jnp.int32, (8, LANES), 1)
        first = jnp.where(lane < HEADS, heads, moved[:, :LANES])
        tail = [hidden[:, :LANES], hidden[:, LANES:], first] + [
            moved[:, j * LANES : (j + 1) * LANES] for j in range(1, 9)
        ]
        for j, piece in enumerate(tail):
            flat_ref[R_LOGIT + j : R_LOGIT + j + 1, :] = (
                piece[0:1] * slope_ref[j : j + 1, :] + lag_ref[j : j + 1, :]
            )
        flat_ref[R_USED:flat_len, :] = jnp.zeros((flat_len - R_USED, LANES), f32)
        for j in range(2):
            flat_ref[pl.ds(flat_len + j, LEN, stride=2), :] = jnp.transpose(
                pos_add[j * LANES : (j + 1) * LANES, :]
            )


def whole_spec():
    return pl.BlockSpec(memory_space=pltpu.VMEM)


def smem_spec():
    return pl.BlockSpec(memory_space=pltpu.SMEM)


def seq_spec():
    return pl.BlockSpec((1, D, LEN), lambda s: (s, 0, 0))


def common_scratch():
    return [
        pltpu.VMEM((C_ROWS, LANES), f32),
        pltpu.VMEM((D, LEN), f32),
        pltpu.VMEM((128, 128), bf16),
        pltpu.VMEM((256, 256), bf16),
    ]


def run_student(n, flat_len, sparse, lengths, factors, lagrange, noise, flat_all, places, target, given):
    seqs = lengths.shape[0]
    slot_rows = n * room(n)
    shapes = [
        jax.ShapeDtypeStruct((flat_len + 2 * LEN, LANES), f32),
        jax.ShapeDtypeStruct((seqs, D, LEN), bf16),
        jax.ShapeDtypeStruct((8, LEN), f32),
    ]
    out_specs = [whole_spec(), seq_spec(), whole_spec()]
    scratch = []
    if sparse:
        shapes.append(jax.ShapeDtypeStruct((slot_rows, D), bf16))
        out_specs.append(whole_spec())
        scratch = [
            pltpu.VMEM((D, slot_rows), bf16),
            pltpu.VMEM((slot_rows, LEN), bf16),
            pltpu.VMEM((8, LEN), jnp.int32),
        ]
    return pl.pallas_call(
        functools.partial(student_kernel, n, flat_len, sparse),
        grid=(seqs,),
        out_shape=tuple(shapes),
        in_specs=[smem_spec()] * 3
        + [whole_spec()] * 3
        + [seq_spec()]
        + [whole_spec()] * len(given),
        out_specs=tuple(out_specs),
        scratch_shapes=scratch
        + [pltpu.VMEM(shape, bf16) for _, shape in STUDENT_W]
        + [pltpu.VMEM(shape, kind) for _, shape, kind in STUDENT_S]
        + [pltpu.VMEM(shape, f32) for _, shape in ACCS]
        + [
            pltpu.VMEM((A_ROWS, LANES), f32),
            pltpu.VMEM((D, LEN), f32),
            pltpu.VMEM((16, LANES), f32),
            pltpu.VMEM((16, LANES), f32),
        ]
        + common_scratch(),
        compiler_params=pltpu.CompilerParams(vmem_limit_bytes=44 * 2**20),
        name="student" if sparse else "student_dense",
    )(lengths, factors, lagrange, noise, flat_all, places, target, *given)


MESH = pl.DeviceIdType.MESH
ROW_CUTS = (8, 8)


def room(n):
    return LANES if 8 * LEN // n >= LANES else 0


def filled(n):
    return room(n) - 16


def greet_all(me, n):
    barrier = pltpu.get_barrier_semaphore()

    def signal(k, carry):
        pl.semaphore_signal(barrier, inc=1, device_id=(me ^ k,), device_id_type=MESH)
        return carry

    lax.fori_loop(1, n, signal, 0)
    pl.semaphore_wait(barrier, n - 1)


def copy_to(source, target, send, receive, device):
    return pltpu.make_async_remote_copy(
        src_ref=source,
        dst_ref=target,
        send_sem=send,
        recv_sem=receive,
        device_id=(device,),
        device_id_type=MESH,
    )


def list_rows(n, owner_ref, local_ref, stat, slot_ref, tile_ref):
    cap = room(n)
    upper = (
        lax.broadcasted_iota(jnp.int32, (256, 256), 0)
        <= lax.broadcasted_iota(jnp.int32, (256, 256), 1)
    ).astype(bf16)

    def sequence(s, state):
        base, listed = state
        for c in range(0, LEN, 256):
            owner = owner_ref[pl.ds(s, 1), c : c + 256]
            mine = (lax.broadcasted_iota(jnp.int32, (n, 256), 0) == owner).astype(f32)
            before = nn(mine.astype(bf16), upper)
            rank = jnp.sum(mine * (before - 1.0 + base), axis=0, keepdims=True).astype(jnp.int32)
            fits = (owner >= 0) & (rank < filled(n))
            slot_ref[pl.ds(s, 1), c : c + 256] = jnp.where(fits, owner * cap + rank, n * cap)
            place = (
                lax.broadcasted_iota(jnp.int32, (LANES, 256), 0) == jnp.where(fits, rank, -1)
            ).astype(f32)
            listed = listed + lax.dot_general(
                mine * local_ref[pl.ds(s, 1), c : c + 256],
                place,
                (((1,), (1,)), ((), ())),
                preferred_element_type=f32,
                precision=lax.Precision.HIGHEST,
            )
            base = base + before[:, 255:256]
        return base, listed

    base, listed = lax.fori_loop(
        0,
        owner_ref.shape[0],
        sequence,
        (jnp.zeros((n, 1), f32), jnp.zeros((n, LANES), f32)),
    )
    over = jnp.max(base, axis=0, keepdims=True) > filled(n)
    lane = lax.broadcasted_iota(jnp.int32, (n, LANES), 1)
    tile_ref[...] = jnp.zeros(tile_ref.shape, jnp.int32)
    tile_ref[pl.ds(0, n, stride=8), :] = (listed + 0.5).astype(jnp.int32) - 1
    tile_ref[pl.ds(1, n, stride=8), :] = jnp.where(
        lane == 0, stat, jnp.where(lane == 1, over.astype(jnp.int32), 0)
    )


def place_parts(vrows):
    parts = []
    for o in range(VOCAB // vrows, (VOCAB + LEN - 1) // vrows + 1):
        low, top = max(VOCAB, o * vrows), min(VOCAB + LEN, (o + 1) * vrows)
        parts.append((o, low - o * vrows, low - VOCAB, top - low))
    return parts


def round_up(value, step):
    return -(-value // step) * step


def pair_lists(list_ref, a, cap):
    return jnp.concatenate(
        [list_ref[pl.ds(pl.multiple_of(a * 16 + 8 * j, 8), 8), :][0:1, :cap] for j in range(2)],
        axis=1,
    )


def fetch_kernel(
    n, flat_len, owner_ref, local_ref, stat_ref, len_ref, block_ref, row_ref, words_in, pos_in, flat_in, table_ref, own_flat, *rest
):
    plane, planes, flat_seg, flat_pad = plan(n, flat_len)[:4]
    cap = room(n)
    vrows = table_ref.shape[0]
    parts = place_parts(vrows)
    out_ref, got_out, flat_out, place_out = rest[:4]
    rest = rest[4:]
    if cap:
        slot_ref, rows_out = rest[:2]
        rest = rest[2:]
    w = {entry[0]: rest[i] for i, entry in enumerate(TEACHER_W)}
    rest = rest[len(TEACHER_W) :]
    sc = {entry[0]: rest[i] for i, entry in enumerate(TEACHER_S)}
    rest = rest[len(TEACHER_S) :]
    tile_ref, got_ref, flat_all, place_all, pad_ref, flat_f32 = rest[:6]
    list_sem, a_sem, b_sem, c_sem, pa_sem, pb_sem, pc_sem = rest[6:13]
    col_ref, pos_ref, eye_one, eye_two = rest[13:17]
    words, picked, word_sem, out_sem = rest[17:21]
    if cap:
        table_turned, row_send, rows_in, row_sem = rest[21:]
    eyes = Eyes(eye_one, eye_two)
    s = pl.program_id(0)
    seqs = owner_ref.shape[0]
    me = lax.axis_index("dp")
    core = lax.rem(me, 2)
    chip = me // 2
    mid = lax.rem(chip, plane)
    high = chip // plane

    def device(h, m, c):
        return (h * plane + m) * 2 + c

    def tile(ref, i):
        return ref.at[pl.ds(pl.multiple_of(i * 8, 8), 8), :]

    def list_copy(k):
        return copy_to(
            tile(tile_ref, me ^ k), tile(got_ref, me), list_sem.at[0, k], list_sem.at[1, k], me ^ k
        )

    def row_copy(k):
        return copy_to(
            row_send.at[me ^ k], rows_in.at[me], row_sem.at[0, k], row_sem.at[1, k], me ^ k
        )

    def flat_copies(stage):
        copies = []
        if stage == 0:
            spot = flat_all.at[core, mid, high]
            for k in range(1, planes):
                to = device(lax.rem(high + k, planes), mid, core)
                copies.append(copy_to(spot, spot, a_sem.at[0, k], a_sem.at[1, k], to))
        elif stage == 1:
            spot = flat_all.at[core, mid]
            for k in range(1, plane):
                to = device(high, lax.rem(mid + k, plane), core)
                copies.append(copy_to(spot, spot, b_sem.at[0, k], b_sem.at[1, k], to))
        else:
            spot = flat_all.at[core]
            copies.append(copy_to(spot, spot, c_sem.at[0], c_sem.at[1], me ^ 1))
        return copies

    def place_copies(stage, i):
        o, _, _, count = parts[i]
        chip_o = o // 2
        high_o, mid_o, core_o = chip_o // plane, chip_o % plane, o % 2
        spot = place_all.at[i, pl.ds(0, round_up(count, 16)), :]
        same_core, same_mid, same_high = core == core_o, mid == mid_o, high == high_o
        copies = []
        if stage == 0:
            for k in range(1, planes):
                to = device((high_o + k) % planes, mid_o, core_o)
                copies.append(copy_to(spot, spot, pa_sem.at[0, i, k], pa_sem.at[1, i, 0], to))
            sends = same_core & same_mid & same_high
            receives = same_core & same_mid & (high != high_o)
        elif stage == 1:
            for k in range(1, plane):
                to = device(high, (mid_o + k) % plane, core_o)
                copies.append(copy_to(spot, spot, pb_sem.at[0, i, k], pb_sem.at[1, i, 0], to))
            sends = same_core & same_mid
            receives = same_core & (mid != mid_o)
        else:
            copies.append(copy_to(spot, spot, pc_sem.at[0, i], pc_sem.at[1, i], me ^ 1))
            sends = same_core
            receives = core != core_o
        return copies, sends, receives

    def start_stage(stage):
        for copy in flat_copies(stage):
            copy.start()
        for i in range(len(parts)):
            copies, sends, _ = place_copies(stage, i)

            @pl.when(sends)
            def _():
                for copy in copies:
                    copy.start()

    def finish_stage(stage):
        for copy in flat_copies(stage):
            copy.wait()
        for i in range(len(parts)):
            copies, sends, receives = place_copies(stage, i)

            @pl.when(sends)
            def _():
                for copy in copies:
                    copy.wait_send()

            @pl.when(receives)
            def _():
                copies[0].wait_recv()

    known = words.shape[0] * 16
    word_copy = pltpu.make_async_copy(
        words_in.at[pl.ds(0, known), :], words.reshape(known, D), word_sem
    )

    @pl.when(s == 0)
    def _():
        word_copy.start()
        picked[...] = jnp.zeros(picked.shape, f32)
        greet_all(me, n)
        pad_ref[...] = jnp.zeros(pad_ref.shape, f32)
        pad_ref[0:flat_seg, :] = own_flat[...]
        flat_all[core, mid, high] = pad_ref[...].astype(bf16)
        for i, (o, at, _, count) in enumerate(parts):

            @pl.when(me == o)
            def _():
                full = round_up(count, 16)
                part = table_ref[at : at + count, :]
                if full > count:
                    part = jnp.concatenate([part, jnp.zeros((full - count, D), f32)], axis=0)
                place_all[i, 0:full, :] = part.astype(bf16)

        start_stage(0)
        if cap:
            list_rows(n, owner_ref, local_ref, stat_ref[0], slot_ref, tile_ref)
        else:
            tile_ref[...] = jnp.zeros(tile_ref.shape, jnp.int32) + stat_ref[0]

        def start_list(k, carry):
            list_copy(k).start()
            return carry

        lax.fori_loop(1, n, start_list, 0)
        own = pl.ds(pl.multiple_of(me * 8, 8), 8)
        got_ref[own, :] = tile_ref[own, :]
        set_up(pos_in, pos_ref, eyes.refs)
        if cap:
            table_turned[...] = nt(eye_two[...], table_ref[...].astype(bf16)).astype(bf16)

        def finish_list(k, carry):
            list_copy(k).wait()
            return carry

        lax.fori_loop(1, n, finish_list, 0)

        def serve(step, carry):
            i = n // 2 - 1 - step
            a = chip ^ i
            pick = (
                lax.broadcasted_iota(jnp.int32, (vrows, 2 * cap), 0) == pair_lists(got_ref, a, cap)
            ).astype(bf16)
            both = nn(table_turned[...], pick).astype(bf16)
            for j in range(2):
                row_send[2 * a + j] = both[:, j * cap : (j + 1) * cap]
                k = 2 * i + (core ^ j)
                pl.when(k > 0)(row_copy(k).start)
            return carry

        if cap:
            lax.fori_loop(0, n // 2, serve, 0)
            rows_in[me] = row_send[me]
        step = 512
        whole = flat_in.shape[0] // step

        def unpack(i, carry):
            rows = pl.ds(pl.multiple_of(i * step, step), step)
            flat_f32[rows, :] = flat_in[rows, :].astype(f32)
            return carry

        lax.fori_loop(0, whole, unpack, 0)
        flat_f32[whole * step :, :] = flat_in[whole * step :, :].astype(f32)
        load_weights(flat_f32, w, col_ref, eye_two, False)
        word_copy.wait()

    @pl.when(s == 1)
    def _():
        finish_stage(0)
        start_stage(1)

    length = len_ref[s]
    from_me = jnp.where(s < seqs // 2, me, n - 1 - me)
    longest = LEN // 3 + (LEN - LEN // 3) * from_me // (n - 1)

    def pick_rows(g, carry):
        for e in range(4):
            rows = []
            for u in range(8):
                at = g * 32 + e * 8 + u
                block = words[block_ref[s, at]].astype(f32)
                mine = lax.broadcasted_iota(jnp.int32, (16, D), 0) == row_ref[s, at]
                rows.append(jnp.sum(jnp.where(mine, block, 0.0), axis=0, keepdims=True))
            picked[pl.ds(pl.multiple_of(g * 32 + e * 8, 8), 8), :] = jnp.concatenate(rows, axis=0)
        return carry

    lax.fori_loop(0, (longest + 31) // 32, pick_rows, 0)

    def embed(c, width):
        return nt(eyes[D], picked[pl.ds(c, width), :].astype(bf16))

    def finish(c, width):
        out_ref[0, :, pl.ds(c, width)] = middle_part(c, width, False, col_ref, w, sc)[0]

    def body(span):
        for c, width in chunks(span):
            start_part(c, width, False, embed, pos_ref, col_ref, w, sc, eyes)
        attend(span, length, False, col_ref, sc)
        for c, width in chunks(span):
            finish(c, width)

    by_span(longest, body)

    @pl.when(s == seqs - 2)
    def _():
        finish_stage(1)
        start_stage(2)

    @pl.when(s == seqs - 1)
    def _():
        finish_stage(2)

        def finish_row(k, carry):
            row_copy(k).wait()
            return carry

        if cap:
            lax.fori_loop(1, n, finish_row, 0)
        pairs = [(got_ref, got_out), (flat_all, flat_out), (place_all, place_out)]
        if cap:
            pairs.append((rows_in, rows_out))
        leaving = [
            pltpu.make_async_copy(source, target, out_sem.at[i])
            for i, (source, target) in enumerate(pairs)
        ]
        for copy in leaving:
            copy.start()
        for copy in leaving:
            copy.wait()


def run_fetch(n, flat_len, owner, local, stat, lengths, blocks, rows, words, places, teacher, table, own_flat):
    plane, planes, flat_seg, flat_pad = plan(n, flat_len)[:4]
    seqs, cap, vrows = owner.shape[0], room(n), table.shape[0]
    parts = place_parts(vrows)
    most = max(round_up(part[3], 16) for part in parts)
    dma = pltpu.SemaphoreType.DMA
    got = ((8 * n, LANES), jnp.int32)
    fetched = ((n, D, cap), bf16)
    flat_all = ((2, plane, planes, flat_pad, LANES), bf16)
    place_all = ((len(parts), most, D), bf16)
    shapes = [((seqs, D, LEN), f32), got, flat_all, place_all]
    far = pl.BlockSpec(memory_space=pl.ANY)
    out_specs = [seq_spec(), far, far, far]
    extra = []
    if cap:
        shapes += [(owner.shape, jnp.int32), fetched]
        out_specs += [whole_spec(), far]
        extra = [
            pltpu.VMEM((D, vrows), bf16),
            pltpu.VMEM(*fetched),
            pltpu.VMEM(*fetched),
            dma((2, n)),
        ]
    return pl.pallas_call(
        functools.partial(fetch_kernel, n, flat_len),
        grid=(seqs,),
        out_shape=tuple(jax.ShapeDtypeStruct(shape, kind) for shape, kind in shapes),
        in_specs=[whole_spec()] * 2
        + [smem_spec()] * 4
        + [pl.BlockSpec(memory_space=pl.ANY)]
        + [whole_spec()] * 4,
        out_specs=tuple(out_specs),
        scratch_shapes=[pltpu.VMEM(shape, bf16) for _, shape in TEACHER_W]
        + [pltpu.VMEM(shape, kind) for _, shape, kind in TEACHER_S]
        + [
            pltpu.VMEM(*got),
            pltpu.VMEM(*got),
            pltpu.VMEM(*flat_all),
            pltpu.VMEM(*place_all),
            pltpu.VMEM((flat_pad, LANES), f32),
            pltpu.VMEM(teacher.shape, f32),
            dma((2, n)),
            dma((2, planes)),
            dma((2, plane)),
            dma((2,)),
            dma((2, len(parts), planes)),
            dma((2, len(parts), plane)),
            dma((2, len(parts))),
        ]
        + common_scratch()
        + [pltpu.VMEM((words.shape[0] // 16, 16, D), bf16), pltpu.VMEM((LEN, D), f32), dma, dma((4,))]
        + extra,
        compiler_params=pltpu.CompilerParams(
            collective_id=1, has_side_effects=True, vmem_limit_bytes=50 * 2**20
        ),
        name="teacher",
    )(owner, local, stat, lengths, blocks, rows, words, places, teacher, table, own_flat)


def plan(n, flat_len):
    chips = n // 2
    plane = 2 ** ((chips.bit_length() - 1) // 2)
    flat_seg = flat_len // n
    flat_pad = round_up(flat_seg, 16)
    place_seg = 2 * LEN // n
    return plane, chips // plane, flat_seg, flat_pad, place_seg, flat_pad + round_up(place_seg, 16)


def place_tile(n):
    return max(8, 2 * LEN // n)


def exchange_kernel(n, flat_len, sparse, *refs):
    plane, planes, flat_seg, flat_pad, place_seg, seg = plan(n, flat_len)
    chips = n // 2
    cap = room(n)
    tile = place_tile(n)
    flat_ref, loss_ref = refs[:2]
    refs = refs[2:]
    if sparse:
        packed_ref, list_ref = refs[:2]
        refs = refs[2:]
    else:
        given_ref = refs[0]
        refs = refs[1:]
    table_ref, sums_ref, stat_out = refs[:3]
    (stage, one_in, two_out, two_in, total, three_out, three_in, place_in, stat_in) = refs[3:12]
    refs = refs[12:]
    if sparse:
        rows_in = refs[0]
        refs = refs[1:]
    one_sem, two_sem, three_sem, place_sem, stat_sem, row_sem = refs
    me = lax.axis_index("dp")
    core = lax.rem(me, 2)
    chip = me // 2
    mid = lax.rem(chip, plane)
    high = chip // plane
    vrows = table_ref.shape[0]

    greet_all(me, n)
    pad = jnp.zeros((16, LANES), f32)
    for o in range(n):
        spot = stage.at[o % 2, o // 2]
        if flat_pad > flat_seg:
            spot[flat_pad - 16 : flat_pad, :] = pad
        if seg > flat_pad + place_seg:
            spot[seg - 16 : seg, :] = pad
        spot[0:flat_seg, :] = flat_ref[o * flat_seg : (o + 1) * flat_seg, :]
        at = flat_len + o * place_seg
        spot[flat_pad : flat_pad + place_seg, :] = flat_ref[at : at + place_seg, :]
    first = copy_to(stage.at[1 - core], one_in, one_sem.at[0], one_sem.at[1], me ^ 1)
    first.start()

    if sparse:

        def bucket(ref, i):
            return ref.at[pl.ds(pl.multiple_of(i * cap, cap), filled(n)), :]

        def row_copy(k):
            return copy_to(
                bucket(packed_ref, me ^ k), bucket(rows_in, me), row_sem.at[0, k], row_sem.at[1, k], me ^ k
            )

        def start_row(i, carry):
            row_copy(n - i).start()
            return carry

        def start_rows(low, top):
            lax.fori_loop(low, top, start_row, 0)

        cuts = [1 + (n - 1) * part // 31 for part in ROW_CUTS] + [n]
        start_rows(1, cuts[0])
        own = pl.ds(pl.multiple_of(me * cap, cap), cap)
        rows_in[own, :] = packed_ref[own, :]

        def unused(i, carry):
            at = pl.multiple_of(i * cap + filled(n), 16)
            rows_in[pl.ds(at, cap - filled(n)), :] = jnp.zeros((cap - filled(n), D), bf16)
            return carry

        lax.fori_loop(0, n, unused, 0)

    first.wait()
    for m in range(plane):
        for h in range(planes):
            c = h * plane + m
            two_out[m, h] = (stage[core, c] + one_in[c]).astype(bf16)
    second = []
    for k in range(1, plane):
        m = lax.rem(mid + k, plane)
        second.append(
            copy_to(
                two_out.at[m],
                two_in.at[k - 1],
                two_sem.at[0, k],
                two_sem.at[1, k],
                (high * plane + m) * 2 + core,
            )
        )
        second[-1].start()
    if sparse:
        start_rows(cuts[0], cuts[1])
    for copy in second:
        copy.wait()
    for h in range(planes):
        c = h * plane + mid
        value = stage[core, c] + one_in[c]
        for k in range(1, plane):
            value = value + two_in[k - 1, h].astype(f32)
        total[h] = value
        three_out[h] = value.astype(bf16)
    third = []
    for k in range(1, planes):
        h = lax.rem(high + k, planes)
        third.append(
            copy_to(
                three_out.at[h],
                three_in.at[k - 1],
                three_sem.at[0, k],
                three_sem.at[1, k],
                (h * plane + mid) * 2 + core,
            )
        )
        third[-1].start()
    if sparse:
        start_rows(cuts[1], cuts[2])
    for copy in third:
        copy.wait()
    value = total[high]
    for k in range(1, planes):
        value = value + three_in[k - 1].astype(f32)
    total[0] = value
    sums_ref[...] = value[:flat_pad]

    owners = range(VOCAB // vrows, (VOCAB + LEN - 1) // vrows + 1)
    place_out = total.at[0, pl.ds(flat_pad, tile), :]
    place_spot = pl.ds(pl.multiple_of(me * tile, 8), tile)
    for i, o in enumerate(owners):
        place_copy = copy_to(
            place_out, place_in.at[place_spot, :], place_sem.at[0, i], place_sem.at[1, me], o
        )
        pl.when(me != o)(place_copy.start)

    squares = jnp.sum(jnp.sum(value * value, axis=0, keepdims=True), axis=1, keepdims=True)
    if sparse:
        def add_pair(i, carry):
            pl.when(i > 0)(lambda: row_copy(2 * i).wait_recv())
            row_copy(2 * i + 1).wait_recv()
            a = chip ^ i
            lists = pair_lists(list_ref, a, cap)
            pick = (lax.broadcasted_iota(jnp.int32, (vrows, 2 * cap), 0) == lists).astype(bf16)
            both = rows_in[pl.ds(pl.multiple_of(a * 2 * cap, 2 * cap), 2 * cap), :]
            table_ref[...] += nn(pick, both)
            return carry

        table_ref[...] = jnp.zeros(table_ref.shape, f32)
        lax.fori_loop(0, chips, add_pair, 0)
    else:
        table_ref[...] = given_ref[...]
    grads = table_ref[...]
    squares = squares + jnp.sum(
        jnp.sum(grads * grads, axis=0, keepdims=True), axis=1, keepdims=True
    )
    loss = jnp.sum(loss_ref[0:1, :], axis=1, keepdims=True)
    lane = lax.broadcasted_iota(jnp.int32, (8, LANES), 1)
    lag = jnp.where(me == 0, loss_ref[1:2, 0:1], 0.0)
    stat_out[...] = jnp.where(
        lane == 0, squares, jnp.where(lane == 1, loss, jnp.where(lane == 2, lag, 0.0))
    )

    def stat_copy(k):
        return copy_to(
            stat_out, stat_in.at[me], stat_sem.at[0, k], stat_sem.at[1, k], me ^ k
        )

    def start_stat(k, carry):
        stat_copy(k).start()
        return carry

    def finish_stat(k, carry):
        stat_copy(k).wait()
        return carry

    lax.fori_loop(1, n, start_stat, 0)
    stat_in[me] = stat_out[...]

    for i, o in enumerate(owners):

        @pl.when(me == o)
        def _():
            place_in[place_spot, :] = place_out[...]

            def wait_place(j, carry):
                copy_to(
                    place_out,
                    place_in.at[pl.ds(pl.multiple_of(j * tile, 8), tile), :],
                    place_sem.at[0, i],
                    place_sem.at[1, j],
                    me ^ 1,
                ).wait_recv()
                return carry

            lax.fori_loop(0, o, wait_place, 0)
            lax.fori_loop(o + 1, n, wait_place, 0)
            low = max(0, o * vrows - VOCAB)
            top = min(LEN, (o + 1) * vrows - VOCAB)
            at = VOCAB + low - o * vrows
            if tile > place_seg:
                for d in range(n):
                    place_in[d * place_seg : (d + 1) * place_seg, :] = place_in[
                        d * tile : d * tile + place_seg, :
                    ]
            for j in range(2):
                table_ref[at : at + top - low, j * LANES : (j + 1) * LANES] += place_in[
                    pl.ds(2 * low + j, top - low, stride=2), :
                ]

    lax.fori_loop(1, n, finish_stat, 0)
    sums = jnp.sum(stat_in[...], axis=0)
    norm = jnp.sqrt(sums[0:1, 0:1])
    clip = jnp.minimum(1.0, clip_norm / (norm + 1e-06))
    stat_out[...] = jnp.where(lane == 0, norm, sums)
    table_ref[...] = table_ref[...] * clip
    sums_ref[...] = sums_ref[...] * clip
    for i, o in enumerate(owners):
        place_copy = copy_to(
            place_out, place_in.at[place_spot, :], place_sem.at[0, i], place_sem.at[1, me], o
        )
        pl.when(me != o)(place_copy.wait_send)
    if sparse:

        def finish_row(k, carry):
            row_copy(k).wait_send()
            return carry

        lax.fori_loop(1, n, finish_row, 0)


def run_exchange(n, vrows, flat_grads, loss_rows, sparse, given):
    flat_len = flat_grads.shape[0] - 2 * LEN
    plane, planes, flat_seg, flat_pad, place_seg, seg = plan(n, flat_len)
    count = len(range(VOCAB // vrows, (VOCAB + LEN - 1) // vrows + 1))
    dma = pltpu.SemaphoreType.DMA
    return pl.pallas_call(
        functools.partial(exchange_kernel, n, flat_len, sparse),
        out_shape=(
            jax.ShapeDtypeStruct((vrows, D), f32),
            jax.ShapeDtypeStruct((flat_pad, LANES), f32),
            jax.ShapeDtypeStruct((8, LANES), f32),
        ),
        in_specs=[whole_spec()] * (2 + len(given)),
        out_specs=(whole_spec(),) * 3,
        scratch_shapes=[
            pltpu.VMEM((2, n // 2, seg, LANES), f32),
            pltpu.VMEM((n // 2, seg, LANES), f32),
            pltpu.VMEM((plane, planes, seg, LANES), bf16),
            pltpu.VMEM((plane - 1, planes, seg, LANES), bf16),
            pltpu.VMEM((planes, seg, LANES), f32),
            pltpu.VMEM((planes, seg, LANES), bf16),
            pltpu.VMEM((planes - 1, seg, LANES), bf16),
            pltpu.VMEM((n * place_tile(n), LANES), f32),
            pltpu.VMEM((n, 8, LANES), f32),
        ]
        + ([pltpu.VMEM((n * room(n), D), bf16)] if sparse else [])
        + [dma((2,)), dma((2, plane)), dma((2, planes)), dma((2, max(n, count))), dma((2, n)), dma((2, n))],
        compiler_params=pltpu.CompilerParams(
            collective_id=2 if sparse else 3, has_side_effects=True, vmem_limit_bytes=24 * 2**20
        ),
        name="exchange" if sparse else "exchange_dense",
    )(flat_grads, loss_rows, *given)


def adam_step(weight, first_old, second, clipped):
    first_new = beta_one * first_old + (1.0 - beta_one) * clipped
    second_new = beta_two * second + (1.0 - beta_two) * clipped * clipped
    first_hat = first_new / (1.0 - beta_one**ADAM_STEP)
    second_hat = second_new / (1.0 - beta_two**ADAM_STEP)
    weight_new = weight - learn_rate * (
        first_hat / (jnp.sqrt(second_hat) + adam_eps) + decay_rate * weight
    )
    return (weight_new, first_new, second_new)


def rows_of(table, ids):
    return table.at[ids.reshape(-1)].get(mode="promise_in_bounds")


def ring_gather(devices, block):
    me = lax.axis_index("dp")
    rows = block.shape[0]
    onward = [(i, (i + 1) % devices) for i in range(devices)]

    def step(i, state):
        block, whole = state
        whole = lax.dynamic_update_slice(whole, block, (lax.rem(me - i + devices, devices) * rows, 0))
        return lax.ppermute(block, "dp", onward), whole

    whole = jnp.zeros((devices * rows, block.shape[1]), block.dtype)
    return lax.fori_loop(0, devices, step, (block, whole))[1]


def ring_scatter(devices, whole):
    me = lax.axis_index("dp")
    rows = whole.shape[0] // devices
    onward = [(i, (i + 1) % devices) for i in range(devices)]

    def part(i):
        at = lax.rem(me - 1 - i + 2 * devices, devices) * rows
        return lax.dynamic_slice(whole, (at, 0), (rows, whole.shape[1]))

    def step(i, total):
        return lax.ppermute(total, "dp", onward) + part(i)

    return lax.fori_loop(1, devices, step, part(0))


def per_device(
    devices,
    token_ids,
    lengths,
    gate_noise,
    lagrange,
    teacher_table,
    teacher_flat,
    word_table,
    table_first,
    table_second,
    layer_flat,
    flat_first,
    flat_second,
):
    seqs = token_ids.shape[0]
    half = seqs // 2
    vrows = word_table.shape[0]
    own = layer_flat.shape[0]
    flat_len = own * devices // LANES

    before = jnp.arange(seqs)[None, :] < jnp.arange(seqs)[:, None]
    longer = (lengths[None, :] > lengths[:, None]) | (
        (lengths[None, :] == lengths[:, None]) & before
    )
    rank = jnp.sum(longer.astype(jnp.int32), axis=1)
    kept = [r for r in range(seqs) if r % 4 in (0, 3)]
    order = jnp.array(kept + [r for r in range(seqs) if r not in kept], jnp.int32)
    chosen = (rank[None, :] == order[:, None]).astype(jnp.int32)
    token_ids = jnp.sum(chosen[:, :, None] * token_ids[None], axis=1)
    lengths = jnp.sum(chosen * lengths[None], axis=1)

    mates = [(i, devices - 1 - i) for i in range(devices)]
    sent = jnp.concatenate(
        [token_ids[half:], jnp.pad(lengths[half:], (0, LEN - half)).reshape(1, LEN)]
    )
    got = lax.ppermute(sent, "dp", mates)
    ids = jnp.concatenate([token_ids[:half], got[:half]])
    lens = jnp.concatenate([lengths[:half], got[half, :half]])

    owner = ids // vrows
    valid = jnp.arange(LEN)[None, :] < lens[:, None]
    target, listed, flat_all, place_all, *routed = run_fetch(
        devices,
        flat_len,
        jnp.where(valid, owner, -1),
        (ids - owner * vrows + 1).astype(f32),
        jnp.sum(lens).reshape(1),
        lens,
        ids // 16,
        ids % 16,
        teacher_table,
        teacher_table[VOCAB : VOCAB + LEN],
        teacher_flat.reshape(-1, LANES),
        word_table,
        layer_flat.reshape(-1, LANES),
    )
    stats = listed.reshape(devices, 8, LANES)[:, 1, :2]
    global_count = jnp.sum(stats[:, 0]).astype(f32)
    lag_weight = jnp.where(lax.axis_index("dp") == 0, 1.0, 0.0).astype(f32)
    factors = jnp.stack([(2.0 / D) / global_count, lag_weight])
    noise = jnp.pad(gate_noise, (0, 16 * LANES - gate_noise.shape[0]), constant_values=0.5)
    places = [place_all[i, : part[3]] for i, part in enumerate(place_parts(vrows))]
    shared = (
        lens,
        factors,
        lagrange,
        noise.reshape(16, LANES),
        flat_all,
        jnp.concatenate(places) if len(places) > 1 else places[0],
        target,
    )

    def from_slots():
        slots, fetched = routed
        flat_grads, _, loss_rows, packed = run_student(
            devices, flat_len, True, *shared, (slots, fetched)
        )
        result = run_exchange(devices, vrows, flat_grads, loss_rows, True, (packed, listed))
        return result

    def from_rows(mark):
        if routed:
            words, _ = lax.optimization_barrier((word_table, mark))
            table = ring_gather(devices, words.astype(bf16))
        else:
            table = lax.all_gather(word_table.astype(bf16), "dp", axis=0, tiled=True)
        flat_grads, grad_rows, loss_rows = run_student(
            devices, flat_len, False, *shared, (rows_of(table, ids),)
        )
        updates = jnp.transpose(grad_rows, (0, 2, 1)).reshape(seqs * LEN, D).astype(f32)
        table = jnp.zeros((devices * vrows, D), f32).at[ids.reshape(-1)].add(updates)
        if routed:
            table = ring_scatter(devices, table)
        else:
            table = lax.psum_scatter(table, "dp", scatter_dimension=0, tiled=True)
        result = run_exchange(devices, vrows, flat_grads, loss_rows, False, (table,))
        return result

    if routed:
        crowded = jnp.max(stats[:, 1])
        _, table_grad, sums, totals = lax.while_loop(
            lambda state: state[0] > 0,
            lambda state: (jnp.zeros_like(state[0]), *from_rows(state[0])),
            (crowded, *from_slots()),
        )
    else:
        table_grad, sums, totals = from_rows(0)
    flat_grad = sums[: own // LANES].reshape(-1)
    grad_norm = totals[0, 0]
    total_loss = totals[0, 1] / global_count + totals[0, 2]
    table_new = adam_step(word_table, table_first, table_second, table_grad)
    flat_new = adam_step(layer_flat, flat_first, flat_second, flat_grad)
    return (*table_new, *flat_new, total_loss, grad_norm)


def solution(mesh):
    row, flat, copied = P("dp", None), P("dp"), P()
    in_specs = (row, flat, copied, copied, copied, copied, row, row, row, flat, flat, flat)
    out_specs = (row, row, row, flat, flat, flat, copied, copied)
    return jax.shard_map(
        functools.partial(per_device, mesh.shape["dp"]),
        mesh=mesh,
        in_specs=in_specs,
        out_specs=out_specs,
        check_vma=False,
    )
```

```python
import functools
import math

import jax
import jax.numpy as jnp
from jax import lax
from jax.experimental import pallas as pl
from jax.experimental.pallas import tpu as pltpu
from jax.sharding import PartitionSpec as P

D = 256
HEADS = 4
HD = D // HEADS
FF = 1024
LEN = 512
VOCAB = 30522
NPAR = 856836
LANES = 128
norm_eps = 1e-12
clip_norm = 0.002
learn_rate = 0.015
beta_one = 0.9
beta_two = 0.999
adam_eps = 1e-08
decay_rate = 0.01
sparse_target = 0.3
ADAM_STEP = 10
relaxation_heat = 2.0 / 3.0
widened_left_limit = -0.1
widened_right_limit = 1.1
f32 = jnp.float32
bf16 = jnp.bfloat16
VMEM_LIMIT = 60 * 2**20

C_GH = 10 * D
C_HEAD = 11 * D
C_BUP = 12 * D
C_GI = 12 * D + FF
C_ROWS = 12 * D + 2 * FF
A_BUP = 10 * D
A_GH = 10 * D + FF
A_HEAD = 11 * D + FF
A_GI = 12 * D + FF
A_ROWS = 12 * D + 2 * FF
R_UP = 5 * 512
R_DOWN = R_UP + 2048
R_VEC = R_DOWN + 2048
R_BUP = R_VEC + 20
R_LOGIT = R_BUP + 8
R_USED = R_LOGIT + 11


def nn(left, right):
    return jnp.dot(left, right, preferred_element_type=f32)


def nt(left, right):
    return lax.dot_general(left, right, (((1,), (1,)), ((), ())), preferred_element_type=f32)


def chunks(span):
    return [(c, min(256, span - c)) for c in range(0, span, 256)]


def wide(col_ref, row, rows, width):
    col = col_ref[row : row + rows, :]
    return jnp.concatenate([col] * (width // LANES), axis=1) if width > LANES else col


def lanes_in(values):
    total = values[:, :LANES]
    for c in range(LANES, values.shape[1], LANES):
        total = total + values[:, c : c + LANES]
    return total


def eye(size):
    return (
        lax.broadcasted_iota(jnp.int32, (size, size), 0)
        == lax.broadcasted_iota(jnp.int32, (size, size), 1)
    ).astype(bf16)


def standardise(x):
    mean = jnp.sum(x, axis=0, keepdims=True) * (1.0 / D)
    centred = x - mean
    variance = jnp.sum(centred * centred, axis=0, keepdims=True) * (1.0 / D)
    scale = lax.rsqrt(variance + norm_eps)
    return centred * scale, scale


def standardise_back(dx, hat, scale):
    mean_one = jnp.sum(dx, axis=0, keepdims=True) * (1.0 / D)
    mean_two = jnp.sum(dx * hat, axis=0, keepdims=True) * (1.0 / D)
    return scale * (dx - mean_one - hat * mean_two)


def gelu_parts(x):
    half_erf = 0.5 * lax.erf(x * (2.0**-0.5)) + 0.5
    return half_erf


def start_part(c, width, student, embed, pos_ref, col_ref, w, sc, eyes):
    cols = pl.ds(c, width)
    embedded = embed(c, width) + pos_ref[:, cols]
    hat, scale = standardise(embedded)
    start = hat * wide(col_ref, 0, D, width) + wide(col_ref, D, D, width)
    if student:
        sc["hat0"][:, cols] = hat
        sc["scale"][0:1, cols] = scale
        start = start * wide(col_ref, C_GH, D, width)
    sc["start"][:, cols] = start
    start_low = start.astype(bf16)
    if student:
        sc["start_low"][:, cols] = start_low
    q = nn(w["qkvT"][0:D, :], start_low) + wide(col_ref, 6 * D, D, width)
    sc["qkv"][0:D, cols] = q.astype(bf16)
    k = nn(w["qkvT"][D : 2 * D, :], start_low).astype(bf16)
    sc["qkv"][D : 2 * D, cols] = k
    v = (nn(w["qkvT"][2 * D : 3 * D, :], start_low) + wide(col_ref, 7 * D, D, width)).astype(bf16)
    sc["qkv"][2 * D : 3 * D, cols] = v
    for h in range(HEADS):
        rows = slice(h * HD, (h + 1) * HD)
        sc["k_rows"][h, cols, :] = nt(eyes[width], k[rows, :]).astype(bf16)
        if student:
            sc["v_rows"][h, cols, :] = nt(eyes[width], v[rows, :]).astype(bf16)


def attend(span, length, student, col_ref, sc):
    for c, width in chunks(span):
        valid = lax.broadcasted_iota(jnp.int32, (span, width), 0) < length
        for h in range(HEADS):
            q_h = sc["qkv"][h * HD : (h + 1) * HD, c : c + width] * bf16(HD**-0.5)
            scores = jnp.where(valid, nn(sc["k_rows"][h, 0:span, :], q_h), -1e30)
            shares = jnp.exp(scores - jnp.max(scores, axis=0, keepdims=True))
            shares_low = (shares * (1.0 / jnp.sum(shares, axis=0, keepdims=True))).astype(bf16)
            if student:
                sc["shares"][h, 0:span, c : c + width] = shares_low
            context = nn(sc["qkv"][2 * D + h * HD : 2 * D + (h + 1) * HD, 0:span], shares_low)
            if student:
                sc["context"][h * HD : (h + 1) * HD, c : c + width] = context
                context = context * wide(col_ref, C_HEAD + h * HD, HD, width)
            sc["gated"][h * HD : (h + 1) * HD, c : c + width] = context.astype(bf16)


def middle_part(c, width, student, col_ref, w, sc):
    cols = pl.ds(c, width)
    branch = nn(w["oT"][...], sc["gated"][:, cols]) + wide(col_ref, 8 * D, D, width)
    if student:
        sc["branch"][:, 0:width] = branch
        branch = branch * wide(col_ref, C_GH, D, width)
    hat, scale = standardise(sc["start"][:, cols] + branch)
    middle = hat * wide(col_ref, 2 * D, D, width) + wide(col_ref, 3 * D, D, width)
    if student:
        sc["hat1"][:, 0:width] = hat
        sc["scale"][1:2, cols] = scale
    middle_low = middle.astype(bf16)
    if student:
        sc["middle_low"][:, 0:width] = middle_low
    for r in range(0, FF, D):
        pre = nn(w["upT"][r : r + D, :], middle_low) + wide(col_ref, C_BUP + r, D, width)
        cdf = 0.5 * lax.erf(pre * (2.0**-0.5)) + 0.5
        act = pre * cdf
        if student:
            inner = wide(col_ref, C_GI + r, D, width)
            pdf = jnp.exp(pre * pre * -0.5) * (1.0 / math.sqrt(2.0 * math.pi))
            sc["act"][r : r + D, 0:width] = act
            sc["slope"][r : r + D, 0:width] = (cdf + pre * pdf) * inner
            act = act * inner
        sc["up"][r : r + D, 0:width] = act.astype(bf16)
    down = nn(w["downT"][...], sc["up"][:, 0:width]) + wide(col_ref, 9 * D, D, width)
    if student:
        sc["down"][:, 0:width] = down
        down = down * wide(col_ref, C_GH, D, width)
    hat, scale = standardise(middle + down)
    out = hat * wide(col_ref, 4 * D, D, width) + wide(col_ref, 5 * D, D, width)
    return out, hat, scale


def add_lanes(add_ref, row, values):
    add_ref[row : row + values.shape[0], :] += lanes_in(values)


def back_part(c, width, length, factor, out, hat, scale, target_ref, col_ref, w, sc, acc, add_ref, loss_ref):
    cols = pl.ds(c, width)
    here = slice(0, width)
    add = functools.partial(add_lanes, add_ref)
    out_low = out.astype(bf16)
    differ = nn(w["aT"][...], out_low) - target_ref[0, :, cols]
    token_valid = (lax.broadcasted_iota(jnp.int32, (1, width), 1) + c < length).astype(f32)
    loss_ref[0:1, cols] += jnp.sum(differ * differ, axis=0, keepdims=True) * (1.0 / D) * token_valid
    d_aligned = (differ * (token_valid * factor)).astype(bf16)
    acc["a"][...] += nt(out_low, d_aligned)
    d_out = nn(w["a"][...], d_aligned)
    add(4 * D, d_out * hat)
    add(5 * D, d_out)
    d_second = standardise_back(d_out * wide(col_ref, 4 * D, D, width), hat, scale)
    add(A_GH, d_second * sc["down"][:, here])
    d_down = (d_second * wide(col_ref, C_GH, D, width)).astype(bf16)
    add(9 * D, d_down.astype(f32))
    acc["down"][...] += nt(sc["up"][:, here], d_down)
    for r in range(0, FF, D):
        d_up = nn(w["down"][r : r + D, :], d_down)
        add(A_GI + r, d_up * sc["act"][r : r + D, here])
        d_pre = (d_up * sc["slope"][r : r + D, here]).astype(bf16)
        sc["d_pre"][r : r + D, here] = d_pre
        add(A_BUP + r, d_pre.astype(f32))
    d_middle = d_second + nn(w["up"][...], sc["d_pre"][:, here])
    acc["up"][...] += nt(sc["middle_low"][:, here], sc["d_pre"][:, here])
    hat = sc["hat1"][:, here]
    add(2 * D, d_middle * hat)
    add(3 * D, d_middle)
    d_first = standardise_back(
        d_middle * wide(col_ref, 2 * D, D, width), hat, sc["scale"][1:2, cols]
    )
    sc["d_first"][:, cols] = d_first
    add(A_GH, d_first * sc["branch"][:, here])
    d_branch = (d_first * wide(col_ref, C_GH, D, width)).astype(bf16)
    add(8 * D, d_branch.astype(f32))
    acc["o"][...] += nt(sc["gated"][:, cols], d_branch)
    d_gated = nn(w["o"][...], d_branch)
    context = sc["context"][:, cols]
    add(A_HEAD, d_gated * context)
    d_context = d_gated * wide(col_ref, C_HEAD, D, width)
    sc["d_context"][:, cols] = d_context.astype(bf16)
    dot_rows = d_context * context
    for h in range(HEADS):
        sc["delta"][h : h + 1, cols] = jnp.sum(
            dot_rows[h * HD : (h + 1) * HD, :], axis=0, keepdims=True
        )


def attend_back(span, sc):
    full = slice(0, span)
    for h in range(HEADS):
        rows = slice(h * HD, (h + 1) * HD)
        d_value = nt(sc["d_context"][rows, full], sc["shares"][h, 0:span, 0:span])
        sc["d_qkv"][2 * D + h * HD : 2 * D + (h + 1) * HD, full] = d_value.astype(bf16)
        d_key = None
        for c, width in chunks(span):
            cols = slice(c, c + width)
            d_shares = nn(sc["v_rows"][h, 0:span, :], sc["d_context"][rows, cols])
            d_scores = (
                sc["shares"][h, 0:span, cols].astype(f32) * (d_shares - sc["delta"][h : h + 1, cols])
            ).astype(bf16)
            sc["d_qkv"][rows, cols] = (
                nn(sc["qkv"][D + h * HD : D + (h + 1) * HD, full], d_scores) * (HD**-0.5)
            ).astype(bf16)
            part = nt(sc["qkv"][rows, cols], d_scores)
            d_key = part if d_key is None else d_key + part
        sc["d_qkv"][D + h * HD : D + (h + 1) * HD, full] = (d_key * (HD**-0.5)).astype(bf16)


def end_part(c, width, col_ref, w, sc, acc, add_ref, grad_ref, pos_add):
    cols = pl.ds(c, width)
    add = functools.partial(add_lanes, add_ref)
    acc["qkv"][...] += nt(sc["start_low"][:, cols], sc["d_qkv"][:, cols])
    add(6 * D, sc["d_qkv"][0:D, cols].astype(f32))
    add(7 * D, sc["d_qkv"][2 * D : 3 * D, cols].astype(f32))
    d_start = sc["d_first"][:, cols] + nn(w["qkv"][...], sc["d_qkv"][:, cols])
    hat = sc["hat0"][:, cols]
    gain = wide(col_ref, 0, D, width)
    add(A_GH, d_start * (hat * gain + wide(col_ref, D, D, width)))
    d_norm = d_start * wide(col_ref, C_GH, D, width)
    add(0, d_norm * hat)
    add(D, d_norm)
    d_embedded = standardise_back(d_norm * gain, hat, sc["scale"][0:1, cols])
    pos_add[:, cols] += d_embedded
    grad_ref[0, :, cols] = d_embedded.astype(bf16)


def by_part(length, body):
    def step(i, carry):
        body(pl.multiple_of(i * 256, 256), 256)
        return carry

    lax.fori_loop(0, jnp.where(length > 384, 2, 1), step, 0)
    pl.when((length > 256) & (length <= 384))(lambda: body(256, 128))


def mark_slots(slot, perm_ref):
    step = 512
    width = slot.shape[1]

    def mark(i, carry):
        rows = pl.ds(pl.multiple_of(i * step, step), step)
        seen = lax.broadcasted_iota(jnp.int32, (step, width), 0) == slot - i * step
        perm_ref[rows, :] = seen.astype(f32).astype(bf16)
        return carry

    lax.fori_loop(0, perm_ref.shape[0] // step, mark, 0)


def pack_rows(span, perm_ref, grad_ref, packed_ref):
    step = 4096

    def add(i, carry):
        rows = pl.ds(pl.multiple_of(i * step, step), step)
        packed_ref[rows, :] += nt(perm_ref[rows, 0:span], grad_ref[0, :, 0:span]).astype(bf16)
        return carry

    lax.fori_loop(0, packed_ref.shape[0] // step, add, 0)


SPANS = (256, 384, 512)


def by_span(length, body):
    for i, span in enumerate(SPANS):
        low = SPANS[i - 1] if i else 0
        test = length > low
        if i == 0:
            test = length <= span
        elif i < len(SPANS) - 1:
            test = (length > low) & (length <= span)
        pl.when(test)(functools.partial(body, span))


def set_up(pos_in, pos_ref, eyes_refs):
    for size, ref in eyes_refs.items():
        ref[...] = eye(size)
    for c in range(0, LEN, 256):
        pos_ref[:, c : c + 256] = nt(eyes_refs[256][...], pos_in[c : c + 256, :])


TEACHER_W = (
    ("qkv", (D, 3 * D)),
    ("qkvT", (3 * D, D)),
    ("o", (D, D)),
    ("oT", (D, D)),
    ("up", (D, FF)),
    ("upT", (FF, D)),
    ("down", (FF, D)),
    ("downT", (D, FF)),
)
STUDENT_W = TEACHER_W + (("a", (D, D)), ("aT", (D, D)))


def spread(col_ref, at, row):
    col_ref[pl.ds(at, LANES), :] = jnp.transpose(jnp.broadcast_to(row, (LANES, LANES)))


def load_weights(flat, w, col_ref, one, student):
    squares = [("qkv", 0), ("qkv", D), ("qkv", 2 * D), ("o", 0)] + ([("a", 0)] if student else [])
    for i, (name, at) in enumerate(squares):
        for j in range(2):
            lanes = slice(at + j * LANES, at + (j + 1) * LANES)
            w[name][:, lanes] = flat[pl.ds(512 * i + j, D, stride=2), :].astype(bf16)
    base = 512 * len(squares)
    for j in range(8):
        w["up"][:, j * LANES : (j + 1) * LANES] = flat[pl.ds(base + j, D, stride=8), :].astype(bf16)
    base = base + 2048
    for j in range(2):
        w["down"][:, j * LANES : (j + 1) * LANES] = flat[pl.ds(base + j, FF, stride=2), :].astype(
            bf16
        )
    base = base + 2048
    for i in range(20):
        spread(col_ref, i * LANES, flat[base + i : base + i + 1, :])
    for j in range(8):
        spread(col_ref, C_BUP + j * LANES, flat[base + 20 + j : base + 21 + j, :])
    unit = one[...]
    for name in ("qkv", "o", "up") + (("a",) if student else ()):
        for b in range(0, w[name].shape[1], D):
            w[name + "T"][b : b + D, :] = nt(unit, w[name][:, b : b + D]).astype(bf16)
    for b in range(0, FF, D):
        w["downT"][:, b : b + D] = nt(unit, w["down"][b : b + D, :]).astype(bf16)


def total_of(x):
    return jnp.sum(jnp.sum(x, axis=0, keepdims=True), axis=1, keepdims=True)


def head_groups():
    return (
        lax.broadcasted_iota(jnp.int32, (D, LANES), 0) // HD
        == lax.broadcasted_iota(jnp.int32, (D, LANES), 1)
    ).astype(f32)


def load_gates(logits, noise, lagrange_ref, lag_weight, col_ref, slope_ref, lag_ref):
    index = lax.broadcasted_iota(
        jnp.int32, logits.shape, 0
    ) * LANES + lax.broadcasted_iota(jnp.int32, logits.shape, 1)
    hidden, heads = index < D, (index >= D) & (index < D + HEADS)
    inner = (index >= D + HEADS) & (index < D + HEADS + FF)
    logistic = jax.nn.sigmoid((jnp.log(noise) - jnp.log(1.0 - noise) + logits) / relaxation_heat)
    spanned = widened_right_limit - widened_left_limit
    stretched = logistic * spanned + widened_left_limit
    gates = jnp.clip(stretched, 0.0, 1.0)
    inside = jnp.where((stretched > 0.0) & (stretched < 1.0), 1.0, 0.0)
    inside = jnp.where((stretched == 0.0) | (stretched == 1.0), 0.5, inside)
    slope_ref[...] = inside * logistic * (1.0 - logistic) * (spanned / relaxation_heat)
    keep = jax.nn.sigmoid(
        logits - relaxation_heat * math.log(-widened_left_limit / widened_right_limit)
    )
    kept = total_of(jnp.where(hidden, keep, 0.0)) * (1.0 / D)
    rest = total_of(jnp.where(heads, keep * (4.0 * HD), 0.0) + jnp.where(inner, keep * 2.0, 0.0))
    scale = 1.0 / (4.0 * D + 2.0 * FF)
    excess = kept * rest * scale - sparse_target
    rate = (lagrange_ref[0] + 2.0 * lagrange_ref[1] * excess) * (scale * lag_weight)
    share = jnp.where(hidden, rest * (1.0 / D), 0.0)
    share = share + kept * (jnp.where(heads, 4.0 * HD, 0.0) + jnp.where(inner, 2.0, 0.0))
    lag_ref[...] = rate * share * (keep * (1.0 - keep))
    for j in range(2):
        spread(col_ref, C_GH + j * LANES, gates[j : j + 1, :])
    wide_heads = lax.dot_general(
        jnp.broadcast_to(gates[2:3, :], (8, LANES)),
        head_groups(),
        (((1,), (1,)), ((), ())),
        preferred_element_type=f32,
        precision=lax.Precision.HIGHEST,
    )
    for j in range(2):
        spread(col_ref, C_HEAD + j * LANES, wide_heads[0:1, j * LANES : (j + 1) * LANES])
    run = jnp.concatenate([gates[j : j + 1, :] for j in range(2, 11)], axis=1)
    run = pltpu.roll(jnp.broadcast_to(run, (8, 9 * LANES)), 9 * LANES - HEADS, 1)
    for j in range(8):
        spread(col_ref, C_GI + j * LANES, run[0:1, j * LANES : (j + 1) * LANES])
    return lagrange_ref[0] * excess + lagrange_ref[1] * excess * excess


TEACHER_S = (
    ("start", (D, LEN), f32),
    ("qkv", (3 * D, LEN), bf16),
    ("k_rows", (HEADS, LEN, HD), bf16),
    ("gated", (D, LEN), bf16),
    ("up", (FF, 256), bf16),
)
STUDENT_S = TEACHER_S + (
    ("start_low", (D, LEN), bf16),
    ("hat0", (D, LEN), f32),
    ("hat1", (D, 256), f32),
    ("scale", (8, LEN), f32),
    ("v_rows", (HEADS, LEN, HD), bf16),
    ("shares", (HEADS, LEN, LEN), bf16),
    ("context", (D, LEN), f32),
    ("branch", (D, 256), f32),
    ("middle_low", (D, 256), bf16),
    ("act", (FF, 256), f32),
    ("slope", (FF, 256), f32),
    ("down", (D, 256), f32),
    ("d_pre", (FF, 256), bf16),
    ("d_first", (D, LEN), f32),
    ("d_context", (D, LEN), bf16),
    ("delta", (8, LEN), f32),
    ("d_qkv", (3 * D, LEN), bf16),
)
ACCS = (
    ("qkv", (D, 3 * D)),
    ("o", (D, D)),
    ("a", (D, D)),
    ("up", (D, FF)),
    ("down", (FF, D)),
)


class Eyes:
    def __init__(self, one, two):
        self.refs = {128: one, 256: two}

    def __getitem__(self, size):
        return self.refs[size][...]


def student_kernel(n, flat_len, sparse, len_ref, fac_ref, lagrange_ref, noise_ref, flat_in, pos_in, target_ref, *rest):
    plane, planes, flat_seg = plan(n, flat_len)[:3]
    cap = room(n)
    if sparse:
        slot_ref, rows_ref = rest[:2]
        rest = rest[2:]
    else:
        rows_ref = rest[0]
        rest = rest[1:]
    flat_ref, grad_ref, loss_ref = rest[:3]
    rest = rest[3:]
    if sparse:
        packed_ref, rows_all, perm_ref, slot_now = rest[:4]
        rest = rest[4:]
    w = {entry[0]: rest[i] for i, entry in enumerate(STUDENT_W)}
    rest = rest[len(STUDENT_W) :]
    sc = {entry[0]: rest[i] for i, entry in enumerate(STUDENT_S)}
    rest = rest[len(STUDENT_S) :]
    acc = {entry[0]: rest[i] for i, entry in enumerate(ACCS)}
    add_ref, pos_add, slope_ref, lag_ref, col_ref, pos_ref, eye_one, eye_two = rest[len(ACCS) :]
    s = pl.program_id(0)
    eyes = Eyes(eye_one, eye_two)

    @pl.when(s == 0)
    def _():
        set_up(pos_in, pos_ref, eyes.refs)
        for o in range(n):
            c = o // 2
            flat_ref[o * flat_seg : (o + 1) * flat_seg, :] = flat_in[
                o % 2, c % plane, c // plane, :, :
            ].astype(f32)[:flat_seg]
        load_weights(flat_ref, w, col_ref, eye_two, True)
        lag_value = load_gates(
            flat_ref[R_LOGIT : R_LOGIT + 16, :],
            noise_ref[...],
            lagrange_ref,
            fac_ref[1],
            col_ref,
            slope_ref,
            lag_ref,
        )
        for ref in list(acc.values()) + [add_ref, pos_add]:
            ref[...] = jnp.zeros(ref.shape, f32)
        row = lax.broadcasted_iota(jnp.int32, (8, LEN), 0)
        loss_ref[...] = jnp.where(row == 1, lag_value, 0.0)
        if sparse:
            packed_ref[...] = jnp.zeros(packed_ref.shape, bf16)
            for o in range(n):
                rows_all[:, o * cap : (o + 1) * cap] = rows_ref[o]

    length = len_ref[s]

    def embed(c, width):
        if sparse:
            mark_slots(slot_now[0:1, pl.ds(c, width)], perm_ref.at[:, pl.ds(c, width)])
            return nn(rows_all[...], perm_ref[:, pl.ds(c, width)])
        at = pl.multiple_of(s * LEN + c, 128)
        return nt(eyes[D], rows_ref[pl.ds(at, width), :])

    def between(c, width):
        out, hat, scale = middle_part(c, width, True, col_ref, w, sc)
        back_part(
            c, width, length, fac_ref[0], out, hat, scale, target_ref, col_ref, w, sc, acc, add_ref, loss_ref
        )

    grad_ref[0, :, 256:LEN] = jnp.zeros((D, LEN - 256), bf16)
    if sparse:
        slot_now[0:1, :] = slot_ref[pl.ds(s, 1), :]
    by_part(
        length, lambda c, width: start_part(c, width, True, embed, pos_ref, col_ref, w, sc, eyes)
    )
    by_span(length, lambda span: attend(span, length, True, col_ref, sc))
    by_part(length, between)
    by_span(length, lambda span: attend_back(span, sc))
    by_part(
        length,
        lambda c, width: end_part(c, width, col_ref, w, sc, acc, add_ref, grad_ref, pos_add),
    )
    if sparse:
        by_span(length, lambda span: pack_rows(span, perm_ref, grad_ref, packed_ref))

    @pl.when(s == pl.num_programs(0) - 1)
    def _():
        for i in range(3):
            for j in range(2):
                at = i * D + j * LANES
                flat_ref[pl.ds(512 * i + j, D, stride=2), :] = acc["qkv"][:, at : at + LANES]
        for j in range(2):
            lanes = slice(j * LANES, (j + 1) * LANES)
            flat_ref[pl.ds(512 * 3 + j, D, stride=2), :] = acc["o"][:, lanes]
            flat_ref[pl.ds(512 * 4 + j, D, stride=2), :] = acc["a"][:, lanes]
            flat_ref[pl.ds(R_DOWN + j, FF, stride=2), :] = acc["down"][:, lanes]
        for j in range(8):
            flat_ref[pl.ds(R_UP + j, D, stride=8), :] = acc["up"][:, j * LANES : (j + 1) * LANES]
        ones = jnp.ones((8, LANES), f32)

        def summed(row, rows):
            return lax.dot_general(
                ones,
                add_ref[row : row + rows, :],
                (((1,), (1,)), ((), ())),
                preferred_element_type=f32,
                precision=lax.Precision.HIGHEST,
            )

        for i in range(10):
            sums = summed(i * D, D)
            for j in range(2):
                flat_ref[R_VEC + 2 * i + j : R_VEC + 2 * i + j + 1, :] = sums[
                    0:1, j * LANES : (j + 1) * LANES
                ]
        sums = summed(A_BUP, FF)
        for j in range(8):
            flat_ref[R_BUP + j : R_BUP + j + 1, :] = sums[0:1, j * LANES : (j + 1) * LANES]
        hidden = summed(A_GH, D)
        heads = jnp.dot(
            summed(A_HEAD, D),
            head_groups(),
            preferred_element_type=f32,
            precision=lax.Precision.HIGHEST,
        )
        inner = summed(A_GI, FF)
        moved = pltpu.roll(jnp.concatenate([inner, jnp.zeros((8, LANES), f32)], axis=1), HEADS, 1)
        lane = lax.broadcasted_iota(jnp.int32, (8, LANES), 1)
        first = jnp.where(lane < HEADS, heads, moved[:, :LANES])
        tail = [hidden[:, :LANES], hidden[:, LANES:], first] + [
            moved[:, j * LANES : (j + 1) * LANES] for j in range(1, 9)
        ]
        for j, piece in enumerate(tail):
            flat_ref[R_LOGIT + j : R_LOGIT + j + 1, :] = (
                piece[0:1] * slope_ref[j : j + 1, :] + lag_ref[j : j + 1, :]
            )
        flat_ref[R_USED:flat_len, :] = jnp.zeros((flat_len - R_USED, LANES), f32)
        for j in range(2):
            flat_ref[pl.ds(flat_len + j, LEN, stride=2), :] = jnp.transpose(
                pos_add[j * LANES : (j + 1) * LANES, :]
            )


def whole_spec():
    return pl.BlockSpec(memory_space=pltpu.VMEM)


def smem_spec():
    return pl.BlockSpec(memory_space=pltpu.SMEM)


def seq_spec():
    return pl.BlockSpec((1, D, LEN), lambda s: (s, 0, 0))


def common_scratch():
    return [
        pltpu.VMEM((C_ROWS, LANES), f32),
        pltpu.VMEM((D, LEN), f32),
        pltpu.VMEM((128, 128), bf16),
        pltpu.VMEM((256, 256), bf16),
    ]


def run_student(n, flat_len, sparse, lengths, factors, lagrange, noise, flat_all, places, target, given):
    seqs = lengths.shape[0]
    slot_rows = n * room(n)
    shapes = [
        jax.ShapeDtypeStruct((flat_len + 2 * LEN, LANES), f32),
        jax.ShapeDtypeStruct((seqs, D, LEN), bf16),
        jax.ShapeDtypeStruct((8, LEN), f32),
    ]
    out_specs = [whole_spec(), seq_spec(), whole_spec()]
    scratch = []
    if sparse:
        shapes.append(jax.ShapeDtypeStruct((slot_rows, D), bf16))
        out_specs.append(whole_spec())
        scratch = [
            pltpu.VMEM((D, slot_rows), bf16),
            pltpu.VMEM((slot_rows, LEN), bf16),
            pltpu.VMEM((8, LEN), jnp.int32),
        ]
    return pl.pallas_call(
        functools.partial(student_kernel, n, flat_len, sparse),
        grid=(seqs,),
        out_shape=tuple(shapes),
        in_specs=[smem_spec()] * 3
        + [whole_spec()] * 3
        + [seq_spec()]
        + [whole_spec()] * len(given),
        out_specs=tuple(out_specs),
        scratch_shapes=scratch
        + [pltpu.VMEM(shape, bf16) for _, shape in STUDENT_W]
        + [pltpu.VMEM(shape, kind) for _, shape, kind in STUDENT_S]
        + [pltpu.VMEM(shape, f32) for _, shape in ACCS]
        + [
            pltpu.VMEM((A_ROWS, LANES), f32),
            pltpu.VMEM((D, LEN), f32),
            pltpu.VMEM((16, LANES), f32),
            pltpu.VMEM((16, LANES), f32),
        ]
        + common_scratch(),
        compiler_params=pltpu.CompilerParams(vmem_limit_bytes=44 * 2**20),
        name="student" if sparse else "student_dense",
    )(lengths, factors, lagrange, noise, flat_all, places, target, *given)


MESH = pl.DeviceIdType.MESH
ROW_CUTS = (8, 8)


def room(n):
    return LANES if 8 * LEN // n >= LANES else 0


def filled(n):
    return room(n) - 16


def greet_all(me, n):
    barrier = pltpu.get_barrier_semaphore()

    def signal(k, carry):
        pl.semaphore_signal(barrier, inc=1, device_id=(me ^ k,), device_id_type=MESH)
        return carry

    lax.fori_loop(1, n, signal, 0)
    pl.semaphore_wait(barrier, n - 1)


def copy_to(source, target, send, receive, device):
    return pltpu.make_async_remote_copy(
        src_ref=source,
        dst_ref=target,
        send_sem=send,
        recv_sem=receive,
        device_id=(device,),
        device_id_type=MESH,
    )


def list_rows(n, owner_ref, local_ref, stat, slot_ref, tile_ref):
    cap = room(n)
    upper = (
        lax.broadcasted_iota(jnp.int32, (256, 256), 0)
        <= lax.broadcasted_iota(jnp.int32, (256, 256), 1)
    ).astype(bf16)

    def sequence(s, state):
        base, listed = state
        for c in range(0, LEN, 256):
            owner = owner_ref[pl.ds(s, 1), c : c + 256]
            mine = (lax.broadcasted_iota(jnp.int32, (n, 256), 0) == owner).astype(f32)
            before = nn(mine.astype(bf16), upper)
            rank = jnp.sum(mine * (before - 1.0 + base), axis=0, keepdims=True).astype(jnp.int32)
            fits = (owner >= 0) & (rank < filled(n))
            slot_ref[pl.ds(s, 1), c : c + 256] = jnp.where(fits, owner * cap + rank, n * cap)
            place = (
                lax.broadcasted_iota(jnp.int32, (LANES, 256), 0) == jnp.where(fits, rank, -1)
            ).astype(f32)
            listed = listed + lax.dot_general(
                mine * local_ref[pl.ds(s, 1), c : c + 256],
                place,
                (((1,), (1,)), ((), ())),
                preferred_element_type=f32,
                precision=lax.Precision.HIGHEST,
            )
            base = base + before[:, 255:256]
        return base, listed

    base, listed = lax.fori_loop(
        0,
        owner_ref.shape[0],
        sequence,
        (jnp.zeros((n, 1), f32), jnp.zeros((n, LANES), f32)),
    )
    over = jnp.max(base, axis=0, keepdims=True) > filled(n)
    lane = lax.broadcasted_iota(jnp.int32, (n, LANES), 1)
    tile_ref[...] = jnp.zeros(tile_ref.shape, jnp.int32)
    tile_ref[pl.ds(0, n, stride=8), :] = (listed + 0.5).astype(jnp.int32) - 1
    tile_ref[pl.ds(1, n, stride=8), :] = jnp.where(
        lane == 0, stat, jnp.where(lane == 1, over.astype(jnp.int32), 0)
    )


def place_parts(vrows):
    parts = []
    for o in range(VOCAB // vrows, (VOCAB + LEN - 1) // vrows + 1):
        low, top = max(VOCAB, o * vrows), min(VOCAB + LEN, (o + 1) * vrows)
        parts.append((o, low - o * vrows, low - VOCAB, top - low))
    return parts


def round_up(value, step):
    return -(-value // step) * step


def pair_lists(list_ref, a, cap):
    return jnp.concatenate(
        [list_ref[pl.ds(pl.multiple_of(a * 16 + 8 * j, 8), 8), :][0:1, :cap] for j in range(2)],
        axis=1,
    )


def fetch_kernel(
    n, flat_len, owner_ref, local_ref, stat_ref, len_ref, block_ref, row_ref, words_in, pos_in, flat_in, table_ref, own_flat, *rest
):
    plane, planes, flat_seg, flat_pad = plan(n, flat_len)[:4]
    cap = room(n)
    vrows = table_ref.shape[0]
    parts = place_parts(vrows)
    out_ref, got_out, flat_out, place_out = rest[:4]
    rest = rest[4:]
    if cap:
        slot_ref, rows_out = rest[:2]
        rest = rest[2:]
    w = {entry[0]: rest[i] for i, entry in enumerate(TEACHER_W)}
    rest = rest[len(TEACHER_W) :]
    sc = {entry[0]: rest[i] for i, entry in enumerate(TEACHER_S)}
    rest = rest[len(TEACHER_S) :]
    tile_ref, got_ref, flat_all, place_all, pad_ref, flat_f32 = rest[:6]
    list_sem, a_sem, b_sem, c_sem, pa_sem, pb_sem, pc_sem = rest[6:13]
    col_ref, pos_ref, eye_one, eye_two = rest[13:17]
    words, picked, word_sem, out_sem = rest[17:21]
    if cap:
        table_turned, row_send, rows_in, row_sem = rest[21:]
    eyes = Eyes(eye_one, eye_two)
    s = pl.program_id(0)
    seqs = owner_ref.shape[0]
    me = lax.axis_index("dp")
    core = lax.rem(me, 2)
    chip = me // 2
    mid = lax.rem(chip, plane)
    high = chip // plane

    def device(h, m, c):
        return (h * plane + m) * 2 + c

    def tile(ref, i):
        return ref.at[pl.ds(pl.multiple_of(i * 8, 8), 8), :]

    def list_copy(k):
        return copy_to(
            tile(tile_ref, me ^ k), tile(got_ref, me), list_sem.at[0, k], list_sem.at[1, k], me ^ k
        )

    def row_copy(k):
        return copy_to(
            row_send.at[me ^ k], rows_in.at[me], row_sem.at[0, k], row_sem.at[1, k], me ^ k
        )

    def flat_copies(stage):
        copies = []
        if stage == 0:
            spot = flat_all.at[core, mid, high]
            for k in range(1, planes):
                to = device(lax.rem(high + k, planes), mid, core)
                copies.append(copy_to(spot, spot, a_sem.at[0, k], a_sem.at[1, k], to))
        elif stage == 1:
            spot = flat_all.at[core, mid]
            for k in range(1, plane):
                to = device(high, lax.rem(mid + k, plane), core)
                copies.append(copy_to(spot, spot, b_sem.at[0, k], b_sem.at[1, k], to))
        else:
            spot = flat_all.at[core]
            copies.append(copy_to(spot, spot, c_sem.at[0], c_sem.at[1], me ^ 1))
        return copies

    def place_copies(stage, i):
        o, _, _, count = parts[i]
        chip_o = o // 2
        high_o, mid_o, core_o = chip_o // plane, chip_o % plane, o % 2
        spot = place_all.at[i, pl.ds(0, round_up(count, 16)), :]
        same_core, same_mid, same_high = core == core_o, mid == mid_o, high == high_o
        copies = []
        if stage == 0:
            for k in range(1, planes):
                to = device((high_o + k) % planes, mid_o, core_o)
                copies.append(copy_to(spot, spot, pa_sem.at[0, i, k], pa_sem.at[1, i, 0], to))
            sends = same_core & same_mid & same_high
            receives = same_core & same_mid & (high != high_o)
        elif stage == 1:
            for k in range(1, plane):
                to = device(high, (mid_o + k) % plane, core_o)
                copies.append(copy_to(spot, spot, pb_sem.at[0, i, k], pb_sem.at[1, i, 0], to))
            sends = same_core & same_mid
            receives = same_core & (mid != mid_o)
        else:
            copies.append(copy_to(spot, spot, pc_sem.at[0, i], pc_sem.at[1, i], me ^ 1))
            sends = same_core
            receives = core != core_o
        return copies, sends, receives

    def start_stage(stage):
        for copy in flat_copies(stage):
            copy.start()
        for i in range(len(parts)):
            copies, sends, _ = place_copies(stage, i)

            @pl.when(sends)
            def _():
                for copy in copies:
                    copy.start()

    def finish_stage(stage):
        for copy in flat_copies(stage):
            copy.wait()
        for i in range(len(parts)):
            copies, sends, receives = place_copies(stage, i)

            @pl.when(sends)
            def _():
                for copy in copies:
                    copy.wait_send()

            @pl.when(receives)
            def _():
                copies[0].wait_recv()

    known = words.shape[0] * 16
    word_copy = pltpu.make_async_copy(
        words_in.at[pl.ds(0, known), :], words.reshape(known, D), word_sem
    )

    @pl.when(s == 0)
    def _():
        word_copy.start()
        picked[...] = jnp.zeros(picked.shape, f32)
        greet_all(me, n)
        pad_ref[...] = jnp.zeros(pad_ref.shape, f32)
        pad_ref[0:flat_seg, :] = own_flat[...]
        flat_all[core, mid, high] = pad_ref[...].astype(bf16)
        for i, (o, at, _, count) in enumerate(parts):

            @pl.when(me == o)
            def _():
                full = round_up(count, 16)
                part = table_ref[at : at + count, :]
                if full > count:
                    part = jnp.concatenate([part, jnp.zeros((full - count, D), f32)], axis=0)
                place_all[i, 0:full, :] = part.astype(bf16)

        start_stage(0)
        if cap:
            list_rows(n, owner_ref, local_ref, stat_ref[0], slot_ref, tile_ref)
        else:
            tile_ref[...] = jnp.zeros(tile_ref.shape, jnp.int32) + stat_ref[0]

        def start_list(k, carry):
            list_copy(k).start()
            return carry

        lax.fori_loop(1, n, start_list, 0)
        own = pl.ds(pl.multiple_of(me * 8, 8), 8)
        got_ref[own, :] = tile_ref[own, :]
        set_up(pos_in, pos_ref, eyes.refs)
        if cap:
            table_turned[...] = nt(eye_two[...], table_ref[...].astype(bf16)).astype(bf16)

        def finish_list(k, carry):
            list_copy(k).wait()
            return carry

        lax.fori_loop(1, n, finish_list, 0)

        def serve(step, carry):
            i = n // 2 - 1 - step
            a = chip ^ i
            pick = (
                lax.broadcasted_iota(jnp.int32, (vrows, 2 * cap), 0) == pair_lists(got_ref, a, cap)
            ).astype(bf16)
            both = nn(table_turned[...], pick).astype(bf16)
            for j in range(2):
                row_send[2 * a + j] = both[:, j * cap : (j + 1) * cap]
                k = 2 * i + (core ^ j)
                pl.when(k > 0)(row_copy(k).start)
            return carry

        if cap:
            lax.fori_loop(0, n // 2, serve, 0)
            rows_in[me] = row_send[me]
        step = 512
        whole = flat_in.shape[0] // step

        def unpack(i, carry):
            rows = pl.ds(pl.multiple_of(i * step, step), step)
            flat_f32[rows, :] = flat_in[rows, :].astype(f32)
            return carry

        lax.fori_loop(0, whole, unpack, 0)
        flat_f32[whole * step :, :] = flat_in[whole * step :, :].astype(f32)
        load_weights(flat_f32, w, col_ref, eye_two, False)
        word_copy.wait()

    @pl.when(s == 1)
    def _():
        finish_stage(0)
        start_stage(1)

    length = len_ref[s]
    from_me = jnp.where(s < seqs // 2, me, n - 1 - me)
    longest = LEN // 3 + (LEN - LEN // 3) * from_me // (n - 1)

    def pick_rows(g, carry):
        for e in range(4):
            rows = []
            for u in range(8):
                at = g * 32 + e * 8 + u
                block = words[block_ref[s, at]].astype(f32)
                mine = lax.broadcasted_iota(jnp.int32, (16, D), 0) == row_ref[s, at]
                rows.append(jnp.sum(jnp.where(mine, block, 0.0), axis=0, keepdims=True))
            picked[pl.ds(pl.multiple_of(g * 32 + e * 8, 8), 8), :] = jnp.concatenate(rows, axis=0)
        return carry

    lax.fori_loop(0, (longest + 31) // 32, pick_rows, 0)

    def embed(c, width):
        return nt(eyes[D], picked[pl.ds(c, width), :].astype(bf16))

    def finish(c, width):
        out_ref[0, :, pl.ds(c, width)] = middle_part(c, width, False, col_ref, w, sc)[0]

    def body(span):
        for c, width in chunks(span):
            start_part(c, width, False, embed, pos_ref, col_ref, w, sc, eyes)
        attend(span, length, False, col_ref, sc)
        for c, width in chunks(span):
            finish(c, width)

    by_span(longest, body)

    @pl.when(s == seqs - 2)
    def _():
        finish_stage(1)
        start_stage(2)

    @pl.when(s == seqs - 1)
    def _():
        finish_stage(2)

        def finish_row(k, carry):
            row_copy(k).wait()
            return carry

        if cap:
            lax.fori_loop(1, n, finish_row, 0)
        pairs = [(got_ref, got_out), (flat_all, flat_out), (place_all, place_out)]
        if cap:
            pairs.append((rows_in, rows_out))
        leaving = [
            pltpu.make_async_copy(source, target, out_sem.at[i])
            for i, (source, target) in enumerate(pairs)
        ]
        for copy in leaving:
            copy.start()
        for copy in leaving:
            copy.wait()


def run_fetch(n, flat_len, owner, local, stat, lengths, blocks, rows, words, places, teacher, table, own_flat):
    plane, planes, flat_seg, flat_pad = plan(n, flat_len)[:4]
    seqs, cap, vrows = owner.shape[0], room(n), table.shape[0]
    parts = place_parts(vrows)
    most = max(round_up(part[3], 16) for part in parts)
    dma = pltpu.SemaphoreType.DMA
    got = ((8 * n, LANES), jnp.int32)
    fetched = ((n, D, cap), bf16)
    flat_all = ((2, plane, planes, flat_pad, LANES), bf16)
    place_all = ((len(parts), most, D), bf16)
    shapes = [((seqs, D, LEN), f32), got, flat_all, place_all]
    far = pl.BlockSpec(memory_space=pl.ANY)
    out_specs = [seq_spec(), far, far, far]
    extra = []
    if cap:
        shapes += [(owner.shape, jnp.int32), fetched]
        out_specs += [whole_spec(), far]
        extra = [
            pltpu.VMEM((D, vrows), bf16),
            pltpu.VMEM(*fetched),
            pltpu.VMEM(*fetched),
            dma((2, n)),
        ]
    return pl.pallas_call(
        functools.partial(fetch_kernel, n, flat_len),
        grid=(seqs,),
        out_shape=tuple(jax.ShapeDtypeStruct(shape, kind) for shape, kind in shapes),
        in_specs=[whole_spec()] * 2
        + [smem_spec()] * 4
        + [pl.BlockSpec(memory_space=pl.ANY)]
        + [whole_spec()] * 4,
        out_specs=tuple(out_specs),
        scratch_shapes=[pltpu.VMEM(shape, bf16) for _, shape in TEACHER_W]
        + [pltpu.VMEM(shape, kind) for _, shape, kind in TEACHER_S]
        + [
            pltpu.VMEM(*got),
            pltpu.VMEM(*got),
            pltpu.VMEM(*flat_all),
            pltpu.VMEM(*place_all),
            pltpu.VMEM((flat_pad, LANES), f32),
            pltpu.VMEM(teacher.shape, f32),
            dma((2, n)),
            dma((2, planes)),
            dma((2, plane)),
            dma((2,)),
            dma((2, len(parts), planes)),
            dma((2, len(parts), plane)),
            dma((2, len(parts))),
        ]
        + common_scratch()
        + [pltpu.VMEM((words.shape[0] // 16, 16, D), bf16), pltpu.VMEM((LEN, D), f32), dma, dma((4,))]
        + extra,
        compiler_params=pltpu.CompilerParams(
            collective_id=1, has_side_effects=True, vmem_limit_bytes=50 * 2**20
        ),
        name="teacher",
    )(owner, local, stat, lengths, blocks, rows, words, places, teacher, table, own_flat)


def plan(n, flat_len):
    chips = n // 2
    plane = 2 ** ((chips.bit_length() - 1) // 2)
    flat_seg = flat_len // n
    flat_pad = round_up(flat_seg, 16)
    place_seg = 2 * LEN // n
    return plane, chips // plane, flat_seg, flat_pad, place_seg, flat_pad + round_up(place_seg, 16)


def place_tile(n):
    return max(8, 2 * LEN // n)


def exchange_kernel(n, flat_len, sparse, *refs):
    plane, planes, flat_seg, flat_pad, place_seg, seg = plan(n, flat_len)
    chips = n // 2
    cap = room(n)
    tile = place_tile(n)
    flat_ref, loss_ref = refs[:2]
    refs = refs[2:]
    if sparse:
        packed_ref, list_ref = refs[:2]
        refs = refs[2:]
    else:
        given_ref = refs[0]
        refs = refs[1:]
    table_ref, sums_ref, stat_out = refs[:3]
    (stage, one_in, two_out, two_in, total, three_out, three_in, place_in, stat_in) = refs[3:12]
    refs = refs[12:]
    if sparse:
        rows_in = refs[0]
        refs = refs[1:]
    one_sem, two_sem, three_sem, place_sem, stat_sem, row_sem = refs
    me = lax.axis_index("dp")
    core = lax.rem(me, 2)
    chip = me // 2
    mid = lax.rem(chip, plane)
    high = chip // plane
    vrows = table_ref.shape[0]

    greet_all(me, n)
    pad = jnp.zeros((16, LANES), f32)
    for o in range(n):
        spot = stage.at[o % 2, o // 2]
        if flat_pad > flat_seg:
            spot[flat_pad - 16 : flat_pad, :] = pad
        if seg > flat_pad + place_seg:
            spot[seg - 16 : seg, :] = pad
        spot[0:flat_seg, :] = flat_ref[o * flat_seg : (o + 1) * flat_seg, :]
        at = flat_len + o * place_seg
        spot[flat_pad : flat_pad + place_seg, :] = flat_ref[at : at + place_seg, :]
    first = copy_to(stage.at[1 - core], one_in, one_sem.at[0], one_sem.at[1], me ^ 1)
    first.start()

    if sparse:

        def bucket(ref, i):
            return ref.at[pl.ds(pl.multiple_of(i * cap, cap), filled(n)), :]

        def row_copy(k):
            return copy_to(
                bucket(packed_ref, me ^ k), bucket(rows_in, me), row_sem.at[0, k], row_sem.at[1, k], me ^ k
            )

        def start_row(i, carry):
            row_copy(n - i).start()
            return carry

        def start_rows(low, top):
            lax.fori_loop(low, top, start_row, 0)

        cuts = [1 + (n - 1) * part // 31 for part in ROW_CUTS] + [n]
        start_rows(1, cuts[0])
        own = pl.ds(pl.multiple_of(me * cap, cap), cap)
        rows_in[own, :] = packed_ref[own, :]

        def unused(i, carry):
            at = pl.multiple_of(i * cap + filled(n), 16)
            rows_in[pl.ds(at, cap - filled(n)), :] = jnp.zeros((cap - filled(n), D), bf16)
            return carry

        lax.fori_loop(0, n, unused, 0)

    first.wait()
    for m in range(plane):
        for h in range(planes):
            c = h * plane + m
            two_out[m, h] = (stage[core, c] + one_in[c]).astype(bf16)
    second = []
    for k in range(1, plane):
        m = lax.rem(mid + k, plane)
        second.append(
            copy_to(
                two_out.at[m],
                two_in.at[k - 1],
                two_sem.at[0, k],
                two_sem.at[1, k],
                (high * plane + m) * 2 + core,
            )
        )
        second[-1].start()
    if sparse:
        start_rows(cuts[0], cuts[1])
    for copy in second:
        copy.wait()
    for h in range(planes):
        c = h * plane + mid
        value = stage[core, c] + one_in[c]
        for k in range(1, plane):
            value = value + two_in[k - 1, h].astype(f32)
        total[h] = value
        three_out[h] = value.astype(bf16)
    third = []
    for k in range(1, planes):
        h = lax.rem(high + k, planes)
        third.append(
            copy_to(
                three_out.at[h],
                three_in.at[k - 1],
                three_sem.at[0, k],
                three_sem.at[1, k],
                (h * plane + mid) * 2 + core,
            )
        )
        third[-1].start()
    if sparse:
        start_rows(cuts[1], cuts[2])
    for copy in third:
        copy.wait()
    value = total[high]
    for k in range(1, planes):
        value = value + three_in[k - 1].astype(f32)
    total[0] = value
    sums_ref[...] = value[:flat_pad]

    owners = range(VOCAB // vrows, (VOCAB + LEN - 1) // vrows + 1)
    place_out = total.at[0, pl.ds(flat_pad, tile), :]
    place_spot = pl.ds(pl.multiple_of(me * tile, 8), tile)
    for i, o in enumerate(owners):
        place_copy = copy_to(
            place_out, place_in.at[place_spot, :], place_sem.at[0, i], place_sem.at[1, me], o
        )
        pl.when(me != o)(place_copy.start)

    squares = jnp.sum(jnp.sum(value * value, axis=0, keepdims=True), axis=1, keepdims=True)
    if sparse:
        def add_pair(i, carry):
            pl.when(i > 0)(lambda: row_copy(2 * i).wait_recv())
            row_copy(2 * i + 1).wait_recv()
            a = chip ^ i
            lists = pair_lists(list_ref, a, cap)
            pick = (lax.broadcasted_iota(jnp.int32, (vrows, 2 * cap), 0) == lists).astype(bf16)
            both = rows_in[pl.ds(pl.multiple_of(a * 2 * cap, 2 * cap), 2 * cap), :]
            table_ref[...] += nn(pick, both)
            return carry

        table_ref[...] = jnp.zeros(table_ref.shape, f32)
        lax.fori_loop(0, chips, add_pair, 0)
    else:
        table_ref[...] = given_ref[...]
    grads = table_ref[...]
    squares = squares + jnp.sum(
        jnp.sum(grads * grads, axis=0, keepdims=True), axis=1, keepdims=True
    )
    loss = jnp.sum(loss_ref[0:1, :], axis=1, keepdims=True)
    lane = lax.broadcasted_iota(jnp.int32, (8, LANES), 1)
    lag = jnp.where(me == 0, loss_ref[1:2, 0:1], 0.0)
    stat_out[...] = jnp.where(
        lane == 0, squares, jnp.where(lane == 1, loss, jnp.where(lane == 2, lag, 0.0))
    )

    def stat_copy(k):
        return copy_to(
            stat_out, stat_in.at[me], stat_sem.at[0, k], stat_sem.at[1, k], me ^ k
        )

    def start_stat(k, carry):
        stat_copy(k).start()
        return carry

    def finish_stat(k, carry):
        stat_copy(k).wait()
        return carry

    lax.fori_loop(1, n, start_stat, 0)
    stat_in[me] = stat_out[...]

    for i, o in enumerate(owners):

        @pl.when(me == o)
        def _():
            place_in[place_spot, :] = place_out[...]

            def wait_place(j, carry):
                copy_to(
                    place_out,
                    place_in.at[pl.ds(pl.multiple_of(j * tile, 8), tile), :],
                    place_sem.at[0, i],
                    place_sem.at[1, j],
                    me ^ 1,
                ).wait_recv()
                return carry

            lax.fori_loop(0, o, wait_place, 0)
            lax.fori_loop(o + 1, n, wait_place, 0)
            low = max(0, o * vrows - VOCAB)
            top = min(LEN, (o + 1) * vrows - VOCAB)
            at = VOCAB + low - o * vrows
            if tile > place_seg:
                for d in range(n):
                    place_in[d * place_seg : (d + 1) * place_seg, :] = place_in[
                        d * tile : d * tile + place_seg, :
                    ]
            for j in range(2):
                table_ref[at : at + top - low, j * LANES : (j + 1) * LANES] += place_in[
                    pl.ds(2 * low + j, top - low, stride=2), :
                ]

    lax.fori_loop(1, n, finish_stat, 0)
    sums = jnp.sum(stat_in[...], axis=0)
    norm = jnp.sqrt(sums[0:1, 0:1])
    clip = jnp.minimum(1.0, clip_norm / (norm + 1e-06))
    stat_out[...] = jnp.where(lane == 0, norm, sums)
    table_ref[...] = table_ref[...] * clip
    sums_ref[...] = sums_ref[...] * clip
    for i, o in enumerate(owners):
        place_copy = copy_to(
            place_out, place_in.at[place_spot, :], place_sem.at[0, i], place_sem.at[1, me], o
        )
        pl.when(me != o)(place_copy.wait_send)
    if sparse:

        def finish_row(k, carry):
            row_copy(k).wait_send()
            return carry

        lax.fori_loop(1, n, finish_row, 0)


def run_exchange(n, vrows, flat_grads, loss_rows, sparse, given):
    flat_len = flat_grads.shape[0] - 2 * LEN
    plane, planes, flat_seg, flat_pad, place_seg, seg = plan(n, flat_len)
    count = len(range(VOCAB // vrows, (VOCAB + LEN - 1) // vrows + 1))
    dma = pltpu.SemaphoreType.DMA
    return pl.pallas_call(
        functools.partial(exchange_kernel, n, flat_len, sparse),
        out_shape=(
            jax.ShapeDtypeStruct((vrows, D), f32),
            jax.ShapeDtypeStruct((flat_pad, LANES), f32),
            jax.ShapeDtypeStruct((8, LANES), f32),
        ),
        in_specs=[whole_spec()] * (2 + len(given)),
        out_specs=(whole_spec(),) * 3,
        scratch_shapes=[
            pltpu.VMEM((2, n // 2, seg, LANES), f32),
            pltpu.VMEM((n // 2, seg, LANES), f32),
            pltpu.VMEM((plane, planes, seg, LANES), bf16),
            pltpu.VMEM((plane - 1, planes, seg, LANES), bf16),
            pltpu.VMEM((planes, seg, LANES), f32),
            pltpu.VMEM((planes, seg, LANES), bf16),
            pltpu.VMEM((planes - 1, seg, LANES), bf16),
            pltpu.VMEM((n * place_tile(n), LANES), f32),
            pltpu.VMEM((n, 8, LANES), f32),
        ]
        + ([pltpu.VMEM((n * room(n), D), bf16)] if sparse else [])
        + [dma((2,)), dma((2, plane)), dma((2, planes)), dma((2, max(n, count))), dma((2, n)), dma((2, n))],
        compiler_params=pltpu.CompilerParams(
            collective_id=2 if sparse else 3, has_side_effects=True, vmem_limit_bytes=24 * 2**20
        ),
        name="exchange" if sparse else "exchange_dense",
    )(flat_grads, loss_rows, *given)


def adam_step(weight, first_old, second, clipped):
    first_new = beta_one * first_old + (1.0 - beta_one) * clipped
    second_new = beta_two * second + (1.0 - beta_two) * clipped * clipped
    first_hat = first_new / (1.0 - beta_one**ADAM_STEP)
    second_hat = second_new / (1.0 - beta_two**ADAM_STEP)
    weight_new = weight - learn_rate * (
        first_hat / (jnp.sqrt(second_hat) + adam_eps) + decay_rate * weight
    )
    return (weight_new, first_new, second_new)


def rows_of(table, ids):
    return table.at[ids.reshape(-1)].get(mode="promise_in_bounds")


def ring_gather(devices, block):
    me = lax.axis_index("dp")
    rows = block.shape[0]
    onward = [(i, (i + 1) % devices) for i in range(devices)]

    def step(i, state):
        block, whole = state
        whole = lax.dynamic_update_slice(whole, block, (lax.rem(me - i + devices, devices) * rows, 0))
        return lax.ppermute(block, "dp", onward), whole

    whole = jnp.zeros((devices * rows, block.shape[1]), block.dtype)
    return lax.fori_loop(0, devices, step, (block, whole))[1]


def ring_scatter(devices, whole):
    me = lax.axis_index("dp")
    rows = whole.shape[0] // devices
    onward = [(i, (i + 1) % devices) for i in range(devices)]

    def part(i):
        at = lax.rem(me - 1 - i + 2 * devices, devices) * rows
        return lax.dynamic_slice(whole, (at, 0), (rows, whole.shape[1]))

    def step(i, total):
        return lax.ppermute(total, "dp", onward) + part(i)

    return lax.fori_loop(1, devices, step, part(0))


def per_device(
    devices,
    token_ids,
    lengths,
    gate_noise,
    lagrange,
    teacher_table,
    teacher_flat,
    word_table,
    table_first,
    table_second,
    layer_flat,
    flat_first,
    flat_second,
):
    seqs = token_ids.shape[0]
    half = seqs // 2
    vrows = word_table.shape[0]
    own = layer_flat.shape[0]
    flat_len = own * devices // LANES

    before = jnp.arange(seqs)[None, :] < jnp.arange(seqs)[:, None]
    longer = (lengths[None, :] > lengths[:, None]) | (
        (lengths[None, :] == lengths[:, None]) & before
    )
    rank = jnp.sum(longer.astype(jnp.int32), axis=1)
    kept = [r for r in range(seqs) if r % 4 in (0, 3)]
    order = jnp.array(kept + [r for r in range(seqs) if r not in kept], jnp.int32)
    chosen = (rank[None, :] == order[:, None]).astype(jnp.int32)
    token_ids = jnp.sum(chosen[:, :, None] * token_ids[None], axis=1)
    lengths = jnp.sum(chosen * lengths[None], axis=1)

    mates = [(i, devices - 1 - i) for i in range(devices)]
    sent = jnp.concatenate(
        [token_ids[half:], jnp.pad(lengths[half:], (0, LEN - half)).reshape(1, LEN)]
    )
    got = lax.ppermute(sent, "dp", mates)
    ids = jnp.concatenate([token_ids[:half], got[:half]])
    lens = jnp.concatenate([lengths[:half], got[half, :half]])

    owner = ids // vrows
    valid = jnp.arange(LEN)[None, :] < lens[:, None]
    target, listed, flat_all, place_all, *routed = run_fetch(
        devices,
        flat_len,
        jnp.where(valid, owner, -1),
        (ids - owner * vrows + 1).astype(f32),
        jnp.sum(lens).reshape(1),
        lens,
        ids // 16,
        ids % 16,
        teacher_table,
        teacher_table[VOCAB : VOCAB + LEN],
        teacher_flat.reshape(-1, LANES),
        word_table,
        layer_flat.reshape(-1, LANES),
    )
    stats = listed.reshape(devices, 8, LANES)[:, 1, :2]
    global_count = jnp.sum(stats[:, 0]).astype(f32)
    lag_weight = jnp.where(lax.axis_index("dp") == 0, 1.0, 0.0).astype(f32)
    factors = jnp.stack([(2.0 / D) / global_count, lag_weight])
    noise = jnp.pad(gate_noise, (0, 16 * LANES - gate_noise.shape[0]), constant_values=0.5)
    places = [place_all[i, : part[3]] for i, part in enumerate(place_parts(vrows))]
    shared = (
        lens,
        factors,
        lagrange,
        noise.reshape(16, LANES),
        flat_all,
        jnp.concatenate(places) if len(places) > 1 else places[0],
        target,
    )

    def from_slots():
        slots, fetched = routed
        flat_grads, _, loss_rows, packed = run_student(
            devices, flat_len, True, *shared, (slots, fetched)
        )
        result = run_exchange(devices, vrows, flat_grads, loss_rows, True, (packed, listed))
        return result

    def from_rows(mark):
        if routed:
            words, _ = lax.optimization_barrier((word_table, mark))
            table = ring_gather(devices, words.astype(bf16))
        else:
            table = lax.all_gather(word_table.astype(bf16), "dp", axis=0, tiled=True)
        flat_grads, grad_rows, loss_rows = run_student(
            devices, flat_len, False, *shared, (rows_of(table, ids),)
        )
        updates = jnp.transpose(grad_rows, (0, 2, 1)).reshape(seqs * LEN, D).astype(f32)
        table = jnp.zeros((devices * vrows, D), f32).at[ids.reshape(-1)].add(updates)
        if routed:
            table = ring_scatter(devices, table)
        else:
            table = lax.psum_scatter(table, "dp", scatter_dimension=0, tiled=True)
        result = run_exchange(devices, vrows, flat_grads, loss_rows, False, (table,))
        return result

    if routed:
        crowded = jnp.max(stats[:, 1])
        _, table_grad, sums, totals = lax.while_loop(
            lambda state: state[0] > 0,
            lambda state: (jnp.zeros_like(state[0]), *from_rows(state[0])),
            (crowded, *from_slots()),
        )
    else:
        table_grad, sums, totals = from_rows(0)
    flat_grad = sums[: own // LANES].reshape(-1)
    grad_norm = totals[0, 0]
    total_loss = totals[0, 1] / global_count + totals[0, 2]
    table_new = adam_step(word_table, table_first, table_second, table_grad)
    flat_new = adam_step(layer_flat, flat_first, flat_second, flat_grad)
    return (*table_new, *flat_new, total_loss, grad_norm)


def solution(mesh):
    row, flat, copied = P("dp", None), P("dp"), P()
    in_specs = (row, flat, copied, copied, copied, copied, row, row, row, flat, flat, flat)
    out_specs = (row, row, row, flat, flat, flat, copied, copied)
    return jax.shard_map(
        functools.partial(per_device, mesh.shape["dp"]),
        mesh=mesh,
        in_specs=in_specs,
        out_specs=out_specs,
        check_vma=False,
    )
```
